32 devices in a mesh: dp: 8 (over z, x), tensor: 4 (over y, core).
Axes of the slice: x: 2, y: 2, z: 4, core: 2. Of those that a mesh axis runs over, the one named last changes fastest.
Arguments:
- tokens: bfloat16 [32, 640, 1024], P('dp', 'tensor'), may hold values from -6 to 6
- token_mask: int32 [32, 640], P('dp'), may hold values from 0 to 1, as said below
- out_grad: bfloat16 [32, 640, 1024], P('dp', 'tensor'), may hold values from -6 to 6
- ln1_gain: float32 [1024], replicated, may hold values from 0.5 to 1.5
- ln1_bias: float32 [1024], replicated, may hold values from -1.75 to 1.75
- w_qkv: bfloat16 [1024, 3, 1024], P('dp', None, 'tensor'), may hold values from -0.1875 to 0.1875
- b_qv: float32 [2, 1024], P(None, 'tensor'), may hold values from -1.75 to 1.75
- w_out: bfloat16 [1024, 1024], P('tensor', 'dp'), may hold values from -0.5 to 0.5
- b_out: float32 [1024], replicated, may hold values from -1.75 to 1.75
- ln2_gain: float32 [1024], replicated, may hold values from 0.5 to 1.5
- ln2_bias: float32 [1024], replicated, may hold values from -1.75 to 1.75
- w_fc1: bfloat16 [1024, 4096], P('dp', 'tensor'), may hold values from -0.1875 to 0.1875
- b_fc1: float32 [4096], P('tensor'), may hold values from -3 to 3
- w_fc2: bfloat16 [4096, 1024], P('tensor', 'dp'), may hold values from -0.09375 to 0.09375
- b_fc2: float32 [1024], replicated, may hold values from -1.75 to 1.75
Outputs:
- layer_out: bfloat16 [32, 640, 1024], P('dp', 'tensor')
- grad_tokens: bfloat16 [32, 640, 1024], P('dp', 'tensor')
- grad_ln1_gain: float32 [1024], replicated
- grad_ln1_bias: float32 [1024], replicated
- grad_w_qkv: float32 [1024, 3, 1024], P('dp', None, 'tensor')
- grad_b_qv: float32 [2, 1024], P(None, 'tensor')
- grad_w_out: float32 [1024, 1024], P('tensor', 'dp')
- grad_b_out: float32 [1024], replicated
- grad_ln2_gain: float32 [1024], replicated
- grad_ln2_bias: float32 [1024], replicated
- grad_w_fc1: float32 [1024, 4096], P('dp', 'tensor')
- grad_b_fc1: float32 [4096], P('tensor')
- grad_w_fc2: float32 [4096, 1024], P('tensor', 'dp')
- grad_b_fc2: float32 [1024], replicated
- stream_rms: float32 [3], replicated
The draws below stay inside these ranges and needn't reach their ends.
Inputs may be any that keep to these rules, and one draw needn't show every extreme that they name: `token_mask`: each row is all zeros, or ones on its first 577 positions and zeros after; at least one row is not all zeros.
All inputs are finite; a program needn't handle non-finite values.
Results may differ from the reference program's by a relative error of at most 0.017.
Values may be sent and summed in bfloat16 or wider, within the bound.
A program may use at most 192 MiB of HBM per device.

```python
import jax
import jax.numpy as jnp
from jax import lax

D = 1024
FF = 4096
HD = 64
HEADS = 16
LEN = 577
SEQ = 640
IMAGES = 32


def draw_token_mask(key, part):
    key = jax.random.fold_in(key, 7)
    key_first, key_second = jax.random.split(key)
    filled = jax.random.randint(key_first, (IMAGES,), 0, 5) > 0
    chosen = jax.random.randint(key_second, (), 0, IMAGES)
    filled = jnp.logical_or(filled, jnp.arange(IMAGES) == chosen)
    places = jnp.arange(SEQ) < LEN
    return jnp.logical_and(filled[:, None], places[None, :]).astype(jnp.int32)


def level_of(own_key, extent, cuts, smallest, top_value):
    loudness, own = 1.0, jax.random.fold_in(own_key, 6)
    for axis_at, blocks in cuts:
        steps = jnp.exp(jax.random.uniform(jax.random.fold_in(own, axis_at), (blocks,), jnp.float32, smallest / len(cuts), top_value / len(cuts)))
        loudness = loudness * jnp.repeat(steps, extent[axis_at] // blocks).reshape([-1 if axis == axis_at else 1 for axis in range(len(extent))])
    return loudness


def scatter_about(own_key, extent, spread, limit, cuts=(), held_as=jnp.bfloat16):
    gain = level_of(own_key, extent, cuts, -0.22, 0.18) if cuts else 1.0
    entries = jax.random.normal(own_key, extent, jnp.float32) * spread * gain
    return jnp.minimum(jnp.maximum(entries, -limit), limit).astype(held_as)


def setup_inputs(seed: int = 0) -> dict:
    key_of = jax.random.split(jax.random.key(seed), 16)
    tokens = scatter_about(key_of[0], (IMAGES, SEQ, D), 1.0, 6.0, ((0, 8), (1, 4)))
    token_mask = draw_token_mask(jax.random.fold_in(key_of[15], 71), 0)
    out_grad = scatter_about(key_of[2], (IMAGES, SEQ, D), 1.0, 6.0, ((0, 8), (1, 4)))
    ln1_gain = jnp.clip(1.0 + 0.1 * jax.random.normal(key_of[3], (D,), jnp.float32), 0.5, 1.5)
    ln1_bias = scatter_about(key_of[4], (D,), 0.3, 1.75, (), jnp.float32)
    w_qkv = scatter_about(key_of[5], (D, 3, D), D ** -0.5, 0.1875, ((0, 8), (2, 4)))
    b_qv = scatter_about(key_of[6], (2, D), 0.3, 1.75, ((1, 4),), jnp.float32)
    w_out = scatter_about(key_of[7], (D, D), (D // 8) ** -0.5, 0.5, ((0, 4), (1, 8)))
    b_out = scatter_about(key_of[8], (D,), 0.3, 1.75, (), jnp.float32)
    ln2_gain = jnp.clip(1.0 + 0.1 * jax.random.normal(key_of[9], (D,), jnp.float32), 0.5, 1.5)
    ln2_bias = scatter_about(key_of[10], (D,), 0.3, 1.75, (), jnp.float32)
    w_fc1 = scatter_about(key_of[11], (D, FF), D ** -0.5, 0.1875, ((0, 8), (1, 4)))
    b_fc1 = scatter_about(key_of[12], (FF,), 0.5, 3.0, ((0, 4),), jnp.float32)
    w_fc2 = scatter_about(key_of[13], (FF, D), FF ** -0.5, 0.09375, ((0, 4), (1, 8)))
    b_fc2 = scatter_about(key_of[14], (D,), 0.3, 1.75, (), jnp.float32)
    return dict(tokens=tokens, token_mask=token_mask, out_grad=out_grad, ln1_gain=ln1_gain, ln1_bias=ln1_bias, w_qkv=w_qkv, b_qv=b_qv, w_out=w_out, b_out=b_out, ln2_gain=ln2_gain, ln2_bias=ln2_bias, w_fc1=w_fc1, b_fc1=b_fc1, w_fc2=w_fc2, b_fc2=b_fc2)


@jax.custom_vjp
def low(v):
    return lax.optimization_barrier(v.astype(jnp.bfloat16)).astype(jnp.float32)

@jax.custom_vjp
def low_back(v):
    return v

def low_keep(v):
    return (low(v), None)

def low_pass(kept, grad):
    return (grad,)

def back_keep(v):
    return (v, None)

def back_low(kept, grad):
    return (low(grad),)
low.defvjp(low_keep, low_pass)
low_back.defvjp(back_keep, back_low)
highest = lax.Precision.HIGHEST
epsilon = 1e-05

def layer_norm(values, gain_vec, bias_vec):
    row_mean = lax.optimization_barrier(jnp.mean(values, axis=-1, keepdims=True))
    centred = values - row_mean
    variance = lax.optimization_barrier(jnp.mean(centred * centred, axis=-1, keepdims=True))
    return centred * lax.rsqrt(variance + epsilon) * gain_vec + bias_vec

def image_layer(stream, mask_row, params):
    ln1_gain, ln1_bias, w_qkv, b_qv, w_out, b_out, ln2_gain, ln2_bias, w_fc1, b_fc1, w_fc2, b_fc2 = params
    is_valid = mask_row > 0
    key_allowed = jnp.logical_or(is_valid, jnp.max(mask_row) == 0)
    normed1 = low(layer_norm(stream, ln1_gain, ln1_bias))
    projected = jnp.dot(normed1, w_qkv.reshape(D, 3 * D), precision=highest).reshape(SEQ, 3, D)
    query = low(low_back(projected[:, 0] + b_qv[0])).reshape(SEQ, HEADS, HD)
    key_rows = low(low_back(projected[:, 1])).reshape(SEQ, HEADS, HD)
    values = low(low_back(projected[:, 2] + b_qv[1])).reshape(SEQ, HEADS, HD)
    raw_scores = low_back(jnp.einsum('qhd,khd->hqk', query, key_rows, precision=highest))
    scores = jnp.where(key_allowed[None, None, :], raw_scores * HD ** (-0.5), -1e+30)
    row_top = lax.optimization_barrier(jnp.max(scores, axis=-1, keepdims=True))
    expo = jnp.exp(scores - row_top)
    probs = low(expo / lax.optimization_barrier(jnp.sum(expo, axis=-1, keepdims=True)))
    attended = jnp.einsum('hqk,khd->qhd', probs, values, precision=highest).reshape(SEQ, D)
    attended = low(low_back(attended))
    branch_attn = low_back(jnp.dot(attended, w_out, precision=highest) + b_out)
    middle = stream + branch_attn
    normed2 = low(layer_norm(middle, ln2_gain, ln2_bias))
    hidden = low_back(jnp.dot(normed2, w_fc1, precision=highest) + b_fc1)
    activated = low(hidden * jax.nn.sigmoid(1.702 * hidden))
    branch_mlp = low_back(jnp.dot(activated, w_fc2, precision=highest) + b_fc2)
    result = middle + branch_mlp
    weight_rows = is_valid.astype(jnp.float32)[:, None]
    squares = jnp.stack([jnp.sum(stream * stream * weight_rows), jnp.sum(branch_attn * branch_attn * weight_rows), jnp.sum(branch_mlp * branch_mlp * weight_rows)])
    return (result, squares)

def reference(tokens, token_mask, out_grad, ln1_gain, ln1_bias, w_qkv, b_qv, w_out, b_out, ln2_gain, ln2_bias, w_fc1, b_fc1, w_fc2, b_fc2):
    params = (ln1_gain.astype(jnp.float32), ln1_bias.astype(jnp.float32), w_qkv.astype(jnp.float32), b_qv.astype(jnp.float32), w_out.astype(jnp.float32), b_out.astype(jnp.float32), ln2_gain.astype(jnp.float32), ln2_bias.astype(jnp.float32), w_fc1.astype(jnp.float32), b_fc1.astype(jnp.float32), w_fc2.astype(jnp.float32), b_fc2.astype(jnp.float32))
    stream_in = tokens.astype(jnp.float32)
    image_fn = jax.checkpoint(image_layer)

    def forward(stream_all, weights):

        def step_fn(carry, item_tuple):
            image_rows, mask_row = item_tuple
            result, squares = image_fn(image_rows, mask_row, weights)
            return (carry + squares, result)
        totals, results = lax.scan(step_fn, jnp.zeros((3,), jnp.float32), (stream_all, token_mask))
        return (results, totals)
    results, pullback, totals = jax.vjp(forward, stream_in, params, has_aux=True)
    mask_float = token_mask.astype(jnp.float32)
    cotangent = out_grad.astype(jnp.float32) * mask_float[:, :, None]
    grad_stream, grads = pullback(cotangent)
    valid_count = jnp.sum(mask_float)
    stream_rms = jnp.sqrt(totals / (valid_count * D))
    return (results.astype(jnp.bfloat16), grad_stream.astype(jnp.bfloat16), grads[0], grads[1], grads[2], grads[3], grads[4], grads[5], grads[6], grads[7], grads[8], grads[9], grads[10], grads[11], stream_rms)
```

```python
import functools

import jax
import jax.numpy as jnp
from jax import lax
from jax.experimental import pallas as pl
from jax.experimental.pallas import tpu as pltpu
from jax.sharding import PartitionSpec as P

HD = 64
MESH = pl.DeviceIdType.MESH
BF = jnp.bfloat16
F32 = jnp.float32


class Place:
    def __init__(self, line):
        self.line = line
        d = lax.axis_index("dp")
        self.t = lax.axis_index("tensor")
        self.a = d // 2
        self.b = lax.rem(d, 2)
        self.d = d
        self.y = self.t // 2
        self.c = lax.rem(self.t, 2)

    def at(self, a, b, t):
        return (a * 2 + b, t)

    def pair(self):
        return self.at(self.a, 1 - self.b, self.t)

    def peer(self, k):
        return (self.d, self.other(k))

    def other(self, k):
        y = self.y if k < 2 else 1 - self.y
        c = self.c if k % 2 == 0 else 1 - self.c
        return y * 2 + c


def greet(place, whole_line=False):
    barrier = pltpu.get_barrier_semaphore()

    def hail(device):
        pl.semaphore_signal(barrier, inc=1, device_id=device, device_id_type=MESH)

    a, line = place.a, place.line
    hail(place.pair())
    for k in range(1, 4):
        hail(place.peer(k))
    if whole_line:
        for k in range(1, line):
            hail(place.at(lax.rem(a + k, line), place.b, place.t))
        pl.semaphore_wait(barrier, 3 + line)
        return
    pl.when(a > 0)(lambda: hail(place.at(a - 1, place.b, place.t)))
    pl.when(a < line - 1)(lambda: hail(place.at(a + 1, place.b, place.t)))
    inner = jnp.logical_and(a > 0, a < line - 1)
    pl.when(inner)(lambda: pl.semaphore_wait(barrier, 6))
    pl.when(jnp.logical_not(inner))(lambda: pl.semaphore_wait(barrier, 5))


class Sends:
    def __init__(self, ssem, rsem):
        self.ssem, self.rsem = ssem, rsem
        self.open = []

    def copy(self, src, dst, slot, device):
        return pltpu.make_async_remote_copy(
            src_ref=src,
            dst_ref=dst,
            send_sem=self.ssem.at[slot],
            recv_sem=self.rsem.at[slot],
            device_id=device,
            device_id_type=MESH,
        )

    def start(self, pred, make):
        if pred is None:
            make().start()
        else:
            pl.when(pred)(lambda: make().start())
        self.open.append((pred, make))

    def finish(self):
        for pred, make in self.open:
            if pred is None:
                make().wait_send()
            else:
                pl.when(pred)(lambda make=make: make().wait_send())
        self.open = []

    def landed(self, ref, slot, device):
        self.copy(ref, ref, slot, device).wait_recv()


def both(p, q):
    if p is None:
        return q
    if q is None:
        return p
    return jnp.logical_and(p, q)


class Gather:
    def __init__(self, place, sends, local_sem, shard, whole, base, cut):
        self.p, self.s = place, sends
        self.shard, self.whole = shard, whole
        self.n = shard.shape[1]
        self.base, self.cut = base, cut
        self.local = pltpu.make_async_copy(shard, self.block(place.a, place.b, place.t), local_sem)

    def block(self, a, b, t, lo=0, hi=None):
        hi = self.n if hi is None else hi
        start = pl.multiple_of(t * self.n + lo, 128)
        return self.whole.at[a, b, :, pl.ds(start, hi - lo)]

    def plane(self, b, t):
        start = pl.multiple_of(t * self.n, 128)
        return self.whole.at[:, b, :, pl.ds(start, self.n)]

    def slot(self, kind, i):
        line = self.p.line
        return self.base + kind * line + i

    def spread(self, pred, a, src):
        p, s = self.p, self.s
        s.start(pred, lambda: s.copy(src(), self.block(a, p.b, p.t), self.slot(2, a), p.pair()))
        s.start(pred, lambda: s.copy(src(), self.block(a, p.b, p.t), self.slot(3, a), p.peer(2)))

    def pass_line(self, pred, a, step, up, src):
        p, s = self.p, self.s
        if step > p.line - 1:
            return
        if up:
            ok = both(pred, p.a < p.line - 1)
            s.start(ok, lambda: s.copy(src(), self.block(a, p.b, p.t), self.slot(0, step), p.at(p.a + 1, p.b, p.t)))
        else:
            ok = both(pred, p.a > 0)
            s.start(ok, lambda: s.copy(src(), self.block(a, p.b, p.t), self.slot(1, step), p.at(p.a - 1, p.b, p.t)))

    def begin(self):
        p = self.p
        self.local.start()
        own = lambda: self.shard
        self.pass_line(None, p.a, 1, True, own)
        self.pass_line(None, p.a, 1, False, own)
        self.spread(None, p.a, own)

    def step(self, k):
        p, s = self.p, self.s
        for up in (True, False):
            chunk = p.a - k if up else p.a + k
            pred = p.a >= k if up else p.a + k <= p.line - 1
            pl.when(pred)(
                lambda up=up, chunk=chunk: s.landed(
                    self.block(chunk, p.b, p.t), self.slot(0 if up else 1, k), p.pair()
                )
            )
            src = lambda chunk=chunk: self.block(chunk, p.b, p.t)
            self.pass_line(pred, chunk, k + 1, up, src)
            self.spread(pred, chunk, src)

    def order(self):
        p = self.p
        yield None, p.a
        for k in range(1, p.line):
            yield p.a >= k, p.a - k
            yield p.a + k <= p.line - 1, p.a + k

    def cross(self):
        p, s = self.p, self.s
        t2 = p.other(2)
        for pred, a in self.order():
            run = (lambda f: f()) if pred is None else pl.when(pred)
            run(lambda a=a: s.landed(self.block(a, 1 - p.b, p.t), self.slot(2, a), p.pair()))
            run(lambda a=a: s.landed(self.block(a, p.b, t2), self.slot(3, a), p.pair()))
            if self.cut > 0:
                s.start(pred, lambda a=a: s.copy(
                    self.block(a, 1 - p.b, p.t, 0, self.cut), self.block(a, 1 - p.b, p.t, 0, self.cut),
                    self.slot(4, a), p.peer(2)))
            if self.cut < self.n:
                s.start(pred, lambda a=a: s.copy(
                    self.block(a, p.b, t2, self.cut, self.n), self.block(a, p.b, t2, self.cut, self.n),
                    self.slot(5, a), p.pair()))

    def core(self, which):
        p, s = self.p, self.s
        for j, (b, t) in enumerate(((p.b, p.t), (1 - p.b, p.t), (p.b, p.other(2)), (1 - p.b, p.other(2)))):
            if j in which:
                s.start(None, lambda b=b, t=t, j=j: s.copy(self.plane(b, t), self.plane(b, t), self.slot(6, j), p.peer(1)))

    def diagonal(self):
        p, s = self.p, self.s
        t2 = p.other(2)
        for pred, a in self.order():
            run = (lambda f: f()) if pred is None else pl.when(pred)
            if self.cut > 0:
                run(lambda a=a: s.landed(self.block(a, 1 - p.b, t2, 0, self.cut), self.slot(4, a), p.pair()))
            if self.cut < self.n:
                run(lambda a=a: s.landed(self.block(a, 1 - p.b, t2, self.cut, self.n), self.slot(5, a), p.pair()))

    def arrive(self):
        p, s = self.p, self.s
        for j, (b, t) in enumerate(((p.b, p.other(1)), (1 - p.b, p.other(1)), (p.b, p.other(3)), (1 - p.b, p.other(3)))):
            s.landed(self.plane(b, t), self.slot(6, j), p.pair())

    def line_phase(self):
        self.begin()
        yield
        for k in range(1, self.p.line):
            self.step(k)
            yield

    def all_steps(self):
        yield from self.line_phase()
        self.cross()
        yield
        self.local.wait()
        self.core((0, 1, 2))
        yield
        self.diagonal()
        self.core((3,))
        yield
        self.arrive()
        yield


CUTS = (256, 128, 384, 384)


def slots_of(line):
    return 6 * line + 4


def gather_kernel(line, toks, grads, small, wq, wo, w1, w2, xin, gin, sml, fq, fo, f1, f2, lsem, ssem, rsem):
    place = Place(line)
    sends = Sends(ssem, rsem)
    per = slots_of(line)
    greet(place)
    mine = [
        pltpu.make_async_copy(toks.at[place.t], xin.at[0], lsem.at[4]),
        pltpu.make_async_copy(grads.at[place.t], gin.at[0], lsem.at[5]),
        pltpu.make_async_copy(small, sml.at[place.t], lsem.at[6]),
    ]
    for m in mine:
        m.start()
    exchange = 4 * per

    def trade(k, j, src, dst):
        sends.start(None, lambda: sends.copy(src, dst, exchange + j * 4 + k, place.peer(k)))

    for k in (2, 3, 1):
        trade(k, 0, toks.at[place.other(k)], xin.at[k])
        trade(k, 2, small, sml.at[place.t])
    ws = [
        Gather(place, sends, lsem.at[i], shard, whole, i * per, CUTS[i])
        for i, (shard, whole) in enumerate(((wq, fq), (wo, fo), (w1, f1), (w2, f2)))
    ]
    gens = [w.all_steps() for w in ws]
    for k in (2, 3, 1):
        trade(k, 1, grads.at[place.other(k)], gin.at[k])
    total = line + 4
    shift = 0
    for tick in range(total + shift * 3):
        for i, g in enumerate(gens):
            if 0 <= tick - shift * i < total:
                next(g)
    for k in (2, 3, 1):
        for j, ref in ((0, xin.at[k]), (1, gin.at[k]), (2, sml.at[place.other(k)])):
            sends.landed(ref, exchange + j * 4 + k, place.pair())
    for m in mine:
        m.wait()
    sends.finish()


def gather_all(line, toks, grads, small, wq, wo, w1, w2):
    images, rows, width = toks.shape
    depth = wq.shape[0]
    wholes = [jax.ShapeDtypeStruct((line, 2, depth, 4 * w.shape[1]), BF) for w in (wq, wo, w1, w2)]
    count = 4 * slots_of(line) + 12
    outs = pl.pallas_call(
        functools.partial(gather_kernel, line),
        out_shape=[
            jax.ShapeDtypeStruct((4, rows, width), BF),
            jax.ShapeDtypeStruct((4, rows, width), BF),
            jax.ShapeDtypeStruct((4,) + small.shape, F32),
            *wholes,
        ],
        in_specs=[pl.BlockSpec(memory_space=pl.ANY)] * 7,
        out_specs=[pl.BlockSpec(memory_space=pl.ANY)] * 7,
        scratch_shapes=[
            pltpu.SemaphoreType.DMA((8,)),
            pltpu.SemaphoreType.DMA((count,)),
            pltpu.SemaphoreType.DMA((count,)),
        ],
        compiler_params=pltpu.CompilerParams(collective_id=0, has_side_effects=True),
        name="gather_all",
    )(toks, grads, small, wq, wo, w1, w2)
    return outs


def add_into(dst, *others):
    rows = dst.shape[0]
    step = min(rows, 32)

    def body(i, _):
        at = pl.ds(pl.multiple_of(i * step, step), step)
        total = dst[at, :]
        for other in others:
            total = total + other[at, :]
        dst[at, :] = total
        return 0

    lax.fori_loop(0, rows // step, body, 0)


class Scatter:
    def __init__(self, place, sends, load_sem, grad, out, bufs, base, cut):
        self.p, self.s = place, sends
        self.grad, self.out = grad, out
        self.acc, self.rc, self.rdx, self.rdy, self.rx, self.ry, self.up, self.dn = bufs
        self.n = out.shape[1]
        self.base, self.cut = base, cut
        self.load_sem = load_sem
        self.loads = []

    def plane(self, b, t):
        start = pl.multiple_of(t * self.n, 128)
        return self.grad.at[:, b, :, pl.ds(start, self.n)]

    def planes(self, far):
        p = self.p
        t, t2 = (p.other(1), p.other(3)) if far else (p.t, p.other(2))
        return ((p.b, t), (1 - p.b, t), (p.b, t2), (1 - p.b, t2))

    def begin(self):
        p, s = self.p, self.s
        for j in (3, 1, 2, 0):
            b, t = self.planes(True)[j]
            s.start(None, lambda b=b, t=t, j=j: s.copy(self.plane(b, t), self.rc.at[j], self.base + j, p.peer(1)))
            b, t = self.planes(False)[j]
            load = pltpu.make_async_copy(self.plane(b, t), self.acc.at[j], self.load_sem.at[j])
            load.start()
            self.loads.append((j, load))

    def fold(self, j):
        dict(self.loads)[j].wait()
        self.s.landed(self.rc.at[j], self.base + j, self.p.pair())
        for a in range(self.p.line):
            add_into(self.acc.at[j, a], self.rc.at[j, a])

    def diagonal(self):
        p, s, cut, n = self.p, self.s, self.cut, self.n
        self.fold(3)
        s.start(None, lambda: s.copy(self.acc.at[3, :, :, pl.ds(0, cut)], self.rdy, self.base + 4, p.peer(2)))
        s.start(None, lambda: s.copy(self.acc.at[3, :, :, pl.ds(cut, n - cut)], self.rdx, self.base + 5, p.pair()))
        self.fold(1)
        late = pl.ds(cut, n - cut)
        s.start(None, lambda: s.copy(self.acc.at[1, :, :, late], self.rx.at[:, :, late], self.base + 6, p.pair()))
        self.fold(2)
        first = pl.ds(0, cut)
        s.start(None, lambda: s.copy(self.acc.at[2, :, :, first], self.ry.at[:, :, first], self.base + 7, p.peer(2)))
        self.fold(0)

    def cross(self):
        p, s, cut, n = self.p, self.s, self.cut, self.n
        first, late = pl.ds(0, cut), pl.ds(cut, n - cut)
        s.landed(self.rdy, self.base + 4, p.pair())
        for a in range(p.line):
            add_into(self.acc.at[1, a, :, first], self.rdy.at[a])
        s.start(None, lambda: s.copy(self.acc.at[1, :, :, first], self.rx.at[:, :, first], self.base + 8, p.pair()))
        s.landed(self.rdx, self.base + 5, p.pair())
        for a in range(p.line):
            add_into(self.acc.at[2, a, :, late], self.rdx.at[a])
        s.start(None, lambda: s.copy(self.acc.at[2, :, :, late], self.ry.at[:, :, late], self.base + 9, p.peer(2)))

    def meet(self):
        p, s, cut, n = self.p, self.s, self.cut, self.n
        first, late = pl.ds(0, cut), pl.ds(cut, n - cut)
        s.landed(self.rx.at[:, :, late], self.base + 6, p.pair())
        s.landed(self.ry.at[:, :, first], self.base + 7, p.pair())
        s.landed(self.rx.at[:, :, first], self.base + 8, p.pair())
        s.landed(self.ry.at[:, :, late], self.base + 9, p.pair())
        for a in range(p.line):
            add_into(self.acc.at[0, a], self.rx.at[a], self.ry.at[a])

    def along(self, j):
        p, s = self.p, self.s
        line = p.line
        for up, chunk in ((True, line - j), (False, j - 1)):
            inner = p.a > 0 if up else p.a < line - 1
            passing = p.a < chunk if up else p.a > chunk
            land = self.up if up else self.dn
            slot = self.base + 10 + (0 if up else line) + chunk
            device = p.at(p.a + 1, p.b, p.t) if up else p.at(p.a - 1, p.b, p.t)

            @pl.when(both(passing, inner))
            def _(land=land, chunk=chunk, slot=slot):
                s.landed(land.at[chunk], slot, p.pair())
                add_into(self.acc.at[0, chunk], land.at[chunk])

            s.start(passing, lambda chunk=chunk, land=land, slot=slot, device=device: s.copy(
                self.acc.at[0, chunk], land.at[chunk], slot, device))

    def close(self):
        p, s = self.p, self.s
        line = p.line
        rows = self.out.shape[0]
        step = min(rows, 16)

        def total(refs):
            def body(i, _):
                at = pl.ds(pl.multiple_of(i * step, step), step)
                value = self.acc[0, p.a, at, :].astype(F32)
                for ref in refs:
                    value = value + ref[p.a, at, :].astype(F32)
                self.out[at, :] = value
                return 0

            lax.fori_loop(0, rows // step, body, 0)

        low, high = p.a == 0, p.a == line - 1

        @pl.when(p.a > 0)
        def _():
            s.landed(self.up.at[p.a], self.base + 10 + p.a, p.pair())

        @pl.when(p.a < line - 1)
        def _():
            s.landed(self.dn.at[p.a], self.base + 10 + line + p.a, p.pair())

        pl.when(low)(lambda: total((self.dn,)))
        pl.when(high)(lambda: total((self.up,)))
        pl.when(jnp.logical_not(jnp.logical_or(low, high)))(lambda: total((self.up, self.dn)))

    def all_steps(self):
        self.begin()
        yield
        self.diagonal()
        yield
        self.cross()
        yield
        self.meet()
        yield
        for j in range(1, self.p.line):
            self.along(j)
            yield
        self.close()
        yield


RS_ORDER = (3, 2, 1, 0)


def scatter_kernel(line, *refs):
    ins, rest = refs[:7], refs[7:]
    gq, go, g1, g2, louts, gtoks, small = ins
    oq, oo, o1, o2, lo, gt, sm = rest[:7]
    scratch = rest[7:]
    bufs = [scratch[i * 8 : i * 8 + 8] for i in range(4)]
    here, cold, coly, colx, ssem, rsem, lsem = scratch[32:]
    place = Place(line)
    sends = Sends(ssem, rsem)
    greet(place, whole_line=True)
    per = 10 + 2 * line
    extra = 4 * per
    mine = [
        pltpu.make_async_copy(louts.at[0], lo.at[place.t], lsem.at[0]),
        pltpu.make_async_copy(gtoks.at[0], gt.at[place.t], lsem.at[1]),
    ]
    for m in mine:
        m.start()
    ws = [
        Scatter(place, sends, lsem.at[pl.ds(2 + 4 * i, 4)], g, o, bufs[i], i * per, CUTS[i])
        for i, (g, o) in enumerate(((gq, oq), (go, oo), (g1, o1), (g2, o2)))
    ]
    gens = [ws[i].all_steps() for i in RS_ORDER]
    total = line + 4
    for k in (2, 3, 1):
        for j, (src, dst) in enumerate(((louts, lo), (gtoks, gt))):
            sends.start(None, lambda src=src, dst=dst, k=k, j=j: sends.copy(
                src.at[k], dst.at[place.t], extra + j * 4 + k, place.peer(k)))
    base = extra + 8
    here[0] = small[...]
    hops = ((cold, place.peer(1)), (colx, place.pair()), (coly, place.peer(2)))

    def hop(i):
        land, device = hops[i]
        sends.start(None, lambda: sends.copy(here.at[i], land, base + i, device))

    def small_steps():
        for i in range(3):
            hop(i)
            yield
            land, device = hops[i]
            sends.landed(land, base + i, place.pair())
            here[i + 1] = here[i] + land[...]
        for k in range(1, line):
            far = lax.rem(place.a + k, line)
            sends.start(None, lambda far=far, k=k: sends.copy(
                here.at[3], sm.at[k], base + 3 + k, place.at(far, place.b, place.t)))
        sm[0] = here[3]
        yield
        for k in range(1, line):
            sends.landed(sm.at[k], base + 3 + k, place.pair())
        yield

    extra_gen = small_steps()
    shift = 1
    for tick in range(total + shift * 3):
        for i, g in enumerate(gens):
            if 0 <= tick - shift * i < total:
                next(g)
        if tick < 5:
            next(extra_gen)
    for k in (2, 3, 1):
        for j, dst in enumerate((lo, gt)):
            sends.landed(dst.at[place.other(k)], extra + j * 4 + k, place.pair())
    for m in mine:
        m.wait()
    sends.finish()


def scatter_all(line, grads, louts, gtoks, small):
    depth = grads[0].shape[2]
    widths = [g.shape[3] // 4 for g in grads]
    rows, lanes = small.shape
    scratch = []
    for n, cut in zip(widths, CUTS):
        scratch += [
            pltpu.VMEM((4, line, depth, n), BF),
            pltpu.VMEM((4, line, depth, n), BF),
            pltpu.VMEM((line, depth, n - cut), BF),
            pltpu.VMEM((line, depth, cut), BF),
            pltpu.VMEM((line, depth, n), BF),
            pltpu.VMEM((line, depth, n), BF),
            pltpu.VMEM((line, depth, n), BF),
            pltpu.VMEM((line, depth, n), BF),
        ]
    count = 4 * (10 + 2 * line) + 8 + 3 + line
    scratch += [
        pltpu.VMEM((4, rows, lanes), F32),
        pltpu.VMEM((rows, lanes), F32),
        pltpu.VMEM((rows, lanes), F32),
        pltpu.VMEM((rows, lanes), F32),
        pltpu.SemaphoreType.DMA((count,)),
        pltpu.SemaphoreType.DMA((count,)),
        pltpu.SemaphoreType.DMA((18,)),
    ]
    hbm, vmem = pl.BlockSpec(memory_space=pl.ANY), pl.BlockSpec(memory_space=pltpu.VMEM)
    return pl.pallas_call(
        functools.partial(scatter_kernel, line),
        out_shape=[jax.ShapeDtypeStruct((depth, n), F32) for n in widths]
        + [
            jax.ShapeDtypeStruct(louts.shape, BF),
            jax.ShapeDtypeStruct(gtoks.shape, BF),
            jax.ShapeDtypeStruct((line, rows, lanes), F32),
        ],
        in_specs=[hbm] * 6 + [vmem],
        out_specs=[vmem] * 4 + [hbm] * 2 + [vmem],
        scratch_shapes=scratch,
        compiler_params=pltpu.CompilerParams(
            collective_id=1, has_side_effects=True, vmem_limit_bytes=60 * 1024 * 1024
        ),
        name="scatter_all",
    )(*grads, louts, gtoks, small)


def heads_forward(q_ref, k_ref, v_ref, allow_ref, o_ref, p_ref):
    q, k, v = q_ref[...], k_ref[...], v_ref[...]
    lane = lax.broadcasted_iota(jnp.int32, k.shape, 1)
    allowed = allow_ref[:, :1] > 0
    outs = []
    for h in range(2):
        mine = (lane // HD) == h
        scores = lax.dot_general(
            jnp.where(mine, k, jnp.zeros_like(k)), q, (((1,), (1,)), ((), ())), preferred_element_type=F32
        )
        scores = jnp.where(allowed, scores, -1e30)
        expo = jnp.exp(scores - jnp.max(scores, axis=0, keepdims=True))
        probs = (expo * (1.0 / jnp.sum(expo, axis=0, keepdims=True))).astype(BF)
        p_ref[0, h] = probs
        outs.append(
            lax.dot_general(v[:, h * HD : (h + 1) * HD], probs, (((0,), (0,)), ((), ())), preferred_element_type=F32)
        )
    o_ref[...] = jnp.concatenate(outs, axis=0).T.astype(BF)


def heads_backward(q_ref, k_ref, v_ref, o_ref, do_ref, p_ref, out_ref):
    q, k, v, do = q_ref[...], k_ref[...], v_ref[...], do_ref[...]
    lane = lax.broadcasted_iota(jnp.int32, k.shape, 1)
    product = do.astype(F32) * o_ref[...].astype(F32)
    zero = jnp.zeros_like(k)
    dq_t, dk, dv = [], [], []
    for h in range(2):
        mine = (lane // HD) == h
        inner = jnp.sum(jnp.where(mine, product, 0.0), axis=1, keepdims=True).T
        dprobs = lax.dot_general(
            jnp.where(mine, v, zero), do, (((1,), (1,)), ((), ())), preferred_element_type=F32
        )
        probs = p_ref[0, h]
        dscores = (probs.astype(F32) * (dprobs - inner)).astype(BF)
        dv.append(jnp.dot(probs, do, preferred_element_type=F32))
        dk.append(jnp.dot(dscores, q, preferred_element_type=F32))
        dq_t.append(
            lax.dot_general(k[:, h * HD : (h + 1) * HD], dscores, (((0,), (0,)), ((), ())), preferred_element_type=F32)
        )
    first = lane < HD
    out_ref[0] = (jnp.concatenate(dq_t, axis=0).T * HD ** (-0.5)).astype(BF)
    out_ref[1] = jnp.where(first, dk[0], dk[1]).astype(BF)
    out_ref[2] = jnp.where(first, dv[0], dv[1]).astype(BF)


def attention(qkv, allow):
    rows = qkv.shape[0]
    pairs = qkv.shape[1] // 384
    block = lambda part: pl.BlockSpec((rows, 128), lambda i: (0, (i // 2) * 6 + part * 2 + i % 2))
    return pl.pallas_call(
        heads_forward,
        grid=(pairs,),
        in_specs=[block(0), block(1), block(2), pl.BlockSpec((rows, 128), lambda i: (0, 0))],
        out_specs=[
            pl.BlockSpec((rows, 128), lambda i: (0, i)),
            pl.BlockSpec((1, 2, rows, rows), lambda i: (i, 0, 0, 0)),
        ],
        out_shape=[
            jax.ShapeDtypeStruct((rows, pairs * 128), BF),
            jax.ShapeDtypeStruct((pairs, 2, rows, rows), BF),
        ],
        compiler_params=pltpu.CompilerParams(vmem_limit_bytes=48 * 1024 * 1024),
        name="heads_forward",
    )(qkv, qkv, qkv, allow)


def attention_back(qkv, o, do, probs):
    rows = qkv.shape[0]
    pairs = qkv.shape[1] // 384
    block = lambda part: pl.BlockSpec((rows, 128), lambda i: (0, (i // 2) * 6 + part * 2 + i % 2))
    own = pl.BlockSpec((rows, 128), lambda i: (0, i))
    return pl.pallas_call(
        heads_backward,
        grid=(pairs,),
        in_specs=[block(0), block(1), block(2), own, own, pl.BlockSpec((1, 2, rows, rows), lambda i: (i, 0, 0, 0))],
        out_specs=pl.BlockSpec((3, rows, 128), lambda i: (0, 0, i)),
        out_shape=jax.ShapeDtypeStruct((3, rows, pairs * 128), BF),
        compiler_params=pltpu.CompilerParams(vmem_limit_bytes=48 * 1024 * 1024),
        name="heads_backward",
    )(qkv, qkv, qkv, o, do, probs)


def norm_rows(values, gain_vec, bias_vec):
    row_mean = jnp.mean(values, axis=-1, keepdims=True)
    centred = values - row_mean
    variance = jnp.mean(centred * centred, axis=-1, keepdims=True)
    inv_std = lax.rsqrt(variance + 1e-05)
    normed = centred * inv_std
    return (normed * gain_vec + bias_vec).astype(BF), normed, inv_std


def norm_back(upstream, normed, inv_std, gain_vec):
    scaled = upstream * gain_vec
    inner_mean = jnp.mean(scaled, axis=-1, keepdims=True)
    cross_mean = jnp.mean(scaled * normed, axis=-1, keepdims=True)
    back = inv_std * (scaled - inner_mean - normed * cross_mean)
    return back, jnp.sum(upstream * normed, axis=0), jnp.sum(upstream, axis=0)


def rows_t(left, right):
    return lax.dot_general(left, right, (((0,), (0,)), ((), ())), preferred_element_type=F32)


def cols_t(left, right):
    return lax.dot_general(left, right, (((1,), (1,)), ((), ())), preferred_element_type=F32)


def shards(
    tokens, token_mask, out_grad, ln1_gain, ln1_bias, w_qkv, b_qv, w_out, b_out,
    ln2_gain, ln2_bias, w_fc1, b_fc1, w_fc2, b_fc2,
):
    images, tok_rows, width = tokens.shape
    parts = lax.axis_size("tensor")
    line = lax.axis_size("dp") // 2
    t = lax.axis_index("tensor")
    depth, _, local = w_qkv.shape
    rows = tok_rows * parts

    small = jnp.zeros((8, w_fc1.shape[1]), F32).at[0].set(b_fc1).at[1, : 2 * local].set(b_qv.reshape(-1))
    xin, gin, sml, fq, fo, f1, f2 = gather_all(
        line, tokens, out_grad, small, w_qkv.reshape(depth, 3 * local), w_out.T, w_fc1, w_fc2.T
    )
    fq, fo, f1, f2 = (f.reshape(width, -1) for f in (fq, fo, f1, f2))
    full_fc1 = sml[:, 0].reshape(-1)
    bq, bv = sml[:, 1, :local], sml[:, 1, local : 2 * local]
    full_qkv = jnp.stack([bq, jnp.zeros_like(bq), bv], axis=1).reshape(-1)
    shrink = jnp.stack([jnp.full_like(bq, HD ** (-0.5)), jnp.ones_like(bq), jnp.ones_like(bq)], axis=1).reshape(-1)

    own = lax.dynamic_index_in_dim(token_mask, t, 0, keepdims=False).reshape(parts, tok_rows)
    y, c = t // 2, lax.rem(t, 2)
    others = [t, y * 2 + 1 - c, (1 - y) * 2 + c, (1 - y) * 2 + 1 - c]
    mask = jnp.concatenate([lax.dynamic_index_in_dim(own, o, 0, keepdims=False) for o in others])
    real = mask.astype(F32)[:, None]
    allow = jnp.where(jnp.max(mask) > 0, mask, 1).astype(F32)
    allow = jnp.broadcast_to(allow[:, None], (rows, 128))

    stream = xin.reshape(rows, width).astype(F32)
    h1, unit1, inv1 = norm_rows(stream, ln1_gain, ln1_bias)
    qkv = (jnp.dot(h1, fq, preferred_element_type=F32) + full_qkv).astype(BF) * shrink.astype(BF)
    o, probs = attention(qkv, allow)
    branch = cols_t(o, fo) + b_out
    middle = stream + branch
    h2, unit2, inv2 = norm_rows(middle, ln2_gain, ln2_bias)
    hidden = jnp.dot(h2, f1, preferred_element_type=F32) + full_fc1
    gate = jax.nn.sigmoid(1.702 * hidden)
    act = (hidden * gate).astype(BF)
    slope = (gate + 1.702 * hidden * gate * (1.0 - gate)).astype(BF)
    mlp = cols_t(act, f2) + b_fc2
    layer_out = (middle + mlp).astype(BF)
    squares = jnp.stack(
        [jnp.sum(v * v * real) for v in (stream, branch, mlp)] + [jnp.sum(real)]
    )

    top = gin.reshape(rows, width) * real.astype(BF)
    top32 = top.astype(F32)
    grad_f2 = rows_t(top, act).astype(BF)
    du = (jnp.dot(top, f2, preferred_element_type=F32) * slope.astype(F32)).astype(BF)
    grad_f1 = rows_t(h2, du).astype(BF)
    dh2 = cols_t(du, f1)
    back2, g_ln2_gain, g_ln2_bias = norm_back(dh2, unit2, inv2, ln2_gain)
    g1 = top32 + back2
    g1b = g1.astype(BF)
    grad_fo = rows_t(g1b, o).astype(BF)
    do = jnp.dot(g1b, fo, preferred_element_type=F32).astype(BF)
    dqkv = attention_back(qkv, o, do, probs)
    dqkv = dqkv.reshape(3, rows, parts, local).transpose(1, 2, 0, 3).reshape(rows, -1)
    grad_fq = rows_t(h1, dqkv).astype(BF)
    dh1 = cols_t(dqkv, fq)
    back1, g_ln1_gain, g_ln1_bias = norm_back(dh1, unit1, inv1, ln1_gain)
    grad_tokens = (g1 + back1).astype(BF)

    bias_sums = jnp.sum(dqkv.astype(F32), axis=0).reshape(parts, 3, local)
    sums = jnp.stack(
        [
            g_ln1_gain,
            g_ln1_bias,
            jnp.sum(g1b.astype(F32), axis=0),
            g_ln2_gain,
            g_ln2_bias,
            jnp.sum(top32, axis=0),
            jnp.zeros((width,), F32).at[:4].set(squares),
            jnp.zeros((width,), F32),
        ]
    )
    sums = jnp.concatenate(
        [
            sums,
            jnp.sum(du.astype(F32), axis=0).reshape(parts, -1),
            bias_sums[:, 0].reshape(1, -1),
            bias_sums[:, 2].reshape(1, -1),
            jnp.zeros((2, width), F32),
        ]
    )
    blocks = lambda g: g.reshape(line, 2, depth, -1)
    sum_q, sum_o, sum_1, sum_2, lo, gt, sm = scatter_all(
        line,
        [blocks(g) for g in (grad_fq, grad_fo, grad_f1, grad_f2)],
        layer_out.reshape(parts, tok_rows, width),
        grad_tokens.reshape(parts, tok_rows, width),
        sums,
    )
    sums = jnp.sum(sm, axis=0)
    rms = jnp.sqrt(sums[6, :3] / (sums[6, 3] * width))
    pick = lambda v: lax.dynamic_slice_in_dim(v, t * local, local, 0)
    return (
        lo,
        gt,
        sums[0],
        sums[1],
        sum_q.reshape(depth, 3, local),
        jnp.stack([pick(sums[12]), pick(sums[13])]),
        sum_o.T,
        sums[2],
        sums[3],
        sums[4],
        sum_1,
        lax.dynamic_index_in_dim(sums[8:12], t, 0, keepdims=False),
        sum_2.T,
        sums[5],
        rms,
    )


def solution(mesh):
    rowwise = P("dp", "tensor", None)
    placed = (
        rowwise, P("dp", None), rowwise, P(), P(), P("dp", None, "tensor"), P(None, "tensor"), P("tensor", "dp"),
        P(), P(), P(), P("dp", "tensor"), P("tensor"), P("tensor", "dp"), P(),
    )
    return jax.shard_map(
        shards,
        mesh=mesh,
        in_specs=placed,
        out_specs=(
            rowwise, rowwise, P(), P(), P("dp", None, "tensor"), P(None, "tensor"), P("tensor", "dp"), P(),
            P(), P(), P("dp", "tensor"), P("tensor"), P("tensor", "dp"), P(), P(),
        ),
        check_vma=False,
    )
```

```python
import functools

import jax
import jax.numpy as jnp
from jax import lax
from jax.experimental import pallas as pl
from jax.experimental.pallas import tpu as pltpu
from jax.sharding import PartitionSpec as P

HD = 64
MESH = pl.DeviceIdType.MESH
BF = jnp.bfloat16
F32 = jnp.float32
ROWS = 64
TILE = 512
MIB = 1024 * 1024


class Place:
    def __init__(self, line):
        self.line = line
        self.d = lax.axis_index("dp")
        self.t = lax.axis_index("tensor")
        self.a = self.d // 2
        self.b = lax.rem(self.d, 2)
        y, c = self.t // 2, lax.rem(self.t, 2)
        self.others = (self.t, y * 2 + 1 - c, (1 - y) * 2 + c, (1 - y) * 2 + 1 - c)
        self.low, self.high = self.a > 0, self.a < line - 1
        self.inner = jnp.logical_and(self.low, self.high)

    def at(self, a, b, t):
        return (a * 2 + b, t)

    def pair(self):
        return self.at(self.a, 1 - self.b, self.t)

    def peer(self, k):
        return (self.d, self.others[k])

    def up(self):
        return self.at(self.a + 1, self.b, self.t)

    def down(self):
        return self.at(self.a - 1, self.b, self.t)


def greet(place, whole_line=False):
    barrier = pltpu.get_barrier_semaphore()

    def hail(device):
        pl.semaphore_signal(barrier, inc=1, device_id=device, device_id_type=MESH)

    line = place.line
    hail(place.pair())
    for k in range(1, 4):
        hail(place.peer(k))
    if whole_line:
        for k in range(1, line):
            hail(place.at(lax.rem(place.a + k, line), place.b, place.t))
        pl.semaphore_wait(barrier, 3 + line)
        return
    pl.when(place.low)(lambda: hail(place.down()))
    pl.when(place.high)(lambda: hail(place.up()))
    pl.when(place.inner)(lambda: pl.semaphore_wait(barrier, 6))
    pl.when(jnp.logical_not(place.inner))(lambda: pl.semaphore_wait(barrier, 5))


def both(p, q):
    if p is None:
        return q
    if q is None:
        return p
    return jnp.logical_and(p, q)


def when(pred, act):
    if pred is None:
        act()
    else:
        pl.when(pred)(act)


class Script:
    def __init__(self, ssem, rsem):
        self.ssem, self.rsem = ssem, rsem
        self.sent = []
        self.steps = []

    def copy(self, src, dst, slot, device):
        return pltpu.make_async_remote_copy(
            src_ref=src,
            dst_ref=dst,
            send_sem=self.ssem.at[slot],
            recv_sem=self.rsem.at[slot],
            device_id=device,
            device_id_type=MESH,
        )

    def step(self):
        self.steps.append([])

    def do(self, pred, act):
        self.steps[-1].append((pred, act))

    def send(self, pred, make):
        self.do(pred, lambda: make().start())
        self.sent.append((pred, make))

    def wait(self, pred, ref, slot, device):
        self.do(pred, lambda: self.copy(ref(), ref(), slot, device).wait_recv())

    def run(self, count=1):
        for _ in range(count):
            for pred, act in self.steps.pop(0):
                when(pred, act)

    def finish(self):
        assert not self.steps
        for pred, make in self.sent:
            when(pred, lambda make=make: make().wait_send())


def thirds(line):
    return [1], [2] if line > 2 else [], list(range(3, line))


def order(place):
    yield None, place.a
    for k in range(1, place.line):
        yield place.a >= k, place.a - k
        yield place.a + k <= place.line - 1, place.a + k


class Gather(Script):
    def __init__(self, place, ssem, rsem, local_sem, shard, whole, base, cut):
        super().__init__(ssem, rsem)
        self.p = place
        self.shard, self.whole = shard, whole
        self.n = shard.shape[1]
        self.base, self.cut = base, cut
        local = pltpu.make_async_copy(shard, self.block(place.a, place.b, place.t), local_sem)
        p = place
        own = lambda: self.shard

        self.step()
        self.do(None, local.start)
        self.pass_line(None, p.a, 1, True, own)
        self.pass_line(None, p.a, 1, False, own)
        self.spread(None, p.a, own)
        for group in thirds(p.line):
            self.step()
            for k in group:
                self.receive(k)
        self.step()
        self.cross()
        self.step()
        self.do(None, local.wait)
        self.core((0, 1, 2))
        self.step()
        self.diagonal()
        self.core((3,))
        self.step()
        self.arrive()

    def block(self, a, b, t, lo=0, hi=None):
        hi = self.n if hi is None else hi
        start = pl.multiple_of(t * self.n + lo, 128)
        return self.whole.at[a, b, :, pl.ds(start, hi - lo)]

    def plane(self, b, t):
        start = pl.multiple_of(t * self.n, 128)
        return self.whole.at[:, b, :, pl.ds(start, self.n)]

    def slot(self, kind, i):
        return self.base + kind * self.p.line + i

    def spread(self, pred, a, src):
        p = self.p
        self.send(pred, lambda: self.copy(src(), self.block(a, p.b, p.t), self.slot(2, a), p.pair()))
        self.send(pred, lambda: self.copy(src(), self.block(a, p.b, p.t), self.slot(3, a), p.peer(2)))

    def pass_line(self, pred, a, step, up, src):
        p = self.p
        if step > p.line - 1:
            return
        ok = both(pred, p.high if up else p.low)
        to = p.up if up else p.down
        self.send(ok, lambda: self.copy(src(), self.block(a, p.b, p.t), self.slot(0 if up else 1, step), to()))

    def receive(self, k):
        p = self.p
        for up in (True, False):
            chunk = p.a - k if up else p.a + k
            pred = p.a >= k if up else p.a + k <= p.line - 1
            src = lambda chunk=chunk: self.block(chunk, p.b, p.t)
            self.wait(pred, src, self.slot(0 if up else 1, k), p.pair())
            self.pass_line(pred, chunk, k + 1, up, src)
            self.spread(pred, chunk, src)

    def cross(self):
        p, t2 = self.p, self.p.others[2]
        for pred, a in order(p):
            self.wait(pred, lambda a=a: self.block(a, 1 - p.b, p.t), self.slot(2, a), p.pair())
            self.wait(pred, lambda a=a: self.block(a, p.b, t2), self.slot(3, a), p.pair())
            one = lambda a=a: self.block(a, 1 - p.b, p.t, 0, self.cut)
            two = lambda a=a: self.block(a, p.b, t2, self.cut, self.n)
            if self.cut > 0:
                self.send(pred, lambda a=a, one=one: self.copy(one(), one(), self.slot(4, a), p.peer(2)))
            if self.cut < self.n:
                self.send(pred, lambda a=a, two=two: self.copy(two(), two(), self.slot(5, a), p.pair()))

    def planes(self, far):
        p = self.p
        t, t2 = (p.others[1], p.others[3]) if far else (p.t, p.others[2])
        return ((p.b, t), (1 - p.b, t), (p.b, t2), (1 - p.b, t2))

    def core(self, which):
        for j in which:
            b, t = self.planes(False)[j]
            src = lambda b=b, t=t: self.plane(b, t)
            self.send(None, lambda j=j, src=src: self.copy(src(), src(), self.slot(6, j), self.p.peer(1)))

    def diagonal(self):
        p, t2 = self.p, self.p.others[2]
        for pred, a in order(p):
            if self.cut > 0:
                self.wait(pred, lambda a=a: self.block(a, 1 - p.b, t2, 0, self.cut), self.slot(4, a), p.pair())
            if self.cut < self.n:
                self.wait(pred, lambda a=a: self.block(a, 1 - p.b, t2, self.cut, self.n), self.slot(5, a), p.pair())

    def arrive(self):
        for j, (b, t) in enumerate(self.planes(True)):
            self.wait(None, lambda b=b, t=t: self.plane(b, t), self.slot(6, j), self.p.pair())


CUTS = (256, 128, 384, 384)


def slots_of(line):
    return 6 * line + 4


def add_into(dst, *others):
    rows = dst.shape[0]
    step = min(rows, 32)

    def body(i, _):
        at = pl.ds(pl.multiple_of(i * step, step), step)
        total = dst[at, :]
        for other in others:
            total = total + other[at, :]
        dst[at, :] = total
        return 0

    lax.fori_loop(0, rows // step, body, 0)


class Scatter(Script):
    def __init__(self, place, ssem, rsem, load_sem, grad, out, bufs, base, cut):
        super().__init__(ssem, rsem)
        self.p = place
        self.grad, self.out = grad, out
        self.acc, self.rc, self.rdx, self.rdy, self.rx, self.ry, self.up, self.dn = bufs
        self.n = out.shape[1]
        self.base, self.cut = base, cut
        self.load_sem = load_sem
        self.step()
        self.begin()
        self.step()
        self.diagonal()
        self.step()
        self.cross()
        self.step()
        self.meet()
        for group in thirds(place.line):
            self.step()
            for j in group:
                self.along(j)
        self.step()
        self.close()

    def plane(self, b, t):
        start = pl.multiple_of(t * self.n, 128)
        return self.grad.at[:, b, :, pl.ds(start, self.n)]

    def planes(self, far):
        p = self.p
        t, t2 = (p.others[1], p.others[3]) if far else (p.t, p.others[2])
        return ((p.b, t), (1 - p.b, t), (p.b, t2), (1 - p.b, t2))

    def load(self, j):
        b, t = self.planes(False)[j]
        return pltpu.make_async_copy(self.plane(b, t), self.acc.at[j], self.load_sem.at[j])

    def begin(self):
        p = self.p
        for j in (3, 1, 2, 0):
            b, t = self.planes(True)[j]
            self.send(None, lambda b=b, t=t, j=j: self.copy(self.plane(b, t), self.rc.at[j], self.base + j, p.peer(1)))
            self.do(None, lambda j=j: self.load(j).start())

    def fold(self, j):
        self.do(None, lambda: self.load(j).wait())
        self.wait(None, lambda: self.rc.at[j], self.base + j, self.p.pair())
        for a in range(self.p.line):
            self.do(None, lambda a=a: add_into(self.acc.at[j, a], self.rc.at[j, a]))

    def diagonal(self):
        p, cut, n = self.p, self.cut, self.n
        first, late = pl.ds(0, cut), pl.ds(cut, n - cut)
        self.fold(3)
        self.send(None, lambda: self.copy(self.acc.at[3, :, :, first], self.rdy, self.base + 4, p.peer(2)))
        self.send(None, lambda: self.copy(self.acc.at[3, :, :, late], self.rdx, self.base + 5, p.pair()))
        self.fold(1)
        self.send(None, lambda: self.copy(self.acc.at[1, :, :, late], self.rx.at[:, :, late], self.base + 6, p.pair()))
        self.fold(2)
        self.send(None, lambda: self.copy(self.acc.at[2, :, :, first], self.ry.at[:, :, first], self.base + 7, p.peer(2)))
        self.fold(0)

    def cross(self):
        p, cut, n = self.p, self.cut, self.n
        first, late = pl.ds(0, cut), pl.ds(cut, n - cut)
        self.wait(None, lambda: self.rdy, self.base + 4, p.pair())
        for a in range(p.line):
            self.do(None, lambda a=a: add_into(self.acc.at[1, a, :, first], self.rdy.at[a]))
        self.send(None, lambda: self.copy(self.acc.at[1, :, :, first], self.rx.at[:, :, first], self.base + 8, p.pair()))
        self.wait(None, lambda: self.rdx, self.base + 5, p.pair())
        for a in range(p.line):
            self.do(None, lambda a=a: add_into(self.acc.at[2, a, :, late], self.rdx.at[a]))
        self.send(None, lambda: self.copy(self.acc.at[2, :, :, late], self.ry.at[:, :, late], self.base + 9, p.peer(2)))

    def meet(self):
        p, cut, n = self.p, self.cut, self.n
        first, late = pl.ds(0, cut), pl.ds(cut, n - cut)
        self.wait(None, lambda: self.rx.at[:, :, late], self.base + 6, p.pair())
        self.wait(None, lambda: self.ry.at[:, :, first], self.base + 7, p.pair())
        self.wait(None, lambda: self.rx.at[:, :, first], self.base + 8, p.pair())
        self.wait(None, lambda: self.ry.at[:, :, late], self.base + 9, p.pair())
        for a in range(p.line):
            self.do(None, lambda a=a: add_into(self.acc.at[0, a], self.rx.at[a], self.ry.at[a]))

    def along(self, j):
        p = self.p
        line = p.line
        for up, chunk in ((True, line - j), (False, j - 1)):
            passing = p.a < chunk if up else p.a > chunk
            inner = both(passing, p.low if up else p.high)
            land = self.up if up else self.dn
            slot = self.base + 10 + (0 if up else line) + chunk
            to = p.up if up else p.down
            self.wait(inner, lambda land=land, chunk=chunk: land.at[chunk], slot, p.pair())
            self.do(inner, lambda land=land, chunk=chunk: add_into(self.acc.at[0, chunk], land.at[chunk]))
            self.send(passing, lambda chunk=chunk, land=land, slot=slot, to=to: self.copy(
                self.acc.at[0, chunk], land.at[chunk], slot, to()))

    def close(self):
        p = self.p
        line = p.line
        rows = self.out.shape[0]
        step = min(rows, 16)

        def total(refs):
            def body(i, _):
                at = pl.ds(pl.multiple_of(i * step, step), step)
                value = self.acc[0, p.a, at, :].astype(F32)
                for ref in refs:
                    value = value + ref[p.a, at, :].astype(F32)
                self.out[at, :] = value
                return 0

            lax.fori_loop(0, rows // step, body, 0)

        self.wait(p.low, lambda: self.up.at[p.a], self.base + 10 + p.a, p.pair())
        self.wait(p.high, lambda: self.dn.at[p.a], self.base + 10 + line + p.a, p.pair())
        self.do(jnp.logical_not(p.low), lambda: total((self.dn,)))
        self.do(jnp.logical_not(p.high), lambda: total((self.up,)))
        self.do(p.inner, lambda: total((self.up, self.dn)))


class Trade(Script):
    pass


def scatter_kernel(line, *refs):
    ins, rest = refs[:7], refs[7:]
    gq, go, g1, g2, louts, gtoks, small = ins
    oq, oo, o1, o2, lo, gt, sm = rest[:7]
    scratch = rest[7:]
    bufs = [scratch[i * 8 : i * 8 + 8] for i in range(4)]
    here, cold, coly, colx, ssem, rsem, lsem = scratch[32:]
    place = Place(line)
    greet(place, whole_line=True)
    per = 10 + 2 * line
    extra = 4 * per
    mine = [
        pltpu.make_async_copy(louts.at[0], lo.at[place.t], lsem.at[0]),
        pltpu.make_async_copy(gtoks.at[0], gt.at[place.t], lsem.at[1]),
    ]
    for m in mine:
        m.start()
    ws = [
        Scatter(place, ssem, rsem, lsem.at[pl.ds(2 + 4 * i, 4)], g, o, bufs[i], i * per, CUTS[i])
        for i, (g, o) in enumerate(((gq, oq), (go, oo), (g1, o1), (g2, o2)))
    ]
    trade = Trade(ssem, rsem)
    trade.step()
    for k in (2, 3, 1):
        for j, (src, dst) in enumerate(((louts, lo), (gtoks, gt))):
            trade.send(None, lambda src=src, dst=dst, k=k, j=j: trade.copy(
                src.at[k], dst.at[place.t], extra + j * 4 + k, place.peer(k)))
    base = extra + 8
    here[0] = small[...]
    hops = ((cold, place.peer(1)), (colx, place.pair()), (coly, place.peer(2)))

    def fold(i, land):
        here[i + 1] = here[i] + land[...]

    for i, (land, device) in enumerate(hops):
        trade.send(None, lambda i=i, land=land, device=device: trade.copy(here.at[i], land, base + i, device))
        trade.step()
        trade.wait(None, lambda land=land: land, base + i, place.pair())
        trade.do(None, lambda i=i, land=land: fold(i, land))
    for k in range(1, line):
        far = lax.rem(place.a + k, line)
        trade.send(None, lambda far=far, k=k: trade.copy(
            here.at[3], sm.at[k], base + 3 + k, place.at(far, place.b, place.t)))

    def keep():
        sm[0] = here[3]

    trade.do(None, keep)
    trade.step()
    for k in range(1, line):
        trade.wait(None, lambda k=k: sm.at[k], base + 3 + k, place.pair())
    trade.step()
    for k in (2, 3, 1):
        for j, dst in enumerate((lo, gt)):
            trade.wait(None, lambda dst=dst, k=k: dst.at[place.others[k]], extra + j * 4 + k, place.pair())
    for m in mine:
        trade.do(None, m.wait)

    for tick in range(8 + 3):
        for i, w in enumerate((3, 2, 1, 0)):
            if 0 <= tick - i < 8:
                ws[w].run()
        if tick < 5:
            trade.run()
    trade.run()
    for script in ws + [trade]:
        script.finish()


def heads_forward(q, k, v, allowed, keep):
    lane = lax.broadcasted_iota(jnp.int32, k.shape, 1)
    outs = []
    for h in range(2):
        mine = (lane // HD) == h
        scores = lax.dot_general(
            jnp.where(mine, k, jnp.zeros_like(k)), q, (((1,), (1,)), ((), ())), preferred_element_type=F32
        )
        scores = jnp.where(allowed, scores, -1e30)
        expo = jnp.exp(scores - jnp.max(scores, axis=0, keepdims=True))
        probs = (expo * (1.0 / jnp.sum(expo, axis=0, keepdims=True))).astype(BF)
        keep(h, probs)
        outs.append(
            lax.dot_general(v[:, h * HD : (h + 1) * HD], probs, (((0,), (0,)), ((), ())), preferred_element_type=F32)
        )
    return jnp.concatenate(outs, axis=0).T.astype(BF)


def norm_stats(values):
    row_mean = jnp.mean(values, axis=-1, keepdims=True)
    centred = values - row_mean
    variance = jnp.mean(centred * centred, axis=-1, keepdims=True)
    inv_std = lax.rsqrt(variance + 1e-05)
    return centred * inv_std, inv_std


def forward_kernel(line, *refs):
    toks, grads, small, wq, wo, w1, w2, vecs, masks = refs[:9]
    xin, gin, fq, fo, f1, f2, qkv_out, p_out, o_out, x1_out, h2_out, act_out, slope_out, g2_out, stats = refs[9:24]
    (sml, xv, gv, gt, h1, wqv, wov, w1v, qkv, pbuf, o, x1, h2, actb, slopeb, g2b, lsem, csem, ssem, rsem) = refs[24:]
    place = Place(line)
    per = slots_of(line)
    rows, width = xv.shape
    part = toks.shape[1]
    third = wqv.shape[-1]
    local = third // 3
    greet(place)
    ws = [
        Gather(place, ssem, rsem, lsem.at[i], shard, whole, i * per, CUTS[i])
        for i, (shard, whole) in enumerate(((wq, fq), (wo, fo), (w1, f1), (w2, f2)))
    ]
    trade = Trade(ssem, rsem)
    slot_of = lambda j, k: 4 * per + j * 4 + k
    pairs_of_rows = ((toks, xin), (grads, gin))
    mine = [pltpu.make_async_copy(src.at[place.t], dst.at[0], lsem.at[4 + j]) for j, (src, dst) in enumerate(pairs_of_rows)]
    mine.append(pltpu.make_async_copy(small, sml.at[place.t], lsem.at[6]))
    for j, (src, dst) in enumerate(pairs_of_rows):
        trade.step()
        trade.do(None, mine[j].start)
        for k in (2, 3, 1):
            trade.send(None, lambda src=src, dst=dst, j=j, k=k: trade.copy(
                src.at[place.others[k]], dst.at[k], slot_of(j, k), place.peer(k)))
        if j == 0:
            trade.do(None, mine[2].start)
            for k in (2, 3, 1):
                trade.send(None, lambda k=k: trade.copy(small, sml.at[place.t], slot_of(2, k), place.peer(k)))
    for j, (src, dst) in enumerate(pairs_of_rows):
        trade.step()
        trade.do(None, mine[j].wait)
        for k in (2, 3, 1):
            trade.wait(None, lambda dst=dst, k=k: dst.at[k], slot_of(j, k), place.pair())
        if j == 0:
            trade.do(None, mine[2].wait)
            for k in (2, 3, 1):
                trade.wait(None, lambda k=k: sml.at[place.others[k]], slot_of(2, k), place.pair())

    def ticks(text):
        for name in text:
            (trade if name == "r" else ws[int(name)]).run()

    def in_loop(i, plan):
        for at, text in plan.items():
            pl.when(i == at)(lambda text=text: ticks(text))

    def fetch_rows(src, dst, first):
        copies = [
            pltpu.make_async_copy(src.at[k], dst.at[pl.ds(k * part, part)], csem.at[first + k]) for k in range(4)
        ]
        for c in copies:
            c.start()
        return copies

    ticks("r0r0102r")
    fetch_x = fetch_rows(xin, xv, 0)
    ticks("0")
    for f in fetch_x:
        f.wait()
    stats[...] = jnp.zeros_like(stats)

    def first_norm(i, _):
        at = pl.ds(pl.multiple_of(i * ROWS, ROWS), ROWS)
        x = xv[at, :].astype(F32)
        unit, _inv = norm_stats(x)
        h1[at, :] = (unit * vecs[0:1, :] + vecs[1:2, :]).astype(BF)
        real = masks[0, at, :1]
        stats[0:1, :] += jnp.sum(x * x * real, axis=0, keepdims=True)
        stats[2:3, :] += jnp.broadcast_to(jnp.sum(real, axis=0, keepdims=True), (1, width))
        return 0

    lax.fori_loop(0, rows // ROWS, first_norm, 0)
    ticks("0113020r")
    fetch_g = fetch_rows(gin, gv, 4)
    ticks("0")
    fetch_q = lambda t: pltpu.make_async_copy(
        fq.at[:, :, :, pl.ds(pl.multiple_of(t * third, 128), third)], wqv.at[t], csem.at[8 + t])
    for t in range(4):
        fetch_q(t).start()
    for f in fetch_g:
        f.wait()

    def mask_rows(i, _):
        at = pl.ds(pl.multiple_of(i * ROWS, ROWS), ROWS)
        g = gv[at, :].astype(F32) * masks[0, at, :1]
        stats[3:4, :] += jnp.sum(g, axis=0, keepdims=True)
        gv[at, :] = g.astype(BF)
        return 0

    lax.fori_loop(0, rows // ROWS, mask_rows, 0)
    gt[...] = gv[...].T
    ticks("2")

    def project(t, _):
        fetch_q(t).wait()
        got = jnp.dot(h1[...], wqv[t].reshape(width, third), preferred_element_type=F32)
        cols = [pl.ds(pl.multiple_of(t * third + j * local, 128), local) for j in range(3)]
        qkv[:, cols[0]] = (got[:, :local] + sml[t, 1:2, :local]).astype(BF) * jnp.asarray(HD ** (-0.5), BF)
        qkv[:, cols[1]] = got[:, local : 2 * local].astype(BF)
        qkv[:, cols[2]] = (got[:, 2 * local :] + sml[t, 1:2, local : 2 * local]).astype(BF)
        in_loop(t, {0: "1", 1: "2", 2: "3", 3: "1"})
        return 0

    lax.fori_loop(0, 4, project, 0)
    save_qkv = pltpu.make_async_copy(qkv, qkv_out, csem.at[0])
    save_qkv.start()
    allowed = masks[1, :, :1] > 0
    pairs = qkv.shape[1] // 384
    keep_copy = lambda i, slot: pltpu.make_async_copy(pbuf.at[slot], p_out.at[i], csem.at[12 + slot])

    def pair_step(i, _):
        slot = lax.rem(i, 2)
        pl.when(i >= 2)(lambda: keep_copy(i - 2, slot).wait())

        def keep(h, probs):
            pbuf[slot, h] = probs

        base = (i // 2) * third + lax.rem(i, 2) * 128
        cols = [pl.ds(pl.multiple_of(base + j * local, 128), 128) for j in range(3)]
        o[:, pl.ds(pl.multiple_of(i * 128, 128), 128)] = heads_forward(
            qkv[:, cols[0]], qkv[:, cols[1]], qkv[:, cols[2]], allowed, keep
        )
        keep_copy(i, slot).start()
        in_loop(i, {0: "2", 1: "1", 2: "3", 3: "2", 4: "1", 5: "3", 6: "2", 7: "3"})
        return 0

    lax.fori_loop(0, pairs, pair_step, 0)
    save_o = pltpu.make_async_copy(o, o_out, csem.at[1])
    save_o.start()
    ticks("1")
    fetch_o = pltpu.make_async_copy(fo, wov, csem.at[2])
    fetch_o.start()
    fetch_o.wait()
    half = rows // 2

    def join(i, _):
        at = pl.ds(pl.multiple_of(i * half, 64), half)
        branch = lax.dot_general(
            o[at, :], wov[...].reshape(width, width), (((1,), (1,)), ((), ())), preferred_element_type=F32
        ) + vecs[4:5, :]
        stats[1:2, :] += jnp.sum(branch * branch * masks[0, at, :1], axis=0, keepdims=True)
        middle = xv[at, :].astype(F32) + branch
        x1[at, :] = middle
        unit, _inv = norm_stats(middle)
        h2[at, :] = (unit * vecs[2:3, :] + vecs[3:4, :]).astype(BF)
        return 0

    lax.fori_loop(0, 2, join, 0)
    save_x1 = pltpu.make_async_copy(x1, x1_out, csem.at[3])
    save_x1.start()
    save_h2 = pltpu.make_async_copy(h2, h2_out, csem.at[4])
    save_h2.start()
    ticks("2")
    tiles = w1v.shape[0]
    fetch_1 = lambda j: pltpu.make_async_copy(
        f1.at[:, :, :, pl.ds(pl.multiple_of(j * TILE, TILE), TILE)], w1v.at[j], csem.at[22 + j])
    for j in range(tiles):
        fetch_1(j).start()

    def saves(j, slot):
        cols = pl.ds(pl.multiple_of(j * TILE, TILE), TILE)
        return (
            pltpu.make_async_copy(actb.at[slot], act_out.at[:, cols], csem.at[14 + slot]),
            pltpu.make_async_copy(slopeb.at[slot], slope_out.at[:, cols], csem.at[16 + slot]),
            pltpu.make_async_copy(g2b.at[slot], g2_out.at[:, cols], csem.at[18 + slot]),
        )

    per_part = sml.shape[2] // TILE

    def hidden_step(j, _):
        slot = lax.rem(j, 2)

        @pl.when(j >= 2)
        def _():
            for save in saves(j - 2, slot):
                save.wait()

        fetch_1(j).wait()
        bias = sml[j // per_part, 0:1, pl.ds(pl.multiple_of(lax.rem(j, per_part) * TILE, TILE), TILE)]
        hidden = jnp.dot(h2[...], w1v[j].reshape(width, TILE), preferred_element_type=F32) + bias
        gate = jax.nn.sigmoid(1.702 * hidden)
        actb[slot] = (hidden * gate).astype(BF)
        slopeb[slot] = (gate + 1.702 * hidden * gate * (1.0 - gate)).astype(BF)
        g2b[slot] = jnp.dot(gt[...], actb[slot], preferred_element_type=F32).astype(BF)
        for save in saves(j, slot):
            save.start()
        in_loop(j, {1: "3", 4: "3"})
        return 0

    lax.fori_loop(0, tiles, hidden_step, 0)
    for j in (tiles - 2, tiles - 1):
        for save in saves(j, j % 2):
            save.wait()
    ticks("3")
    for save in (save_qkv, save_o, save_x1, save_h2, keep_copy(pairs - 2, pairs % 2), keep_copy(pairs - 1, (pairs - 1) % 2)):
        save.wait()
    for script in ws + [trade]:
        script.finish()


def forward(line, toks, grads, small, wq, wo, w1, w2, vecs, masks):
    images, part, width = toks.shape
    rows = 4 * part
    depth = wq.shape[0]
    hidden = 4 * w1.shape[1]
    heads = wo.shape[1] * 4 // HD
    wholes = [jax.ShapeDtypeStruct((line, 2, depth, 4 * w.shape[1]), BF) for w in (wq, wo, w1, w2)]
    count = 4 * slots_of(line) + 12
    hbm, vmem = pl.BlockSpec(memory_space=pl.ANY), pl.BlockSpec(memory_space=pltpu.VMEM)
    sds = jax.ShapeDtypeStruct
    return pl.pallas_call(
        functools.partial(forward_kernel, line),
        out_shape=[
            sds((4, part, width), BF),
            sds((4, part, width), BF),
            *wholes,
            sds((rows, 3 * width), BF),
            sds((heads // 2, 2, rows, rows), BF),
            sds((rows, width), BF),
            sds((rows, width), F32),
            sds((rows, width), BF),
            sds((rows, hidden), BF),
            sds((rows, hidden), BF),
            sds((width, hidden), BF),
            sds((8, width), F32),
        ],
        in_specs=[hbm] * 7 + [vmem] * 2,
        out_specs=[hbm] * 14 + [vmem],
        scratch_shapes=[
            pltpu.VMEM((4,) + small.shape, F32),
            pltpu.VMEM((rows, width), BF),
            pltpu.VMEM((rows, width), BF),
            pltpu.VMEM((width, rows), BF),
            pltpu.VMEM((rows, width), BF),
            pltpu.VMEM((4, line, 2, depth, wq.shape[1]), BF),
            pltpu.VMEM((line, 2, depth, width), BF),
            pltpu.VMEM((hidden // TILE, line, 2, depth, TILE), BF),
            pltpu.VMEM((rows, 3 * width), BF),
            pltpu.VMEM((2, 2, rows, rows), BF),
            pltpu.VMEM((rows, width), BF),
            pltpu.VMEM((rows, width), F32),
            pltpu.VMEM((rows, width), BF),
            pltpu.VMEM((2, rows, TILE), BF),
            pltpu.VMEM((2, rows, TILE), BF),
            pltpu.VMEM((2, width, TILE), BF),
            pltpu.SemaphoreType.DMA((8,)),
            pltpu.SemaphoreType.DMA((22 + hidden // TILE,)),
            pltpu.SemaphoreType.DMA((count,)),
            pltpu.SemaphoreType.DMA((count,)),
        ],
        compiler_params=pltpu.CompilerParams(
            collective_id=0, has_side_effects=True, vmem_limit_bytes=62 * MIB
        ),
        name="forward",
    )(toks, grads, small, wq, wo, w1, w2, vecs, masks)


def scatter_all(line, grads, louts, gtoks, small):
    depth = grads[0].shape[2]
    widths = [g.shape[3] // 4 for g in grads]
    rows, lanes = small.shape
    scratch = []
    for n, cut in zip(widths, CUTS):
        scratch += [
            pltpu.VMEM((4, line, depth, n), BF),
            pltpu.VMEM((4, line, depth, n), BF),
            pltpu.VMEM((line, depth, n - cut), BF),
            pltpu.VMEM((line, depth, cut), BF),
            pltpu.VMEM((line, depth, n), BF),
            pltpu.VMEM((line, depth, n), BF),
            pltpu.VMEM((line, depth, n), BF),
            pltpu.VMEM((line, depth, n), BF),
        ]
    count = 4 * (10 + 2 * line) + 8 + 3 + line
    scratch += [
        pltpu.VMEM((4, rows, lanes), F32),
        pltpu.VMEM((rows, lanes), F32),
        pltpu.VMEM((rows, lanes), F32),
        pltpu.VMEM((rows, lanes), F32),
        pltpu.SemaphoreType.DMA((count,)),
        pltpu.SemaphoreType.DMA((count,)),
        pltpu.SemaphoreType.DMA((18,)),
    ]
    hbm, vmem = pl.BlockSpec(memory_space=pl.ANY), pl.BlockSpec(memory_space=pltpu.VMEM)
    return pl.pallas_call(
        functools.partial(scatter_kernel, line),
        out_shape=[jax.ShapeDtypeStruct((depth, n), F32) for n in widths]
        + [
            jax.ShapeDtypeStruct(louts.shape, BF),
            jax.ShapeDtypeStruct(gtoks.shape, BF),
            jax.ShapeDtypeStruct((line, rows, lanes), F32),
        ],
        in_specs=[hbm] * 6 + [vmem],
        out_specs=[vmem] * 4 + [hbm] * 2 + [vmem],
        scratch_shapes=scratch,
        compiler_params=pltpu.CompilerParams(
            collective_id=1, has_side_effects=True, vmem_limit_bytes=60 * 1024 * 1024
        ),
        name="scatter_all",
    )(*grads, louts, gtoks, small)


def heads_backward(q_ref, k_ref, v_ref, o_ref, do_ref, p_ref, out_ref):
    q, k, v, do = q_ref[...], k_ref[...], v_ref[...], do_ref[...]
    lane = lax.broadcasted_iota(jnp.int32, k.shape, 1)
    product = do.astype(F32) * o_ref[...].astype(F32)
    zero = jnp.zeros_like(k)
    dq_t, dk, dv = [], [], []
    for h in range(2):
        mine = (lane // HD) == h
        inner = jnp.sum(jnp.where(mine, product, 0.0), axis=1, keepdims=True).T
        dprobs = lax.dot_general(
            jnp.where(mine, v, zero), do, (((1,), (1,)), ((), ())), preferred_element_type=F32
        )
        probs = p_ref[0, h]
        dscores = (probs.astype(F32) * (dprobs - inner)).astype(BF)
        dv.append(jnp.dot(probs, do, preferred_element_type=F32))
        dk.append(jnp.dot(dscores, q, preferred_element_type=F32))
        dq_t.append(
            lax.dot_general(k[:, h * HD : (h + 1) * HD], dscores, (((0,), (0,)), ((), ())), preferred_element_type=F32)
        )
    first = lane < HD
    out_ref[0] = (jnp.concatenate(dq_t, axis=0).T * HD ** (-0.5)).astype(BF)
    out_ref[1] = jnp.where(first, dk[0], dk[1]).astype(BF)
    out_ref[2] = jnp.where(first, dv[0], dv[1]).astype(BF)


def attention_back(qkv, o, do, probs):
    rows = qkv.shape[0]
    pairs = qkv.shape[1] // 384
    block = lambda part: pl.BlockSpec((rows, 128), lambda i: (0, (i // 2) * 6 + part * 2 + i % 2))
    own = pl.BlockSpec((rows, 128), lambda i: (0, i))
    return pl.pallas_call(
        heads_backward,
        grid=(pairs,),
        in_specs=[block(0), block(1), block(2), own, own, pl.BlockSpec((1, 2, rows, rows), lambda i: (i, 0, 0, 0))],
        out_specs=pl.BlockSpec((3, rows, 128), lambda i: (0, 0, i)),
        out_shape=jax.ShapeDtypeStruct((3, rows, pairs * 128), BF),
        compiler_params=pltpu.CompilerParams(vmem_limit_bytes=48 * 1024 * 1024),
        name="heads_backward",
    )(qkv, qkv, qkv, o, do, probs)


def norm_rows(values, gain_vec, bias_vec):
    row_mean = jnp.mean(values, axis=-1, keepdims=True)
    centred = values - row_mean
    variance = jnp.mean(centred * centred, axis=-1, keepdims=True)
    inv_std = lax.rsqrt(variance + 1e-05)
    normed = centred * inv_std
    return (normed * gain_vec + bias_vec).astype(BF), normed, inv_std


def norm_back(upstream, normed, inv_std, gain_vec):
    scaled = upstream * gain_vec
    inner_mean = jnp.mean(scaled, axis=-1, keepdims=True)
    cross_mean = jnp.mean(scaled * normed, axis=-1, keepdims=True)
    back = inv_std * (scaled - inner_mean - normed * cross_mean)
    return back, jnp.sum(upstream * normed, axis=0), jnp.sum(upstream, axis=0)


def rows_t(left, right):
    return lax.dot_general(left, right, (((0,), (0,)), ((), ())), preferred_element_type=F32)


def cols_t(left, right):
    return lax.dot_general(left, right, (((1,), (1,)), ((), ())), preferred_element_type=F32)


def shards(
    tokens, token_mask, out_grad, ln1_gain, ln1_bias, w_qkv, b_qv, w_out, b_out,
    ln2_gain, ln2_bias, w_fc1, b_fc1, w_fc2, b_fc2,
):
    images, tok_rows, width = tokens.shape
    parts = lax.axis_size("tensor")
    line = lax.axis_size("dp") // 2
    t = lax.axis_index("tensor")
    depth, _, local = w_qkv.shape
    rows = tok_rows * parts

    small = jnp.zeros((8, w_fc1.shape[1]), F32).at[0].set(b_fc1).at[1, : 2 * local].set(b_qv.reshape(-1))
    vecs = jnp.stack([ln1_gain, ln1_bias, ln2_gain, ln2_bias, b_out, b_fc2, b_out, b_out])
    own = lax.dynamic_index_in_dim(token_mask, t, 0, keepdims=False).reshape(parts, tok_rows)
    y, c = t // 2, lax.rem(t, 2)
    others = [t, y * 2 + 1 - c, (1 - y) * 2 + c, (1 - y) * 2 + 1 - c]
    mask = jnp.concatenate([lax.dynamic_index_in_dim(own, o, 0, keepdims=False) for o in others])
    real = mask.astype(F32)[:, None]
    allow = jnp.where(jnp.max(mask) > 0, mask, 1).astype(F32)
    masks = jnp.broadcast_to(jnp.stack([mask.astype(F32), allow])[:, :, None], (2, rows, 128))
    xin, gin, fq, fo, f1, f2, qkv, probs, o, middle, h2, act, slope, grad_f2, stats = forward(
        line, tokens, out_grad, small, w_qkv.reshape(depth, 3 * local), w_out.T, w_fc1, w_fc2.T, vecs, masks
    )
    fq, fo, f1, f2 = (f.reshape(width, -1) for f in (fq, fo, f1, f2))
    stream = xin.reshape(rows, width).astype(F32)
    h1, unit1, inv1 = norm_rows(stream, ln1_gain, ln1_bias)
    _, unit2, inv2 = norm_rows(middle, ln2_gain, ln2_bias)
    mlp = cols_t(act, f2) + b_fc2
    layer_out = (middle + mlp).astype(BF)
    squares = jnp.stack([jnp.sum(stats[0]), jnp.sum(stats[1]), jnp.sum(mlp * mlp * real), stats[2, 0]])

    top = gin.reshape(rows, width) * real.astype(BF)
    top32 = top.astype(F32)
    du = (jnp.dot(top, f2, preferred_element_type=F32) * slope.astype(F32)).astype(BF)
    grad_f1 = rows_t(h2, du).astype(BF)
    dh2 = cols_t(du, f1)
    back2, g_ln2_gain, g_ln2_bias = norm_back(dh2, unit2, inv2, ln2_gain)
    g1 = top32 + back2
    g1b = g1.astype(BF)
    grad_fo = rows_t(g1b, o).astype(BF)
    do = jnp.dot(g1b, fo, preferred_element_type=F32).astype(BF)
    dqkv = attention_back(qkv, o, do, probs)
    dqkv = dqkv.reshape(3, rows, parts, local).transpose(1, 2, 0, 3).reshape(rows, -1)
    grad_fq = rows_t(h1, dqkv).astype(BF)
    dh1 = cols_t(dqkv, fq)
    back1, g_ln1_gain, g_ln1_bias = norm_back(dh1, unit1, inv1, ln1_gain)
    grad_tokens = (g1 + back1).astype(BF)

    bias_sums = jnp.sum(dqkv.astype(F32), axis=0).reshape(parts, 3, local)
    sums = jnp.stack(
        [
            g_ln1_gain,
            g_ln1_bias,
            jnp.sum(g1b.astype(F32), axis=0),
            g_ln2_gain,
            g_ln2_bias,
            stats[3],
            jnp.zeros((width,), F32).at[:4].set(squares),
            jnp.zeros((width,), F32),
        ]
    )
    sums = jnp.concatenate(
        [
            sums,
            jnp.sum(du.astype(F32), axis=0).reshape(parts, -1),
            bias_sums[:, 0].reshape(1, -1),
            bias_sums[:, 2].reshape(1, -1),
            jnp.zeros((2, width), F32),
        ]
    )
    blocks = lambda g: g.reshape(line, 2, depth, -1)
    sum_q, sum_o, sum_1, sum_2, lo, gt, sm = scatter_all(
        line,
        [blocks(g) for g in (grad_fq, grad_fo, grad_f1, grad_f2)],
        layer_out.reshape(parts, tok_rows, width),
        grad_tokens.reshape(parts, tok_rows, width),
        sums,
    )
    sums = jnp.sum(sm, axis=0)
    rms = jnp.sqrt(sums[6, :3] / (sums[6, 3] * width))
    pick = lambda v: lax.dynamic_slice_in_dim(v, t * local, local, 0)
    return (
        lo,
        gt,
        sums[0],
        sums[1],
        sum_q.reshape(depth, 3, local),
        jnp.stack([pick(sums[12]), pick(sums[13])]),
        sum_o.T,
        sums[2],
        sums[3],
        sums[4],
        sum_1,
        lax.dynamic_index_in_dim(sums[8:12], t, 0, keepdims=False),
        sum_2.T,
        sums[5],
        rms,
    )


def solution(mesh):
    rowwise = P("dp", "tensor", None)
    placed = (
        rowwise, P("dp", None), rowwise, P(), P(), P("dp", None, "tensor"), P(None, "tensor"), P("tensor", "dp"),
        P(), P(), P(), P("dp", "tensor"), P("tensor"), P("tensor", "dp"), P(),
    )
    return jax.shard_map(
        shards,
        mesh=mesh,
        in_specs=placed,
        out_specs=(
            rowwise, rowwise, P(), P(), P("dp", None, "tensor"), P(None, "tensor"), P("tensor", "dp"), P(),
            P(), P(), P("dp", "tensor"), P("tensor"), P("tensor", "dp"), P(), P(),
        ),
        check_vma=False,
    )
```

```python
import functools

import jax
import jax.numpy as jnp
from jax import lax
from jax.experimental import pallas as pl
from jax.experimental.pallas import tpu as pltpu
from jax.sharding import PartitionSpec as P

HD = 64
MESH = pl.DeviceIdType.MESH
BF = jnp.bfloat16
F32 = jnp.float32
ROWS = 64
TILE = 512
MIB = 1024 * 1024


class Place:
    def __init__(self, line):
        self.line = line
        self.d = lax.axis_index("dp")
        self.t = lax.axis_index("tensor")
        self.a = self.d // 2
        self.b = lax.rem(self.d, 2)
        y, c = self.t // 2, lax.rem(self.t, 2)
        self.others = (self.t, y * 2 + 1 - c, (1 - y) * 2 + c, (1 - y) * 2 + 1 - c)
        self.low, self.high = self.a > 0, self.a < line - 1
        self.inner = jnp.logical_and(self.low, self.high)

    def at(self, a, b, t):
        return (a * 2 + b, t)

    def pair(self):
        return self.at(self.a, 1 - self.b, self.t)

    def peer(self, k):
        return (self.d, self.others[k])

    def up(self):
        return self.at(self.a + 1, self.b, self.t)

    def down(self):
        return self.at(self.a - 1, self.b, self.t)


def greet(place, whole_line=False):
    barrier = pltpu.get_barrier_semaphore()

    def hail(device):
        pl.semaphore_signal(barrier, inc=1, device_id=device, device_id_type=MESH)

    line = place.line
    hail(place.pair())
    for k in range(1, 4):
        hail(place.peer(k))
    if whole_line:
        for k in range(1, line):
            hail(place.at(lax.rem(place.a + k, line), place.b, place.t))
        pl.semaphore_wait(barrier, 3 + line)
        return
    pl.when(place.low)(lambda: hail(place.down()))
    pl.when(place.high)(lambda: hail(place.up()))
    pl.when(place.inner)(lambda: pl.semaphore_wait(barrier, 6))
    pl.when(jnp.logical_not(place.inner))(lambda: pl.semaphore_wait(barrier, 5))


def both(p, q):
    if p is None:
        return q
    if q is None:
        return p
    return jnp.logical_and(p, q)


def when(pred, act):
    if pred is None:
        act()
    else:
        pl.when(pred)(act)


class Script:
    def __init__(self, ssem, rsem):
        self.ssem, self.rsem = ssem, rsem
        self.sent = []
        self.steps = []

    def copy(self, src, dst, slot, device):
        return pltpu.make_async_remote_copy(
            src_ref=src,
            dst_ref=dst,
            send_sem=self.ssem.at[slot],
            recv_sem=self.rsem.at[slot],
            device_id=device,
            device_id_type=MESH,
        )

    def step(self):
        self.steps.append([])

    def do(self, pred, act):
        self.steps[-1].append((pred, act))

    def send(self, pred, make):
        self.do(pred, lambda: make().start())
        self.sent.append((pred, make))

    def wait(self, pred, ref, slot, device):
        self.do(pred, lambda: self.copy(ref(), ref(), slot, device).wait_recv())

    def run(self, count=1):
        for _ in range(count):
            for pred, act in self.steps.pop(0):
                when(pred, act)

    def finish(self):
        assert not self.steps
        for pred, make in self.sent:
            when(pred, lambda make=make: make().wait_send())


def thirds(line):
    return [1], [2] if line > 2 else [], list(range(3, line))


def order(place):
    yield None, place.a
    for k in range(1, place.line):
        yield place.a >= k, place.a - k
        yield place.a + k <= place.line - 1, place.a + k


class Gather(Script):
    def __init__(self, place, ssem, rsem, local_sem, shard, whole, base, cut):
        super().__init__(ssem, rsem)
        self.p = place
        self.shard, self.whole = shard, whole
        self.n = shard.shape[1]
        self.base, self.cut = base, cut
        local = pltpu.make_async_copy(shard, self.block(place.a, place.b, place.t), local_sem)
        p = place
        own = lambda: self.shard

        self.step()
        self.do(None, local.start)
        self.pass_line(None, p.a, 1, True, own)
        self.pass_line(None, p.a, 1, False, own)
        self.spread(None, p.a, own)
        for group in thirds(p.line):
            self.step()
            for k in group:
                self.receive(k)
        self.step()
        self.cross()
        self.step()
        self.do(None, local.wait)
        self.core((0, 1, 2))
        self.step()
        self.diagonal()
        self.core((3,))
        self.step()
        self.arrive()

    def block(self, a, b, t, lo=0, hi=None):
        hi = self.n if hi is None else hi
        start = pl.multiple_of(t * self.n + lo, 128)
        return self.whole.at[a, b, :, pl.ds(start, hi - lo)]

    def plane(self, b, t):
        start = pl.multiple_of(t * self.n, 128)
        return self.whole.at[:, b, :, pl.ds(start, self.n)]

    def slot(self, kind, i):
        return self.base + kind * self.p.line + i

    def spread(self, pred, a, src):
        p = self.p
        self.send(pred, lambda: self.copy(src(), self.block(a, p.b, p.t), self.slot(2, a), p.pair()))
        self.send(pred, lambda: self.copy(src(), self.block(a, p.b, p.t), self.slot(3, a), p.peer(2)))

    def pass_line(self, pred, a, step, up, src):
        p = self.p
        if step > p.line - 1:
            return
        ok = both(pred, p.high if up else p.low)
        to = p.up if up else p.down
        self.send(ok, lambda: self.copy(src(), self.block(a, p.b, p.t), self.slot(0 if up else 1, step), to()))

    def receive(self, k):
        p = self.p
        for up in (True, False):
            chunk = p.a - k if up else p.a + k
            pred = p.a >= k if up else p.a + k <= p.line - 1
            src = lambda chunk=chunk: self.block(chunk, p.b, p.t)
            self.wait(pred, src, self.slot(0 if up else 1, k), p.pair())
            self.pass_line(pred, chunk, k + 1, up, src)
            self.spread(pred, chunk, src)

    def cross(self):
        p, t2 = self.p, self.p.others[2]
        for pred, a in order(p):
            self.wait(pred, lambda a=a: self.block(a, 1 - p.b, p.t), self.slot(2, a), p.pair())
            self.wait(pred, lambda a=a: self.block(a, p.b, t2), self.slot(3, a), p.pair())
            one = lambda a=a: self.block(a, 1 - p.b, p.t, 0, self.cut)
            two = lambda a=a: self.block(a, p.b, t2, self.cut, self.n)
            if self.cut > 0:
                self.send(pred, lambda a=a, one=one: self.copy(one(), one(), self.slot(4, a), p.peer(2)))
            if self.cut < self.n:
                self.send(pred, lambda a=a, two=two: self.copy(two(), two(), self.slot(5, a), p.pair()))

    def planes(self, far):
        p = self.p
        t, t2 = (p.others[1], p.others[3]) if far else (p.t, p.others[2])
        return ((p.b, t), (1 - p.b, t), (p.b, t2), (1 - p.b, t2))

    def core(self, which):
        for j in which:
            b, t = self.planes(False)[j]
            src = lambda b=b, t=t: self.plane(b, t)
            self.send(None, lambda j=j, src=src: self.copy(src(), src(), self.slot(6, j), self.p.peer(1)))

    def diagonal(self):
        p, t2 = self.p, self.p.others[2]
        for pred, a in order(p):
            if self.cut > 0:
                self.wait(pred, lambda a=a: self.block(a, 1 - p.b, t2, 0, self.cut), self.slot(4, a), p.pair())
            if self.cut < self.n:
                self.wait(pred, lambda a=a: self.block(a, 1 - p.b, t2, self.cut, self.n), self.slot(5, a), p.pair())

    def arrive(self):
        for j, (b, t) in enumerate(self.planes(True)):
            self.wait(None, lambda b=b, t=t: self.plane(b, t), self.slot(6, j), self.p.pair())


CUTS = (256, 128, 384, 384)


def slots_of(line):
    return 6 * line + 4


def add_into(dst, *others):
    rows = dst.shape[0]
    step = min(rows, 32)

    def body(i, _):
        at = pl.ds(pl.multiple_of(i * step, step), step)
        total = dst[at, :]
        for other in others:
            total = total + other[at, :]
        dst[at, :] = total
        return 0

    lax.fori_loop(0, rows // step, body, 0)


def block_of(place, q):
    y, c = place.t // 2, lax.rem(place.t, 2)
    return lax.rem(y + 1 + q, 2) * 2 + lax.rem(c + 1 - q // 2, 2)


class Scatter(Script):
    def __init__(self, place, ssem, rsem, far, met, acc, out, bufs, base, cut):
        super().__init__(ssem, rsem)
        self.p = place
        self.acc, self.out = acc, out
        self.rdx, self.rdy, self.rx, self.ry, self.up, self.dn = bufs
        self.n = out.shape[1]
        self.base, self.cut = base, cut
        self.own = lambda *at: acc.at[(1, at[0], place.b) + at[1:]]
        self.by_pair = lambda *at: acc.at[(1, at[0], 1 - place.b) + at[1:]]
        self.by_y = lambda *at: acc.at[(0, at[0], place.b) + at[1:]]
        self.by_both = lambda *at: acc.at[(0, at[0], 1 - place.b) + at[1:]]
        if far is not None:
            for i in range(2):
                self.step()
                self.send(None, lambda i=i: self.copy(far(i), met.at[i], base + i, place.peer(1)))
            for i in range(2):
                self.step()
                self.wait(None, lambda i=i: met.at[i], base + i, place.pair())
        every, first, late = slice(None), pl.ds(0, cut), pl.ds(cut, self.n - cut)
        pair, y = place.pair(), place.peer(2)
        self.step()
        self.send(None, lambda: self.copy(self.by_both(every, every, first), self.rdy, base + 4, y))
        self.send(None, lambda: self.copy(self.by_both(every, every, late), self.rdx, base + 5, pair))
        self.send(None, lambda: self.copy(self.by_y(every, every, first), self.ry.at[:, :, first], base + 7, y))
        self.step()
        self.send(None, lambda: self.copy(self.by_pair(every, every, late), self.rx.at[:, :, late], base + 6, pair))
        self.step()
        self.wait(None, lambda: self.rdy, base + 4, pair)
        for a in range(place.line):
            self.do(None, lambda a=a: add_into(self.by_pair(a, every, first), self.rdy.at[a]))
        self.send(None, lambda: self.copy(self.by_pair(every, every, first), self.rx.at[:, :, first], base + 8, pair))
        self.wait(None, lambda: self.rdx, base + 5, pair)
        for a in range(place.line):
            self.do(None, lambda a=a: add_into(self.by_y(a, every, late), self.rdx.at[a]))
        self.send(None, lambda: self.copy(self.by_y(every, every, late), self.ry.at[:, :, late], base + 9, y))
        self.step()
        self.wait(None, lambda: self.rx.at[:, :, late], base + 6, pair)
        self.wait(None, lambda: self.ry.at[:, :, first], base + 7, pair)
        self.wait(None, lambda: self.rx.at[:, :, first], base + 8, pair)
        self.wait(None, lambda: self.ry.at[:, :, late], base + 9, pair)
        for a in range(place.line):
            self.do(None, lambda a=a: add_into(self.own(a), self.rx.at[a], self.ry.at[a]))
        for group in thirds(place.line):
            self.step()
            for j in group:
                self.along(j)
        self.step()
        self.close()

    def along(self, j):
        p = self.p
        line = p.line
        for up, chunk in ((True, line - j), (False, j - 1)):
            passing = p.a < chunk if up else p.a > chunk
            inner = both(passing, p.low if up else p.high)
            land = self.up if up else self.dn
            slot = self.base + 10 + (0 if up else line) + chunk
            to = p.up if up else p.down
            self.wait(inner, lambda land=land, chunk=chunk: land.at[chunk], slot, p.pair())
            self.do(inner, lambda land=land, chunk=chunk: add_into(self.own(chunk), land.at[chunk]))
            self.send(passing, lambda chunk=chunk, land=land, slot=slot, to=to: self.copy(
                self.own(chunk), land.at[chunk], slot, to()))

    def close(self):
        p = self.p
        line = p.line
        rows = self.out.shape[0]
        step = min(rows, 16)

        def total(refs):
            def body(i, _):
                at = pl.ds(pl.multiple_of(i * step, step), step)
                value = self.acc[1, p.a, p.b, at, :].astype(F32)
                for ref in refs:
                    value = value + ref[p.a, at, :].astype(F32)
                self.out[at, :] = value
                return 0

            lax.fori_loop(0, rows // step, body, 0)

        self.wait(p.low, lambda: self.up.at[p.a], self.base + 10 + p.a, p.pair())
        self.wait(p.high, lambda: self.dn.at[p.a], self.base + 10 + line + p.a, p.pair())
        self.do(jnp.logical_not(p.low), lambda: total((self.dn,)))
        self.do(jnp.logical_not(p.high), lambda: total((self.up,)))
        self.do(p.inner, lambda: total((self.up, self.dn)))


def landing(line, depth, n, cut):
    return [
        pltpu.VMEM((line, depth, n - cut), BF),
        pltpu.VMEM((line, depth, cut), BF),
        pltpu.VMEM((line, depth, n), BF),
        pltpu.VMEM((line, depth, n), BF),
        pltpu.VMEM((line, depth, n), BF),
        pltpu.VMEM((line, depth, n), BF),
    ]


def sums_of(line):
    return 10 + 2 * line


class Trade(Script):
    pass


def heads_forward(q, k, v, allowed, keep):
    lane = lax.broadcasted_iota(jnp.int32, k.shape, 1)
    outs = []
    for h in range(2):
        mine = (lane // HD) == h
        scores = lax.dot_general(
            jnp.where(mine, k, jnp.zeros_like(k)), q, (((1,), (1,)), ((), ())), preferred_element_type=F32
        )
        scores = jnp.where(allowed, scores, -1e30)
        expo = jnp.exp(scores - jnp.max(scores, axis=0, keepdims=True))
        probs = (expo * (1.0 / jnp.sum(expo, axis=0, keepdims=True))).astype(BF)
        keep(h, probs)
        outs.append(
            lax.dot_general(v[:, h * HD : (h + 1) * HD], probs, (((0,), (0,)), ((), ())), preferred_element_type=F32)
        )
    return jnp.concatenate(outs, axis=0).T.astype(BF)


def norm_stats(values):
    row_mean = jnp.mean(values, axis=-1, keepdims=True)
    centred = values - row_mean
    variance = jnp.mean(centred * centred, axis=-1, keepdims=True)
    inv_std = lax.rsqrt(variance + 1e-05)
    return centred * inv_std, inv_std


def forward_kernel(line, *refs):
    toks, grads, small, wq, wo, w1, w2, vecs, masks = refs[:9]
    xin, gin, fq, fo, f1, f2, qkv_out, p_out, o_out, x1_out, h2_out, act_out, slope_out, g2_out, h1_out, g_out, stats = refs[9:26]
    (sml, xv, gv, gt, h1, wqv, wov, w1v, qkv, pbuf, o, x1, h2, actb, slopeb, g2b, far, met, lsem, csem, ssem, rsem) = refs[26:]
    place = Place(line)
    per = slots_of(line)
    rows, width = xv.shape
    part = toks.shape[1]
    third = wqv.shape[-1]
    local = third // 3
    greet(place)
    ws = [
        Gather(place, ssem, rsem, lsem.at[i], shard, whole, i * per, CUTS[i])
        for i, (shard, whole) in enumerate(((wq, fq), (wo, fo), (w1, f1), (w2, f2)))
    ]
    trade = Trade(ssem, rsem)
    slot_of = lambda j, k: 4 * per + j * 4 + k
    pairs_of_rows = ((toks, xin), (grads, gin))
    mine = [pltpu.make_async_copy(src.at[place.t], dst.at[0], lsem.at[4 + j]) for j, (src, dst) in enumerate(pairs_of_rows)]
    mine.append(pltpu.make_async_copy(small, sml.at[place.t], lsem.at[6]))
    for j, (src, dst) in enumerate(pairs_of_rows):
        trade.step()
        trade.do(None, mine[j].start)
        for k in (2, 3, 1):
            trade.send(None, lambda src=src, dst=dst, j=j, k=k: trade.copy(
                src.at[place.others[k]], dst.at[k], slot_of(j, k), place.peer(k)))
        if j == 0:
            trade.do(None, mine[2].start)
            for k in (2, 3, 1):
                trade.send(None, lambda k=k: trade.copy(small, sml.at[place.t], slot_of(2, k), place.peer(k)))
    for j, (src, dst) in enumerate(pairs_of_rows):
        trade.step()
        trade.do(None, mine[j].wait)
        for k in (2, 3, 1):
            trade.wait(None, lambda dst=dst, k=k: dst.at[k], slot_of(j, k), place.pair())
        if j == 0:
            trade.do(None, mine[2].wait)
            for k in (2, 3, 1):
                trade.wait(None, lambda k=k: sml.at[place.others[k]], slot_of(2, k), place.pair())

    core = Script(ssem, rsem)
    for i in range(2):
        core.step()
        core.send(None, lambda i=i: core.copy(far.at[i], met.at[i], 4 * per + 12 + i, place.peer(1)))
    for i in range(2):
        core.step()
        core.wait(None, lambda i=i: met.at[i], 4 * per + 12 + i, place.pair())
    by_name = {"r": trade, "c": core, **{str(i): w for i, w in enumerate(ws)}}

    def ticks(text):
        for name in text:
            by_name[name].run()

    def in_loop(i, plan):
        for at, text in plan.items():
            pl.when(i == at)(lambda text=text: ticks(text))

    def fetch_rows(src, dst, first):
        copies = [
            pltpu.make_async_copy(src.at[k], dst.at[pl.ds(k * part, part)], csem.at[first + k]) for k in range(4)
        ]
        for c in copies:
            c.start()
        return copies

    ticks("r0r0102r")
    fetch_x = fetch_rows(xin, xv, 0)
    ticks("0")
    for f in fetch_x:
        f.wait()
    stats[...] = jnp.zeros_like(stats)

    def first_norm(i, _):
        at = pl.ds(pl.multiple_of(i * ROWS, ROWS), ROWS)
        x = xv[at, :].astype(F32)
        unit, _inv = norm_stats(x)
        h1[at, :] = (unit * vecs[0:1, :] + vecs[1:2, :]).astype(BF)
        real = masks[0, at, :1]
        stats[0:1, :] += jnp.sum(x * x * real, axis=0, keepdims=True)
        stats[2:3, :] += jnp.broadcast_to(jnp.sum(real, axis=0, keepdims=True), (1, width))
        return 0

    lax.fori_loop(0, rows // ROWS, first_norm, 0)
    save_h1 = pltpu.make_async_copy(h1, h1_out, csem.at[20])
    save_h1.start()
    ticks("0113020r")
    fetch_g = fetch_rows(gin, gv, 4)
    ticks("0")
    fetch_q = lambda t: pltpu.make_async_copy(
        fq.at[:, :, :, pl.ds(pl.multiple_of(t * third, 128), third)], wqv.at[t], csem.at[8 + t])
    for t in range(4):
        fetch_q(t).start()
    for f in fetch_g:
        f.wait()

    def mask_rows(i, _):
        at = pl.ds(pl.multiple_of(i * ROWS, ROWS), ROWS)
        g = gv[at, :].astype(F32) * masks[0, at, :1]
        stats[3:4, :] += jnp.sum(g, axis=0, keepdims=True)
        gv[at, :] = g.astype(BF)
        return 0

    lax.fori_loop(0, rows // ROWS, mask_rows, 0)
    save_g = pltpu.make_async_copy(gv, g_out, csem.at[21])
    save_g.start()
    gt[...] = gv[...].T
    ticks("2")

    def project(t, _):
        fetch_q(t).wait()
        got = jnp.dot(h1[...], wqv[t].reshape(width, third), preferred_element_type=F32)
        cols = [pl.ds(pl.multiple_of(t * third + j * local, 128), local) for j in range(3)]
        qkv[:, cols[0]] = (got[:, :local] + sml[t, 1:2, :local]).astype(BF) * jnp.asarray(HD ** (-0.5), BF)
        qkv[:, cols[1]] = got[:, local : 2 * local].astype(BF)
        qkv[:, cols[2]] = (got[:, 2 * local :] + sml[t, 1:2, local : 2 * local]).astype(BF)
        in_loop(t, {0: "1", 1: "2", 2: "3", 3: "1"})
        return 0

    lax.fori_loop(0, 4, project, 0)
    save_qkv = pltpu.make_async_copy(qkv, qkv_out, csem.at[0])
    save_qkv.start()
    allowed = masks[1, :, :1] > 0
    pairs = qkv.shape[1] // 384
    keep_copy = lambda i, slot: pltpu.make_async_copy(pbuf.at[slot], p_out.at[i], csem.at[12 + slot])

    def pair_step(i, _):
        slot = lax.rem(i, 2)
        pl.when(i >= 2)(lambda: keep_copy(i - 2, slot).wait())

        def keep(h, probs):
            pbuf[slot, h] = probs

        base = (i // 2) * third + lax.rem(i, 2) * 128
        cols = [pl.ds(pl.multiple_of(base + j * local, 128), 128) for j in range(3)]
        o[:, pl.ds(pl.multiple_of(i * 128, 128), 128)] = heads_forward(
            qkv[:, cols[0]], qkv[:, cols[1]], qkv[:, cols[2]], allowed, keep
        )
        keep_copy(i, slot).start()
        in_loop(i, {0: "2", 1: "1", 2: "3", 3: "2", 4: "1", 5: "3", 6: "2", 7: "3"})
        return 0

    lax.fori_loop(0, pairs, pair_step, 0)
    save_o = pltpu.make_async_copy(o, o_out, csem.at[1])
    save_o.start()
    ticks("1")
    fetch_o = pltpu.make_async_copy(fo, wov, csem.at[2])
    fetch_o.start()
    fetch_o.wait()
    half = rows // 2

    def join(i, _):
        at = pl.ds(pl.multiple_of(i * half, 64), half)
        branch = lax.dot_general(
            o[at, :], wov[...].reshape(width, width), (((1,), (1,)), ((), ())), preferred_element_type=F32
        ) + vecs[4:5, :]
        stats[1:2, :] += jnp.sum(branch * branch * masks[0, at, :1], axis=0, keepdims=True)
        middle = xv[at, :].astype(F32) + branch
        x1[at, :] = middle
        unit, _inv = norm_stats(middle)
        h2[at, :] = (unit * vecs[2:3, :] + vecs[3:4, :]).astype(BF)
        return 0

    lax.fori_loop(0, 2, join, 0)
    save_x1 = pltpu.make_async_copy(x1, x1_out, csem.at[3])
    save_x1.start()
    save_h2 = pltpu.make_async_copy(h2, h2_out, csem.at[4])
    save_h2.start()
    ticks("2")
    tiles = w1v.shape[0]
    n1 = w1.shape[1]
    fetch_1 = lambda j: pltpu.make_async_copy(f1.at[:, :, :, place_of(j)[3]], w1v.at[j], csem.at[22 + j])
    half_block = n1 // TILE

    def place_of(j):
        q, h = j // half_block, lax.rem(j, half_block)
        block = block_of(place, q)
        return q, block, h, pl.ds(pl.multiple_of(block * n1 + h * TILE, TILE), TILE)

    for j in range(tiles):
        fetch_1(j).start()

    def saves(j, slot):
        q, block, h, cols = place_of(j)
        return (
            pltpu.make_async_copy(actb.at[slot], act_out.at[:, cols], csem.at[14 + slot]),
            pltpu.make_async_copy(slopeb.at[slot], slope_out.at[:, cols], csem.at[16 + slot]),
        )

    def save_g2(j, slot):
        q, block, h, cols = place_of(j)
        at = pl.ds(pl.multiple_of(h * TILE, TILE), TILE)
        return pltpu.make_async_copy(g2b.at[slot], g2_out.at[q - 2, :, :, :, at], csem.at[18 + slot])

    def hidden_step(j, _):
        slot = lax.rem(j, 2)

        @pl.when(j >= 2)
        def _():
            for save in saves(j - 2, slot):
                save.wait()

        q, block, h, cols = place_of(j)
        fetch_1(j).wait()
        at = pl.ds(pl.multiple_of(h * TILE, TILE), TILE)
        bias = sml[block, 0:1, at]
        hidden = jnp.dot(h2[...], w1v[j].reshape(width, TILE), preferred_element_type=F32) + bias
        gate = jax.nn.sigmoid(1.702 * hidden)
        actb[slot] = (hidden * gate).astype(BF)
        slopeb[slot] = (gate + 1.702 * hidden * gate * (1.0 - gate)).astype(BF)
        for save in saves(j, slot):
            save.start()
        product = jnp.dot(gt[...], actb[slot], preferred_element_type=F32)

        @pl.when(q < 2)
        def _():
            far[q, :, :, :, at] = product.astype(BF).reshape(far.shape[1:4] + (TILE,))

        @pl.when(q >= 2)
        def _():
            pl.when(j >= 2 * half_block + 2)(lambda: save_g2(j - 2, slot).wait())
            g2b[slot] = (product.reshape(far.shape[1:4] + (TILE,)) + met[q - 2, :, :, :, at].astype(F32)).astype(BF)
            save_g2(j, slot).start()

        in_loop(j, {half_block - 1: "c", half_block: "3", 2 * half_block - 1: "cc", 3 * half_block - 2: "3", 3 * half_block - 1: "c"})
        return 0

    lax.fori_loop(0, tiles, hidden_step, 0)
    for j in (tiles - 2, tiles - 1):
        for save in saves(j, j % 2) + (save_g2(j, j % 2),):
            save.wait()
    ticks("3")
    for save in (save_h1, save_g, save_qkv, save_o, save_x1, save_h2, keep_copy(pairs - 2, pairs % 2), keep_copy(pairs - 1, (pairs - 1) % 2)):
        save.wait()
    for script in ws + [trade, core]:
        script.finish()


def forward(line, toks, grads, small, wq, wo, w1, w2, vecs, masks):
    images, part, width = toks.shape
    rows = 4 * part
    depth = wq.shape[0]
    hidden = 4 * w1.shape[1]
    heads = wo.shape[1] * 4 // HD
    wholes = [jax.ShapeDtypeStruct((line, 2, depth, 4 * w.shape[1]), BF) for w in (wq, wo, w1, w2)]
    count = 4 * slots_of(line) + 14
    hbm, vmem = pl.BlockSpec(memory_space=pl.ANY), pl.BlockSpec(memory_space=pltpu.VMEM)
    sds = jax.ShapeDtypeStruct
    return pl.pallas_call(
        functools.partial(forward_kernel, line),
        out_shape=[
            sds((4, part, width), BF),
            sds((4, part, width), BF),
            *wholes,
            sds((rows, 3 * width), BF),
            sds((heads // 2, 2, rows, rows), BF),
            sds((rows, width), BF),
            sds((rows, width), F32),
            sds((rows, width), BF),
            sds((rows, hidden), BF),
            sds((rows, hidden), BF),
            sds((2, line, 2, depth, w2.shape[1]), BF),
            sds((rows, width), BF),
            sds((rows, width), BF),
            sds((8, width), F32),
        ],
        in_specs=[hbm] * 7 + [vmem] * 2,
        out_specs=[hbm] * 16 + [vmem],
        scratch_shapes=[
            pltpu.VMEM((4,) + small.shape, F32),
            pltpu.VMEM((rows, width), BF),
            pltpu.VMEM((rows, width), BF),
            pltpu.VMEM((width, rows), BF),
            pltpu.VMEM((rows, width), BF),
            pltpu.VMEM((4, line, 2, depth, wq.shape[1]), BF),
            pltpu.VMEM((line, 2, depth, width), BF),
            pltpu.VMEM((hidden // TILE, line, 2, depth, TILE), BF),
            pltpu.VMEM((rows, 3 * width), BF),
            pltpu.VMEM((2, 2, rows, rows), BF),
            pltpu.VMEM((rows, width), BF),
            pltpu.VMEM((rows, width), F32),
            pltpu.VMEM((rows, width), BF),
            pltpu.VMEM((2, rows, TILE), BF),
            pltpu.VMEM((2, rows, TILE), BF),
            pltpu.VMEM((2, line, 2, depth, TILE), BF),
            pltpu.VMEM((2, line, 2, depth, w2.shape[1]), BF),
            pltpu.VMEM((2, line, 2, depth, w2.shape[1]), BF),
            pltpu.SemaphoreType.DMA((8,)),
            pltpu.SemaphoreType.DMA((22 + hidden // TILE,)),
            pltpu.SemaphoreType.DMA((count,)),
            pltpu.SemaphoreType.DMA((count,)),
        ],
        compiler_params=pltpu.CompilerParams(
            collective_id=0, has_side_effects=True, vmem_limit_bytes=62 * MIB
        ),
        name="forward",
    )(toks, grads, small, wq, wo, w1, w2, vecs, masks)


def heads_backward(q, k, v, o, do, probs_of):
    lane = lax.broadcasted_iota(jnp.int32, k.shape, 1)
    product = do.astype(F32) * o.astype(F32)
    zero = jnp.zeros_like(k)
    dq_t, dk, dv = [], [], []
    for h in range(2):
        mine = (lane // HD) == h
        inner = jnp.sum(jnp.where(mine, product, 0.0), axis=1, keepdims=True).T
        dprobs = lax.dot_general(
            jnp.where(mine, v, zero), do, (((1,), (1,)), ((), ())), preferred_element_type=F32
        )
        probs = probs_of(h)
        dscores = (probs.astype(F32) * (dprobs - inner)).astype(BF)
        dv.append(jnp.dot(probs, do, preferred_element_type=F32))
        dk.append(jnp.dot(dscores, q, preferred_element_type=F32))
        dq_t.append(
            lax.dot_general(k[:, h * HD : (h + 1) * HD], dscores, (((0,), (0,)), ((), ())), preferred_element_type=F32)
        )
    first = lane < HD
    return (
        (jnp.concatenate(dq_t, axis=0).T * HD ** (-0.5)).astype(BF),
        jnp.where(first, dk[0], dk[1]).astype(BF),
        jnp.where(first, dv[0], dv[1]).astype(BF),
    )


def norm_back(upstream, unit, inv_std, gain):
    scaled = upstream * gain
    inner_mean = jnp.mean(scaled, axis=-1, keepdims=True)
    cross_mean = jnp.mean(scaled * unit, axis=-1, keepdims=True)
    return inv_std * (scaled - inner_mean - unit * cross_mean)


def middle_kernel(line, *refs):
    g_in, f1, f2, fo, act, slope, h2, x1, o_in, qkv, probs, g2, vecs, masks = refs[:14]
    s1, s2, so, lo, dqkv, g1_out, stats = refs[14:21]
    big1, met1, bigo, meto, acc2 = refs[21:26]
    bufs = [refs[26 + 6 * i : 32 + 6 * i] for i in range(3)]
    g, dh2, ml, g1b, low, lsem, ssem, rsem = refs[44:]
    place = Place(line)
    per = sums_of(line)
    rows, width = g.shape
    part = rows // 4
    n1, no = s1.shape[1], so.shape[1]
    local = no
    greet(place)
    two = lambda ref: ref.at[pl.ds(2, 2)]
    ws = {
        "2": Scatter(place, ssem, rsem, None, None, acc2, s2, bufs[2], 2 * per, CUTS[3]),
        "1": Scatter(place, ssem, rsem, lambda i: big1.at[i], met1, two(big1), s1, bufs[0], 0, CUTS[2]),
        "o": Scatter(place, ssem, rsem, lambda i: bigo.at[i], meto, two(bigo), so, bufs[1], per, CUTS[1]),
    }
    trade = Trade(ssem, rsem)
    slot_of = lambda k: 3 * per + k
    mine = pltpu.make_async_copy(low.at[pl.ds(0, part)], lo.at[place.t], lsem.at[0])
    trade.step()
    trade.do(None, mine.start)
    for k in (2, 3, 1):
        trade.send(None, lambda k=k: trade.copy(
            low.at[pl.ds(k * part, part)], lo.at[place.t], slot_of(k), place.peer(k)))
    trade.step()
    trade.do(None, mine.wait)
    for k in (2, 3, 1):
        trade.wait(None, lambda k=k: lo.at[place.others[k]], slot_of(k), place.pair())
    ws["r"] = trade

    def ticks(text):
        for name in text:
            ws[name].run()

    def in_loop(i, plan):
        for at, text in plan.items():
            pl.when(i == at)(lambda text=text: ticks(text))

    start = [
        pltpu.make_async_copy(g2.at[0], acc2.at[0], lsem.at[1]),
        pltpu.make_async_copy(g2.at[1], acc2.at[1], lsem.at[2]),
        pltpu.make_async_copy(g_in, g, lsem.at[3]),
        pltpu.make_async_copy(x1, ml, lsem.at[4]),
    ]
    for c in start:
        c.start()
    start[0].wait()
    ticks("2")
    start[1].wait()
    ticks("2")
    stats[...] = jnp.zeros_like(stats)
    dh2[...] = jnp.zeros_like(dh2)
    half_block = n1 // TILE
    tiles = 4 * half_block

    def feed_forward(h2t, f1t, f2t, actt, slopet, sem):
        def place_of(j):
            q, h = j // half_block, lax.rem(j, half_block)
            block = block_of(place, q)
            return q, block, h, pl.ds(pl.multiple_of(block * n1 + h * TILE, TILE), TILE)

        def fetch(j, slot):
            cols = place_of(j)[3]
            return (
                pltpu.make_async_copy(f1.at[:, :, :, cols], f1t.at[slot], sem.at[slot]),
                pltpu.make_async_copy(f2.at[:, :, :, cols], f2t.at[slot], sem.at[2 + slot]),
                pltpu.make_async_copy(act.at[:, cols], actt.at[slot], sem.at[4 + slot]),
                pltpu.make_async_copy(slope.at[:, cols], slopet.at[slot], sem.at[6 + slot]),
            )

        load = pltpu.make_async_copy(h2, low, sem.at[8])
        load.start()
        for c in fetch(0, 0):
            c.start()
        load.wait()
        h2t[...] = low[...].T
        start[2].wait()
        start[3].wait()

        def tile(j, _):
            slot = lax.rem(j, 2)

            @pl.when(j + 1 < tiles)
            def _():
                for c in fetch(j + 1, 1 - slot):
                    c.start()

            for c in fetch(j, slot):
                c.wait()
            q, block, h, cols = place_of(j)
            at = pl.ds(pl.multiple_of(h * TILE, TILE), TILE)
            w2 = f2t[slot].reshape(width, TILE)
            du = jnp.dot(g[...], w2, preferred_element_type=F32) * slopet[slot].astype(F32)
            du = du.astype(BF)
            stats[pl.ds(block, 1), at] = jnp.sum(du.astype(F32), axis=0, keepdims=True)
            product = jnp.dot(h2t[...], du, preferred_element_type=F32).reshape(big1.shape[1:4] + (TILE,))

            @pl.when(q < 2)
            def _():
                big1[q, :, :, :, at] = product.astype(BF)

            @pl.when(q >= 2)
            def _():
                big1[q, :, :, :, at] = (product + met1[q - 2, :, :, :, at].astype(F32)).astype(BF)

            dh2[...] += lax.dot_general(
                du, f1t[slot].reshape(width, TILE), (((1,), (1,)), ((), ())), preferred_element_type=F32
            )
            ml[...] += lax.dot_general(actt[slot], w2, (((1,), (1,)), ((), ())), preferred_element_type=F32)
            in_loop(j, {
                half_block - 1: "1",
                2 * half_block - 1: "112",
                3 * half_block - 1: "11",
                4 * half_block - 1: "1",
            })
            return 0

        lax.fori_loop(0, tiles, tile, 0)

    pl.run_scoped(
        feed_forward,
        pltpu.VMEM((width, rows), BF),
        pltpu.VMEM((2,) + big1.shape[1:4] + (TILE,), BF),
        pltpu.VMEM((2,) + big1.shape[1:4] + (TILE,), BF),
        pltpu.VMEM((2, rows, TILE), BF),
        pltpu.VMEM((2, rows, TILE), BF),
        pltpu.SemaphoreType.DMA((9,)),
    )

    def second_norm(xt, sem):
        fetch = lambda i, slot: pltpu.make_async_copy(
            x1.at[pl.ds(pl.multiple_of(i * ROWS, ROWS), ROWS)], xt.at[slot], sem.at[slot])
        count = rows // ROWS
        fetch(0, 0).start()

        def some_rows(i, _):
            slot = lax.rem(i, 2)
            pl.when(i + 1 < count)(lambda: fetch(i + 1, 1 - slot).start())
            fetch(i, slot).wait()
            at = pl.ds(pl.multiple_of(i * ROWS, ROWS), ROWS)
            x = xt[slot]
            out = ml[at, :] + vecs[5:6, :]
            low[at, :] = out.astype(BF)
            m = out - x
            stats[7:8, :] += jnp.sum(m * m * masks[0, at, :1], axis=0, keepdims=True)
            unit, inv = norm_stats(x)
            up = dh2[at, :]
            stats[4:5, :] += jnp.sum(up * unit, axis=0, keepdims=True)
            stats[5:6, :] += jnp.sum(up, axis=0, keepdims=True)
            g1 = g[at, :].astype(F32) + norm_back(up, unit, inv, vecs[2:3, :])
            rounded = g1.astype(BF)
            g1b[at, :] = rounded
            stats[6:7, :] += jnp.sum(rounded.astype(F32), axis=0, keepdims=True)
            dh2[at, :] = g1
            return 0

        lax.fori_loop(0, count, some_rows, 0)

    pl.run_scoped(second_norm, pltpu.VMEM((2, ROWS, width), F32), pltpu.SemaphoreType.DMA((3,)))
    save_g1 = pltpu.make_async_copy(dh2, g1_out, lsem.at[1])
    save_g1.start()
    ticks("r")

    def heads(g1t, o, wov, do, pt, qt, out, sem):
        load_o = pltpu.make_async_copy(o_in, o, sem.at[0])
        load_w = pltpu.make_async_copy(fo, wov, sem.at[1])
        load_o.start()
        load_w.start()
        pairs = width // 128

        def fetch(i, slot):
            base = (i // 2) * 3 * local + lax.rem(i, 2) * 128
            return [
                pltpu.make_async_copy(
                    qkv.at[:, pl.ds(pl.multiple_of(base + j * local, 128), 128)], qt.at[slot, j], sem.at[2 + 2 * j + slot])
                for j in range(3)
            ]

        head = lambda i, h: pltpu.make_async_copy(probs.at[i, h], pt.at[h], sem.at[8 + h])
        for c in fetch(0, 0) + [head(0, 0), head(0, 1)]:
            c.start()
        g1t[...] = g1b[...].T
        load_o.wait()
        load_w.wait()

        def output_weight(q, _):
            block = block_of(place, q)
            cols = pl.ds(pl.multiple_of(block * no, 128), no)
            product = jnp.dot(g1t[...], o[:, cols], preferred_element_type=F32).reshape(bigo.shape[1:])

            @pl.when(q < 2)
            def _():
                bigo[q] = product.astype(BF)

            @pl.when(q >= 2)
            def _():
                bigo[q] = (product + meto[q - 2].astype(F32)).astype(BF)

            in_loop(q, {0: "o", 1: "oo", 2: "oo", 3: "o"})
            return 0

        lax.fori_loop(0, 4, output_weight, 0)
        do[...] = jnp.dot(g1b[...], wov[...].reshape(width, width), preferred_element_type=F32).astype(BF)

        def save(i, slot):
            base = (i // 2) * 3 * local + lax.rem(i, 2) * 128
            return [
                pltpu.make_async_copy(
                    out.at[slot, j], dqkv.at[:, pl.ds(pl.multiple_of(base + j * local, 128), 128)], sem.at[10 + 2 * j + slot])
                for j in range(3)
            ]

        def pair_step(i, _):
            slot = lax.rem(i, 2)

            @pl.when(i + 1 < pairs)
            def _():
                for c in fetch(i + 1, 1 - slot):
                    c.start()

            @pl.when(i >= 2)
            def _():
                for c in save(i - 2, slot):
                    c.wait()

            for c in fetch(i, slot) + [head(i, 0), head(i, 1)]:
                c.wait()
            cols = pl.ds(pl.multiple_of(i * 128, 128), 128)
            got = heads_backward(qt[slot, 0], qt[slot, 1], qt[slot, 2], o[:, cols], do[:, cols], lambda h: pt[h])
            for j in range(3):
                out[slot, j] = got[j]

            @pl.when(i + 1 < pairs)
            def _():
                for h in range(2):
                    head(i + 1, h).start()

            for c in save(i, slot):
                c.start()
            in_loop(i, {0: "2", 1: "2", 2: "1", 3: "2", 4: "o", 5: "2", 6: "1", 7: "2o"})
            return 0

        lax.fori_loop(0, pairs, pair_step, 0)
        for i in (pairs - 2, pairs - 1):
            for c in save(i, i % 2):
                c.wait()

    pl.run_scoped(
        heads,
        pltpu.VMEM((width, rows), BF),
        pltpu.VMEM((rows, width), BF),
        pltpu.VMEM(fo.shape, BF),
        pltpu.VMEM((rows, width), BF),
        pltpu.VMEM((2, rows, rows), BF),
        pltpu.VMEM((2, 3, rows, 128), BF),
        pltpu.VMEM((2, 3, rows, 128), BF),
        pltpu.SemaphoreType.DMA((16,)),
    )
    ticks("1o1o1o1or")
    save_g1.wait()
    for script in ws.values():
        script.finish()


def middle(line, g, f1, f2, fo, act, slope, h2, x1, o, qkv, probs, g2, vecs, masks):
    rows, width = g.shape
    part = rows // 4
    depth = f1.shape[2]
    n1, no = f1.shape[3] // 4, fo.shape[3] // 4
    hbm, vmem = pl.BlockSpec(memory_space=pl.ANY), pl.BlockSpec(memory_space=pltpu.VMEM)
    sds = jax.ShapeDtypeStruct
    block = lambda count, n: pltpu.VMEM((count, line, 2, depth, n), BF)
    count = 3 * sums_of(line) + 4
    return pl.pallas_call(
        functools.partial(middle_kernel, line),
        out_shape=[
            sds((depth, n1), F32),
            sds((depth, n1), F32),
            sds((depth, no), F32),
            sds((4, part, width), BF),
            sds((rows, 3 * width), BF),
            sds((rows, width), F32),
            sds((8, width), F32),
        ],
        in_specs=[hbm] * 12 + [vmem] * 2,
        out_specs=[vmem] * 3 + [hbm] * 3 + [vmem],
        scratch_shapes=[
            block(4, n1),
            block(2, n1),
            block(4, no),
            block(2, no),
            block(2, n1),
            *landing(line, depth, n1, CUTS[2]),
            *landing(line, depth, no, CUTS[1]),
            *landing(line, depth, n1, CUTS[3]),
            pltpu.VMEM((rows, width), BF),
            pltpu.VMEM((rows, width), F32),
            pltpu.VMEM((rows, width), F32),
            pltpu.VMEM((rows, width), BF),
            pltpu.VMEM((rows, width), BF),
            pltpu.SemaphoreType.DMA((5,)),
            pltpu.SemaphoreType.DMA((count,)),
            pltpu.SemaphoreType.DMA((count,)),
        ],
        compiler_params=pltpu.CompilerParams(collective_id=1, has_side_effects=True, vmem_limit_bytes=63 * MIB),
        name="middle",
    )(g, f1, f2, fo, act, slope, h2, x1, o, qkv, probs, g2, vecs, masks)


def first_kernel(line, *refs):
    xin, h1, dqkv, fq, g1_in, vecs, small = refs[:7]
    sq, gtok, sm = refs[7:10]
    big, met = refs[10:12]
    bufs = refs[12:18]
    x, ht, dv, wqv, dh1, g1, low, here, cold, colx, coly, lsem, ssem, rsem = refs[18:]
    place = Place(line)
    per = sums_of(line)
    rows, width = x.shape
    part = rows // 4
    n = sq.shape[1]
    local = n // 3
    greet(place, whole_line=True)
    total = Scatter(place, ssem, rsem, lambda i: big.at[i], met, big.at[pl.ds(2, 2)], sq, bufs, 0, CUTS[0])
    trade = Trade(ssem, rsem)
    slot_of = lambda k: per + k
    mine = pltpu.make_async_copy(low.at[pl.ds(0, part)], gtok.at[place.t], lsem.at[0])
    trade.step()
    trade.do(None, mine.start)
    for k in (2, 3, 1):
        trade.send(None, lambda k=k: trade.copy(
            low.at[pl.ds(k * part, part)], gtok.at[place.t], slot_of(k), place.peer(k)))
    trade.step()
    trade.do(None, mine.wait)
    for k in (2, 3, 1):
        trade.wait(None, lambda k=k: gtok.at[place.others[k]], slot_of(k), place.pair())
    base = per + 4
    few = Trade(ssem, rsem)
    hops = ((cold, place.peer(1)), (colx, place.pair()), (coly, place.peer(2)))

    def fold(i, land):
        here[i + 1] = here[i] + land[...]

    few.step()
    for i, (land, device) in enumerate(hops):
        few.send(None, lambda i=i, land=land, device=device: few.copy(here.at[i], land, base + i, device))
        few.step()
        few.wait(None, lambda land=land: land, base + i, place.pair())
        few.do(None, lambda i=i, land=land: fold(i, land))
    for k in range(1, line):
        far = lax.rem(place.a + k, line)
        few.send(None, lambda far=far, k=k: few.copy(
            here.at[3], sm.at[k], base + 3 + k, place.at(far, place.b, place.t)))

    def keep():
        sm[0] = here[3]

    few.do(None, keep)
    few.step()
    for k in range(1, line):
        few.wait(None, lambda k=k: sm.at[k], base + 3 + k, place.pair())

    block_cols = lambda q: pl.ds(pl.multiple_of(block_of(place, q) * n, 128), n)
    load_h = pltpu.make_async_copy(h1, low, lsem.at[1])
    load_h.start()
    load_d = lambda q: pltpu.make_async_copy(dqkv.at[:, block_cols(q)], dv.at[q], lsem.at[4 + q])
    load_w = lambda q: pltpu.make_async_copy(fq.at[:, :, :, block_cols(q)], wqv.at[q], lsem.at[8 + q])
    for q in range(4):
        load_d(q).start()
    for q in range(4):
        load_w(q).start()
    load_x = [pltpu.make_async_copy(xin.at[k], x.at[pl.ds(k * part, part)], lsem.at[12 + k]) for k in range(4)]
    load_g = pltpu.make_async_copy(g1_in, g1, lsem.at[2])
    for c in load_x + [load_g]:
        c.start()
    here[0] = small[...]
    load_h.wait()
    ht[...] = low[...].T

    def weight(q, _):
        load_d(q).wait()
        got = dv[q]
        product = jnp.dot(ht[...], got, preferred_element_type=F32).reshape(big.shape[1:])
        sums = jnp.sum(got.astype(F32), axis=0, keepdims=True)
        cols = pl.ds(pl.multiple_of(block_of(place, q) * local, 128), local)
        here[0, 14:15, cols] = sums[:, :local]
        here[0, 15:16, cols] = sums[:, 2 * local :]

        @pl.when(q < 2)
        def _():
            big[q] = product.astype(BF)

        @pl.when(q >= 2)
        def _():
            big[q] = (product + met[q - 2].astype(F32)).astype(BF)

        for at, count in {0: 1, 1: 2, 2: 2, 3: 1}.items():
            pl.when(q == at)(lambda count=count: total.run(count))
        return 0

    lax.fori_loop(0, 4, weight, 0)

    def back(q, _):
        load_w(q).wait()
        product = lax.dot_general(
            dv[q], wqv[q].reshape(width, n), (((1,), (1,)), ((), ())), preferred_element_type=F32
        )

        @pl.when(q == 0)
        def _():
            dh1[...] = product

        @pl.when(q > 0)
        def _():
            dh1[...] += product

        pl.when(q == 2)(lambda: total.run())
        return 0

    lax.fori_loop(0, 4, back, 0)
    for c in load_x + [load_g]:
        c.wait()
    here[0, 12:14, :] = jnp.zeros((2, width), F32)

    def some_rows(i, _):
        at = pl.ds(pl.multiple_of(i * ROWS, ROWS), ROWS)
        unit, inv = norm_stats(x[at, :].astype(F32))
        up = dh1[at, :]
        here[0, 12:13, :] += jnp.sum(up * unit, axis=0, keepdims=True)
        here[0, 13:14, :] += jnp.sum(up, axis=0, keepdims=True)
        low[at, :] = (g1[at, :] + norm_back(up, unit, inv, vecs[0:1, :])).astype(BF)
        return 0

    lax.fori_loop(0, rows // ROWS, some_rows, 0)
    few.run()
    trade.run()
    few.run()
    total.run()
    few.run()
    total.run()
    few.run()
    total.run()
    few.run()
    total.run()
    total.run()
    trade.run()
    for script in (total, trade, few):
        script.finish()


def first(line, xin, h1, dqkv, fq, g1, vecs, small):
    rows, width = h1.shape
    part = rows // 4
    depth = fq.shape[2]
    n = fq.shape[3] // 4
    hbm, vmem = pl.BlockSpec(memory_space=pl.ANY), pl.BlockSpec(memory_space=pltpu.VMEM)
    sds = jax.ShapeDtypeStruct
    block = lambda count: pltpu.VMEM((count, line, 2, depth, n), BF)
    count = sums_of(line) + 4 + 3 + line
    few = small.shape
    return pl.pallas_call(
        functools.partial(first_kernel, line),
        out_shape=[sds((depth, n), F32), sds((4, part, width), BF), sds((line,) + few, F32)],
        in_specs=[hbm] * 5 + [vmem] * 2,
        out_specs=[vmem, hbm, vmem],
        scratch_shapes=[
            block(4),
            block(2),
            *landing(line, depth, n, CUTS[0]),
            pltpu.VMEM((rows, width), BF),
            pltpu.VMEM((width, rows), BF),
            pltpu.VMEM((4, rows, n), BF),
            pltpu.VMEM((4, line, 2, depth, n), BF),
            pltpu.VMEM((rows, width), F32),
            pltpu.VMEM((rows, width), F32),
            pltpu.VMEM((rows, width), BF),
            pltpu.VMEM((4,) + few, F32),
            pltpu.VMEM(few, F32),
            pltpu.VMEM(few, F32),
            pltpu.VMEM(few, F32),
            pltpu.SemaphoreType.DMA((16,)),
            pltpu.SemaphoreType.DMA((count,)),
            pltpu.SemaphoreType.DMA((count,)),
        ],
        compiler_params=pltpu.CompilerParams(collective_id=2, has_side_effects=True, vmem_limit_bytes=60 * MIB),
        name="first",
    )(xin, h1, dqkv, fq, g1, vecs, small)


def shards(
    tokens, token_mask, out_grad, ln1_gain, ln1_bias, w_qkv, b_qv, w_out, b_out,
    ln2_gain, ln2_bias, w_fc1, b_fc1, w_fc2, b_fc2,
):
    images, tok_rows, width = tokens.shape
    parts = lax.axis_size("tensor")
    line = lax.axis_size("dp") // 2
    t = lax.axis_index("tensor")
    depth, _, local = w_qkv.shape
    rows = tok_rows * parts

    small = jnp.zeros((8, w_fc1.shape[1]), F32).at[0].set(b_fc1).at[1, : 2 * local].set(b_qv.reshape(-1))
    vecs = jnp.stack([ln1_gain, ln1_bias, ln2_gain, ln2_bias, b_out, b_fc2, b_out, b_out])
    own = lax.dynamic_index_in_dim(token_mask, t, 0, keepdims=False).reshape(parts, tok_rows)
    y, c = t // 2, lax.rem(t, 2)
    others = [t, y * 2 + 1 - c, (1 - y) * 2 + c, (1 - y) * 2 + 1 - c]
    mask = jnp.concatenate([lax.dynamic_index_in_dim(own, o, 0, keepdims=False) for o in others])
    allow = jnp.where(jnp.max(mask) > 0, mask, 1).astype(F32)
    masks = jnp.broadcast_to(jnp.stack([mask.astype(F32), allow])[:, :, None], (2, rows, 128))
    xin, _, fq, fo, f1, f2, qkv, probs, o, x1, h2, act, slope, g2, h1, g, stats = forward(
        line, tokens, out_grad, small, w_qkv.reshape(depth, 3 * local), w_out.T, w_fc1, w_fc2.T, vecs, masks
    )
    sum_1, sum_2, sum_o, layer_out, dqkv, g1, more = middle(
        line, g, f1, f2, fo, act, slope, h2, x1, o, qkv, probs, g2, vecs, masks
    )
    few = jnp.concatenate([stats[:4], more, jnp.zeros((4, width), F32)])
    sum_q, grad_tokens, sm = first(line, xin, h1, dqkv, fq, g1, vecs, few)
    sums = jnp.sum(sm, axis=0)
    squares = jnp.stack([jnp.sum(sums[0]), jnp.sum(sums[1]), jnp.sum(sums[11])])
    pick = lambda v: lax.dynamic_slice_in_dim(v, t * local, local, 0)
    return (
        layer_out,
        grad_tokens,
        sums[12],
        sums[13],
        sum_q.reshape(depth, 3, local),
        jnp.stack([pick(sums[14]), pick(sums[15])]),
        sum_o.T,
        sums[10],
        sums[8],
        sums[9],
        sum_1,
        lax.dynamic_index_in_dim(sums[4:8], t, 0, keepdims=False),
        sum_2.T,
        sums[3],
        jnp.sqrt(squares / (sums[2, 0] * width)),
    )


def solution(mesh):
    rowwise = P("dp", "tensor", None)
    placed = (
        rowwise, P("dp", None), rowwise, P(), P(), P("dp", None, "tensor"), P(None, "tensor"), P("tensor", "dp"),
        P(), P(), P(), P("dp", "tensor"), P("tensor"), P("tensor", "dp"), P(),
    )
    return jax.shard_map(
        shards,
        mesh=mesh,
        in_specs=placed,
        out_specs=(
            rowwise, rowwise, P(), P(), P("dp", None, "tensor"), P(None, "tensor"), P("tensor", "dp"), P(),
            P(), P(), P("dp", "tensor"), P("tensor"), P("tensor", "dp"), P(), P(),
        ),
        check_vma=False,
    )
```

```python
import functools

import jax
import jax.numpy as jnp
from jax import lax
from jax.experimental import pallas as pl
from jax.experimental.pallas import tpu as pltpu
from jax.sharding import PartitionSpec as P

HD = 64
MESH = pl.DeviceIdType.MESH
BF = jnp.bfloat16
F32 = jnp.float32
ROWS = 64
TILE = 512
MIB = 1024 * 1024


class Place:
    def __init__(self, line):
        self.line = line
        self.d = lax.axis_index("dp")
        self.t = lax.axis_index("tensor")
        self.a = self.d // 2
        self.b = lax.rem(self.d, 2)
        y, c = self.t // 2, lax.rem(self.t, 2)
        self.others = (self.t, y * 2 + 1 - c, (1 - y) * 2 + c, (1 - y) * 2 + 1 - c)
        self.low, self.high = self.a > 0, self.a < line - 1
        self.inner = jnp.logical_and(self.low, self.high)

    def at(self, a, b, t):
        return (a * 2 + b, t)

    def pair(self):
        return self.at(self.a, 1 - self.b, self.t)

    def peer(self, k):
        return (self.d, self.others[k])

    def up(self):
        return self.at(self.a + 1, self.b, self.t)

    def down(self):
        return self.at(self.a - 1, self.b, self.t)


def greet(place, whole_line=False):
    barrier = pltpu.get_barrier_semaphore()

    def hail(device):
        pl.semaphore_signal(barrier, inc=1, device_id=device, device_id_type=MESH)

    line = place.line
    hail(place.pair())
    for k in range(1, 4):
        hail(place.peer(k))
    if whole_line:
        for k in range(1, line):
            hail(place.at(lax.rem(place.a + k, line), place.b, place.t))
        pl.semaphore_wait(barrier, 3 + line)
        return
    pl.when(place.low)(lambda: hail(place.down()))
    pl.when(place.high)(lambda: hail(place.up()))
    pl.when(place.inner)(lambda: pl.semaphore_wait(barrier, 6))
    pl.when(jnp.logical_not(place.inner))(lambda: pl.semaphore_wait(barrier, 5))


def both(p, q):
    if p is None:
        return q
    if q is None:
        return p
    return jnp.logical_and(p, q)


def when(pred, act):
    if pred is None:
        act()
    else:
        pl.when(pred)(act)


class Script:
    def __init__(self, ssem, rsem):
        self.ssem, self.rsem = ssem, rsem
        self.sent = []
        self.steps = []

    def copy(self, src, dst, slot, device):
        return pltpu.make_async_remote_copy(
            src_ref=src,
            dst_ref=dst,
            send_sem=self.ssem.at[slot],
            recv_sem=self.rsem.at[slot],
            device_id=device,
            device_id_type=MESH,
        )

    def step(self):
        self.steps.append([])

    def do(self, pred, act):
        self.steps[-1].append((pred, act))

    def send(self, pred, make):
        self.do(pred, lambda: make().start())
        self.sent.append((pred, make))

    def wait(self, pred, ref, slot, device):
        self.do(pred, lambda: self.copy(ref(), ref(), slot, device).wait_recv())

    def run(self, count=1):
        for _ in range(count):
            for pred, act in self.steps.pop(0):
                when(pred, act)

    def wait_sent(self, count):
        for pred, make in self.sent[:count]:
            when(pred, lambda make=make: make().wait_send())
        self.sent = self.sent[count:]

    def finish(self):
        assert not self.steps
        for pred, make in self.sent:
            when(pred, lambda make=make: make().wait_send())


def thirds(line):
    return [1], [2] if line > 2 else [], list(range(3, line))


def order(place):
    yield None, place.a
    for k in range(1, place.line):
        yield place.a >= k, place.a - k
        yield place.a + k <= place.line - 1, place.a + k


class Gather(Script):
    def __init__(self, place, ssem, rsem, local_sem, shard, whole, base, cut, by_line):
        super().__init__(ssem, rsem)
        self.p = place
        self.shard, self.whole = shard, whole
        self.n = shard.shape[1]
        self.base, self.cut = base, cut
        p = place
        t2 = p.others[2]
        local = pltpu.make_async_copy(shard, self.block(p.a, p.b, p.t), local_sem)
        own = lambda: self.shard
        groups = thirds(p.line)

        def line_step(group):
            for k in group:
                self.receive(k, 0, p.b, p.t, True)

        self.step()
        self.pass_line(None, p.a, 1, True, own, 0, p.b, p.t)
        self.pass_line(None, p.a, 1, False, own, 0, p.b, p.t)
        self.spread(None, p.a, own)
        self.do(None, local.start)
        self.step()
        line_step(groups[0])
        if by_line:
            self.step()
            self.cross([(None, p.a)])
            self.step()
            line_step(groups[1])
            self.step()
            self.landed([(None, p.a)])
            diagonal = lambda: self.block(p.a, 1 - p.b, t2)
            self.pass_line(None, p.a, 1, True, diagonal, 7, 1 - p.b, t2)
            self.pass_line(None, p.a, 1, False, diagonal, 7, 1 - p.b, t2)
            self.step()
            line_step(groups[2])
            for group in groups:
                self.step()
                for k in group:
                    self.receive(k, 7, 1 - p.b, t2, False)
            self.step()
            self.settle([i for i in order(p)][1:])
        else:
            for group in groups[1:]:
                self.step()
                line_step(group)
            self.step()
            self.cross(list(order(p)))
            self.step()
        self.do(None, local.wait)
        self.core((0, 1, 2))
        self.step()
        if not by_line:
            self.landed(list(order(p)))
        self.core((3,))
        self.step()
        self.arrive()

    def block(self, a, b, t, lo=0, hi=None):
        hi = self.n if hi is None else hi
        start = pl.multiple_of(t * self.n + lo, 128)
        return self.whole.at[a, b, :, pl.ds(start, hi - lo)]

    def plane(self, b, t):
        start = pl.multiple_of(t * self.n, 128)
        return self.whole.at[:, b, :, pl.ds(start, self.n)]

    def slot(self, kind, i):
        return self.base + kind * max(self.p.line, 4) + i

    def spread(self, pred, a, src):
        p = self.p
        self.send(pred, lambda: self.copy(src(), self.block(a, p.b, p.t), self.slot(2, a), p.pair()))
        self.send(pred, lambda: self.copy(src(), self.block(a, p.b, p.t), self.slot(3, a), p.peer(2)))

    def pass_line(self, pred, a, step, up, src, kind, b, t):
        p = self.p
        if step > p.line - 1:
            return
        ok = both(pred, p.high if up else p.low)
        to = p.up if up else p.down
        slot = self.slot(kind if up else kind + 1, step)
        self.send(ok, lambda: self.copy(src(), self.block(a, b, t), slot, to()))

    def receive(self, k, kind, b, t, spread):
        p = self.p
        for up in (True, False):
            chunk = p.a - k if up else p.a + k
            pred = p.a >= k if up else p.a + k <= p.line - 1
            src = lambda chunk=chunk: self.block(chunk, b, t)
            self.wait(pred, src, self.slot(kind if up else kind + 1, k), p.pair())
            self.pass_line(pred, chunk, k + 1, up, src, kind, b, t)
            if spread:
                self.spread(pred, chunk, src)

    def settle(self, chunks):
        p = self.p
        for pred, a in chunks:
            self.wait(pred, lambda a=a: self.block(a, 1 - p.b, p.t), self.slot(2, a), p.pair())
            self.wait(pred, lambda a=a: self.block(a, p.b, p.others[2]), self.slot(3, a), p.pair())

    def cross(self, chunks):
        p, t2 = self.p, self.p.others[2]
        for pred, a in chunks:
            self.settle([(pred, a)])
            one = lambda a=a: self.block(a, 1 - p.b, p.t, 0, self.cut)
            two = lambda a=a: self.block(a, p.b, t2, self.cut, self.n)
            if self.cut > 0:
                self.send(pred, lambda a=a, one=one: self.copy(one(), one(), self.slot(4, a), p.peer(2)))
            if self.cut < self.n:
                self.send(pred, lambda a=a, two=two: self.copy(two(), two(), self.slot(5, a), p.pair()))

    def planes(self, far):
        p = self.p
        t, t2 = (p.others[1], p.others[3]) if far else (p.t, p.others[2])
        return ((p.b, t), (1 - p.b, t), (p.b, t2), (1 - p.b, t2))

    def core(self, which):
        for j in which:
            b, t = self.planes(False)[j]
            src = lambda b=b, t=t: self.plane(b, t)
            self.send(None, lambda j=j, src=src: self.copy(src(), src(), self.slot(6, j), self.p.peer(1)))

    def landed(self, chunks):
        p, t2 = self.p, self.p.others[2]
        for pred, a in chunks:
            if self.cut > 0:
                self.wait(pred, lambda a=a: self.block(a, 1 - p.b, t2, 0, self.cut), self.slot(4, a), p.pair())
            if self.cut < self.n:
                self.wait(pred, lambda a=a: self.block(a, 1 - p.b, t2, self.cut, self.n), self.slot(5, a), p.pair())

    def arrive(self):
        for j, (b, t) in enumerate(self.planes(True)):
            self.wait(None, lambda b=b, t=t: self.plane(b, t), self.slot(6, j), self.p.pair())


GATHER_CUTS = (256, 0, 0, 0)
BY_LINE = (False, True, True, True)
CUTS = (256, 128, 384, 384)


def slots_of(line):
    return 9 * max(line, 4)


def add_into(dst, *others):
    rows = dst.shape[0]
    step = min(rows, 32)

    def body(i, _):
        at = pl.ds(pl.multiple_of(i * step, step), step)
        total = dst[at, :]
        for other in others:
            total = total + other[at, :]
        dst[at, :] = total
        return 0

    lax.fori_loop(0, rows // step, body, 0)


def block_of(place, q):
    y, c = place.t // 2, lax.rem(place.t, 2)
    return lax.rem(y + 1 + q, 2) * 2 + lax.rem(c + 1 - q // 2, 2)


class Scatter(Script):
    def __init__(
        self, place, ssem, rsem, far, met, acc, out, bufs, base, cut, before_cross=None, before_line=None, release=None
    ):
        super().__init__(ssem, rsem)
        self.p = place
        self.acc, self.out = acc, out
        self.rdx, self.rdy, self.rx, self.ry, self.near = bufs
        self.n = out.shape[1]
        self.base, self.cut = base, cut
        self.own = lambda *at: acc.at[(1, at[0], place.b) + at[1:]]
        self.by_pair = lambda *at: acc.at[(1, at[0], 1 - place.b) + at[1:]]
        self.by_y = lambda *at: acc.at[(0, at[0], place.b) + at[1:]]
        self.by_both = lambda *at: acc.at[(0, at[0], 1 - place.b) + at[1:]]
        if far is not None:
            for i in range(2):
                self.step()
                self.send(None, lambda i=i: self.copy(far(i), met.at[i], base + i, place.peer(1)))
            for i in range(2):
                self.step()
                self.wait(None, lambda i=i: met.at[i], base + i, place.pair())
        every, first, late = slice(None), pl.ds(0, cut), pl.ds(cut, self.n - cut)
        pair, y = place.pair(), place.peer(2)
        lines = range(place.line)

        def give(src, dst, slot, device):
            self.send(None, lambda: self.copy(src(), dst(), base + slot, device))

        def take(ref, slot):
            self.wait(None, ref, base + slot, pair)

        def add(dst, *others):
            for a in lines:
                self.do(None, lambda a=a: add_into(dst(a), *[other(a) for other in others]))

        some, rest = cut > 0, cut < self.n
        self.step()
        if before_cross is not None:
            before_cross(self)
        if some:
            give(lambda: self.by_both(every, every, first), lambda: self.rdy, 4, y)
        if rest:
            give(lambda: self.by_both(every, every, late), lambda: self.rdx, 5, pair)
        if some:
            give(lambda: self.by_y(every, every, first), lambda: self.ry.at[:, :, first], 7, y)
        self.step()
        if rest:
            give(lambda: self.by_pair(every, every, late), lambda: self.rx.at[:, :, late], 6, pair)
        self.step()
        if some:
            take(lambda: self.rdy, 4)
            add(lambda a: self.by_pair(a, every, first), lambda a: self.rdy.at[a])
            give(lambda: self.by_pair(every, every, first), lambda: self.rx.at[:, :, first], 8, pair)
        self.step()
        if rest:
            take(lambda: self.rdx, 5)
            add(lambda a: self.by_y(a, every, late), lambda a: self.rdx.at[a])
            give(lambda: self.by_y(every, every, late), lambda: self.ry.at[:, :, late], 9, y)
        self.step()
        if rest:
            take(lambda: self.rx.at[:, :, late], 6)
        if some:
            take(lambda: self.ry.at[:, :, first], 7)
            take(lambda: self.rx.at[:, :, first], 8)
        if rest:
            take(lambda: self.ry.at[:, :, late], 9)
        if before_line is not None:
            before_line(self)
        for pred, chunk in reversed(list(order(place))[1:]):
            self.do(pred, lambda chunk=chunk: add_into(self.own(chunk), self.rx.at[chunk], self.ry.at[chunk]))
            self.send(pred, lambda chunk=chunk: self.copy(
                self.own(chunk), self.near.at[place.a], base + 10 + place.a, place.at(chunk, place.b, place.t)))
        self.do(None, lambda: add_into(self.own(place.a), self.rx.at[place.a], self.ry.at[place.a]))
        self.step()
        for pred, a in list(order(place))[1:]:
            self.wait(pred, lambda a=a: self.near.at[a], base + 10 + a, pair)
        self.do(None, self.close)
        if release is not None:
            sent, self.sent = self.sent, []
            for pred, make in sent:
                self.do(pred, lambda make=make: make().wait_send())
            release(self)

    def close(self):
        p = self.p
        rows = self.out.shape[0]
        step = min(rows, 16)

        def body(i, _):
            at = pl.ds(pl.multiple_of(i * step, step), step)
            value = self.acc[1, p.a, p.b, at, :].astype(F32)
            for k in range(1, p.line):
                value = value + self.near[lax.rem(p.a + k, p.line), at, :].astype(F32)
            self.out[at, :] = value
            return 0

        lax.fori_loop(0, rows // step, body, 0)


def landing(line, depth, n, cut):
    return [
        pltpu.VMEM((line, depth, max(n - cut, 128)), BF),
        pltpu.VMEM((line, depth, max(cut, 128)), BF),
        pltpu.VMEM((line, depth, n), BF),
        pltpu.VMEM((line, depth, n), BF),
        pltpu.VMEM((line, depth, n), BF),
    ]


def sums_of(line):
    return 10 + line


class Trade(Script):
    pass


def heads_forward(q, k, v, allowed, keep):
    lane = lax.broadcasted_iota(jnp.int32, k.shape, 1)
    outs = []
    for h in range(2):
        mine = (lane // HD) == h
        scores = lax.dot_general(
            jnp.where(mine, k, jnp.zeros_like(k)), q, (((1,), (1,)), ((), ())), preferred_element_type=F32
        )
        scores = jnp.where(allowed, scores, -1e30)
        expo = jnp.exp(scores - jnp.max(scores, axis=0, keepdims=True))
        probs = (expo * (1.0 / jnp.sum(expo, axis=0, keepdims=True))).astype(BF)
        keep(h, probs)
        outs.append(
            lax.dot_general(v[:, h * HD : (h + 1) * HD], probs, (((0,), (0,)), ((), ())), preferred_element_type=F32)
        )
    return jnp.concatenate(outs, axis=0).T.astype(BF)


def norm_stats(values):
    row_mean = jnp.mean(values, axis=-1, keepdims=True)
    centred = values - row_mean
    variance = jnp.mean(centred * centred, axis=-1, keepdims=True)
    inv_std = lax.rsqrt(variance + 1e-05)
    return centred * inv_std, inv_std


class Schedule:
    def __init__(self, text, scripts):
        self.after = {}
        at = ("", 0)
        counts = {}
        for ch in "".join(text):
            if ch.isupper():
                at = (ch, counts.get(ch, 0))
                counts[ch] = at[1] + 1
            else:
                self.after.setdefault(at, []).extend(scripts[ch].steps.pop(0))

    def run(self, name="", i=0):
        for pred, act in self.after.pop((name, i), ()):
            when(pred, act)

    def run_at(self, name, i):
        for at in sorted(k for n, k in self.after if n == name):
            pl.when(i == at)(lambda at=at: self.run(name, at))


FORWARD = ("01020r002r101rL12031021P1PP2P2H3", "HH2HrH11123H13H22H3G12O332F3FcF3", "33FccFFcFF3")
BACKWARD = ("G2TT12TT11T2T211TTNUU1ooo2oUUDAA", "1W1AAW2qqoAAqWoAqqAooWq1qEEEqEoM", "YYYYsYYY1YqZfffrofrsqf")


def forward_kernel(line, *refs):
    toks, grads, small, wq, wo, w1, w2, vecs, masks = refs[:9]
    xin, gin, fq, fo, f1, f2, qkv_out, p_out, o_out, x1_out, h2_out, act_out, slope_out, g2_out, h1_out, g_out, stats = refs[9:26]
    (sml, xv, gv, gt, h1, wqv, wov, w1v, qkv, pbuf, o, x1, h2, actb, slopeb, g2b, far, met, lsem, csem, ssem, rsem) = refs[26:]
    place = Place(line)
    per = slots_of(line)
    rows, width = xv.shape
    part = toks.shape[1]
    third = wqv.shape[-1]
    local = third // 3
    greet(place)
    ws = [
        Gather(place, ssem, rsem, lsem.at[i], shard, whole, i * per, GATHER_CUTS[i], BY_LINE[i])
        for i, (shard, whole) in enumerate(((wq, fq), (wo, fo), (w1, f1), (w2, f2)))
    ]
    trade = Trade(ssem, rsem)
    slot_of = lambda j, k: 4 * per + j * 4 + k
    pairs_of_rows = ((toks, xin), (grads, gin))
    mine = [pltpu.make_async_copy(src.at[place.t], dst.at[0], lsem.at[4 + j]) for j, (src, dst) in enumerate(pairs_of_rows)]
    mine.append(pltpu.make_async_copy(small, sml.at[place.t], lsem.at[6]))
    for j, (src, dst) in enumerate(pairs_of_rows):
        trade.step()
        trade.do(None, mine[j].start)
        for k in (2, 3, 1):
            trade.send(None, lambda src=src, dst=dst, j=j, k=k: trade.copy(
                src.at[place.others[k]], dst.at[k], slot_of(j, k), place.peer(k)))
        if j == 0:
            trade.do(None, mine[2].start)
            for k in (2, 3, 1):
                trade.send(None, lambda k=k: trade.copy(small, sml.at[place.t], slot_of(2, k), place.peer(k)))
    for j, (src, dst) in enumerate(pairs_of_rows):
        trade.step()
        trade.do(None, mine[j].wait)
        for k in (2, 3, 1):
            trade.wait(None, lambda dst=dst, k=k: dst.at[k], slot_of(j, k), place.pair())
        if j == 0:
            trade.do(None, mine[2].wait)
            for k in (2, 3, 1):
                trade.wait(None, lambda k=k: sml.at[place.others[k]], slot_of(2, k), place.pair())

    core = Script(ssem, rsem)
    for i in range(2):
        core.step()
        core.send(None, lambda i=i: core.copy(far.at[i], met.at[i], 4 * per + 12 + i, place.peer(1)))
    for i in range(2):
        core.step()
        core.wait(None, lambda i=i: met.at[i], 4 * per + 12 + i, place.pair())
    plan = Schedule(FORWARD, {"r": trade, "c": core, **{str(i): w for i, w in enumerate(ws)}})

    def fetch_rows(src, dst, first):
        copies = [
            pltpu.make_async_copy(src.at[k], dst.at[pl.ds(k * part, part)], csem.at[first + k]) for k in range(4)
        ]
        for c in copies:
            c.start()
        return copies

    plan.run()
    fetch_x = fetch_rows(xin, xv, 0)
    for f in fetch_x:
        f.wait()
    stats[...] = jnp.zeros_like(stats)

    def first_norm(i, _):
        at = pl.ds(pl.multiple_of(i * ROWS, ROWS), ROWS)
        x = xv[at, :].astype(F32)
        unit, _inv = norm_stats(x)
        h1[at, :] = (unit * vecs[0:1, :] + vecs[1:2, :]).astype(BF)
        real = masks[0, at, :1]
        stats[0:1, :] += jnp.sum(x * x * real, axis=0, keepdims=True)
        stats[2:3, :] += jnp.broadcast_to(jnp.sum(real, axis=0, keepdims=True), (1, width))
        return 0

    lax.fori_loop(0, rows // ROWS, first_norm, 0)
    save_h1 = pltpu.make_async_copy(h1, h1_out, csem.at[20])
    save_h1.start()
    plan.run("L")
    fetch_q = lambda t: pltpu.make_async_copy(
        fq.at[:, :, :, pl.ds(pl.multiple_of(t * third, 128), third)], wqv.at[t], csem.at[8 + t])
    for t in range(4):
        fetch_q(t).start()
    def project(t, _):
        fetch_q(t).wait()
        got = jnp.dot(h1[...], wqv[t].reshape(width, third), preferred_element_type=F32)
        cols = [pl.ds(pl.multiple_of(t * third + j * local, 128), local) for j in range(3)]
        qkv[:, cols[0]] = (got[:, :local] + sml[t, 1:2, :local]).astype(BF) * jnp.asarray(HD ** (-0.5), BF)
        qkv[:, cols[1]] = got[:, local : 2 * local].astype(BF)
        qkv[:, cols[2]] = (got[:, 2 * local :] + sml[t, 1:2, local : 2 * local]).astype(BF)
        plan.run_at("P", t)
        return 0

    lax.fori_loop(0, 4, project, 0)
    save_qkv = pltpu.make_async_copy(qkv, qkv_out, csem.at[0])
    save_qkv.start()
    allowed = masks[1, :, :1] > 0
    pairs = qkv.shape[1] // 384
    keep_copy = lambda i, slot: pltpu.make_async_copy(pbuf.at[slot], p_out.at[i], csem.at[12 + slot])

    def pair_step(i, _):
        slot = lax.rem(i, 2)
        pl.when(i >= 2)(lambda: keep_copy(i - 2, slot).wait())

        def keep(h, probs):
            pbuf[slot, h] = probs

        base = (i // 2) * third + lax.rem(i, 2) * 128
        cols = [pl.ds(pl.multiple_of(base + j * local, 128), 128) for j in range(3)]
        o[:, pl.ds(pl.multiple_of(i * 128, 128), 128)] = heads_forward(
            qkv[:, cols[0]], qkv[:, cols[1]], qkv[:, cols[2]], allowed, keep
        )
        keep_copy(i, slot).start()
        plan.run_at("H", i)
        return 0

    lax.fori_loop(0, pairs, pair_step, 0)
    save_o = pltpu.make_async_copy(o, o_out, csem.at[1])
    save_o.start()
    fetch_g = fetch_rows(gin, gv, 4)
    for f in fetch_g:
        f.wait()

    def mask_rows(i, _):
        at = pl.ds(pl.multiple_of(i * ROWS, ROWS), ROWS)
        g = gv[at, :].astype(F32) * masks[0, at, :1]
        stats[3:4, :] += jnp.sum(g, axis=0, keepdims=True)
        gv[at, :] = g.astype(BF)
        return 0

    lax.fori_loop(0, rows // ROWS, mask_rows, 0)
    save_g = pltpu.make_async_copy(gv, g_out, csem.at[21])
    save_g.start()
    gt[...] = gv[...].T
    plan.run("G")
    fetch_o = pltpu.make_async_copy(fo, wov, csem.at[2])
    fetch_o.start()
    fetch_o.wait()
    half = rows // 2

    def join(i, _):
        at = pl.ds(pl.multiple_of(i * half, 64), half)
        branch = lax.dot_general(
            o[at, :], wov[...].reshape(width, width), (((1,), (1,)), ((), ())), preferred_element_type=F32
        ) + vecs[4:5, :]
        stats[1:2, :] += jnp.sum(branch * branch * masks[0, at, :1], axis=0, keepdims=True)
        middle = xv[at, :].astype(F32) + branch
        x1[at, :] = middle
        unit, _inv = norm_stats(middle)
        h2[at, :] = (unit * vecs[2:3, :] + vecs[3:4, :]).astype(BF)
        return 0

    lax.fori_loop(0, 2, join, 0)
    save_x1 = pltpu.make_async_copy(x1, x1_out, csem.at[3])
    save_x1.start()
    save_h2 = pltpu.make_async_copy(h2, h2_out, csem.at[4])
    save_h2.start()
    plan.run("O")
    tiles = w1v.shape[0]
    n1 = w1.shape[1]
    fetch_1 = lambda j: pltpu.make_async_copy(f1.at[:, :, :, place_of(j)[3]], w1v.at[j], csem.at[22 + j])
    half_block = n1 // TILE

    def place_of(j):
        q, h = j // half_block, lax.rem(j, half_block)
        block = block_of(place, q)
        return q, block, h, pl.ds(pl.multiple_of(block * n1 + h * TILE, TILE), TILE)

    for j in range(tiles):
        fetch_1(j).start()

    def saves(j, slot):
        q, block, h, cols = place_of(j)
        return (
            pltpu.make_async_copy(actb.at[slot], act_out.at[:, cols], csem.at[14 + slot]),
            pltpu.make_async_copy(slopeb.at[slot], slope_out.at[:, cols], csem.at[16 + slot]),
        )

    def save_g2(j, slot):
        q, block, h, cols = place_of(j)
        at = pl.ds(pl.multiple_of(h * TILE, TILE), TILE)
        return pltpu.make_async_copy(g2b.at[slot], g2_out.at[q - 2, :, :, :, at], csem.at[18 + slot])

    def hidden_step(j, _):
        slot = lax.rem(j, 2)

        @pl.when(j >= 2)
        def _():
            for save in saves(j - 2, slot):
                save.wait()

        q, block, h, cols = place_of(j)
        fetch_1(j).wait()
        at = pl.ds(pl.multiple_of(h * TILE, TILE), TILE)
        bias = sml[block, 0:1, at]
        hidden = jnp.dot(h2[...], w1v[j].reshape(width, TILE), preferred_element_type=F32) + bias
        gate = jax.nn.sigmoid(1.702 * hidden)
        actb[slot] = (hidden * gate).astype(BF)
        slopeb[slot] = (gate + 1.702 * hidden * gate * (1.0 - gate)).astype(BF)
        for save in saves(j, slot):
            save.start()
        product = jnp.dot(gt[...], actb[slot], preferred_element_type=F32)

        @pl.when(q < 2)
        def _():
            far[q, :, :, :, at] = product.astype(BF).reshape(far.shape[1:4] + (TILE,))

        @pl.when(q >= 2)
        def _():
            pl.when(j >= 2 * half_block + 2)(lambda: save_g2(j - 2, slot).wait())
            g2b[slot] = (product.reshape(far.shape[1:4] + (TILE,)) + met[q - 2, :, :, :, at].astype(F32)).astype(BF)
            save_g2(j, slot).start()

        plan.run_at("F", j)
        return 0

    lax.fori_loop(0, tiles, hidden_step, 0)
    for j in (tiles - 2, tiles - 1):
        for save in saves(j, j % 2) + (save_g2(j, j % 2),):
            save.wait()
    for save in (save_h1, save_g, save_qkv, save_o, save_x1, save_h2, keep_copy(pairs - 2, pairs % 2), keep_copy(pairs - 1, (pairs - 1) % 2)):
        save.wait()
    for script in ws + [trade, core]:
        script.finish()


def forward(line, toks, grads, small, wq, wo, w1, w2, vecs, masks):
    images, part, width = toks.shape
    rows = 4 * part
    depth = wq.shape[0]
    hidden = 4 * w1.shape[1]
    heads = wo.shape[1] * 4 // HD
    wholes = [jax.ShapeDtypeStruct((line, 2, depth, 4 * w.shape[1]), BF) for w in (wq, wo, w1, w2)]
    count = 4 * slots_of(line) + 14
    hbm, vmem = pl.BlockSpec(memory_space=pl.ANY), pl.BlockSpec(memory_space=pltpu.VMEM)
    sds = jax.ShapeDtypeStruct
    return pl.pallas_call(
        functools.partial(forward_kernel, line),
        out_shape=[
            sds((4, part, width), BF),
            sds((4, part, width), BF),
            *wholes,
            sds((rows, 3 * width), BF),
            sds((heads // 2, 2, rows, rows), BF),
            sds((rows, width), BF),
            sds((rows, width), F32),
            sds((rows, width), BF),
            sds((rows, hidden), BF),
            sds((rows, hidden), BF),
            sds((2, line, 2, depth, w2.shape[1]), BF),
            sds((rows, width), BF),
            sds((rows, width), BF),
            sds((8, width), F32),
        ],
        in_specs=[hbm] * 7 + [vmem] * 2,
        out_specs=[hbm] * 16 + [vmem],
        scratch_shapes=[
            pltpu.VMEM((4,) + small.shape, F32),
            pltpu.VMEM((rows, width), BF),
            pltpu.VMEM((rows, width), BF),
            pltpu.VMEM((width, rows), BF),
            pltpu.VMEM((rows, width), BF),
            pltpu.VMEM((4, line, 2, depth, wq.shape[1]), BF),
            pltpu.VMEM((line, 2, depth, width), BF),
            pltpu.VMEM((hidden // TILE, line, 2, depth, TILE), BF),
            pltpu.VMEM((rows, 3 * width), BF),
            pltpu.VMEM((2, 2, rows, rows), BF),
            pltpu.VMEM((rows, width), BF),
            pltpu.VMEM((rows, width), F32),
            pltpu.VMEM((rows, width), BF),
            pltpu.VMEM((2, rows, TILE), BF),
            pltpu.VMEM((2, rows, TILE), BF),
            pltpu.VMEM((2, line, 2, depth, TILE), BF),
            pltpu.VMEM((2, line, 2, depth, w2.shape[1]), BF),
            pltpu.VMEM((2, line, 2, depth, w2.shape[1]), BF),
            pltpu.SemaphoreType.DMA((8,)),
            pltpu.SemaphoreType.DMA((22 + hidden // TILE,)),
            pltpu.SemaphoreType.DMA((count,)),
            pltpu.SemaphoreType.DMA((count,)),
        ],
        compiler_params=pltpu.CompilerParams(
            collective_id=0, has_side_effects=True, vmem_limit_bytes=62 * MIB
        ),
        name="forward",
    )(toks, grads, small, wq, wo, w1, w2, vecs, masks)


def heads_backward(q, k, v, o, do, probs_of):
    lane = lax.broadcasted_iota(jnp.int32, k.shape, 1)
    product = do.astype(F32) * o.astype(F32)
    zero = jnp.zeros_like(k)
    dq_t, dk, dv = [], [], []
    for h in range(2):
        mine = (lane // HD) == h
        inner = jnp.sum(jnp.where(mine, product, 0.0), axis=1, keepdims=True).T
        dprobs = lax.dot_general(
            jnp.where(mine, v, zero), do, (((1,), (1,)), ((), ())), preferred_element_type=F32
        )
        probs = probs_of(h)
        dscores = (probs.astype(F32) * (dprobs - inner)).astype(BF)
        dv.append(jnp.dot(probs, do, preferred_element_type=F32))
        dk.append(jnp.dot(dscores, q, preferred_element_type=F32))
        dq_t.append(
            lax.dot_general(k[:, h * HD : (h + 1) * HD], dscores, (((0,), (0,)), ((), ())), preferred_element_type=F32)
        )
    first = lane < HD
    return (
        (jnp.concatenate(dq_t, axis=0).T * HD ** (-0.5)).astype(BF),
        jnp.where(first, dk[0], dk[1]).astype(BF),
        jnp.where(first, dv[0], dv[1]).astype(BF),
    )


def norm_back(upstream, unit, inv_std, gain):
    scaled = upstream * gain
    inner_mean = jnp.mean(scaled, axis=-1, keepdims=True)
    cross_mean = jnp.mean(scaled * unit, axis=-1, keepdims=True)
    return inv_std * (scaled - inner_mean - unit * cross_mean)


def backward_kernel(line, *refs):
    g_in, f1, f2, fo, fq, act, slope, h1, h2, x1, xin, o_in, qkv, probs, g2, vecs, masks, small = refs[:18]
    sq, so, s1, s2, lo, gtok, sums = refs[18:25]
    big1, met1, bigo, meto, acc2, dqkv = refs[25:31]
    bufs = [refs[31 + 5 * i : 36 + 5 * i] for i in range(3)]
    g, dh2, g1b, low, here, cold, colx, coly, far_sums, lsem, ssem, rsem, free = refs[46:]
    place = Place(line)
    per = sums_of(line)
    rows, width = g.shape
    part = rows // 4
    n1, no, nq = s1.shape[1], so.shape[1], sq.shape[1]
    local = no
    cq, co, c1, c2 = CUTS
    greet(place, whole_line=True)

    def tell(i, device):
        pl.semaphore_signal(free.at[i], inc=1, device_id=device, device_id_type=MESH)

    def hear(i):
        pl.semaphore_wait(free.at[i], 1)

    def release(script):
        script.do(None, lambda: tell(1, place.pair()))
        script.do(None, lambda: tell(2, place.peer(2)))
        for k in range(1, line):
            script.do(None, lambda k=k: tell(3 + place.a, place.at(lax.rem(place.a + k, line), place.b, place.t)))

    def before_cross(script):
        script.do(None, lambda: hear(1))
        script.do(None, lambda: hear(2))

    def before_line(script):
        for k in range(1, line):
            script.do(None, lambda k=k: hear(3 + lax.rem(place.a + k, line)))

    cols_q = pl.ds(0, nq)
    two = lambda ref: ref.at[pl.ds(2, 2)]
    rdx, rdy, rx, ry, near = bufs[2]
    bufs_q = (
        rdx.at[:, :, pl.ds(0, nq - cq)] if cq < nq else rdx,
        rdy.at[:, :, pl.ds(0, cq)] if cq > 0 else rdy,
        *[ref.at[:, :, cols_q] for ref in (rx, ry, near)],
    )
    w2 = Scatter(place, ssem, rsem, None, None, acc2, s2, bufs[2], 2 * per, c2, release=release)
    w1 = Scatter(place, ssem, rsem, lambda i: big1.at[i], met1, two(big1), s1, bufs[0], 0, c1)
    wo = Scatter(place, ssem, rsem, lambda i: bigo.at[i], meto, two(bigo), so, bufs[1], per, co)
    wq = Scatter(
        place, ssem, rsem, lambda i: big1.at[i, :, :, :, cols_q], met1.at[:, :, :, :, cols_q],
        acc2.at[:, :, :, :, cols_q], sq, bufs_q, 3 * per, cq, before_cross=before_cross, before_line=before_line,
    )

    def rows_home(src, dst, first, sem):
        trade = Trade(ssem, rsem)
        mine = pltpu.make_async_copy(src.at[pl.ds(0, part)], dst.at[place.t], sem)
        trade.step()
        trade.do(None, mine.start)
        for k in (2, 3, 1):
            trade.send(None, lambda k=k: trade.copy(
                src.at[pl.ds(k * part, part)], dst.at[place.t], first + k, place.peer(k)))
        trade.step()
        trade.do(None, mine.wait)
        for k in (2, 3, 1):
            trade.wait(None, lambda k=k: dst.at[place.others[k]], first + k, place.pair())
        return trade

    token_rows = rows_home(low, gtok, 4 * per, lsem.at[0])
    out_rows = rows_home(g, lo, 4 * per + 4, lsem.at[1])

    base = 4 * per + 8
    few = Trade(ssem, rsem)
    hops = ((cold, place.peer(1)), (colx, place.pair()), (coly, place.peer(2)))

    def fold(i, land):
        here[i + 1] = here[i] + land[...]

    few.step()
    for i, (land, device) in enumerate(hops):
        few.send(None, lambda i=i, land=land, device=device: few.copy(here.at[i], land, base + i, device))
        few.step()
        few.wait(None, lambda land=land: land, base + i, place.pair())
        few.do(None, lambda i=i, land=land: fold(i, land))
    for k in range(1, line):
        far = lax.rem(place.a + k, line)
        few.send(None, lambda far=far, k=k: few.copy(
            here.at[3], far_sums.at[k], base + 3 + k, place.at(far, place.b, place.t)))
    few.step()
    for k in range(1, line):
        few.wait(None, lambda k=k: far_sums.at[k], base + 3 + k, place.pair())

    plan = Schedule(BACKWARD, {"q": wq, "o": wo, "1": w1, "2": w2, "r": out_rows, "s": token_rows, "f": few})
    half_block = n1 // TILE
    tiles = 4 * half_block

    def tile_of(j):
        q, h = j // half_block, lax.rem(j, half_block)
        block = block_of(place, q)
        at = pl.ds(pl.multiple_of(h * TILE, TILE), TILE)
        return q, block, at, pl.ds(pl.multiple_of(block * n1 + h * TILE, TILE), TILE)

    start = [
        pltpu.make_async_copy(g2.at[0], acc2.at[0], lsem.at[2]),
        pltpu.make_async_copy(g2.at[1], acc2.at[1], lsem.at[3]),
        pltpu.make_async_copy(g_in, g, lsem.at[4]),
    ]
    for c in start:
        c.start()
    here[0] = jnp.concatenate([small[:4, :], jnp.zeros((12, width), F32)], axis=0)
    dh2[...] = jnp.zeros_like(dh2)

    def feed_forward(h2t, f1t, f2t, slopet, sem):
        def fetch(j, slot):
            cols = tile_of(j)[3]
            return (
                pltpu.make_async_copy(f1.at[:, :, :, cols], f1t.at[slot], sem.at[slot]),
                pltpu.make_async_copy(f2.at[:, :, :, cols], f2t.at[slot], sem.at[2 + slot]),
                pltpu.make_async_copy(slope.at[:, cols], slopet.at[slot], sem.at[4 + slot]),
            )

        load = pltpu.make_async_copy(h2, low, sem.at[6])
        load.start()
        for c in fetch(0, 0):
            c.start()
        start[0].wait()
        start[1].wait()
        plan.run("G")
        load.wait()
        h2t[...] = low[...].T
        start[2].wait()

        def tile(j, _):
            slot = lax.rem(j, 2)

            @pl.when(j + 1 < tiles)
            def _():
                for c in fetch(j + 1, 1 - slot):
                    c.start()

            for c in fetch(j, slot):
                c.wait()
            q, block, at, cols = tile_of(j)
            du = jnp.dot(g[...], f2t[slot].reshape(width, TILE), preferred_element_type=F32)
            du = (du * slopet[slot].astype(F32)).astype(BF)
            here[0, pl.ds(4 + block, 1), at] = jnp.sum(du.astype(F32), axis=0, keepdims=True)
            product = jnp.dot(h2t[...], du, preferred_element_type=F32).reshape(big1.shape[1:4] + (TILE,))

            @pl.when(q < 2)
            def _():
                big1[q, :, :, :, at] = product.astype(BF)

            @pl.when(q >= 2)
            def _():
                big1[q, :, :, :, at] = (product + met1[q - 2, :, :, :, at].astype(F32)).astype(BF)

            dh2[...] += lax.dot_general(
                du, f1t[slot].reshape(width, TILE), (((1,), (1,)), ((), ())), preferred_element_type=F32
            )
            plan.run_at("T", j)
            return 0

        lax.fori_loop(0, tiles, tile, 0)

    block_shape = big1.shape[1:4]
    pl.run_scoped(
        feed_forward,
        pltpu.VMEM((width, rows), BF),
        pltpu.VMEM((2,) + block_shape + (TILE,), BF),
        pltpu.VMEM((2,) + block_shape + (TILE,), BF),
        pltpu.VMEM((2, rows, TILE), BF),
        pltpu.SemaphoreType.DMA((7,)),
    )
    tell(0, place.peer(1))

    def second_norm(xt, sem):
        fetch = lambda i, slot: pltpu.make_async_copy(
            x1.at[pl.ds(pl.multiple_of(i * ROWS, ROWS), ROWS)], xt.at[slot], sem.at[slot])
        count = rows // ROWS
        fetch(0, 0).start()

        def some_rows(i, _):
            slot = lax.rem(i, 2)
            pl.when(i + 1 < count)(lambda: fetch(i + 1, 1 - slot).start())
            fetch(i, slot).wait()
            at = pl.ds(pl.multiple_of(i * ROWS, ROWS), ROWS)
            unit, inv = norm_stats(xt[slot])
            up = dh2[at, :]
            here[0, 8:9, :] += jnp.sum(up * unit, axis=0, keepdims=True)
            here[0, 9:10, :] += jnp.sum(up, axis=0, keepdims=True)
            g1 = g[at, :].astype(F32) + norm_back(up, unit, inv, vecs[2:3, :])
            rounded = g1.astype(BF)
            g1b[at, :] = rounded
            here[0, 10:11, :] += jnp.sum(rounded.astype(F32), axis=0, keepdims=True)
            dh2[at, :] = g1
            return 0

        lax.fori_loop(0, count, some_rows, 0)

    pl.run_scoped(second_norm, pltpu.VMEM((2, ROWS, width), F32), pltpu.SemaphoreType.DMA((2,)))
    plan.run("N")

    def heads(tall, o, wov, do, pt, qt, sem):
        load_o = pltpu.make_async_copy(o_in, o, sem.at[0])
        load_w = pltpu.make_async_copy(fo, wov, sem.at[1])
        load_h = pltpu.make_async_copy(h1, low, sem.at[10])
        for c in (load_o, load_w, load_h):
            c.start()
        pairs = width // 128

        def cols_of(i, j):
            start = block_of(place, i // 2) * nq + lax.rem(i, 2) * 128 + j * local
            return pl.ds(pl.multiple_of(start, 128), 128)

        def heads_of(i):
            return block_of(place, i // 2) * 2 + lax.rem(i, 2)

        def fetch(i, slot):
            return [
                pltpu.make_async_copy(qkv.at[:, cols_of(i, j)], qt.at[slot, j], sem.at[2 + 2 * j + slot]) for j in range(3)
            ]

        head = lambda i, h: pltpu.make_async_copy(probs.at[heads_of(i), h], pt.at[h], sem.at[8 + h])
        for c in fetch(0, 0) + [head(0, 0), head(0, 1)]:
            c.start()
        tall[...] = g1b[...].T
        load_o.wait()
        load_w.wait()

        def output_weight(q, _):
            cols = pl.ds(pl.multiple_of(block_of(place, q) * no, 128), no)
            product = jnp.dot(tall[...], o[:, cols], preferred_element_type=F32).reshape(bigo.shape[1:])

            @pl.when(q < 2)
            def _():
                bigo[q] = product.astype(BF)

            @pl.when(q >= 2)
            def _():
                bigo[q] = (product + meto[q - 2].astype(F32)).astype(BF)

            plan.run_at("U", q)
            return 0

        lax.fori_loop(0, 4, output_weight, 0)
        do[...] = jnp.dot(g1b[...], wov[...].reshape(width, width), preferred_element_type=F32).astype(BF)
        plan.run("D")
        load_h.wait()
        tall[...] = low[...].T
        w1.wait_sent(2)
        hear(0)

        def pair_step(i, _):
            slot = lax.rem(i, 2)
            q = i // 2

            @pl.when(i + 1 < pairs)
            def _():
                for c in fetch(i + 1, 1 - slot):
                    c.start()

            for c in fetch(i, slot) + [head(i, 0), head(i, 1)]:
                c.wait()
            cols = pl.ds(pl.multiple_of(heads_of(i) * 128, 128), 128)
            got = heads_backward(qt[slot, 0], qt[slot, 1], qt[slot, 2], o[:, cols], do[:, cols], lambda h: pt[h])
            for j in range(3):
                dqkv[q, :, pl.ds(pl.multiple_of(j * local + slot * 128, 128), 128)] = got[j]

            @pl.when(i + 1 < pairs)
            def _():
                for h in range(2):
                    head(i + 1, h).start()

            plan.run_at("A", i)

            @pl.when(slot == 1)
            def _():
                block = block_of(place, q)
                got = dqkv[q]
                product = jnp.dot(tall[...], got, preferred_element_type=F32).reshape(block_shape + (nq,))
                total = jnp.sum(got.astype(F32), axis=0, keepdims=True)
                at = pl.ds(pl.multiple_of(block * local, 128), local)
                here[0, 14:15, at] = total[:, :local]
                here[0, 15:16, at] = total[:, 2 * local :]

                @pl.when(q < 2)
                def _():
                    big1[q, :, :, :, cols_q] = product.astype(BF)

                @pl.when(q >= 2)
                def _():
                    met = met1[q - 2, :, :, :, cols_q].astype(F32)
                    acc2[q - 2, :, :, :, cols_q] = (product + met).astype(BF)

                plan.run_at("W", q)

            return 0

        lax.fori_loop(0, pairs, pair_step, 0)

    pl.run_scoped(
        heads,
        pltpu.VMEM((width, rows), BF),
        pltpu.VMEM((rows, width), BF),
        pltpu.VMEM(fo.shape, BF),
        pltpu.VMEM((rows, width), BF),
        pltpu.VMEM((2, rows, rows), BF),
        pltpu.VMEM((2, 3, rows, 128), BF),
        pltpu.SemaphoreType.DMA((11,)),
    )

    def last(dh1, wqv, x, f2t, actt, sem):
        fetch_w = lambda q, slot: pltpu.make_async_copy(
            fq.at[:, :, :, pl.ds(pl.multiple_of(block_of(place, q) * nq, 128), nq)], wqv.at[slot], sem.at[slot])
        load_x = [pltpu.make_async_copy(xin.at[k], x.at[pl.ds(k * part, part)], sem.at[2 + k]) for k in range(4)]
        fetch_w(0, 0).start()
        for c in load_x:
            c.start()
        dh1[...] = jnp.zeros_like(dh1)

        def back(q, _):
            slot = lax.rem(q, 2)
            pl.when(q < 3)(lambda: fetch_w(q + 1, 1 - slot).start())
            fetch_w(q, slot).wait()
            dh1[...] += lax.dot_general(
                dqkv[q], wqv[slot].reshape(width, nq), (((1,), (1,)), ((), ())), preferred_element_type=F32
            )
            plan.run_at("E", q)
            return 0

        lax.fori_loop(0, 4, back, 0)
        for c in load_x:
            c.wait()

        def some_rows(i, _):
            at = pl.ds(pl.multiple_of(i * ROWS, ROWS), ROWS)
            unit, inv = norm_stats(x[at, :].astype(F32))
            up = dh1[at, :]
            here[0, 12:13, :] += jnp.sum(up * unit, axis=0, keepdims=True)
            here[0, 13:14, :] += jnp.sum(up, axis=0, keepdims=True)
            low[at, :] = (dh2[at, :] + norm_back(up, unit, inv, vecs[0:1, :])).astype(BF)
            return 0

        lax.fori_loop(0, rows // ROWS, some_rows, 0)
        plan.run("M")

        def fetch(j, slot):
            cols = tile_of(j)[3]
            return (
                pltpu.make_async_copy(f2.at[:, :, :, cols], f2t.at[slot], sem.at[6 + slot]),
                pltpu.make_async_copy(act.at[:, cols], actt.at[slot], sem.at[8 + slot]),
            )

        load = pltpu.make_async_copy(x1, dh2, sem.at[10])
        load.start()
        for c in fetch(0, 0):
            c.start()
        dh1[...] = jnp.zeros_like(dh1)

        def second_product(j, _):
            slot = lax.rem(j, 2)

            @pl.when(j + 1 < tiles)
            def _():
                for c in fetch(j + 1, 1 - slot):
                    c.start()

            for c in fetch(j, slot):
                c.wait()
            dh1[...] += lax.dot_general(
                actt[slot], f2t[slot].reshape(width, TILE), (((1,), (1,)), ((), ())), preferred_element_type=F32
            )
            plan.run_at("Y", j)
            return 0

        lax.fori_loop(0, tiles, second_product, 0)
        load.wait()

        def join(i, _):
            at = pl.ds(pl.multiple_of(i * ROWS, ROWS), ROWS)
            m = dh1[at, :] + vecs[5:6, :]
            g[at, :] = (dh2[at, :] + m).astype(BF)
            here[0, 11:12, :] += jnp.sum(m * m * masks[0, at, :1], axis=0, keepdims=True)
            return 0

        lax.fori_loop(0, rows // ROWS, join, 0)
        plan.run("Z")

    pl.run_scoped(
        last,
        pltpu.VMEM((rows, width), F32),
        pltpu.VMEM((2,) + block_shape + (nq,), BF),
        pltpu.VMEM((rows, width), BF),
        pltpu.VMEM((2,) + block_shape + (TILE,), BF),
        pltpu.VMEM((2, rows, TILE), BF),
        pltpu.SemaphoreType.DMA((11,)),
    )
    total = here[3]
    for k in range(1, line):
        total = total + far_sums[k]
    sums[...] = total
    for script in (w2, w1, wo, wq, token_rows, out_rows, few):
        script.finish()


def backward(line, g, f1, f2, fo, fq, act, slope, h1, h2, x1, xin, o, qkv, probs, g2, vecs, masks, small):
    rows, width = g.shape
    part = rows // 4
    depth = f1.shape[2]
    n1, no, nq = f1.shape[3] // 4, fo.shape[3] // 4, fq.shape[3] // 4
    hbm, vmem = pl.BlockSpec(memory_space=pl.ANY), pl.BlockSpec(memory_space=pltpu.VMEM)
    sds = jax.ShapeDtypeStruct
    block = lambda count, n: pltpu.VMEM((count, line, 2, depth, n), BF)
    few = (16, width)
    count = 4 * sums_of(line) + 8 + 3 + line
    return pl.pallas_call(
        functools.partial(backward_kernel, line),
        out_shape=[
            sds((depth, nq), F32),
            sds((depth, no), F32),
            sds((depth, n1), F32),
            sds((depth, n1), F32),
            sds((4, part, width), BF),
            sds((4, part, width), BF),
            sds(few, F32),
        ],
        in_specs=[hbm] * 15 + [vmem] * 3,
        out_specs=[vmem] * 4 + [hbm] * 2 + [vmem],
        scratch_shapes=[
            block(4, n1),
            block(2, n1),
            block(4, no),
            block(2, no),
            block(2, n1),
            pltpu.VMEM((4, rows, nq), BF),
            *landing(line, depth, n1, CUTS[2]),
            *landing(line, depth, no, CUTS[1]),
            *landing(line, depth, n1, CUTS[3]),
            pltpu.VMEM((rows, width), BF),
            pltpu.VMEM((rows, width), F32),
            pltpu.VMEM((rows, width), BF),
            pltpu.VMEM((rows, width), BF),
            pltpu.VMEM((4,) + few, F32),
            pltpu.VMEM(few, F32),
            pltpu.VMEM(few, F32),
            pltpu.VMEM(few, F32),
            pltpu.VMEM((line,) + few, F32),
            pltpu.SemaphoreType.DMA((5,)),
            pltpu.SemaphoreType.DMA((count,)),
            pltpu.SemaphoreType.DMA((count,)),
            pltpu.SemaphoreType.REGULAR((3 + line,)),
        ],
        compiler_params=pltpu.CompilerParams(collective_id=1, has_side_effects=True, vmem_limit_bytes=63 * MIB),
        name="backward",
    )(g, f1, f2, fo, fq, act, slope, h1, h2, x1, xin, o, qkv, probs, g2, vecs, masks, small)


def shards(
    tokens, token_mask, out_grad, ln1_gain, ln1_bias, w_qkv, b_qv, w_out, b_out,
    ln2_gain, ln2_bias, w_fc1, b_fc1, w_fc2, b_fc2,
):
    images, tok_rows, width = tokens.shape
    parts = lax.axis_size("tensor")
    line = lax.axis_size("dp") // 2
    t = lax.axis_index("tensor")
    depth, _, local = w_qkv.shape
    rows = tok_rows * parts

    small = jnp.zeros((8, w_fc1.shape[1]), F32).at[0].set(b_fc1).at[1, : 2 * local].set(b_qv.reshape(-1))
    vecs = jnp.stack([ln1_gain, ln1_bias, ln2_gain, ln2_bias, b_out, b_fc2, b_out, b_out])
    own = lax.dynamic_index_in_dim(token_mask, t, 0, keepdims=False).reshape(parts, tok_rows)
    y, c = t // 2, lax.rem(t, 2)
    others = [t, y * 2 + 1 - c, (1 - y) * 2 + c, (1 - y) * 2 + 1 - c]
    mask = jnp.concatenate([lax.dynamic_index_in_dim(own, o, 0, keepdims=False) for o in others])
    allow = jnp.where(jnp.max(mask) > 0, mask, 1).astype(F32)
    masks = jnp.broadcast_to(jnp.stack([mask.astype(F32), allow])[:, :, None], (2, rows, 128))
    xin, _, fq, fo, f1, f2, qkv, probs, o, x1, h2, act, slope, g2, h1, g, stats = forward(
        line, tokens, out_grad, small, w_qkv.reshape(depth, 3 * local), w_out.T, w_fc1, w_fc2.T, vecs, masks
    )
    sum_q, sum_o, sum_1, sum_2, layer_out, grad_tokens, sums = backward(
        line, g, f1, f2, fo, fq, act, slope, h1, h2, x1, xin, o, qkv, probs, g2, vecs, masks, stats
    )
    squares = jnp.stack([jnp.sum(sums[0]), jnp.sum(sums[1]), jnp.sum(sums[11])])
    pick = lambda v: lax.dynamic_slice_in_dim(v, t * local, local, 0)
    return (
        layer_out,
        grad_tokens,
        sums[12],
        sums[13],
        sum_q.reshape(depth, 3, local),
        jnp.stack([pick(sums[14]), pick(sums[15])]),
        sum_o.T,
        sums[10],
        sums[8],
        sums[9],
        sum_1,
        lax.dynamic_index_in_dim(sums[4:8], t, 0, keepdims=False),
        sum_2.T,
        sums[3],
        jnp.sqrt(squares / (sums[2, 0] * width)),
    )


def solution(mesh):
    rowwise = P("dp", "tensor", None)
    placed = (
        rowwise, P("dp", None), rowwise, P(), P(), P("dp", None, "tensor"), P(None, "tensor"), P("tensor", "dp"),
        P(), P(), P(), P("dp", "tensor"), P("tensor"), P("tensor", "dp"), P(),
    )
    return jax.shard_map(
        shards,
        mesh=mesh,
        in_specs=placed,
        out_specs=(
            rowwise, rowwise, P(), P(), P("dp", None, "tensor"), P(None, "tensor"), P("tensor", "dp"), P(),
            P(), P(), P("dp", "tensor"), P("tensor"), P("tensor", "dp"), P(), P(),
        ),
        check_vma=False,
    )
```

```python
import functools

import jax
import jax.numpy as jnp
from jax import lax
from jax.experimental import pallas as pl
from jax.experimental.pallas import tpu as pltpu
from jax.sharding import PartitionSpec as P

HD = 64
MESH = pl.DeviceIdType.MESH
BF = jnp.bfloat16
F32 = jnp.float32
ROWS = 64
TILE = 512
MIB = 1024 * 1024


class Place:
    def __init__(self, line):
        self.line = line
        self.d = lax.axis_index("dp")
        self.t = lax.axis_index("tensor")
        self.a = self.d // 2
        self.b = lax.rem(self.d, 2)
        y, c = self.t // 2, lax.rem(self.t, 2)
        self.others = (self.t, y * 2 + 1 - c, (1 - y) * 2 + c, (1 - y) * 2 + 1 - c)
        self.low, self.high = self.a > 0, self.a < line - 1
        self.inner = jnp.logical_and(self.low, self.high)

    def at(self, a, b, t):
        return (a * 2 + b, t)

    def pair(self):
        return self.at(self.a, 1 - self.b, self.t)

    def peer(self, k):
        return (self.d, self.others[k])

    def up(self):
        return self.at(self.a + 1, self.b, self.t)

    def down(self):
        return self.at(self.a - 1, self.b, self.t)


def greet(place, whole_line=False):
    barrier = pltpu.get_barrier_semaphore()

    def hail(device):
        pl.semaphore_signal(barrier, inc=1, device_id=device, device_id_type=MESH)

    line = place.line
    hail(place.pair())
    for k in range(1, 4):
        hail(place.peer(k))
    if whole_line:
        for k in range(1, line):
            hail(place.at(lax.rem(place.a + k, line), place.b, place.t))
        pl.semaphore_wait(barrier, 3 + line)
        return
    pl.when(place.low)(lambda: hail(place.down()))
    pl.when(place.high)(lambda: hail(place.up()))
    pl.when(place.inner)(lambda: pl.semaphore_wait(barrier, 6))
    pl.when(jnp.logical_not(place.inner))(lambda: pl.semaphore_wait(barrier, 5))


def both(p, q):
    if p is None:
        return q
    if q is None:
        return p
    return jnp.logical_and(p, q)


def when(pred, act):
    if pred is None:
        act()
    else:
        pl.when(pred)(act)


class Script:
    def __init__(self, ssem, rsem):
        self.ssem, self.rsem = ssem, rsem
        self.sent = []
        self.steps = []

    def copy(self, src, dst, slot, device):
        return pltpu.make_async_remote_copy(
            src_ref=src,
            dst_ref=dst,
            send_sem=self.ssem.at[slot],
            recv_sem=self.rsem.at[slot],
            device_id=device,
            device_id_type=MESH,
        )

    def step(self):
        self.steps.append([])

    def do(self, pred, act):
        self.steps[-1].append((pred, act))

    def send(self, pred, make):
        self.do(pred, lambda: make().start())
        self.sent.append((pred, make))

    def wait(self, pred, ref, slot, device):
        self.do(pred, lambda: self.copy(ref(), ref(), slot, device).wait_recv())

    def run(self, count=1):
        for _ in range(count):
            for pred, act in self.steps.pop(0):
                when(pred, act)

    def wait_sent(self, count):
        for pred, make in self.sent[:count]:
            when(pred, lambda make=make: make().wait_send())
        self.sent = self.sent[count:]

    def finish(self):
        assert not self.steps
        for pred, make in self.sent:
            when(pred, lambda make=make: make().wait_send())


def thirds(line):
    return [1], [2] if line > 2 else [], list(range(3, line))


def order(place):
    yield None, place.a
    for k in range(1, place.line):
        yield place.a >= k, place.a - k
        yield place.a + k <= place.line - 1, place.a + k


class Gather(Script):
    def __init__(self, place, ssem, rsem, local_sem, shard, whole, base, cut, by_line):
        super().__init__(ssem, rsem)
        self.p = place
        self.shard, self.whole = shard, whole
        self.n = shard.shape[1]
        self.base, self.cut = base, cut
        p = place
        t2 = p.others[2]
        local = pltpu.make_async_copy(shard, self.block(p.a, p.b, p.t), local_sem)
        own = lambda: self.shard
        groups = thirds(p.line)

        def line_step(group):
            for k in group:
                self.receive(k, 0, p.b, p.t, True)

        self.step()
        self.pass_line(None, p.a, 1, True, own, 0, p.b, p.t)
        self.pass_line(None, p.a, 1, False, own, 0, p.b, p.t)
        self.spread(None, p.a, own)
        self.do(None, local.start)
        self.step()
        line_step(groups[0])
        if by_line:
            self.step()
            self.cross([(None, p.a)])
            self.step()
            line_step(groups[1])
            self.step()
            self.landed([(None, p.a)])
            diagonal = lambda: self.block(p.a, 1 - p.b, t2)
            self.pass_line(None, p.a, 1, True, diagonal, 7, 1 - p.b, t2)
            self.pass_line(None, p.a, 1, False, diagonal, 7, 1 - p.b, t2)
            self.step()
            line_step(groups[2])
            for group in groups:
                self.step()
                for k in group:
                    self.receive(k, 7, 1 - p.b, t2, False)
            self.step()
            self.settle([i for i in order(p)][1:])
        else:
            for group in groups[1:]:
                self.step()
                line_step(group)
            self.step()
            self.cross(list(order(p)))
            self.step()
        self.do(None, local.wait)
        self.core((0, 1, 2))
        self.step()
        if not by_line:
            self.landed(list(order(p)))
        self.core((3,))
        self.step()
        self.arrive()

    def block(self, a, b, t, lo=0, hi=None):
        hi = self.n if hi is None else hi
        start = pl.multiple_of(t * self.n + lo, 128)
        return self.whole.at[a, b, :, pl.ds(start, hi - lo)]

    def plane(self, b, t):
        start = pl.multiple_of(t * self.n, 128)
        return self.whole.at[:, b, :, pl.ds(start, self.n)]

    def slot(self, kind, i):
        return self.base + kind * max(self.p.line, 4) + i

    def spread(self, pred, a, src):
        p = self.p
        self.send(pred, lambda: self.copy(src(), self.block(a, p.b, p.t), self.slot(2, a), p.pair()))
        self.send(pred, lambda: self.copy(src(), self.block(a, p.b, p.t), self.slot(3, a), p.peer(2)))

    def pass_line(self, pred, a, step, up, src, kind, b, t):
        p = self.p
        if step > p.line - 1:
            return
        ok = both(pred, p.high if up else p.low)
        to = p.up if up else p.down
        slot = self.slot(kind if up else kind + 1, step)
        self.send(ok, lambda: self.copy(src(), self.block(a, b, t), slot, to()))

    def receive(self, k, kind, b, t, spread):
        p = self.p
        for up in (True, False):
            chunk = p.a - k if up else p.a + k
            pred = p.a >= k if up else p.a + k <= p.line - 1
            src = lambda chunk=chunk: self.block(chunk, b, t)
            self.wait(pred, src, self.slot(kind if up else kind + 1, k), p.pair())
            self.pass_line(pred, chunk, k + 1, up, src, kind, b, t)
            if spread:
                self.spread(pred, chunk, src)

    def settle(self, chunks):
        p = self.p
        for pred, a in chunks:
            self.wait(pred, lambda a=a: self.block(a, 1 - p.b, p.t), self.slot(2, a), p.pair())
            self.wait(pred, lambda a=a: self.block(a, p.b, p.others[2]), self.slot(3, a), p.pair())

    def cross(self, chunks):
        p, t2 = self.p, self.p.others[2]
        for pred, a in chunks:
            self.settle([(pred, a)])
            one = lambda a=a: self.block(a, 1 - p.b, p.t, 0, self.cut)
            two = lambda a=a: self.block(a, p.b, t2, self.cut, self.n)
            if self.cut > 0:
                self.send(pred, lambda a=a, one=one: self.copy(one(), one(), self.slot(4, a), p.peer(2)))
            if self.cut < self.n:
                self.send(pred, lambda a=a, two=two: self.copy(two(), two(), self.slot(5, a), p.pair()))

    def planes(self, far):
        p = self.p
        t, t2 = (p.others[1], p.others[3]) if far else (p.t, p.others[2])
        return ((p.b, t), (1 - p.b, t), (p.b, t2), (1 - p.b, t2))

    def core(self, which):
        for j in which:
            b, t = self.planes(False)[j]
            src = lambda b=b, t=t: self.plane(b, t)
            self.send(None, lambda j=j, src=src: self.copy(src(), src(), self.slot(6, j), self.p.peer(1)))

    def landed(self, chunks):
        p, t2 = self.p, self.p.others[2]
        for pred, a in chunks:
            if self.cut > 0:
                self.wait(pred, lambda a=a: self.block(a, 1 - p.b, t2, 0, self.cut), self.slot(4, a), p.pair())
            if self.cut < self.n:
                self.wait(pred, lambda a=a: self.block(a, 1 - p.b, t2, self.cut, self.n), self.slot(5, a), p.pair())

    def arrive(self):
        for j, (b, t) in enumerate(self.planes(True)):
            self.wait(None, lambda b=b, t=t: self.plane(b, t), self.slot(6, j), self.p.pair())


GATHER_CUTS = (256, 0, 0, 0)
BY_LINE = (False, True, True, True)
CUTS = (256, 128, 384, 384)


def slots_of(line):
    return 9 * max(line, 4)


def add_into(dst, *others):
    rows = dst.shape[0]
    step = min(rows, 32)

    def body(i, _):
        at = pl.ds(pl.multiple_of(i * step, step), step)
        total = dst[at, :]
        for other in others:
            total = total + other[at, :]
        dst[at, :] = total
        return 0

    lax.fori_loop(0, rows // step, body, 0)


def block_of(place, q):
    y, c = place.t // 2, lax.rem(place.t, 2)
    return lax.rem(y + 1 + q, 2) * 2 + lax.rem(c + 1 - q // 2, 2)


class Scatter(Script):
    def __init__(
        self, place, ssem, rsem, far, met, acc, out, bufs, base, cut, before_cross=None, before_line=None, release=None
    ):
        super().__init__(ssem, rsem)
        self.p = place
        self.acc, self.out = acc, out
        self.rdx, self.rdy, self.rx, self.ry, self.near = bufs
        self.n = out.shape[1]
        self.base, self.cut = base, cut
        self.own = lambda *at: acc.at[(1, at[0], place.b) + at[1:]]
        self.by_pair = lambda *at: acc.at[(1, at[0], 1 - place.b) + at[1:]]
        self.by_y = lambda *at: acc.at[(0, at[0], place.b) + at[1:]]
        self.by_both = lambda *at: acc.at[(0, at[0], 1 - place.b) + at[1:]]
        if far is not None:
            for i in range(2):
                self.step()
                self.send(None, lambda i=i: self.copy(far(i), met.at[i], base + i, place.peer(1)))
            for i in range(2):
                self.step()
                self.wait(None, lambda i=i: met.at[i], base + i, place.pair())
        every, first, late = slice(None), pl.ds(0, cut), pl.ds(cut, self.n - cut)
        pair, y = place.pair(), place.peer(2)
        lines = range(place.line)

        def give(src, dst, slot, device):
            self.send(None, lambda: self.copy(src(), dst(), base + slot, device))

        def take(ref, slot):
            self.wait(None, ref, base + slot, pair)

        def add(dst, *others):
            for a in lines:
                self.do(None, lambda a=a: add_into(dst(a), *[other(a) for other in others]))

        some, rest = cut > 0, cut < self.n
        self.step()
        if before_cross is not None:
            before_cross(self)
        if some:
            give(lambda: self.by_both(every, every, first), lambda: self.rdy, 4, y)
        if rest:
            give(lambda: self.by_both(every, every, late), lambda: self.rdx, 5, pair)
        if some:
            give(lambda: self.by_y(every, every, first), lambda: self.ry.at[:, :, first], 7, y)
        self.step()
        if rest:
            give(lambda: self.by_pair(every, every, late), lambda: self.rx.at[:, :, late], 6, pair)
        self.step()
        if some:
            take(lambda: self.rdy, 4)
            add(lambda a: self.by_pair(a, every, first), lambda a: self.rdy.at[a])
            give(lambda: self.by_pair(every, every, first), lambda: self.rx.at[:, :, first], 8, pair)
        self.step()
        if rest:
            take(lambda: self.rdx, 5)
            add(lambda a: self.by_y(a, every, late), lambda a: self.rdx.at[a])
            give(lambda: self.by_y(every, every, late), lambda: self.ry.at[:, :, late], 9, y)
        self.step()
        if rest:
            take(lambda: self.rx.at[:, :, late], 6)
        if some:
            take(lambda: self.ry.at[:, :, first], 7)
            take(lambda: self.rx.at[:, :, first], 8)
        if rest:
            take(lambda: self.ry.at[:, :, late], 9)
        if before_line is not None:
            before_line(self)
        for pred, chunk in reversed(list(order(place))[1:]):
            self.do(pred, lambda chunk=chunk: add_into(self.own(chunk), self.rx.at[chunk], self.ry.at[chunk]))
            self.send(pred, lambda chunk=chunk: self.copy(
                self.own(chunk), self.near.at[place.a], base + 10 + place.a, place.at(chunk, place.b, place.t)))
        self.do(None, lambda: add_into(self.own(place.a), self.rx.at[place.a], self.ry.at[place.a]))
        self.step()
        for pred, a in list(order(place))[1:]:
            self.wait(pred, lambda a=a: self.near.at[a], base + 10 + a, pair)
        self.do(None, self.close)
        if release is not None:
            sent, self.sent = self.sent, []
            for pred, make in sent:
                self.do(pred, lambda make=make: make().wait_send())
            release(self)

    def close(self):
        p = self.p
        rows = self.out.shape[0]
        step = min(rows, 16)

        def body(i, _):
            at = pl.ds(pl.multiple_of(i * step, step), step)
            value = self.acc[1, p.a, p.b, at, :].astype(F32)
            for k in range(1, p.line):
                value = value + self.near[lax.rem(p.a + k, p.line), at, :].astype(F32)
            self.out[at, :] = value
            return 0

        lax.fori_loop(0, rows // step, body, 0)


def landing(line, depth, n, cut):
    return [
        pltpu.VMEM((line, depth, max(n - cut, 128)), BF),
        pltpu.VMEM((line, depth, max(cut, 128)), BF),
        pltpu.VMEM((line, depth, n), BF),
        pltpu.VMEM((line, depth, n), BF),
        pltpu.VMEM((line, depth, n), BF),
    ]


def sums_of(line):
    return 10 + line


class Trade(Script):
    pass


def heads_forward(q, k, v, allowed, keep):
    lane = lax.broadcasted_iota(jnp.int32, k.shape, 1)
    outs = []
    for h in range(2):
        mine = (lane // HD) == h
        scores = lax.dot_general(
            jnp.where(mine, k, jnp.zeros_like(k)), q, (((1,), (1,)), ((), ())), preferred_element_type=F32
        )
        scores = jnp.where(allowed, scores, -1e30)
        expo = jnp.exp(scores - jnp.max(scores, axis=0, keepdims=True))
        probs = (expo * (1.0 / jnp.sum(expo, axis=0, keepdims=True))).astype(BF)
        keep(h, probs)
        outs.append(
            lax.dot_general(v[:, h * HD : (h + 1) * HD], probs, (((0,), (0,)), ((), ())), preferred_element_type=F32)
        )
    return jnp.concatenate(outs, axis=0).T.astype(BF)


def norm_stats(values):
    row_mean = jnp.mean(values, axis=-1, keepdims=True)
    centred = values - row_mean
    variance = jnp.mean(centred * centred, axis=-1, keepdims=True)
    inv_std = lax.rsqrt(variance + 1e-05)
    return centred * inv_std, inv_std


class Schedule:
    def __init__(self, text, scripts):
        self.after = {}
        at = ("", 0)
        counts = {}
        for ch in "".join(text):
            if ch.isupper():
                at = (ch, counts.get(ch, 0))
                counts[ch] = at[1] + 1
            else:
                self.after.setdefault(at, []).extend(scripts[ch].steps.pop(0))

    def run(self, name="", i=0):
        for pred, act in self.after.pop((name, i), ()):
            when(pred, act)

    def run_at(self, name, i):
        for at in sorted(k for n, k in self.after if n == name):
            pl.when(i == at)(lambda at=at: self.run(name, at))


FORWARD = ("0K1020r002r101rL12031021P1PP2P2H", "3HH2HrH11123H13H22H3G12O332F3FcF", "333FccFFcFF3")
BACKWARD = ("G2TT12TT11T2T211TTNUU1ooo2oUUDAA", "1W1AAW2qqoAAqWoAqqAooWq1qEEEqEoM", "YYYYsYYY1YqZfffrofrsqf")


def forward_kernel(line, *refs):
    toks, grads, raw_q, w1, raw_o, raw_2, marks, b_fc1, b_qv = refs[:9]
    vectors = refs[9:15]
    xin, gin, fq, fo, f1, f2, qkv_out, p_out, o_out, x1_out, h2_out, act_out, slope_out, g2_out, h1_out, g_out, stats, vecs, masks = refs[15:34]
    (sml, xv, gv, gt, h1, wqv, wov, w1v, qkv, pbuf, o, x1, h2, actb, slopeb, g2b, far, met, small, wq, wo, w2, marked, lsem, csem, ssem, rsem) = refs[34:]
    place = Place(line)
    per = slots_of(line)
    rows, width = xv.shape
    part = toks.shape[1]
    third = wqv.shape[-1]
    local = third // 3
    greet(place)
    ws = [
        Gather(place, ssem, rsem, lsem.at[i], shard, whole, i * per, GATHER_CUTS[i], BY_LINE[i])
        for i, (shard, whole) in enumerate(((wq, fq), (wo, fo), (w1, f1), (w2, f2)))
    ]
    trade = Trade(ssem, rsem)
    slot_of = lambda j, k: 4 * per + j * 4 + k
    pairs_of_rows = ((toks, xin), (grads, gin))
    mine = [pltpu.make_async_copy(src.at[place.t], dst.at[0], lsem.at[4 + j]) for j, (src, dst) in enumerate(pairs_of_rows)]
    mine.append(pltpu.make_async_copy(small, sml.at[place.t], lsem.at[6]))
    for j, (src, dst) in enumerate(pairs_of_rows):
        trade.step()
        trade.do(None, mine[j].start)
        for k in (2, 3, 1):
            trade.send(None, lambda src=src, dst=dst, j=j, k=k: trade.copy(
                src.at[place.others[k]], dst.at[k], slot_of(j, k), place.peer(k)))
        if j == 0:
            trade.do(None, mine[2].start)
            for k in (2, 3, 1):
                trade.send(None, lambda k=k: trade.copy(small, sml.at[place.t], slot_of(2, k), place.peer(k)))
    for j, (src, dst) in enumerate(pairs_of_rows):
        trade.step()
        trade.do(None, mine[j].wait)
        for k in (2, 3, 1):
            trade.wait(None, lambda dst=dst, k=k: dst.at[k], slot_of(j, k), place.pair())
        if j == 0:
            trade.do(None, mine[2].wait)
            for k in (2, 3, 1):
                trade.wait(None, lambda k=k: sml.at[place.others[k]], slot_of(2, k), place.pair())

    core = Script(ssem, rsem)
    for i in range(2):
        core.step()
        core.send(None, lambda i=i: core.copy(far.at[i], met.at[i], 4 * per + 12 + i, place.peer(1)))
    for i in range(2):
        core.step()
        core.wait(None, lambda i=i: met.at[i], 4 * per + 12 + i, place.pair())
    plan = Schedule(FORWARD, {"r": trade, "c": core, **{str(i): w for i, w in enumerate(ws)}})

    def fetch_rows(src, dst, first):
        copies = [
            pltpu.make_async_copy(src.at[k], dst.at[pl.ds(k * part, part)], csem.at[first + k]) for k in range(4)
        ]
        for c in copies:
            c.start()
        return copies

    small[...] = jnp.zeros_like(small)
    small[0:1, :] = b_fc1[...].reshape(1, -1)
    small[1:2, :local] = b_qv[0:1, :]
    small[1:2, local : 2 * local] = b_qv[1:2, :]
    for j in range(3):
        wq[:, j * local : (j + 1) * local] = raw_q[j]
    plan.run()
    wo[...] = raw_o[...].T
    w2[...] = raw_2[...].T
    plan.run("K")
    for i, vector in enumerate(vectors):
        vecs[i : i + 1, :] = vector[...].reshape(1, -1)
    mark = marks[pl.ds(place.t, 1), :].astype(F32)
    marked[...] = jnp.broadcast_to(mark, (128, rows)).T
    for k in range(4):
        at = pl.ds(k * part, part)
        masks[0, at, :] = marked[pl.ds(pl.multiple_of(place.others[k] * part, 32), part), :]
    masks[1] = jnp.where(jnp.max(mark, axis=1, keepdims=True) > 0, masks[0], 1.0)
    fetch_x = fetch_rows(xin, xv, 0)
    for f in fetch_x:
        f.wait()
    stats[...] = jnp.zeros_like(stats)

    def first_norm(i, _):
        at = pl.ds(pl.multiple_of(i * ROWS, ROWS), ROWS)
        x = xv[at, :].astype(F32)
        unit, _inv = norm_stats(x)
        h1[at, :] = (unit * vecs[0:1, :] + vecs[1:2, :]).astype(BF)
        real = masks[0, at, :1]
        stats[0:1, :] += jnp.sum(x * x * real, axis=0, keepdims=True)
        stats[2:3, :] += jnp.broadcast_to(jnp.sum(real, axis=0, keepdims=True), (1, width))
        return 0

    lax.fori_loop(0, rows // ROWS, first_norm, 0)
    save_h1 = pltpu.make_async_copy(h1, h1_out, csem.at[20])
    save_h1.start()
    plan.run("L")
    fetch_q = lambda t: pltpu.make_async_copy(
        fq.at[:, :, :, pl.ds(pl.multiple_of(t * third, 128), third)], wqv.at[t], csem.at[8 + t])
    for t in range(4):
        fetch_q(t).start()
    def project(t, _):
        fetch_q(t).wait()
        got = jnp.dot(h1[...], wqv[t].reshape(width, third), preferred_element_type=F32)
        cols = [pl.ds(pl.multiple_of(t * third + j * local, 128), local) for j in range(3)]
        qkv[:, cols[0]] = (got[:, :local] + sml[t, 1:2, :local]).astype(BF) * jnp.asarray(HD ** (-0.5), BF)
        qkv[:, cols[1]] = got[:, local : 2 * local].astype(BF)
        qkv[:, cols[2]] = (got[:, 2 * local :] + sml[t, 1:2, local : 2 * local]).astype(BF)
        plan.run_at("P", t)
        return 0

    lax.fori_loop(0, 4, project, 0)
    save_qkv = pltpu.make_async_copy(qkv, qkv_out, csem.at[0])
    save_qkv.start()
    allowed = masks[1, :, :1] > 0
    pairs = qkv.shape[1] // 384
    keep_copy = lambda i, slot: pltpu.make_async_copy(pbuf.at[slot], p_out.at[i], csem.at[12 + slot])

    def pair_step(i, _):
        slot = lax.rem(i, 2)
        pl.when(i >= 2)(lambda: keep_copy(i - 2, slot).wait())

        def keep(h, probs):
            pbuf[slot, h] = probs

        base = (i // 2) * third + lax.rem(i, 2) * 128
        cols = [pl.ds(pl.multiple_of(base + j * local, 128), 128) for j in range(3)]
        o[:, pl.ds(pl.multiple_of(i * 128, 128), 128)] = heads_forward(
            qkv[:, cols[0]], qkv[:, cols[1]], qkv[:, cols[2]], allowed, keep
        )
        keep_copy(i, slot).start()
        plan.run_at("H", i)
        return 0

    lax.fori_loop(0, pairs, pair_step, 0)
    save_o = pltpu.make_async_copy(o, o_out, csem.at[1])
    save_o.start()
    fetch_g = fetch_rows(gin, gv, 4)
    for f in fetch_g:
        f.wait()

    def mask_rows(i, _):
        at = pl.ds(pl.multiple_of(i * ROWS, ROWS), ROWS)
        g = gv[at, :].astype(F32) * masks[0, at, :1]
        stats[3:4, :] += jnp.sum(g, axis=0, keepdims=True)
        gv[at, :] = g.astype(BF)
        return 0

    lax.fori_loop(0, rows // ROWS, mask_rows, 0)
    save_g = pltpu.make_async_copy(gv, g_out, csem.at[21])
    save_g.start()
    gt[...] = gv[...].T
    plan.run("G")
    fetch_o = pltpu.make_async_copy(fo, wov, csem.at[2])
    fetch_o.start()
    fetch_o.wait()
    half = rows // 2

    def join(i, _):
        at = pl.ds(pl.multiple_of(i * half, 64), half)
        branch = lax.dot_general(
            o[at, :], wov[...].reshape(width, width), (((1,), (1,)), ((), ())), preferred_element_type=F32
        ) + vecs[4:5, :]
        stats[1:2, :] += jnp.sum(branch * branch * masks[0, at, :1], axis=0, keepdims=True)
        middle = xv[at, :].astype(F32) + branch
        x1[at, :] = middle
        unit, _inv = norm_stats(middle)
        h2[at, :] = (unit * vecs[2:3, :] + vecs[3:4, :]).astype(BF)
        return 0

    lax.fori_loop(0, 2, join, 0)
    save_x1 = pltpu.make_async_copy(x1, x1_out, csem.at[3])
    save_x1.start()
    save_h2 = pltpu.make_async_copy(h2, h2_out, csem.at[4])
    save_h2.start()
    plan.run("O")
    tiles = w1v.shape[0]
    n1 = w1.shape[1]
    fetch_1 = lambda j: pltpu.make_async_copy(f1.at[:, :, :, place_of(j)[3]], w1v.at[j], csem.at[22 + j])
    half_block = n1 // TILE

    def place_of(j):
        q, h = j // half_block, lax.rem(j, half_block)
        block = block_of(place, q)
        return q, block, h, pl.ds(pl.multiple_of(block * n1 + h * TILE, TILE), TILE)

    for j in range(tiles):
        fetch_1(j).start()

    def saves(j, slot):
        q, block, h, cols = place_of(j)
        return (
            pltpu.make_async_copy(actb.at[slot], act_out.at[:, cols], csem.at[14 + slot]),
            pltpu.make_async_copy(slopeb.at[slot], slope_out.at[:, cols], csem.at[16 + slot]),
        )

    def save_g2(j, slot):
        q, block, h, cols = place_of(j)
        at = pl.ds(pl.multiple_of(h * TILE, TILE), TILE)
        return pltpu.make_async_copy(g2b.at[slot], g2_out.at[q - 2, :, :, :, at], csem.at[18 + slot])

    def hidden_step(j, _):
        slot = lax.rem(j, 2)

        @pl.when(j >= 2)
        def _():
            for save in saves(j - 2, slot):
                save.wait()

        q, block, h, cols = place_of(j)
        fetch_1(j).wait()
        at = pl.ds(pl.multiple_of(h * TILE, TILE), TILE)
        bias = sml[block, 0:1, at]
        hidden = jnp.dot(h2[...], w1v[j].reshape(width, TILE), preferred_element_type=F32) + bias
        gate = jax.nn.sigmoid(1.702 * hidden)
        actb[slot] = (hidden * gate).astype(BF)
        slopeb[slot] = (gate + 1.702 * hidden * gate * (1.0 - gate)).astype(BF)
        for save in saves(j, slot):
            save.start()
        product = jnp.dot(gt[...], actb[slot], preferred_element_type=F32)

        @pl.when(q < 2)
        def _():
            far[q, :, :, :, at] = product.astype(BF).reshape(far.shape[1:4] + (TILE,))

        @pl.when(q >= 2)
        def _():
            pl.when(j >= 2 * half_block + 2)(lambda: save_g2(j - 2, slot).wait())
            g2b[slot] = (product.reshape(far.shape[1:4] + (TILE,)) + met[q - 2, :, :, :, at].astype(F32)).astype(BF)
            save_g2(j, slot).start()

        plan.run_at("F", j)
        return 0

    lax.fori_loop(0, tiles, hidden_step, 0)
    for j in (tiles - 2, tiles - 1):
        for save in saves(j, j % 2) + (save_g2(j, j % 2),):
            save.wait()
    for save in (save_h1, save_g, save_qkv, save_o, save_x1, save_h2, keep_copy(pairs - 2, pairs % 2), keep_copy(pairs - 1, (pairs - 1) % 2)):
        save.wait()
    for script in ws + [trade, core]:
        script.finish()


def forward(line, toks, grads, w_qkv, w1, w_out, w_fc2, marks, b_fc1, b_qv, *vectors):
    images, part, width = toks.shape
    rows = 4 * part
    depth = w1.shape[0]
    hidden = 4 * w1.shape[1]
    no, n2, nq = w_out.shape[0], w_fc2.shape[0], 3 * w_qkv.shape[2]
    heads = no * 4 // HD
    wholes = [jax.ShapeDtypeStruct((line, 2, depth, 4 * n), BF) for n in (nq, no, w1.shape[1], n2)]
    count = 4 * slots_of(line) + 14
    hbm, vmem = pl.BlockSpec(memory_space=pl.ANY), pl.BlockSpec(memory_space=pltpu.VMEM)
    sds = jax.ShapeDtypeStruct
    return pl.pallas_call(
        functools.partial(forward_kernel, line),
        out_shape=[
            sds((4, part, width), BF),
            sds((4, part, width), BF),
            *wholes,
            sds((rows, 3 * width), BF),
            sds((heads // 2, 2, rows, rows), BF),
            sds((rows, width), BF),
            sds((rows, width), F32),
            sds((rows, width), BF),
            sds((rows, hidden), BF),
            sds((rows, hidden), BF),
            sds((2, line, 2, depth, n2), BF),
            sds((rows, width), BF),
            sds((rows, width), BF),
            sds((8, width), F32),
            sds((8, width), F32),
            sds((2, rows, 128), F32),
        ],
        in_specs=[hbm] * 2 + [vmem] + [hbm] + [vmem] * 11,
        out_specs=[hbm] * 16 + [vmem] * 3,
        scratch_shapes=[
            pltpu.VMEM((4, 8, w1.shape[1]), F32),
            pltpu.VMEM((rows, width), BF),
            pltpu.VMEM((rows, width), BF),
            pltpu.VMEM((width, rows), BF),
            pltpu.VMEM((rows, width), BF),
            pltpu.VMEM((4, line, 2, depth, nq), BF),
            pltpu.VMEM((line, 2, depth, width), BF),
            pltpu.VMEM((hidden // TILE, line, 2, depth, TILE), BF),
            pltpu.VMEM((rows, 3 * width), BF),
            pltpu.VMEM((2, 2, rows, rows), BF),
            pltpu.VMEM((rows, width), BF),
            pltpu.VMEM((rows, width), F32),
            pltpu.VMEM((rows, width), BF),
            pltpu.VMEM((2, rows, TILE), BF),
            pltpu.VMEM((2, rows, TILE), BF),
            pltpu.VMEM((2, line, 2, depth, TILE), BF),
            pltpu.VMEM((2, line, 2, depth, n2), BF),
            pltpu.VMEM((2, line, 2, depth, n2), BF),
            pltpu.VMEM((8, w1.shape[1]), F32),
            pltpu.VMEM((depth, nq), BF),
            pltpu.VMEM((depth, no), BF),
            pltpu.VMEM((depth, n2), BF),
            pltpu.VMEM((rows, 128), F32),
            pltpu.SemaphoreType.DMA((8,)),
            pltpu.SemaphoreType.DMA((22 + hidden // TILE,)),
            pltpu.SemaphoreType.DMA((count,)),
            pltpu.SemaphoreType.DMA((count,)),
        ],
        compiler_params=pltpu.CompilerParams(
            collective_id=0, has_side_effects=True, vmem_limit_bytes=62 * MIB
        ),
        name="forward",
    )(toks, grads, w_qkv, w1, w_out, w_fc2, marks, b_fc1, b_qv, *vectors)


def heads_backward(q, k, v, o, do, probs_of):
    lane = lax.broadcasted_iota(jnp.int32, k.shape, 1)
    product = do.astype(F32) * o.astype(F32)
    zero = jnp.zeros_like(k)
    dq_t, dk, dv = [], [], []
    for h in range(2):
        mine = (lane // HD) == h
        inner = jnp.sum(jnp.where(mine, product, 0.0), axis=1, keepdims=True).T
        dprobs = lax.dot_general(
            jnp.where(mine, v, zero), do, (((1,), (1,)), ((), ())), preferred_element_type=F32
        )
        probs = probs_of(h)
        dscores = (probs.astype(F32) * (dprobs - inner)).astype(BF)
        dv.append(jnp.dot(probs, do, preferred_element_type=F32))
        dk.append(jnp.dot(dscores, q, preferred_element_type=F32))
        dq_t.append(
            lax.dot_general(k[:, h * HD : (h + 1) * HD], dscores, (((0,), (0,)), ((), ())), preferred_element_type=F32)
        )
    first = lane < HD
    return (
        (jnp.concatenate(dq_t, axis=0).T * HD ** (-0.5)).astype(BF),
        jnp.where(first, dk[0], dk[1]).astype(BF),
        jnp.where(first, dv[0], dv[1]).astype(BF),
    )


def norm_back(upstream, unit, inv_std, gain):
    scaled = upstream * gain
    inner_mean = jnp.mean(scaled, axis=-1, keepdims=True)
    cross_mean = jnp.mean(scaled * unit, axis=-1, keepdims=True)
    return inv_std * (scaled - inner_mean - unit * cross_mean)


def backward_kernel(line, *refs):
    g_in, f1, f2, fo, fq, act, slope, h1, h2, x1, xin, o_in, qkv, probs, g2, vecs, masks, small = refs[:18]
    sq, so, s1, s2, lo, gtok, sums = refs[18:25]
    big1, met1, bigo, meto, acc2, dqkv = refs[25:31]
    bufs = [refs[31 + 5 * i : 36 + 5 * i] for i in range(3)]
    g, dh2, g1b, low, here, cold, colx, coly, far_sums, lsem, ssem, rsem, free = refs[46:]
    place = Place(line)
    per = sums_of(line)
    rows, width = g.shape
    part = rows // 4
    n1, no, nq = s1.shape[1], so.shape[1], sq.shape[1]
    local = no
    cq, co, c1, c2 = CUTS
    greet(place, whole_line=True)

    def tell(i, device):
        pl.semaphore_signal(free.at[i], inc=1, device_id=device, device_id_type=MESH)

    def hear(i):
        pl.semaphore_wait(free.at[i], 1)

    def release(script):
        script.do(None, lambda: tell(1, place.pair()))
        script.do(None, lambda: tell(2, place.peer(2)))
        for k in range(1, line):
            script.do(None, lambda k=k: tell(3 + place.a, place.at(lax.rem(place.a + k, line), place.b, place.t)))

    def before_cross(script):
        script.do(None, lambda: hear(1))
        script.do(None, lambda: hear(2))

    def before_line(script):
        for k in range(1, line):
            script.do(None, lambda k=k: hear(3 + lax.rem(place.a + k, line)))

    cols_q = pl.ds(0, nq)
    two = lambda ref: ref.at[pl.ds(2, 2)]
    rdx, rdy, rx, ry, near = bufs[2]
    bufs_q = (
        rdx.at[:, :, pl.ds(0, nq - cq)] if cq < nq else rdx,
        rdy.at[:, :, pl.ds(0, cq)] if cq > 0 else rdy,
        *[ref.at[:, :, cols_q] for ref in (rx, ry, near)],
    )
    w2 = Scatter(place, ssem, rsem, None, None, acc2, s2, bufs[2], 2 * per, c2, release=release)
    w1 = Scatter(place, ssem, rsem, lambda i: big1.at[i], met1, two(big1), s1, bufs[0], 0, c1)
    wo = Scatter(place, ssem, rsem, lambda i: bigo.at[i], meto, two(bigo), so, bufs[1], per, co)
    wq = Scatter(
        place, ssem, rsem, lambda i: big1.at[i, :, :, :, cols_q], met1.at[:, :, :, :, cols_q],
        acc2.at[:, :, :, :, cols_q], sq, bufs_q, 3 * per, cq, before_cross=before_cross, before_line=before_line,
    )

    def rows_home(src, dst, first, sem):
        trade = Trade(ssem, rsem)
        mine = pltpu.make_async_copy(src.at[pl.ds(0, part)], dst.at[place.t], sem)
        trade.step()
        trade.do(None, mine.start)
        for k in (2, 3, 1):
            trade.send(None, lambda k=k: trade.copy(
                src.at[pl.ds(k * part, part)], dst.at[place.t], first + k, place.peer(k)))
        trade.step()
        trade.do(None, mine.wait)
        for k in (2, 3, 1):
            trade.wait(None, lambda k=k: dst.at[place.others[k]], first + k, place.pair())
        return trade

    token_rows = rows_home(low, gtok, 4 * per, lsem.at[0])
    out_rows = rows_home(g, lo, 4 * per + 4, lsem.at[1])

    base = 4 * per + 8
    few = Trade(ssem, rsem)
    hops = ((cold, place.peer(1)), (colx, place.pair()), (coly, place.peer(2)))

    def fold(i, land):
        here[i + 1] = here[i] + land[...]

    few.step()
    for i, (land, device) in enumerate(hops):
        few.send(None, lambda i=i, land=land, device=device: few.copy(here.at[i], land, base + i, device))
        few.step()
        few.wait(None, lambda land=land: land, base + i, place.pair())
        few.do(None, lambda i=i, land=land: fold(i, land))
    for k in range(1, line):
        far = lax.rem(place.a + k, line)
        few.send(None, lambda far=far, k=k: few.copy(
            here.at[3], far_sums.at[k], base + 3 + k, place.at(far, place.b, place.t)))
    few.step()
    for k in range(1, line):
        few.wait(None, lambda k=k: far_sums.at[k], base + 3 + k, place.pair())

    plan = Schedule(BACKWARD, {"q": wq, "o": wo, "1": w1, "2": w2, "r": out_rows, "s": token_rows, "f": few})
    half_block = n1 // TILE
    tiles = 4 * half_block

    def tile_of(j):
        q, h = j // half_block, lax.rem(j, half_block)
        block = block_of(place, q)
        at = pl.ds(pl.multiple_of(h * TILE, TILE), TILE)
        return q, block, at, pl.ds(pl.multiple_of(block * n1 + h * TILE, TILE), TILE)

    start = [
        pltpu.make_async_copy(g2.at[0], acc2.at[0], lsem.at[2]),
        pltpu.make_async_copy(g2.at[1], acc2.at[1], lsem.at[3]),
        pltpu.make_async_copy(g_in, g, lsem.at[4]),
    ]
    for c in start:
        c.start()
    here[0] = jnp.concatenate([small[:4, :], jnp.zeros((12, width), F32)], axis=0)
    dh2[...] = jnp.zeros_like(dh2)

    def feed_forward(h2t, f1t, f2t, slopet, sem):
        def fetch(j, slot):
            cols = tile_of(j)[3]
            return (
                pltpu.make_async_copy(f1.at[:, :, :, cols], f1t.at[slot], sem.at[slot]),
                pltpu.make_async_copy(f2.at[:, :, :, cols], f2t.at[slot], sem.at[2 + slot]),
                pltpu.make_async_copy(slope.at[:, cols], slopet.at[slot], sem.at[4 + slot]),
            )

        load = pltpu.make_async_copy(h2, low, sem.at[6])
        load.start()
        for c in fetch(0, 0):
            c.start()
        start[0].wait()
        start[1].wait()
        plan.run("G")
        load.wait()
        h2t[...] = low[...].T
        start[2].wait()

        def tile(j, _):
            slot = lax.rem(j, 2)

            @pl.when(j + 1 < tiles)
            def _():
                for c in fetch(j + 1, 1 - slot):
                    c.start()

            for c in fetch(j, slot):
                c.wait()
            q, block, at, cols = tile_of(j)
            du = jnp.dot(g[...], f2t[slot].reshape(width, TILE), preferred_element_type=F32)
            du = (du * slopet[slot].astype(F32)).astype(BF)
            here[0, pl.ds(4 + block, 1), at] = jnp.sum(du.astype(F32), axis=0, keepdims=True)
            product = jnp.dot(h2t[...], du, preferred_element_type=F32).reshape(big1.shape[1:4] + (TILE,))

            @pl.when(q < 2)
            def _():
                big1[q, :, :, :, at] = product.astype(BF)

            @pl.when(q >= 2)
            def _():
                big1[q, :, :, :, at] = (product + met1[q - 2, :, :, :, at].astype(F32)).astype(BF)

            dh2[...] += lax.dot_general(
                du, f1t[slot].reshape(width, TILE), (((1,), (1,)), ((), ())), preferred_element_type=F32
            )
            plan.run_at("T", j)
            return 0

        lax.fori_loop(0, tiles, tile, 0)

    block_shape = big1.shape[1:4]
    pl.run_scoped(
        feed_forward,
        pltpu.VMEM((width, rows), BF),
        pltpu.VMEM((2,) + block_shape + (TILE,), BF),
        pltpu.VMEM((2,) + block_shape + (TILE,), BF),
        pltpu.VMEM((2, rows, TILE), BF),
        pltpu.SemaphoreType.DMA((7,)),
    )
    tell(0, place.peer(1))

    def second_norm(xt, sem):
        fetch = lambda i, slot: pltpu.make_async_copy(
            x1.at[pl.ds(pl.multiple_of(i * ROWS, ROWS), ROWS)], xt.at[slot], sem.at[slot])
        count = rows // ROWS
        fetch(0, 0).start()

        def some_rows(i, _):
            slot = lax.rem(i, 2)
            pl.when(i + 1 < count)(lambda: fetch(i + 1, 1 - slot).start())
            fetch(i, slot).wait()
            at = pl.ds(pl.multiple_of(i * ROWS, ROWS), ROWS)
            unit, inv = norm_stats(xt[slot])
            up = dh2[at, :]
            here[0, 8:9, :] += jnp.sum(up * unit, axis=0, keepdims=True)
            here[0, 9:10, :] += jnp.sum(up, axis=0, keepdims=True)
            g1 = g[at, :].astype(F32) + norm_back(up, unit, inv, vecs[2:3, :])
            rounded = g1.astype(BF)
            g1b[at, :] = rounded
            here[0, 10:11, :] += jnp.sum(rounded.astype(F32), axis=0, keepdims=True)
            dh2[at, :] = g1
            return 0

        lax.fori_loop(0, count, some_rows, 0)

    pl.run_scoped(second_norm, pltpu.VMEM((2, ROWS, width), F32), pltpu.SemaphoreType.DMA((2,)))
    plan.run("N")

    def heads(tall, o, wov, do, pt, qt, sem):
        load_o = pltpu.make_async_copy(o_in, o, sem.at[0])
        load_w = pltpu.make_async_copy(fo, wov, sem.at[1])
        load_h = pltpu.make_async_copy(h1, low, sem.at[10])
        for c in (load_o, load_w, load_h):
            c.start()
        pairs = width // 128

        def cols_of(i, j):
            start = block_of(place, i // 2) * nq + lax.rem(i, 2) * 128 + j * local
            return pl.ds(pl.multiple_of(start, 128), 128)

        def heads_of(i):
            return block_of(place, i // 2) * 2 + lax.rem(i, 2)

        def fetch(i, slot):
            return [
                pltpu.make_async_copy(qkv.at[:, cols_of(i, j)], qt.at[slot, j], sem.at[2 + 2 * j + slot]) for j in range(3)
            ]

        head = lambda i, h: pltpu.make_async_copy(probs.at[heads_of(i), h], pt.at[h], sem.at[8 + h])
        for c in fetch(0, 0) + [head(0, 0), head(0, 1)]:
            c.start()
        tall[...] = g1b[...].T
        load_o.wait()
        load_w.wait()

        def output_weight(q, _):
            cols = pl.ds(pl.multiple_of(block_of(place, q) * no, 128), no)
            product = jnp.dot(tall[...], o[:, cols], preferred_element_type=F32).reshape(bigo.shape[1:])

            @pl.when(q < 2)
            def _():
                bigo[q] = product.astype(BF)

            @pl.when(q >= 2)
            def _():
                bigo[q] = (product + meto[q - 2].astype(F32)).astype(BF)

            plan.run_at("U", q)
            return 0

        lax.fori_loop(0, 4, output_weight, 0)
        do[...] = jnp.dot(g1b[...], wov[...].reshape(width, width), preferred_element_type=F32).astype(BF)
        plan.run("D")
        load_h.wait()
        tall[...] = low[...].T
        w1.wait_sent(2)
        hear(0)

        def pair_step(i, _):
            slot = lax.rem(i, 2)
            q = i // 2

            @pl.when(i + 1 < pairs)
            def _():
                for c in fetch(i + 1, 1 - slot):
                    c.start()

            for c in fetch(i, slot) + [head(i, 0), head(i, 1)]:
                c.wait()
            cols = pl.ds(pl.multiple_of(heads_of(i) * 128, 128), 128)
            got = heads_backward(qt[slot, 0], qt[slot, 1], qt[slot, 2], o[:, cols], do[:, cols], lambda h: pt[h])
            for j in range(3):
                dqkv[q, :, pl.ds(pl.multiple_of(j * local + slot * 128, 128), 128)] = got[j]

            @pl.when(i + 1 < pairs)
            def _():
                for h in range(2):
                    head(i + 1, h).start()

            plan.run_at("A", i)

            @pl.when(slot == 1)
            def _():
                block = block_of(place, q)
                got = dqkv[q]
                product = jnp.dot(tall[...], got, preferred_element_type=F32).reshape(block_shape + (nq,))
                total = jnp.sum(got.astype(F32), axis=0, keepdims=True)
                at = pl.ds(pl.multiple_of(block * local, 128), local)
                here[0, 14:15, at] = total[:, :local]
                here[0, 15:16, at] = total[:, 2 * local :]

                @pl.when(q < 2)
                def _():
                    big1[q, :, :, :, cols_q] = product.astype(BF)

                @pl.when(q >= 2)
                def _():
                    met = met1[q - 2, :, :, :, cols_q].astype(F32)
                    acc2[q - 2, :, :, :, cols_q] = (product + met).astype(BF)

                plan.run_at("W", q)

            return 0

        lax.fori_loop(0, pairs, pair_step, 0)

    pl.run_scoped(
        heads,
        pltpu.VMEM((width, rows), BF),
        pltpu.VMEM((rows, width), BF),
        pltpu.VMEM(fo.shape, BF),
        pltpu.VMEM((rows, width), BF),
        pltpu.VMEM((2, rows, rows), BF),
        pltpu.VMEM((2, 3, rows, 128), BF),
        pltpu.SemaphoreType.DMA((11,)),
    )

    def last(dh1, wqv, x, f2t, actt, sem):
        fetch_w = lambda q, slot: pltpu.make_async_copy(
            fq.at[:, :, :, pl.ds(pl.multiple_of(block_of(place, q) * nq, 128), nq)], wqv.at[slot], sem.at[slot])
        load_x = [pltpu.make_async_copy(xin.at[k], x.at[pl.ds(k * part, part)], sem.at[2 + k]) for k in range(4)]
        fetch_w(0, 0).start()
        for c in load_x:
            c.start()
        dh1[...] = jnp.zeros_like(dh1)

        def back(q, _):
            slot = lax.rem(q, 2)
            pl.when(q < 3)(lambda: fetch_w(q + 1, 1 - slot).start())
            fetch_w(q, slot).wait()
            dh1[...] += lax.dot_general(
                dqkv[q], wqv[slot].reshape(width, nq), (((1,), (1,)), ((), ())), preferred_element_type=F32
            )
            plan.run_at("E", q)
            return 0

        lax.fori_loop(0, 4, back, 0)
        for c in load_x:
            c.wait()

        def some_rows(i, _):
            at = pl.ds(pl.multiple_of(i * ROWS, ROWS), ROWS)
            unit, inv = norm_stats(x[at, :].astype(F32))
            up = dh1[at, :]
            here[0, 12:13, :] += jnp.sum(up * unit, axis=0, keepdims=True)
            here[0, 13:14, :] += jnp.sum(up, axis=0, keepdims=True)
            low[at, :] = (dh2[at, :] + norm_back(up, unit, inv, vecs[0:1, :])).astype(BF)
            return 0

        lax.fori_loop(0, rows // ROWS, some_rows, 0)
        plan.run("M")

        def fetch(j, slot):
            cols = tile_of(j)[3]
            return (
                pltpu.make_async_copy(f2.at[:, :, :, cols], f2t.at[slot], sem.at[6 + slot]),
                pltpu.make_async_copy(act.at[:, cols], actt.at[slot], sem.at[8 + slot]),
            )

        load = pltpu.make_async_copy(x1, dh2, sem.at[10])
        load.start()
        for c in fetch(0, 0):
            c.start()
        dh1[...] = jnp.zeros_like(dh1)

        def second_product(j, _):
            slot = lax.rem(j, 2)

            @pl.when(j + 1 < tiles)
            def _():
                for c in fetch(j + 1, 1 - slot):
                    c.start()

            for c in fetch(j, slot):
                c.wait()
            dh1[...] += lax.dot_general(
                actt[slot], f2t[slot].reshape(width, TILE), (((1,), (1,)), ((), ())), preferred_element_type=F32
            )
            plan.run_at("Y", j)
            return 0

        lax.fori_loop(0, tiles, second_product, 0)
        load.wait()

        def join(i, _):
            at = pl.ds(pl.multiple_of(i * ROWS, ROWS), ROWS)
            m = dh1[at, :] + vecs[5:6, :]
            g[at, :] = (dh2[at, :] + m).astype(BF)
            here[0, 11:12, :] += jnp.sum(m * m * masks[0, at, :1], axis=0, keepdims=True)
            return 0

        lax.fori_loop(0, rows // ROWS, join, 0)
        plan.run("Z")

    pl.run_scoped(
        last,
        pltpu.VMEM((rows, width), F32),
        pltpu.VMEM((2,) + block_shape + (nq,), BF),
        pltpu.VMEM((rows, width), BF),
        pltpu.VMEM((2,) + block_shape + (TILE,), BF),
        pltpu.VMEM((2, rows, TILE), BF),
        pltpu.SemaphoreType.DMA((11,)),
    )
    total = here[3]
    for k in range(1, line):
        total = total + far_sums[k]
    sums[...] = total
    for script in (w2, w1, wo, wq, token_rows, out_rows, few):
        script.finish()


def backward(line, g, f1, f2, fo, fq, act, slope, h1, h2, x1, xin, o, qkv, probs, g2, vecs, masks, small):
    rows, width = g.shape
    part = rows // 4
    depth = f1.shape[2]
    n1, no, nq = f1.shape[3] // 4, fo.shape[3] // 4, fq.shape[3] // 4
    hbm, vmem = pl.BlockSpec(memory_space=pl.ANY), pl.BlockSpec(memory_space=pltpu.VMEM)
    sds = jax.ShapeDtypeStruct
    block = lambda count, n: pltpu.VMEM((count, line, 2, depth, n), BF)
    few = (16, width)
    count = 4 * sums_of(line) + 8 + 3 + line
    return pl.pallas_call(
        functools.partial(backward_kernel, line),
        out_shape=[
            sds((depth, nq), F32),
            sds((depth, no), F32),
            sds((depth, n1), F32),
            sds((depth, n1), F32),
            sds((4, part, width), BF),
            sds((4, part, width), BF),
            sds(few, F32),
        ],
        in_specs=[hbm] * 15 + [vmem] * 3,
        out_specs=[vmem] * 4 + [hbm] * 2 + [vmem],
        scratch_shapes=[
            block(4, n1),
            block(2, n1),
            block(4, no),
            block(2, no),
            block(2, n1),
            pltpu.VMEM((4, rows, nq), BF),
            *landing(line, depth, n1, CUTS[2]),
            *landing(line, depth, no, CUTS[1]),
            *landing(line, depth, n1, CUTS[3]),
            pltpu.VMEM((rows, width), BF),
            pltpu.VMEM((rows, width), F32),
            pltpu.VMEM((rows, width), BF),
            pltpu.VMEM((rows, width), BF),
            pltpu.VMEM((4,) + few, F32),
            pltpu.VMEM(few, F32),
            pltpu.VMEM(few, F32),
            pltpu.VMEM(few, F32),
            pltpu.VMEM((line,) + few, F32),
            pltpu.SemaphoreType.DMA((5,)),
            pltpu.SemaphoreType.DMA((count,)),
            pltpu.SemaphoreType.DMA((count,)),
            pltpu.SemaphoreType.REGULAR((3 + line,)),
        ],
        compiler_params=pltpu.CompilerParams(collective_id=1, has_side_effects=True, vmem_limit_bytes=63 * MIB),
        name="backward",
    )(g, f1, f2, fo, fq, act, slope, h1, h2, x1, xin, o, qkv, probs, g2, vecs, masks, small)


def finish_kernel(sq, so, s1, s2, lo, gtok, sums, lo_out, gtok_out, *refs):
    out, (rows, sem) = refs[:-2], refs[-2:]
    g_ln1, b_ln1, q, b_qv, o, b_out, g_ln2, b_ln2, one, b_fc1, two, b_fc2, rms = out
    pairs = ((lo, lo_out), (gtok, gtok_out))
    load = [pltpu.make_async_copy(src, rows.at[i], sem.at[i]) for i, (src, dst) in enumerate(pairs)]
    save = [pltpu.make_async_copy(rows.at[i], dst, sem.at[2 + i]) for i, (src, dst) in enumerate(pairs)]
    for c in load:
        c.start()
    t = lax.axis_index("tensor")
    local = b_qv.shape[1]
    for ref, at in ((g_ln1, 12), (b_ln1, 13), (b_out, 10), (g_ln2, 8), (b_ln2, 9), (b_fc2, 3)):
        ref[...] = sums[at, :]
    for l, s in zip(load, save):
        l.wait()
        s.start()
    b_fc1[...] = sums[pl.ds(4 + t, 1), :].reshape(-1)
    at = pl.ds(pl.multiple_of(t * local, 128), local)
    b_qv[0:1, :] = sums[14:15, at]
    b_qv[1:2, :] = sums[15:16, at]
    for j in range(3):
        q[j] = sq[:, j * local : (j + 1) * local]
    one[...] = s1[...]
    o[...] = so[...].T
    two[...] = s2[...].T
    count = sums[2:3, 0:1] * sums.shape[1]
    squares = [jnp.sum(sums[i : i + 1, :], axis=1, keepdims=True) for i in (0, 1, 11)]
    lane = lax.broadcasted_iota(jnp.int32, rms.shape, 1)
    total = jnp.where(lane == 0, squares[0], jnp.where(lane == 1, squares[1], squares[2]))
    rms[...] = jnp.sqrt(total / count)
    for s in save:
        s.wait()


def finish(sum_q, sum_o, sum_1, sum_2, layer_out, grad_tokens, sums):
    width = sums.shape[1]
    depth, no = sum_o.shape
    n2 = sum_2.shape[1]
    sds = jax.ShapeDtypeStruct
    row = sds((width,), F32)
    hbm, vmem = pl.BlockSpec(memory_space=pl.ANY), pl.BlockSpec(memory_space=pltpu.VMEM)
    lo, gtok, g_ln1, b_ln1, q, b_qv, o, b_out, g_ln2, b_ln2, one, b_fc1, two, b_fc2, rms = pl.pallas_call(
        finish_kernel,
        out_shape=[
            sds(layer_out.shape, BF), sds(grad_tokens.shape, BF), row, row, sds((3, depth, no), F32), sds((2, no), F32),
            sds((no, depth), F32), row, row, row, sds(sum_1.shape, F32), sds((sum_1.shape[1],), F32),
            sds((n2, depth), F32), row, sds((1, 128), F32),
        ],
        in_specs=[vmem] * 4 + [hbm] * 2 + [vmem],
        out_specs=[hbm] * 2 + [vmem] * 13,
        scratch_shapes=[pltpu.VMEM((2,) + layer_out.shape, BF), pltpu.SemaphoreType.DMA((4,))],
        compiler_params=pltpu.CompilerParams(vmem_limit_bytes=63 * MIB),
        name="finish",
    )(sum_q, sum_o, sum_1, sum_2, layer_out, grad_tokens, sums)
    return (
        lo, gtok, g_ln1, b_ln1, q.transpose(1, 0, 2), b_qv, o, b_out, g_ln2, b_ln2, one, b_fc1, two, b_fc2, rms[0, :3]
    )


def shards(
    tokens, token_mask, out_grad, ln1_gain, ln1_bias, w_qkv, b_qv, w_out, b_out,
    ln2_gain, ln2_bias, w_fc1, b_fc1, w_fc2, b_fc2,
):
    line = lax.axis_size("dp") // 2
    depth, _, local = w_qkv.shape
    xin, _, fq, fo, f1, f2, qkv, probs, o, x1, h2, act, slope, g2, h1, g, stats, vecs, masks = forward(
        line, tokens, out_grad, w_qkv.transpose(1, 0, 2), w_fc1, w_out, w_fc2, token_mask, b_fc1, b_qv,
        ln1_gain, ln1_bias, ln2_gain, ln2_bias, b_out, b_fc2,
    )
    sum_q, sum_o, sum_1, sum_2, layer_out, grad_tokens, sums = backward(
        line, g, f1, f2, fo, fq, act, slope, h1, h2, x1, xin, o, qkv, probs, g2, vecs, masks, stats
    )
    return finish(sum_q, sum_o, sum_1, sum_2, layer_out, grad_tokens, sums)


def solution(mesh):
    rowwise = P("dp", "tensor", None)
    placed = (
        rowwise, P("dp", None), rowwise, P(), P(), P("dp", None, "tensor"), P(None, "tensor"), P("tensor", "dp"),
        P(), P(), P(), P("dp", "tensor"), P("tensor"), P("tensor", "dp"), P(),
    )
    return jax.shard_map(
        shards,
        mesh=mesh,
        in_specs=placed,
        out_specs=(
            rowwise, rowwise, P(), P(), P("dp", None, "tensor"), P(None, "tensor"), P("tensor", "dp"), P(),
            P(), P(), P("dp", "tensor"), P("tensor"), P("tensor", "dp"), P(), P(),
        ),
        check_vma=False,
    )
```

```python
import functools

import jax
import jax.numpy as jnp
from jax import lax
from jax.experimental import pallas as pl
from jax.experimental.pallas import tpu as pltpu
from jax.sharding import PartitionSpec as P

HD = 64
MESH = pl.DeviceIdType.MESH
BF = jnp.bfloat16
F32 = jnp.float32
ROWS = 64
TILE = 512
UNROLL = 2
MIB = 1024 * 1024


class Place:
    def __init__(self, line):
        self.line = line
        self.d = lax.axis_index("dp")
        self.t = lax.axis_index("tensor")
        self.a = self.d // 2
        self.b = lax.rem(self.d, 2)
        y, c = self.t // 2, lax.rem(self.t, 2)
        self.others = (self.t, y * 2 + 1 - c, (1 - y) * 2 + c, (1 - y) * 2 + 1 - c)
        self.low, self.high = self.a > 0, self.a < line - 1
        self.inner = jnp.logical_and(self.low, self.high)

    def at(self, a, b, t):
        return (a * 2 + b, t)

    def pair(self):
        return self.at(self.a, 1 - self.b, self.t)

    def peer(self, k):
        return (self.d, self.others[k])

    def up(self):
        return self.at(self.a + 1, self.b, self.t)

    def down(self):
        return self.at(self.a - 1, self.b, self.t)


def greet(place, whole_line=False):
    barrier = pltpu.get_barrier_semaphore()

    def hail(device):
        pl.semaphore_signal(barrier, inc=1, device_id=device, device_id_type=MESH)

    line = place.line
    hail(place.pair())
    for k in range(1, 4):
        hail(place.peer(k))
    if whole_line:
        for k in range(1, line):
            hail(place.at(lax.rem(place.a + k, line), place.b, place.t))
        pl.semaphore_wait(barrier, 3 + line)
        return
    pl.when(place.low)(lambda: hail(place.down()))
    pl.when(place.high)(lambda: hail(place.up()))
    pl.when(place.inner)(lambda: pl.semaphore_wait(barrier, 6))
    pl.when(jnp.logical_not(place.inner))(lambda: pl.semaphore_wait(barrier, 5))


def both(p, q):
    if p is None:
        return q
    if q is None:
        return p
    return jnp.logical_and(p, q)


def when(pred, act):
    if pred is None:
        act()
    else:
        pl.when(pred)(act)


class Script:
    def __init__(self, ssem, rsem):
        self.ssem, self.rsem = ssem, rsem
        self.sent = []
        self.steps = []

    def copy(self, src, dst, slot, device):
        return pltpu.make_async_remote_copy(
            src_ref=src,
            dst_ref=dst,
            send_sem=self.ssem.at[slot],
            recv_sem=self.rsem.at[slot],
            device_id=device,
            device_id_type=MESH,
        )

    def step(self):
        self.steps.append([])

    def do(self, pred, act):
        self.steps[-1].append((pred, act))

    def send(self, pred, make):
        self.do(pred, lambda: make().start())
        self.sent.append((pred, make))

    def wait(self, pred, ref, slot, device):
        self.do(pred, lambda: self.copy(ref(), ref(), slot, device).wait_recv())

    def run(self, count=1):
        for _ in range(count):
            for pred, act in self.steps.pop(0):
                when(pred, act)

    def wait_sent(self, count):
        for pred, make in self.sent[:count]:
            when(pred, lambda make=make: make().wait_send())
        self.sent = self.sent[count:]

    def finish(self):
        assert not self.steps
        for pred, make in self.sent:
            when(pred, lambda make=make: make().wait_send())


def thirds(line):
    return [1], [2] if line > 2 else [], list(range(3, line))


def order(place):
    yield None, place.a
    for k in range(1, place.line):
        yield place.a >= k, place.a - k
        yield place.a + k <= place.line - 1, place.a + k


class Gather(Script):
    def __init__(self, place, ssem, rsem, local_sem, shard, whole, base, cut, by_line, first=0):
        super().__init__(ssem, rsem)
        self.p = place
        self.shard, self.whole = shard, whole
        self.n = shard.shape[1]
        self.first, self.apart = first, whole.shape[3] // 4
        self.base, self.cut, self.by_line = base, cut, by_line
        line, few = place.line, 1 if by_line else place.line
        sizes = (line, line, line, line, few, few, 4, line if by_line else 0, 0)
        self.offsets = [sum(sizes[:kind]) for kind in range(9)]
        p = place
        t2 = p.others[2]
        local = pltpu.make_async_copy(shard, self.block(p.a, p.b, p.t), local_sem)
        own = lambda: self.shard
        groups = thirds(p.line)
        apart = list(order(p))
        rings = [[i for k in group for i in apart[2 * k - 1 : 2 * k + 1]] for group in groups]

        def along(group, kind, b, t, spread):
            for up in (True, False):
                self.step()
                for k in group:
                    self.receive(k, kind, b, t, spread, up)

        self.step()
        self.pass_line(None, p.a, 1, True, own, 0, p.b, p.t)
        self.pass_line(None, p.a, 1, False, own, 0, p.b, p.t)
        self.spread(None, p.a, own)
        self.do(None, local.start)
        along(groups[0], 0, p.b, p.t, True)
        self.step()
        self.cross(apart[:1])
        along(groups[1], 0, p.b, p.t, True)
        self.step()
        if by_line:
            self.landed(apart[:1])
            diagonal = lambda: self.block(p.a, 1 - p.b, t2)
            self.pass_line(None, p.a, 1, True, diagonal, 7, 1 - p.b, t2)
            self.pass_line(None, p.a, 1, False, diagonal, 7, 1 - p.b, t2)
        else:
            self.cross(rings[0])
        along(groups[2], 0, p.b, p.t, True)
        if by_line:
            for group in groups:
                along(group, 7, 1 - p.b, t2, False)
        for ring in rings if by_line else rings[1:]:
            self.step()
            (self.settle if by_line else self.cross)(ring)
        self.do(None, local.wait)
        for j in range(3):
            self.step()
            self.core((j,))
        self.step()
        if not by_line:
            self.landed(apart)
        self.core((3,))
        self.step()
        self.arrive()

    def block(self, a, b, t, lo=0, hi=None):
        hi = self.n if hi is None else hi
        start = pl.multiple_of(t * self.apart + self.first + lo, 128)
        return self.whole.at[a, b, :, pl.ds(start, hi - lo)]

    def plane(self, b, t):
        start = pl.multiple_of(t * self.apart + self.first, 128)
        return self.whole.at[:, b, :, pl.ds(start, self.n)]

    def slot(self, kind, i):
        return self.base + self.offsets[kind] + (0 if self.by_line and kind in (4, 5) else i)

    def spread(self, pred, a, src):
        p = self.p
        self.send(pred, lambda: self.copy(src(), self.block(a, p.b, p.t), self.slot(2, a), p.pair()))
        self.send(pred, lambda: self.copy(src(), self.block(a, p.b, p.t), self.slot(3, a), p.peer(2)))

    def pass_line(self, pred, a, step, up, src, kind, b, t):
        p = self.p
        if step > p.line - 1:
            return
        ok = both(pred, p.high if up else p.low)
        to = p.up if up else p.down
        slot = self.slot(kind if up else kind + 1, step)
        self.send(ok, lambda: self.copy(src(), self.block(a, b, t), slot, to()))

    def receive(self, k, kind, b, t, spread, up):
        p = self.p
        chunk = p.a - k if up else p.a + k
        pred = p.a >= k if up else p.a + k <= p.line - 1
        src = lambda: self.block(chunk, b, t)
        self.wait(pred, src, self.slot(kind if up else kind + 1, k), p.pair())
        self.pass_line(pred, chunk, k + 1, up, src, kind, b, t)
        if spread:
            self.spread(pred, chunk, src)

    def settle(self, chunks):
        p = self.p
        for pred, a in chunks:
            self.wait(pred, lambda a=a: self.block(a, 1 - p.b, p.t), self.slot(2, a), p.pair())
            self.wait(pred, lambda a=a: self.block(a, p.b, p.others[2]), self.slot(3, a), p.pair())

    def cross(self, chunks):
        p, t2 = self.p, self.p.others[2]
        for pred, a in chunks:
            self.settle([(pred, a)])
            one = lambda a=a: self.block(a, 1 - p.b, p.t, 0, self.cut)
            two = lambda a=a: self.block(a, p.b, t2, self.cut, self.n)
            if self.cut > 0:
                self.send(pred, lambda a=a, one=one: self.copy(one(), one(), self.slot(4, a), p.peer(2)))
            if self.cut < self.n:
                self.send(pred, lambda a=a, two=two: self.copy(two(), two(), self.slot(5, a), p.pair()))

    def planes(self, far):
        p = self.p
        t, t2 = (p.others[1], p.others[3]) if far else (p.t, p.others[2])
        return ((p.b, t), (1 - p.b, t), (p.b, t2), (1 - p.b, t2))

    def core(self, which):
        for j in which:
            b, t = self.planes(False)[j]
            src = lambda b=b, t=t: self.plane(b, t)
            self.send(None, lambda j=j, src=src: self.copy(src(), src(), self.slot(6, j), self.p.peer(1)))

    def landed(self, chunks):
        p, t2 = self.p, self.p.others[2]
        for pred, a in chunks:
            if self.cut > 0:
                self.wait(pred, lambda a=a: self.block(a, 1 - p.b, t2, 0, self.cut), self.slot(4, a), p.pair())
            if self.cut < self.n:
                self.wait(pred, lambda a=a: self.block(a, 1 - p.b, t2, self.cut, self.n), self.slot(5, a), p.pair())

    def arrive(self):
        for j, (b, t) in enumerate(self.planes(True)):
            self.wait(None, lambda b=b, t=t: self.plane(b, t), self.slot(6, j), self.p.pair())


GATHER_CUTS = (256, 0, 0, 0, 0, 0)
BY_LINE = (False, False, True, True, True, True)
CUTS = (128, 128, 128, 256, 128, 128, 256)


def slots_of(line):
    return 6 * line + 6


def add_into(dst, *others):
    rows = dst.shape[0]
    step = min(rows, 32)

    def body(i, _):
        at = pl.ds(pl.multiple_of(i * step, step), step)
        total = dst[at, :]
        for other in others:
            total = total + other[at, :]
        dst[at, :] = total
        return 0

    lax.fori_loop(0, rows // step, body, 0)


def block_of(place, q):
    y, c = place.t // 2, lax.rem(place.t, 2)
    return lax.rem(y + 1 + q, 2) * 2 + lax.rem(c + 1 - q // 2, 2)


class Scatter(Script):
    def __init__(
        self, place, ssem, rsem, far, met, acc, out, bufs, base, cut,
        before_far=None, before_cross=None, before_line=None, release=None,
    ):
        super().__init__(ssem, rsem)
        self.p = place
        self.acc, self.out = acc, out
        self.rdx, self.rdy, self.rx, self.ry, self.near = bufs
        self.n = out.shape[1]
        self.base, self.cut = base, cut
        self.own = lambda *at: acc.at[(1, at[0], place.b) + at[1:]]
        self.by_pair = lambda *at: acc.at[(1, at[0], 1 - place.b) + at[1:]]
        self.by_y = lambda *at: acc.at[(0, at[0], place.b) + at[1:]]
        self.by_both = lambda *at: acc.at[(0, at[0], 1 - place.b) + at[1:]]
        if far is not None:
            for i in range(2):
                self.step()
                if i == 0 and before_far is not None:
                    before_far(self)
                self.send(None, lambda i=i: self.copy(far(i), met.at[i], base + i, place.peer(1)))
            for i in range(2):
                self.step()
                self.wait(None, lambda i=i: met.at[i], base + i, place.pair())
        every, first, late = slice(None), pl.ds(0, cut), pl.ds(cut, self.n - cut)
        pair, y = place.pair(), place.peer(2)
        lines = range(place.line)

        def give(src, dst, slot, device):
            self.send(None, lambda: self.copy(src(), dst(), base + slot, device))

        def take(ref, slot):
            self.wait(None, ref, base + slot, pair)

        def add(dst, *others):
            for a in lines:
                self.do(None, lambda a=a: add_into(dst(a), *[other(a) for other in others]))

        some, rest = cut > 0, cut < self.n
        self.step()
        if before_cross is not None:
            before_cross(self)
        if some:
            give(lambda: self.by_both(every, every, first), lambda: self.rdy, 4, y)
        if rest:
            give(lambda: self.by_both(every, every, late), lambda: self.rdx, 5, pair)
        if some:
            give(lambda: self.by_y(every, every, first), lambda: self.ry.at[:, :, first], 7, y)
        self.step()
        if rest:
            give(lambda: self.by_pair(every, every, late), lambda: self.rx.at[:, :, late], 6, pair)
        self.step()
        if some:
            take(lambda: self.rdy, 4)
            add(lambda a: self.by_pair(a, every, first), lambda a: self.rdy.at[a])
            give(lambda: self.by_pair(every, every, first), lambda: self.rx.at[:, :, first], 8, pair)
        self.step()
        if rest:
            take(lambda: self.rdx, 5)
            add(lambda a: self.by_y(a, every, late), lambda a: self.rdx.at[a])
            give(lambda: self.by_y(every, every, late), lambda: self.ry.at[:, :, late], 9, y)
        self.step()
        if rest:
            take(lambda: self.rx.at[:, :, late], 6)
        if some:
            take(lambda: self.ry.at[:, :, first], 7)
            take(lambda: self.rx.at[:, :, first], 8)
        if rest:
            take(lambda: self.ry.at[:, :, late], 9)
        if before_line is not None:
            before_line(self)
        for pred, chunk in reversed(list(order(place))[1:]):
            self.do(pred, lambda chunk=chunk: add_into(self.own(chunk), self.rx.at[chunk], self.ry.at[chunk]))
            self.send(pred, lambda chunk=chunk: self.copy(
                self.own(chunk), self.near.at[place.a], base + 10 + place.a, place.at(chunk, place.b, place.t)))
        self.do(None, lambda: add_into(self.own(place.a), self.rx.at[place.a], self.ry.at[place.a]))
        self.step()
        for pred, a in list(order(place))[1:]:
            self.wait(pred, lambda a=a: self.near.at[a], base + 10 + a, pair)
        self.do(None, self.close)
        if release is not None:
            sent, self.sent = self.sent[2:], self.sent[:2]
            for pred, make in sent:
                self.do(pred, lambda make=make: make().wait_send())
            release(self)

    def close(self):
        p = self.p
        rows = self.out.shape[0]
        step = min(rows, 16)

        def body(i, _):
            at = pl.ds(pl.multiple_of(i * step, step), step)
            value = self.acc[1, p.a, p.b, at, :].astype(F32)
            for k in range(1, p.line):
                value = value + self.near[lax.rem(p.a + k, p.line), at, :].astype(F32)
            self.out[at, :] = value
            return 0

        lax.fori_loop(0, rows // step, body, 0)


def landing(line, depth, n, by_pair, by_y):
    widths = (max(by_pair, 128), max(by_y, 128), n, n, n)
    return [pltpu.VMEM((line, depth, width), BF) for width in widths]


def sums_of(line):
    return 10 + line


class Trade(Script):
    pass


def heads_forward(q, k, v, allowed, keep):
    lane = lax.broadcasted_iota(jnp.int32, k.shape, 1)
    outs = []
    for h in range(2):
        mine = (lane // HD) == h
        scores = lax.dot_general(
            jnp.where(mine, k, jnp.zeros_like(k)), q, (((1,), (1,)), ((), ())), preferred_element_type=F32
        )
        scores = jnp.where(allowed, scores, -1e30)
        expo = jnp.exp(scores - jnp.max(scores, axis=0, keepdims=True))
        share = 1.0 / jnp.sum(expo, axis=0, keepdims=True)
        expo = expo.astype(BF)
        keep(h, expo, share)
        out = lax.dot_general(v[:, h * HD : (h + 1) * HD], expo, (((0,), (0,)), ((), ())), preferred_element_type=F32)
        outs.append(out * share)
    return jnp.concatenate(outs, axis=0).T.astype(BF)


def norm_stats(values):
    row_mean = jnp.mean(values, axis=-1, keepdims=True)
    centred = values - row_mean
    variance = jnp.mean(centred * centred, axis=-1, keepdims=True)
    inv_std = lax.rsqrt(variance + 1e-05)
    return centred * inv_std, inv_std


class Schedule:
    def __init__(self, text, scripts):
        self.after = {}
        at = ("", 0)
        counts = {}
        for ch in "".join(text):
            if ch.isupper():
                at = (ch, counts.get(ch, 0))
                counts[ch] = at[1] + 1
            else:
                self.after.setdefault(at, []).extend(scripts[ch].steps.pop(0))

    def run(self, name="", i=0):
        for pred, act in self.after.pop((name, i), ()):
            when(pred, act)

    def run_at(self, name, i):
        for at in sorted(k for n, k in self.after if n == name):
            pl.when(i == at)(lambda at=at: self.run(name, at))


ORDER = (
    "20K220001140021r4144000022222101",
    "10214220434145rr0LPH2344403HP2H1",
    "12244222202H133P25H154HP2415135H",
    "33H14344444r45G3O3Fd535F3d55dF45",
    "33333333ddFF5e5dFe555535d5de555F",
    "eeF3TueTu5duTeueTTvTvuevTvvTNUod",
    "vUuovvuoeUuoUDAWqAWoqAoqWAqWoAWw",
    "vAquWwwqoAWAwWwEEqqEEwwwMYosqYYY",
    "YYYYZfwfqfvoutwftfs",
)


def heads_backward(q, k, v, o, do, expo, shares):
    lane = lax.broadcasted_iota(jnp.int32, k.shape, 1)
    first = lane < HD
    column = shares.T
    do = (do.astype(F32) * jnp.where(first, column[:, :1], column[:, 1:2])).astype(BF)
    product = do.astype(F32) * o.astype(F32)
    zero = jnp.zeros_like(k)
    dq_t, dk, dv = [], [], []
    for h in range(2):
        mine = (lane // HD) == h
        inner = jnp.sum(jnp.where(mine, product, 0.0), axis=1, keepdims=True).T
        dprobs = lax.dot_general(
            jnp.where(mine, v, zero), do, (((1,), (1,)), ((), ())), preferred_element_type=F32
        )
        got = expo[h]
        dscores = (got.astype(F32) * (dprobs - inner)).astype(BF)
        dv.append(jnp.dot(got, do, preferred_element_type=F32))
        dk.append(jnp.dot(dscores, q, preferred_element_type=F32))
        dq_t.append(
            lax.dot_general(k[:, h * HD : (h + 1) * HD], dscores, (((0,), (0,)), ((), ())), preferred_element_type=F32)
        )
    return (
        (jnp.concatenate(dq_t, axis=0).T * HD ** (-0.5)).astype(BF),
        jnp.where(first, dk[0], dk[1]).astype(BF),
        jnp.where(first, dv[0], dv[1]).astype(BF),
    )


def norm_back(upstream, unit, inv_std, gain):
    scaled = upstream * gain
    inner_mean = jnp.mean(scaled, axis=-1, keepdims=True)
    cross_mean = jnp.mean(scaled * unit, axis=-1, keepdims=True)
    return inv_std * (scaled - inner_mean - unit * cross_mean)


def layer_kernel(line, *refs):
    toks, grads, raw_q, w1, raw_o, raw_2, marks, b_fc1, b_qv = refs[:9]
    vectors = refs[9:15]
    sq, so, s1, s2, lo, gtok, sums = refs[15:22]
    xin, gin, fq, fo, f1, f2, qkv_kept, probs, o_kept, x1_kept, h1_kept, h2_kept, act, slope = refs[22:36]
    big1, met1, bigo, meto, acc2, dqkv = refs[36:42]
    bufs = [refs[42 + 5 * i : 47 + 5 * i] for i in range(5)]
    g, dh2, g1b, low, here, cold, colx, coly, far_sums = refs[67:76]
    sml, small, wq, wo, w2, marked, vecs, masks, shares, lsem, ssem, rsem, free = refs[76:]
    place = Place(line)
    rows, width = g.shape
    part = rows // 4
    n1, no, nq = s1.shape[1], so.shape[1], sq.shape[1]
    local = no
    pairs = width // 128
    half_block = n1 // TILE
    tiles = 4 * half_block
    block_shape = big1.shape[1:4]
    greet(place, whole_line=True)

    per = slots_of(line)
    part_of = lambda ref, h: ref.at[:, pl.ds(h * TILE, TILE)]
    pieces = [(wq, fq, 0), (wo, fo, 0)]
    for h in range(half_block):
        pieces += [(part_of(w1, h), f1, h * TILE), (part_of(w2, h), f2, h * TILE)]
    gathers = [
        Gather(place, ssem, rsem, lsem.at[i], shard, whole, i * per, GATHER_CUTS[i], BY_LINE[i], first)
        for i, (shard, whole, first) in enumerate(pieces)
    ]
    rows_at = len(pieces) * per
    rows_sem = len(pieces)
    trade = Trade(ssem, rsem)
    slot_of = lambda j, k: rows_at + j * 4 + k
    pairs_of_rows = ((toks, xin), (grads, gin))
    mine = [pltpu.make_async_copy(src.at[place.t], dst.at[0], lsem.at[rows_sem + j]) for j, (src, dst) in enumerate(pairs_of_rows)]
    mine.append(pltpu.make_async_copy(small, sml.at[place.t], lsem.at[rows_sem + 2]))
    for j, (src, dst) in enumerate(pairs_of_rows):
        trade.step()
        trade.do(None, mine[j].start)
        for k in (2, 3, 1):
            trade.send(None, lambda src=src, dst=dst, j=j, k=k: trade.copy(
                src.at[place.others[k]], dst.at[k], slot_of(j, k), place.peer(k)))
        if j == 0:
            trade.do(None, mine[2].start)
            for k in (2, 3, 1):
                trade.send(None, lambda k=k: trade.copy(small, sml.at[place.t], slot_of(2, k), place.peer(k)))
    for j, (src, dst) in enumerate(pairs_of_rows):
        trade.step()
        trade.do(None, mine[j].wait)
        for k in (2, 3, 1):
            trade.wait(None, lambda dst=dst, k=k: dst.at[k], slot_of(j, k), place.pair())
        if j == 0:
            trade.do(None, mine[2].wait)
            for k in (2, 3, 1):
                trade.wait(None, lambda k=k: sml.at[place.others[k]], slot_of(2, k), place.pair())

    def tell(i, device):
        pl.semaphore_signal(free.at[i], inc=1, device_id=device, device_id_type=MESH)

    def hear(i):
        pl.semaphore_wait(free.at[i], 1)

    pair_at = lambda h: 4 + 2 * h
    line_at = lambda h: 8 + line * h

    def release(h):
        def add(script):
            script.do(None, lambda: tell(pair_at(h), place.pair()))
            script.do(None, lambda: tell(pair_at(h) + 1, place.peer(2)))
            for k in range(1, line):
                to = place.at(lax.rem(place.a + k, line), place.b, place.t)
                script.do(None, lambda to=to: tell(line_at(h) + place.a, to))

        return add

    def before_far(i):
        return lambda script: script.do(None, lambda: hear(i))

    def before_cross(h):
        def add(script):
            script.do(None, lambda: hear(pair_at(h)))
            script.do(None, lambda: hear(pair_at(h) + 1))

        return add

    def before_line(h):
        def add(script):
            for k in range(1, line):
                script.do(None, lambda k=k: hear(line_at(h) + lax.rem(place.a + k, line)))

        return add

    base = rows_at + 12
    each = sums_of(line)
    nh = nq // 2
    two = lambda ref: ref.at[pl.ds(2, 2)]
    last = lambda ref, cols: ref.at[:, :, :, :, cols]
    scatter = lambda *args, **more: Scatter(place, ssem, rsem, *args, **more)
    sum_u, sum_d, sum_q = [], [], []
    for h in range(2):
        cols = pl.ds(h * TILE, TILE)
        cols_q = pl.ds(h * TILE, nh)
        cq, cu, cd = CUTS[h], CUTS[3 + h], CUTS[5 + h]
        rdx, rdy, rx, ry, near = bufs[3 + h]
        sum_u.append(scatter(
            lambda i, cols=cols: big1.at[i, :, :, :, cols], last(met1, cols), last(two(big1), cols), part_of(s1, h),
            bufs[1 + h], base + (1 + h) * each, cu, before_far=before_far(2 + h),
        ))
        sum_d.append(scatter(
            lambda i, cols=cols: big1.at[i, :, :, :, cols], last(met1, cols), last(acc2, cols), part_of(s2, h),
            (rdx.at[:, :, pl.ds(0, TILE - cd)], rdy.at[:, :, pl.ds(0, cd)], rx, ry, near),
            base + (3 + h) * each, cd, release=release(h),
        ))
        sum_q.append(scatter(
            lambda i, cols=cols_q: big1.at[i, :, :, :, cols], last(met1, cols_q), last(acc2, cols_q),
            sq.at[:, pl.ds(h * nh, nh)],
            (
                rdx.at[:, :, pl.ds(0, nh - cq)],
                rdy.at[:, :, pl.ds(0, cq)] if cq > 0 else rdy,
                *[ref.at[:, :, pl.ds(0, nh)] for ref in (rx, ry, near)],
            ),
            base + (5 + h) * each, cq,
            before_far=before_far(h), before_cross=before_cross(h), before_line=before_line(h),
        ))
    sum_o = scatter(lambda i: bigo.at[i], meto, two(bigo), so, bufs[0], base, CUTS[2])

    def rows_home(src, dst, first, sem):
        home = Trade(ssem, rsem)
        stay = pltpu.make_async_copy(src.at[pl.ds(0, part)], dst.at[place.t], sem)
        home.step()
        home.do(None, stay.start)
        for k in (2, 3, 1):
            home.send(None, lambda k=k: home.copy(
                src.at[pl.ds(k * part, part)], dst.at[place.t], first + k, place.peer(k)))
        home.step()
        home.do(None, stay.wait)
        for k in (2, 3, 1):
            home.wait(None, lambda k=k: dst.at[place.others[k]], first + k, place.pair())
        return home

    base = base + 7 * each
    token_rows = rows_home(low, gtok, base, lsem.at[rows_sem + 3])
    out_rows = rows_home(g, lo, base + 4, lsem.at[rows_sem + 4])

    base = base + 8
    few = Trade(ssem, rsem)
    hops = ((cold, place.peer(1)), (colx, place.pair()), (coly, place.peer(2)))

    def fold(i, land):
        here[i + 1] = here[i] + land[...]

    few.step()
    for i, (land, device) in enumerate(hops):
        few.send(None, lambda i=i, land=land, device=device: few.copy(here.at[i], land, base + i, device))
        few.step()
        few.wait(None, lambda land=land: land, base + i, place.pair())
        few.do(None, lambda i=i, land=land: fold(i, land))
    for k in range(1, line):
        far = lax.rem(place.a + k, line)
        few.send(None, lambda far=far, k=k: few.copy(
            here.at[3], far_sums.at[k], base + 3 + k, place.at(far, place.b, place.t)))
    few.step()
    for k in range(1, line):
        few.wait(None, lambda k=k: far_sums.at[k], base + 3 + k, place.pair())

    scripts = {str(i): w for i, w in enumerate(gathers)}
    scripts.update(
        {
            "r": trade, "q": sum_q[0], "w": sum_q[1], "o": sum_o, "u": sum_u[0], "v": sum_u[1], "d": sum_d[0],
            "e": sum_d[1], "s": token_rows, "t": out_rows, "f": few,
        }
    )
    plan = Schedule(ORDER, scripts)

    def tile_of(j):
        h, q = j // 4, lax.rem(j, 4)
        block = block_of(place, q)
        at = pl.ds(pl.multiple_of(h * TILE, TILE), TILE)
        return q, block, at, pl.ds(pl.multiple_of(block * n1 + h * TILE, TILE), TILE)

    def some(count, body, unroll=1):
        lax.fori_loop(0, count, lambda i, _: (body(i), 0)[1], 0, unroll=unroll)

    def by_rows(body):
        some(rows // ROWS, lambda i: body(i, pl.ds(pl.multiple_of(i * ROWS, ROWS), ROWS)), UNROLL)

    def fetch_rows(src, dst, sem):
        copies = [pltpu.make_async_copy(src.at[k], dst.at[pl.ds(k * part, part)], sem.at[k]) for k in range(4)]
        for c in copies:
            c.start()
        for c in copies:
            c.wait()

    small[...] = jnp.zeros_like(small)
    small[0:1, :] = b_fc1[...].reshape(1, -1)
    small[1:2, :local] = b_qv[0:1, :]
    small[1:2, local : 2 * local] = b_qv[1:2, :]
    for h in range(2):
        for j in range(3):
            wq[:, (h * 3 + j) * 128 : (h * 3 + j + 1) * 128] = raw_q[j, :, h * 128 : (h + 1) * 128]
    plan.run()
    wo[...] = raw_o[...].T
    w2[...] = raw_2[...].T
    plan.run("K")
    for i, vector in enumerate(vectors):
        vecs[i : i + 1, :] = vector[...].reshape(1, -1)
    mark = marks[pl.ds(place.t, 1), :].astype(F32)
    marked[...] = jnp.broadcast_to(mark, (128, rows)).T
    for k in range(4):
        at = pl.ds(k * part, part)
        masks[0, at, :] = marked[pl.ds(pl.multiple_of(place.others[k] * part, 32), part), :]
    masks[1] = jnp.where(jnp.max(mark, axis=1, keepdims=True) > 0, masks[0], 1.0)
    here[0] = jnp.zeros_like(here[0])

    def heads_part(h1, wqv, pbuf, sem):
        fetch_rows(xin, low, sem)

        def first_norm(i, at):
            x = low[at, :].astype(F32)
            unit, _inv = norm_stats(x)
            h1[at, :] = (unit * vecs[0:1, :] + vecs[1:2, :]).astype(BF)
            real = masks[0, at, :1]
            here[0, 0:1, :] += jnp.sum(x * x * real, axis=0, keepdims=True)
            here[0, 2:3, :] += jnp.broadcast_to(jnp.sum(real, axis=0, keepdims=True), (1, width))

        by_rows(first_norm)
        save_h1 = pltpu.make_async_copy(h1, h1_kept, sem.at[4])
        save_h1.start()
        plan.run("L")
        block_at = lambda i: block_of(place, 3 - i)
        fetch = lambda i, slot: pltpu.make_async_copy(
            fq.at[:, :, :, pl.ds(pl.multiple_of(block_at(i) * nq, 128), nq)], wqv.at[slot], sem.at[5 + slot])
        fetch(0, 0).start()
        allowed = masks[1, :, :1] > 0
        save = lambda i, h: pltpu.make_async_copy(pbuf.at[h], probs.at[block_at(i) * 2 + h], sem.at[8 + h])

        def heads_block(i):
            block, slot = block_at(i), lax.rem(i, 2)
            fetch(i, slot).wait()
            got = jnp.dot(h1[...], wqv[slot].reshape(width, nq), preferred_element_type=F32)
            bias = sml[pl.ds(block, 1), 1, : 2 * local]
            for h in range(2):
                q, k, v = (slice((h * 3 + j) * 128, (h * 3 + j + 1) * 128) for j in range(3))
                bq, bv = bias[:, h * 128 : (h + 1) * 128], bias[:, local + h * 128 : local + (h + 1) * 128]
                dqkv[block, :, q] = (got[:, q] + bq).astype(BF) * jnp.asarray(HD ** (-0.5), BF)
                dqkv[block, :, k] = got[:, k].astype(BF)
                dqkv[block, :, v] = (got[:, v] + bv).astype(BF)
            plan.run_at("P", i)

            def pair_step(h):
                pl.when(i >= 1)(lambda: save(i - 1, h).wait())

                def keep(head, got, share):
                    pbuf[h, head] = got
                    shares[block * 2 + h, head : head + 1, :] = share

                cols = [pl.ds(pl.multiple_of((h * 3 + j) * 128, 128), 128) for j in range(3)]
                q, k, v = (dqkv[block, :, c] for c in cols)
                at = pl.ds(pl.multiple_of(block * local + h * 128, 128), 128)
                g1b[:, at] = heads_forward(q, k, v, allowed, keep)
                save(i, h).start()
                plan.run_at("H", 2 * i + h)
                pl.when(jnp.logical_and(h == 0, i < 3))(lambda: fetch(i + 1, 1 - slot).start())

            some(2, pair_step)

        some(4, heads_block)
        save_qkv = pltpu.make_async_copy(dqkv, qkv_kept, sem.at[7])
        save_qkv.start()
        for wait in (save_h1, save_qkv, save(3, 0), save(3, 1)):
            wait.wait()

    pl.run_scoped(
        heads_part,
        pltpu.VMEM((rows, width), BF),
        pltpu.VMEM((2,) + block_shape + (nq,), BF),
        pltpu.VMEM((2, 2, rows, rows), BF),
        pltpu.SemaphoreType.DMA((10,)),
    )

    def hidden_part(wov, h2, gt, w1t, actb, slopeb, sem):
        save_o = pltpu.make_async_copy(g1b, o_kept, sem.at[4])
        save_o.start()
        fetch_o = pltpu.make_async_copy(fo, wov, sem.at[5])
        fetch_o.start()
        fetch_rows(gin, g, sem)

        def mask_rows(i, at):
            masked = g[at, :].astype(F32) * masks[0, at, :1]
            here[0, 3:4, :] += jnp.sum(masked, axis=0, keepdims=True)
            g[at, :] = masked.astype(BF)

        by_rows(mask_rows)
        gt[...] = g[...].T
        plan.run("G")
        fetch_o.wait()
        half = rows // 2

        def join(i):
            at = pl.ds(pl.multiple_of(i * half, 64), half)
            branch = lax.dot_general(
                g1b[at, :], wov[...].reshape(width, width), (((1,), (1,)), ((), ())), preferred_element_type=F32
            ) + vecs[4:5, :]
            here[0, 1:2, :] += jnp.sum(branch * branch * masks[0, at, :1], axis=0, keepdims=True)
            middle = low[at, :].astype(F32) + branch
            dh2[at, :] = middle
            unit, _inv = norm_stats(middle)
            h2[at, :] = (unit * vecs[2:3, :] + vecs[3:4, :]).astype(BF)

        some(2, join)
        save_x1 = pltpu.make_async_copy(dh2, x1_kept, sem.at[6])
        save_h2 = pltpu.make_async_copy(h2, h2_kept, sem.at[7])
        save_x1.start()
        save_h2.start()
        plan.run("O")
        fetch = lambda j, slot: pltpu.make_async_copy(f1.at[:, :, :, tile_of(j)[3]], w1t.at[slot], sem.at[8 + slot])
        fetch(0, 0).start()

        def saves(j, slot):
            cols = tile_of(j)[3]
            return (
                pltpu.make_async_copy(actb.at[slot], act.at[:, cols], sem.at[10 + slot]),
                pltpu.make_async_copy(slopeb.at[slot], slope.at[:, cols], sem.at[12 + slot]),
            )

        def hidden_step(j):
            slot = lax.rem(j, 2)
            pl.when(j + 1 < tiles)(lambda: fetch(j + 1, 1 - slot).start())

            @pl.when(j >= 2)
            def _():
                for save in saves(j - 2, slot):
                    save.wait()

            q, block, at, cols = tile_of(j)
            fetch(j, slot).wait()
            hidden = jnp.dot(h2[...], w1t[slot].reshape(width, TILE), preferred_element_type=F32) + sml[block, 0:1, at]
            gate = jax.nn.sigmoid(1.702 * hidden)
            actb[slot] = (hidden * gate).astype(BF)
            slopeb[slot] = (gate + 1.702 * hidden * gate * (1.0 - gate)).astype(BF)
            for save in saves(j, slot):
                save.start()
            product = jnp.dot(gt[...], actb[slot], preferred_element_type=F32).reshape(block_shape + (TILE,))

            @pl.when(q < 2)
            def _():
                big1[q, :, :, :, at] = product.astype(BF)

            @pl.when(q >= 2)
            def _():
                acc2[q - 2, :, :, :, at] = (product + met1[q - 2, :, :, :, at].astype(F32)).astype(BF)

            plan.run_at("F", j)

        some(tiles, hidden_step)
        for wait in saves(tiles - 2, tiles % 2) + saves(tiles - 1, (tiles - 1) % 2) + (save_o, save_x1, save_h2):
            wait.wait()

    pl.run_scoped(
        hidden_part,
        pltpu.VMEM(fo.shape, BF),
        pltpu.VMEM((rows, width), BF),
        pltpu.VMEM((width, rows), BF),
        pltpu.VMEM((2,) + block_shape + (TILE,), BF),
        pltpu.VMEM((2, rows, TILE), BF),
        pltpu.VMEM((2, rows, TILE), BF),
        pltpu.SemaphoreType.DMA((14,)),
    )
    for h in range(2):
        tell(2 + h, place.peer(1))
        sum_d[h].wait_sent(2)

    dh2[...] = jnp.zeros_like(dh2)

    def feed_forward(h2t, f1t, f2t, slopet, sem):
        def fetch(j, slot):
            cols = tile_of(j)[3]
            return (
                pltpu.make_async_copy(f1.at[:, :, :, cols], f1t.at[slot], sem.at[slot]),
                pltpu.make_async_copy(f2.at[:, :, :, cols], f2t.at[slot], sem.at[2 + slot]),
                pltpu.make_async_copy(slope.at[:, cols], slopet.at[slot], sem.at[4 + slot]),
            )

        load = pltpu.make_async_copy(h2_kept, low, sem.at[6])
        load.start()
        for c in fetch(0, 0):
            c.start()
        load.wait()
        h2t[...] = low[...].T

        def tile(j):
            slot = lax.rem(j, 2)

            @pl.when(j + 1 < tiles)
            def _():
                for c in fetch(j + 1, 1 - slot):
                    c.start()

            for c in fetch(j, slot):
                c.wait()
            q, block, at, cols = tile_of(j)
            du = jnp.dot(g[...], f2t[slot].reshape(width, TILE), preferred_element_type=F32)
            du = (du * slopet[slot].astype(F32)).astype(BF)
            here[0, pl.ds(4 + block, 1), at] = jnp.sum(du.astype(F32), axis=0, keepdims=True)
            product = jnp.dot(h2t[...], du, preferred_element_type=F32).reshape(block_shape + (TILE,))

            @pl.when(q < 2)
            def _():
                big1[q, :, :, :, at] = product.astype(BF)

            @pl.when(q >= 2)
            def _():
                big1[q, :, :, :, at] = (product + met1[q - 2, :, :, :, at].astype(F32)).astype(BF)

            dh2[...] += lax.dot_general(
                du, f1t[slot].reshape(width, TILE), (((1,), (1,)), ((), ())), preferred_element_type=F32
            )
            plan.run_at("T", j)

        some(tiles, tile)

    pl.run_scoped(
        feed_forward,
        pltpu.VMEM((width, rows), BF),
        pltpu.VMEM((2,) + block_shape + (TILE,), BF),
        pltpu.VMEM((2,) + block_shape + (TILE,), BF),
        pltpu.VMEM((2, rows, TILE), BF),
        pltpu.SemaphoreType.DMA((7,)),
    )
    for h in range(2):
        tell(h, place.peer(1))

    def second_norm(xt, sem):
        fetch = lambda i, slot: pltpu.make_async_copy(
            x1_kept.at[pl.ds(pl.multiple_of(i * ROWS, ROWS), ROWS)], xt.at[slot], sem.at[slot])
        fetch(0, 0).start()

        def some_rows(i, at):
            slot = lax.rem(i, 2)
            pl.when(i + 1 < rows // ROWS)(lambda: fetch(i + 1, 1 - slot).start())
            fetch(i, slot).wait()
            unit, inv = norm_stats(xt[slot])
            up = dh2[at, :]
            here[0, 8:9, :] += jnp.sum(up * unit, axis=0, keepdims=True)
            here[0, 9:10, :] += jnp.sum(up, axis=0, keepdims=True)
            g1 = g[at, :].astype(F32) + norm_back(up, unit, inv, vecs[2:3, :])
            rounded = g1.astype(BF)
            g1b[at, :] = rounded
            here[0, 10:11, :] += jnp.sum(rounded.astype(F32), axis=0, keepdims=True)
            dh2[at, :] = g1

        by_rows(some_rows)

    pl.run_scoped(second_norm, pltpu.VMEM((2, ROWS, width), F32), pltpu.SemaphoreType.DMA((2,)))
    plan.run("N")

    def heads(tall, o, wov, do, pt, qt, sem):
        load_o = pltpu.make_async_copy(o_kept, o, sem.at[0])
        load_w = pltpu.make_async_copy(fo, wov, sem.at[1])
        load_h = pltpu.make_async_copy(h1_kept, low, sem.at[6])
        for c in (load_o, load_w, load_h):
            c.start()

        def heads_of(i):
            return block_of(place, lax.rem(i, 4)) * 2 + i // 4

        def fetch(i, slot):
            cols = pl.ds(pl.multiple_of((i // 4) * nh, 128), nh)
            return [
                pltpu.make_async_copy(
                    qkv_kept.at[block_of(place, lax.rem(i, 4)), :, cols], qt.at[slot], sem.at[2 + slot]),
                pltpu.make_async_copy(probs.at[heads_of(i)], pt.at[slot], sem.at[4 + slot]),
            ]

        for c in fetch(0, 0):
            c.start()
        tall[...] = g1b[...].T
        load_o.wait()
        load_w.wait()

        def output_weight(q):
            cols = pl.ds(pl.multiple_of(block_of(place, q) * no, 128), no)
            product = jnp.dot(tall[...], o[:, cols], preferred_element_type=F32).reshape(bigo.shape[1:])

            @pl.when(q < 2)
            def _():
                bigo[q] = product.astype(BF)

            @pl.when(q >= 2)
            def _():
                bigo[q] = (product + meto[q - 2].astype(F32)).astype(BF)

            plan.run_at("U", q)

        some(4, output_weight)
        do[...] = jnp.dot(g1b[...], wov[...].reshape(width, width), preferred_element_type=F32).astype(BF)
        plan.run("D")
        load_h.wait()
        tall[...] = low[...].T
        for script in sum_u:
            script.wait_sent(2)

        def pair_step(i):
            slot = lax.rem(i, 2)
            h, q = i // 4, lax.rem(i, 4)

            @pl.when(i + 1 < pairs)
            def _():
                for c in fetch(i + 1, 1 - slot):
                    c.start()

            for c in fetch(i, slot):
                c.wait()
            cols = pl.ds(pl.multiple_of(heads_of(i) * 128, 128), 128)
            got = heads_backward(
                qt[slot, :, :128], qt[slot, :, 128:256], qt[slot, :, 256:], o[:, cols], do[:, cols], pt[slot],
                shares[heads_of(i)],
            )
            mine = pl.ds(pl.multiple_of(h * nh, 128), nh)
            dqkv[q, :, mine] = jnp.concatenate(got, axis=1)
            plan.run_at("A", i)
            block = block_of(place, q)
            got = dqkv[q, :, mine]
            product = jnp.dot(tall[...], got, preferred_element_type=F32).reshape(block_shape + (nh,))
            total = jnp.sum(got.astype(F32), axis=0, keepdims=True)
            at = pl.ds(pl.multiple_of(block * local + h * 128, 128), 128)
            here[0, 14:15, at] = total[:, :128]
            here[0, 15:16, at] = total[:, 256:]
            to = pl.ds(pl.multiple_of(h * TILE, 128), nh)

            @pl.when(q < 2)
            def _():
                big1[q, :, :, :, to] = product.astype(BF)

            @pl.when(q >= 2)
            def _():
                acc2[q - 2, :, :, :, to] = (product + met1[q - 2, :, :, :, to].astype(F32)).astype(BF)

            plan.run_at("W", i)

        some(pairs, pair_step)

    pl.run_scoped(
        heads,
        pltpu.VMEM((width, rows), BF),
        pltpu.VMEM((rows, width), BF),
        pltpu.VMEM(fo.shape, BF),
        pltpu.VMEM((rows, width), BF),
        pltpu.VMEM((2, 2, rows, rows), BF),
        pltpu.VMEM((2, rows, nh), BF),
        pltpu.SemaphoreType.DMA((7,)),
    )

    def last(dh1, wqv, x, f2t, actt, sem):
        fetch_w = lambda q, slot: pltpu.make_async_copy(
            fq.at[:, :, :, pl.ds(pl.multiple_of(block_of(place, q) * nq, 128), nq)], wqv.at[slot], sem.at[slot])
        load_x = [pltpu.make_async_copy(xin.at[k], x.at[pl.ds(k * part, part)], sem.at[2 + k]) for k in range(4)]
        fetch_w(0, 0).start()
        for c in load_x:
            c.start()
        dh1[...] = jnp.zeros_like(dh1)

        def back(q):
            slot = lax.rem(q, 2)
            pl.when(q < 3)(lambda: fetch_w(q + 1, 1 - slot).start())
            fetch_w(q, slot).wait()
            dh1[...] += lax.dot_general(
                dqkv[q], wqv[slot].reshape(width, nq), (((1,), (1,)), ((), ())), preferred_element_type=F32
            )
            plan.run_at("E", q)

        some(4, back)
        for c in load_x:
            c.wait()

        def some_rows(i, at):
            unit, inv = norm_stats(x[at, :].astype(F32))
            up = dh1[at, :]
            here[0, 12:13, :] += jnp.sum(up * unit, axis=0, keepdims=True)
            here[0, 13:14, :] += jnp.sum(up, axis=0, keepdims=True)
            low[at, :] = (dh2[at, :] + norm_back(up, unit, inv, vecs[0:1, :])).astype(BF)

        by_rows(some_rows)
        plan.run("M")

        def fetch(j, slot):
            cols = tile_of(j)[3]
            return (
                pltpu.make_async_copy(f2.at[:, :, :, cols], f2t.at[slot], sem.at[6 + slot]),
                pltpu.make_async_copy(act.at[:, cols], actt.at[slot], sem.at[8 + slot]),
            )

        load = pltpu.make_async_copy(x1_kept, dh2, sem.at[10])
        load.start()
        for c in fetch(0, 0):
            c.start()
        dh1[...] = jnp.zeros_like(dh1)

        def second_product(j):
            slot = lax.rem(j, 2)

            @pl.when(j + 1 < tiles)
            def _():
                for c in fetch(j + 1, 1 - slot):
                    c.start()

            for c in fetch(j, slot):
                c.wait()
            dh1[...] += lax.dot_general(
                actt[slot], f2t[slot].reshape(width, TILE), (((1,), (1,)), ((), ())), preferred_element_type=F32
            )
            plan.run_at("Y", j)

        some(tiles, second_product)
        load.wait()

        def join(i, at):
            m = dh1[at, :] + vecs[5:6, :]
            g[at, :] = (dh2[at, :] + m).astype(BF)
            here[0, 11:12, :] += jnp.sum(m * m * masks[0, at, :1], axis=0, keepdims=True)

        by_rows(join)
        plan.run("Z")

    pl.run_scoped(
        last,
        pltpu.VMEM((rows, width), F32),
        pltpu.VMEM((2,) + block_shape + (nq,), BF),
        pltpu.VMEM((rows, width), BF),
        pltpu.VMEM((2,) + block_shape + (TILE,), BF),
        pltpu.VMEM((2, rows, TILE), BF),
        pltpu.SemaphoreType.DMA((11,)),
    )
    total = here[3]
    for k in range(1, line):
        total = total + far_sums[k]
    sums[...] = total
    for script in scripts.values():
        script.finish()


def layer(line, toks, grads, w_qkv, w1, w_out, w_fc2, marks, b_fc1, b_qv, *vectors):
    images, part, width = toks.shape
    rows = 4 * part
    depth, n1 = w1.shape
    no, n2, nq = w_out.shape[0], w_fc2.shape[0], 3 * w_qkv.shape[2]
    hidden = 4 * n1
    hbm, vmem = pl.BlockSpec(memory_space=pl.ANY), pl.BlockSpec(memory_space=pltpu.VMEM)
    sds = jax.ShapeDtypeStruct
    block = lambda count, n: pltpu.VMEM((count, line, 2, depth, n), BF)
    few = (16, width)
    count = 6 * slots_of(line) + 12 + 7 * sums_of(line) + 8 + 3 + line
    kept = [
        sds((4, part, width), BF),
        sds((4, part, width), BF),
        *[sds((line, 2, depth, 4 * n), BF) for n in (nq, no, n1, n2)],
        sds((4, rows, nq), BF),
        sds((width // 128, 2, rows, rows), BF),
        sds((rows, width), BF),
        sds((rows, width), F32),
        sds((rows, width), BF),
        sds((rows, width), BF),
        sds((rows, hidden), BF),
        sds((rows, hidden), BF),
    ]
    return pl.pallas_call(
        functools.partial(layer_kernel, line),
        out_shape=[
            sds((depth, nq), F32),
            sds((depth, no), F32),
            sds((depth, n1), F32),
            sds((depth, n2), F32),
            sds((4, part, width), BF),
            sds((4, part, width), BF),
            sds(few, F32),
            *kept,
        ],
        in_specs=[hbm] * 2 + [vmem] + [hbm] + [vmem] * 11,
        out_specs=[vmem] * 4 + [hbm] * 2 + [vmem] + [hbm] * len(kept),
        scratch_shapes=[
            block(4, n1),
            block(2, n1),
            block(4, no),
            block(2, no),
            block(2, n2),
            pltpu.VMEM((4, rows, nq), BF),
            *landing(line, depth, no, no - CUTS[2], CUTS[2]),
            *landing(line, depth, TILE, TILE - CUTS[3], CUTS[3]),
            *landing(line, depth, TILE, TILE - CUTS[4], CUTS[4]),
            *landing(line, depth, TILE, max(TILE - CUTS[5], nq // 2 - CUTS[0]), max(CUTS[5], CUTS[0])),
            *landing(line, depth, TILE, max(TILE - CUTS[6], nq // 2 - CUTS[1]), max(CUTS[6], CUTS[1])),
            pltpu.VMEM((rows, width), BF),
            pltpu.VMEM((rows, width), F32),
            pltpu.VMEM((rows, width), BF),
            pltpu.VMEM((rows, width), BF),
            pltpu.VMEM((4,) + few, F32),
            pltpu.VMEM(few, F32),
            pltpu.VMEM(few, F32),
            pltpu.VMEM(few, F32),
            pltpu.VMEM((line,) + few, F32),
            pltpu.VMEM((4, 8, n1), F32),
            pltpu.VMEM((8, n1), F32),
            pltpu.VMEM((depth, nq), BF),
            pltpu.VMEM((depth, no), BF),
            pltpu.VMEM((depth, n2), BF),
            pltpu.VMEM((rows, 128), F32),
            pltpu.VMEM((8, width), F32),
            pltpu.VMEM((2, rows, 128), F32),
            pltpu.VMEM((width // 128, 2, rows), F32),
            pltpu.SemaphoreType.DMA((11,)),
            pltpu.SemaphoreType.DMA((count,)),
            pltpu.SemaphoreType.DMA((count,)),
            pltpu.SemaphoreType.REGULAR((8 + 2 * line,)),
        ],
        compiler_params=pltpu.CompilerParams(collective_id=0, has_side_effects=True, vmem_limit_bytes=63 * MIB),
        name="layer",
    )(toks, grads, w_qkv, w1, w_out, w_fc2, marks, b_fc1, b_qv, *vectors)[:7]


def finish_kernel(sq, so, s1, s2, lo, gtok, sums, lo_out, gtok_out, *refs):
    out, (rows, sem) = refs[:-2], refs[-2:]
    g_ln1, b_ln1, q, b_qv, o, b_out, g_ln2, b_ln2, one, b_fc1, two, b_fc2, rms = out
    pairs = ((lo, lo_out), (gtok, gtok_out))
    load = [pltpu.make_async_copy(src, rows.at[i], sem.at[i]) for i, (src, dst) in enumerate(pairs)]
    save = [pltpu.make_async_copy(rows.at[i], dst, sem.at[2 + i]) for i, (src, dst) in enumerate(pairs)]
    for c in load:
        c.start()
    t = lax.axis_index("tensor")
    local = b_qv.shape[1]
    for ref, at in ((g_ln1, 12), (b_ln1, 13), (b_out, 10), (g_ln2, 8), (b_ln2, 9), (b_fc2, 3)):
        ref[...] = sums[at, :]
    for l, s in zip(load, save):
        l.wait()
        s.start()
    b_fc1[...] = sums[pl.ds(4 + t, 1), :].reshape(-1)
    at = pl.ds(pl.multiple_of(t * local, 128), local)
    b_qv[0:1, :] = sums[14:15, at]
    b_qv[1:2, :] = sums[15:16, at]
    for h in range(2):
        for j in range(3):
            q[j, :, h * 128 : (h + 1) * 128] = sq[:, (h * 3 + j) * 128 : (h * 3 + j + 1) * 128]
    one[...] = s1[...]
    o[...] = so[...].T
    two[...] = s2[...].T
    count = sums[2:3, 0:1] * sums.shape[1]
    squares = [jnp.sum(sums[i : i + 1, :], axis=1, keepdims=True) for i in (0, 1, 11)]
    lane = lax.broadcasted_iota(jnp.int32, rms.shape, 1)
    total = jnp.where(lane == 0, squares[0], jnp.where(lane == 1, squares[1], squares[2]))
    rms[...] = jnp.sqrt(total / count)
    for s in save:
        s.wait()


def finish(sum_q, sum_o, sum_1, sum_2, layer_out, grad_tokens, sums):
    width = sums.shape[1]
    depth, no = sum_o.shape
    n2 = sum_2.shape[1]
    sds = jax.ShapeDtypeStruct
    row = sds((width,), F32)
    hbm, vmem = pl.BlockSpec(memory_space=pl.ANY), pl.BlockSpec(memory_space=pltpu.VMEM)
    lo, gtok, g_ln1, b_ln1, q, b_qv, o, b_out, g_ln2, b_ln2, one, b_fc1, two, b_fc2, rms = pl.pallas_call(
        finish_kernel,
        out_shape=[
            sds(layer_out.shape, BF), sds(grad_tokens.shape, BF), row, row, sds((3, depth, no), F32), sds((2, no), F32),
            sds((no, depth), F32), row, row, row, sds(sum_1.shape, F32), sds((sum_1.shape[1],), F32),
            sds((n2, depth), F32), row, sds((1, 128), F32),
        ],
        in_specs=[vmem] * 4 + [hbm] * 2 + [vmem],
        out_specs=[hbm] * 2 + [vmem] * 13,
        scratch_shapes=[pltpu.VMEM((2,) + layer_out.shape, BF), pltpu.SemaphoreType.DMA((4,))],
        compiler_params=pltpu.CompilerParams(vmem_limit_bytes=63 * MIB),
        name="finish",
    )(sum_q, sum_o, sum_1, sum_2, layer_out, grad_tokens, sums)
    return (
        lo, gtok, g_ln1, b_ln1, q.transpose(1, 0, 2), b_qv, o, b_out, g_ln2, b_ln2, one, b_fc1, two, b_fc2, rms[0, :3]
    )


def shards(
    tokens, token_mask, out_grad, ln1_gain, ln1_bias, w_qkv, b_qv, w_out, b_out,
    ln2_gain, ln2_bias, w_fc1, b_fc1, w_fc2, b_fc2,
):
    line = lax.axis_size("dp") // 2
    sums = layer(
        line, tokens, out_grad, w_qkv.transpose(1, 0, 2), w_fc1, w_out, w_fc2, token_mask, b_fc1, b_qv,
        ln1_gain, ln1_bias, ln2_gain, ln2_bias, b_out, b_fc2,
    )
    return finish(*sums)


def solution(mesh):
    rowwise = P("dp", "tensor", None)
    placed = (
        rowwise, P("dp", None), rowwise, P(), P(), P("dp", None, "tensor"), P(None, "tensor"), P("tensor", "dp"),
        P(), P(), P(), P("dp", "tensor"), P("tensor"), P("tensor", "dp"), P(),
    )
    return jax.shard_map(
        shards,
        mesh=mesh,
        in_specs=placed,
        out_specs=(
            rowwise, rowwise, P(), P(), P("dp", None, "tensor"), P(None, "tensor"), P("tensor", "dp"), P(),
            P(), P(), P("dp", "tensor"), P("tensor"), P("tensor", "dp"), P(), P(),
        ),
        check_vma=False,
    )
```

```python
import functools

import jax
import jax.numpy as jnp
from jax import lax
from jax.experimental import pallas as pl
from jax.experimental.pallas import tpu as pltpu
from jax.sharding import PartitionSpec as P

HD = 64
MESH = pl.DeviceIdType.MESH
BF = jnp.bfloat16
F32 = jnp.float32
ROWS = 64
TILE = 512
UNROLL = 2
MIB = 1024 * 1024


class Place:
    def __init__(self, line):
        self.line = line
        self.d = lax.axis_index("dp")
        self.t = lax.axis_index("tensor")
        self.a = self.d // 2
        self.b = lax.rem(self.d, 2)
        y, c = self.t // 2, lax.rem(self.t, 2)
        self.others = (self.t, y * 2 + 1 - c, (1 - y) * 2 + c, (1 - y) * 2 + 1 - c)
        self.low, self.high = self.a > 0, self.a < line - 1
        self.inner = jnp.logical_and(self.low, self.high)

    def at(self, a, b, t):
        return (a * 2 + b, t)

    def pair(self):
        return self.at(self.a, 1 - self.b, self.t)

    def peer(self, k):
        return (self.d, self.others[k])

    def up(self):
        return self.at(self.a + 1, self.b, self.t)

    def down(self):
        return self.at(self.a - 1, self.b, self.t)


def greet(place, whole_line=False):
    barrier = pltpu.get_barrier_semaphore()

    def hail(device):
        pl.semaphore_signal(barrier, inc=1, device_id=device, device_id_type=MESH)

    line = place.line
    hail(place.pair())
    for k in range(1, 4):
        hail(place.peer(k))
    if whole_line:
        for k in range(1, line):
            hail(place.at(lax.rem(place.a + k, line), place.b, place.t))
        pl.semaphore_wait(barrier, 3 + line)
        return
    pl.when(place.low)(lambda: hail(place.down()))
    pl.when(place.high)(lambda: hail(place.up()))
    pl.when(place.inner)(lambda: pl.semaphore_wait(barrier, 6))
    pl.when(jnp.logical_not(place.inner))(lambda: pl.semaphore_wait(barrier, 5))


def both(p, q):
    if p is None:
        return q
    if q is None:
        return p
    return jnp.logical_and(p, q)


def when(pred, act):
    if pred is None:
        act()
    else:
        pl.when(pred)(act)


class Script:
    def __init__(self, ssem, rsem):
        self.ssem, self.rsem = ssem, rsem
        self.sent = []
        self.steps = []

    def copy(self, src, dst, slot, device):
        return pltpu.make_async_remote_copy(
            src_ref=src,
            dst_ref=dst,
            send_sem=self.ssem.at[slot],
            recv_sem=self.rsem.at[slot],
            device_id=device,
            device_id_type=MESH,
        )

    def step(self):
        self.steps.append([])

    def do(self, pred, act):
        self.steps[-1].append((pred, act))

    def send(self, pred, make):
        self.do(pred, lambda: make().start())
        self.sent.append((pred, make))

    def wait(self, pred, ref, slot, device):
        self.do(pred, lambda: self.copy(ref(), ref(), slot, device).wait_recv())

    def run(self, count=1):
        for _ in range(count):
            for pred, act in self.steps.pop(0):
                when(pred, act)

    def wait_sent(self, count):
        for pred, make in self.sent[:count]:
            when(pred, lambda make=make: make().wait_send())
        self.sent = self.sent[count:]

    def finish(self):
        assert not self.steps
        for pred, make in self.sent:
            when(pred, lambda make=make: make().wait_send())


def thirds(line):
    return [1], [2] if line > 2 else [], list(range(3, line))


def order(place):
    yield None, place.a
    for k in range(1, place.line):
        yield place.a >= k, place.a - k
        yield place.a + k <= place.line - 1, place.a + k


class Gather(Script):
    def __init__(self, place, ssem, rsem, local_sem, shard, whole, base, cut, by_line, first=0):
        super().__init__(ssem, rsem)
        self.p = place
        self.shard, self.whole = shard, whole
        self.n = shard.shape[1]
        self.first, self.apart = first, whole.shape[3] // 4
        self.base, self.cut, self.by_line = base, cut, by_line
        line, few = place.line, 1 if by_line else place.line
        sizes = (line, line, line, line, few, few, 4, line if by_line else 0, 0)
        self.offsets = [sum(sizes[:kind]) for kind in range(9)]
        p = place
        t2 = p.others[2]
        local = pltpu.make_async_copy(shard, self.block(p.a, p.b, p.t), local_sem)
        own = lambda: self.shard
        groups = thirds(p.line)
        apart = list(order(p))
        rings = [[i for k in group for i in apart[2 * k - 1 : 2 * k + 1]] for group in groups]

        def along(group, kind, b, t, spread):
            for up in (True, False):
                self.step()
                for k in group:
                    self.receive(k, kind, b, t, spread, up)

        self.step()
        self.pass_line(None, p.a, 1, True, own, 0, p.b, p.t)
        self.pass_line(None, p.a, 1, False, own, 0, p.b, p.t)
        self.spread(None, p.a, own)
        self.do(None, local.start)
        along(groups[0], 0, p.b, p.t, True)
        self.step()
        self.cross(apart[:1])
        along(groups[1], 0, p.b, p.t, True)
        self.step()
        if by_line:
            self.landed(apart[:1])
            diagonal = lambda: self.block(p.a, 1 - p.b, t2)
            self.pass_line(None, p.a, 1, True, diagonal, 7, 1 - p.b, t2)
            self.pass_line(None, p.a, 1, False, diagonal, 7, 1 - p.b, t2)
        else:
            self.cross(rings[0])
        along(groups[2], 0, p.b, p.t, True)
        if by_line:
            for group in groups:
                along(group, 7, 1 - p.b, t2, False)
        for ring in rings if by_line else rings[1:]:
            self.step()
            (self.settle if by_line else self.cross)(ring)
        self.do(None, local.wait)
        for j in range(3):
            self.step()
            self.core((j,))
        self.step()
        if not by_line:
            self.landed(apart)
        self.core((3,))
        self.step()
        self.arrive()

    def block(self, a, b, t, lo=0, hi=None):
        hi = self.n if hi is None else hi
        start = pl.multiple_of(t * self.apart + self.first + lo, 128)
        return self.whole.at[a, b, :, pl.ds(start, hi - lo)]

    def plane(self, b, t):
        start = pl.multiple_of(t * self.apart + self.first, 128)
        return self.whole.at[:, b, :, pl.ds(start, self.n)]

    def slot(self, kind, i):
        return self.base + self.offsets[kind] + (0 if self.by_line and kind in (4, 5) else i)

    def spread(self, pred, a, src):
        p = self.p
        self.send(pred, lambda: self.copy(src(), self.block(a, p.b, p.t), self.slot(2, a), p.pair()))
        self.send(pred, lambda: self.copy(src(), self.block(a, p.b, p.t), self.slot(3, a), p.peer(2)))

    def pass_line(self, pred, a, step, up, src, kind, b, t):
        p = self.p
        if step > p.line - 1:
            return
        ok = both(pred, p.high if up else p.low)
        to = p.up if up else p.down
        slot = self.slot(kind if up else kind + 1, step)
        self.send(ok, lambda: self.copy(src(), self.block(a, b, t), slot, to()))

    def receive(self, k, kind, b, t, spread, up):
        p = self.p
        chunk = p.a - k if up else p.a + k
        pred = p.a >= k if up else p.a + k <= p.line - 1
        src = lambda: self.block(chunk, b, t)
        self.wait(pred, src, self.slot(kind if up else kind + 1, k), p.pair())
        self.pass_line(pred, chunk, k + 1, up, src, kind, b, t)
        if spread:
            self.spread(pred, chunk, src)

    def settle(self, chunks):
        p = self.p
        for pred, a in chunks:
            self.wait(pred, lambda a=a: self.block(a, 1 - p.b, p.t), self.slot(2, a), p.pair())
            self.wait(pred, lambda a=a: self.block(a, p.b, p.others[2]), self.slot(3, a), p.pair())

    def cross(self, chunks):
        p, t2 = self.p, self.p.others[2]
        for pred, a in chunks:
            self.settle([(pred, a)])
            one = lambda a=a: self.block(a, 1 - p.b, p.t, 0, self.cut)
            two = lambda a=a: self.block(a, p.b, t2, self.cut, self.n)
            if self.cut > 0:
                self.send(pred, lambda a=a, one=one: self.copy(one(), one(), self.slot(4, a), p.peer(2)))
            if self.cut < self.n:
                self.send(pred, lambda a=a, two=two: self.copy(two(), two(), self.slot(5, a), p.pair()))

    def planes(self, far):
        p = self.p
        t, t2 = (p.others[1], p.others[3]) if far else (p.t, p.others[2])
        return ((p.b, t), (1 - p.b, t), (p.b, t2), (1 - p.b, t2))

    def core(self, which):
        for j in which:
            b, t = self.planes(False)[j]
            src = lambda b=b, t=t: self.plane(b, t)
            self.send(None, lambda j=j, src=src: self.copy(src(), src(), self.slot(6, j), self.p.peer(1)))

    def landed(self, chunks):
        p, t2 = self.p, self.p.others[2]
        for pred, a in chunks:
            if self.cut > 0:
                self.wait(pred, lambda a=a: self.block(a, 1 - p.b, t2, 0, self.cut), self.slot(4, a), p.pair())
            if self.cut < self.n:
                self.wait(pred, lambda a=a: self.block(a, 1 - p.b, t2, self.cut, self.n), self.slot(5, a), p.pair())

    def arrive(self):
        for j, (b, t) in enumerate(self.planes(True)):
            self.wait(None, lambda b=b, t=t: self.plane(b, t), self.slot(6, j), self.p.pair())


GATHER_CUTS = (256, 0, 0, 0, 0, 0)
BY_LINE = (False, True, True, True, True, True)
CUTS = (0, 128, 128, 256, 128, 128, 256)


def slots_of(line):
    return 6 * line + 6


def add_into(dst, *others):
    rows = dst.shape[0]
    step = min(rows, 32)

    def body(i, _):
        at = pl.ds(pl.multiple_of(i * step, step), step)
        total = dst[at, :]
        for other in others:
            total = total + other[at, :]
        dst[at, :] = total
        return 0

    lax.fori_loop(0, rows // step, body, 0)


def block_of(place, q):
    y, c = place.t // 2, lax.rem(place.t, 2)
    return lax.rem(y + 1 + q, 2) * 2 + lax.rem(c + 1 - q // 2, 2)


class Scatter(Script):
    def __init__(
        self, place, ssem, rsem, far, met, acc, out, bufs, base, cut,
        before_far=None, before_cross=None, before_line=None, release=None,
    ):
        super().__init__(ssem, rsem)
        self.p = place
        self.acc, self.out = acc, out
        self.rdx, self.rdy, self.rx, self.ry, self.near = bufs
        self.n = out.shape[1]
        self.base, self.cut = base, cut
        self.own = lambda *at: acc.at[(1, at[0], place.b) + at[1:]]
        self.by_pair = lambda *at: acc.at[(1, at[0], 1 - place.b) + at[1:]]
        self.by_y = lambda *at: acc.at[(0, at[0], place.b) + at[1:]]
        self.by_both = lambda *at: acc.at[(0, at[0], 1 - place.b) + at[1:]]
        if far is not None:
            for i in range(2):
                self.step()
                if i == 0 and before_far is not None:
                    before_far(self)
                self.send(None, lambda i=i: self.copy(far(i), met.at[i], base + i, place.peer(1)))
            for i in range(2):
                self.step()
                self.wait(None, lambda i=i: met.at[i], base + i, place.pair())
        every, first, late = slice(None), pl.ds(0, cut), pl.ds(cut, self.n - cut)
        pair, y = place.pair(), place.peer(2)
        lines = range(place.line)

        def give(src, dst, slot, device):
            self.send(None, lambda: self.copy(src(), dst(), base + slot, device))

        def take(ref, slot):
            self.wait(None, ref, base + slot, pair)

        def add(dst, *others):
            for a in lines:
                self.do(None, lambda a=a: add_into(dst(a), *[other(a) for other in others]))

        some, rest = cut > 0, cut < self.n
        self.step()
        if before_cross is not None:
            before_cross(self)
        if some:
            give(lambda: self.by_both(every, every, first), lambda: self.rdy, 4, y)
        if rest:
            give(lambda: self.by_both(every, every, late), lambda: self.rdx, 5, pair)
        if some:
            give(lambda: self.by_y(every, every, first), lambda: self.ry.at[:, :, first], 7, y)
        self.step()
        if rest:
            give(lambda: self.by_pair(every, every, late), lambda: self.rx.at[:, :, late], 6, pair)
        self.step()
        if some:
            take(lambda: self.rdy, 4)
            add(lambda a: self.by_pair(a, every, first), lambda a: self.rdy.at[a])
            give(lambda: self.by_pair(every, every, first), lambda: self.rx.at[:, :, first], 8, pair)
        self.step()
        if rest:
            take(lambda: self.rdx, 5)
            add(lambda a: self.by_y(a, every, late), lambda a: self.rdx.at[a])
            give(lambda: self.by_y(every, every, late), lambda: self.ry.at[:, :, late], 9, y)
        self.step()
        if rest:
            take(lambda: self.rx.at[:, :, late], 6)
        if some:
            take(lambda: self.ry.at[:, :, first], 7)
            take(lambda: self.rx.at[:, :, first], 8)
        if rest:
            take(lambda: self.ry.at[:, :, late], 9)
        if before_line is not None:
            before_line(self)
        for pred, chunk in reversed(list(order(place))[1:]):
            self.do(pred, lambda chunk=chunk: add_into(self.own(chunk), self.rx.at[chunk], self.ry.at[chunk]))
            self.send(pred, lambda chunk=chunk: self.copy(
                self.own(chunk), self.near.at[place.a], base + 10 + place.a, place.at(chunk, place.b, place.t)))
        self.do(None, lambda: add_into(self.own(place.a), self.rx.at[place.a], self.ry.at[place.a]))
        self.step()
        for pred, a in list(order(place))[1:]:
            self.wait(pred, lambda a=a: self.near.at[a], base + 10 + a, pair)
        self.do(None, self.close)
        if release is not None:
            sent, self.sent = self.sent[2:], self.sent[:2]
            for pred, make in sent:
                self.do(pred, lambda make=make: make().wait_send())
            release(self)

    def close(self):
        p = self.p
        rows = self.out.shape[0]
        step = min(rows, 16)

        def body(i, _):
            at = pl.ds(pl.multiple_of(i * step, step), step)
            value = self.acc[1, p.a, p.b, at, :].astype(F32)
            for k in range(1, p.line):
                value = value + self.near[lax.rem(p.a + k, p.line), at, :].astype(F32)
            self.out[at, :] = value
            return 0

        lax.fori_loop(0, rows // step, body, 0)


def landing(line, depth, n, by_pair, by_y):
    widths = (max(by_pair, 128), max(by_y, 128), n, n, n)
    return [pltpu.VMEM((line, depth, width), BF) for width in widths]


def sums_of(line):
    return 10 + line


class Trade(Script):
    pass


def heads_forward(q, k, v, allowed, keep):
    lane = lax.broadcasted_iota(jnp.int32, k.shape, 1)
    outs = []
    for h in range(2):
        mine = (lane // HD) == h
        scores = lax.dot_general(
            jnp.where(mine, k, jnp.zeros_like(k)), q, (((1,), (1,)), ((), ())), preferred_element_type=F32
        )
        scores = jnp.where(allowed, scores, -1e30)
        expo = jnp.exp(scores - jnp.max(scores, axis=0, keepdims=True))
        share = 1.0 / jnp.sum(expo, axis=0, keepdims=True)
        expo = expo.astype(BF)
        keep(h, expo, share)
        out = lax.dot_general(v[:, h * HD : (h + 1) * HD], expo, (((0,), (0,)), ((), ())), preferred_element_type=F32)
        outs.append(out * share)
    return jnp.concatenate(outs, axis=0).T.astype(BF)


def norm_stats(values):
    row_mean = jnp.mean(values, axis=-1, keepdims=True)
    centred = values - row_mean
    variance = jnp.mean(centred * centred, axis=-1, keepdims=True)
    inv_std = lax.rsqrt(variance + 1e-05)
    return centred * inv_std, inv_std


class Schedule:
    def __init__(self, text, scripts):
        self.after = {}
        at = ("", 0)
        counts = {}
        for ch in "".join(text):
            if ch.isupper():
                at = (ch, counts.get(ch, 0))
                counts[ch] = at[1] + 1
            else:
                self.after.setdefault(at, []).extend(scripts[ch].steps.pop(0))

    def run(self, name="", i=0):
        for pred, act in self.after.pop((name, i), ()):
            when(pred, act)

    def run_at(self, name, i):
        for at in sorted(k for n, k in self.after if n == name):
            pl.when(i == at)(lambda at=at: self.run(name, at))


ORDER = (
    "0K12002020210114r002022041112042",
    "22413501210rr042LP22H104H112P4H4",
    "14310131H44221352211P5H2313H4142",
    "5PH3H312544345rG43344444O5Fd353F",
    "d55d3353333F34353ddF5Fe5Fedd5ed5",
    "555555FeF3eTuTeudueT5euTuuTvTvue",
    "vTvvTuNUoeUouvdoUvvoUoDAWqAoWqAv",
    "toqWAoqqWAWwqAWuwAqwqWAwowWEwEEq",
    "EwwtMffwvqofsfwsf",
)


def heads_backward(q, k, v, o, do, expo, shares):
    lane = lax.broadcasted_iota(jnp.int32, k.shape, 1)
    first = lane < HD
    column = shares.T
    do = (do.astype(F32) * jnp.where(first, column[:, :1], column[:, 1:2])).astype(BF)
    product = do.astype(F32) * o.astype(F32)
    zero = jnp.zeros_like(k)
    dq_t, dk, dv = [], [], []
    for h in range(2):
        mine = (lane // HD) == h
        inner = jnp.sum(jnp.where(mine, product, 0.0), axis=1, keepdims=True).T
        dprobs = lax.dot_general(
            jnp.where(mine, v, zero), do, (((1,), (1,)), ((), ())), preferred_element_type=F32
        )
        got = expo[h]
        dscores = (got.astype(F32) * (dprobs - inner)).astype(BF)
        dv.append(jnp.dot(got, do, preferred_element_type=F32))
        dk.append(jnp.dot(dscores, q, preferred_element_type=F32))
        dq_t.append(
            lax.dot_general(k[:, h * HD : (h + 1) * HD], dscores, (((0,), (0,)), ((), ())), preferred_element_type=F32)
        )
    return (
        (jnp.concatenate(dq_t, axis=0).T * HD ** (-0.5)).astype(BF),
        jnp.where(first, dk[0], dk[1]).astype(BF),
        jnp.where(first, dv[0], dv[1]).astype(BF),
    )


def norm_back(upstream, unit, inv_std, gain):
    scaled = upstream * gain
    inner_mean = jnp.mean(scaled, axis=-1, keepdims=True)
    cross_mean = jnp.mean(scaled * unit, axis=-1, keepdims=True)
    return inv_std * (scaled - inner_mean - unit * cross_mean)


def layer_kernel(line, *refs):
    toks, grads, w1 = refs[0], refs[1], refs[3]
    given, held = refs[2:3] + refs[4:15], refs[-18:-6]
    raw_q, raw_o, raw_2, marks, b_fc1, b_qv = held[:6]
    vectors = held[6:]
    lo, gtok = refs[19:21]
    wanted, made = refs[15:19] + refs[21:22], refs[-6:-1]
    sq, so, s1, s2, sums = made
    io_sem = refs[-1]
    refs = refs[:-18]
    takes = [pltpu.make_async_copy(src, dst, io_sem.at[i]) for i, (src, dst) in enumerate(zip(given, held))]
    for c in takes:
        c.start()
    xin, gin, fq, fo, f1, f2, qkv_kept, probs, o_kept, x1_kept, h1_kept, h2_kept, act, slope = refs[22:36]
    big1, met1, bigo, meto, acc2, dqkv = refs[36:42]
    bufs = [refs[42 + 5 * i : 47 + 5 * i] for i in range(5)]
    g, dh2, g1b, low, here, cold, colx, coly, far_sums = refs[67:76]
    sml, small, wq, wo, w2, marked, vecs, masks, shares, lsem, ssem, rsem, free = refs[76:]
    place = Place(line)
    rows, width = g.shape
    part = rows // 4
    n1, no, nq = s1.shape[1], so.shape[1], sq.shape[1]
    local = no
    pairs = width // 128
    half_block = n1 // TILE
    tiles = 4 * half_block
    block_shape = big1.shape[1:4]
    greet(place, whole_line=True)

    per = slots_of(line)
    part_of = lambda ref, h: ref.at[:, pl.ds(h * TILE, TILE)]
    pieces = [(wq, fq, 0), (wo, fo, 0)]
    for h in range(half_block):
        pieces += [(part_of(w1, h), f1, h * TILE), (part_of(w2, h), f2, h * TILE)]
    gathers = [
        Gather(place, ssem, rsem, lsem.at[i], shard, whole, i * per, GATHER_CUTS[i], BY_LINE[i], first)
        for i, (shard, whole, first) in enumerate(pieces)
    ]
    rows_at = len(pieces) * per
    rows_sem = len(pieces)
    trade = Trade(ssem, rsem)
    slot_of = lambda j, k: rows_at + j * 4 + k
    pairs_of_rows = ((toks, xin), (grads, gin))
    mine = [pltpu.make_async_copy(src.at[place.t], dst.at[0], lsem.at[rows_sem + j]) for j, (src, dst) in enumerate(pairs_of_rows)]
    mine.append(pltpu.make_async_copy(small, sml.at[place.t], lsem.at[rows_sem + 2]))
    for j, (src, dst) in enumerate(pairs_of_rows):
        trade.step()
        trade.do(None, mine[j].start)
        for k in (2, 3, 1):
            trade.send(None, lambda src=src, dst=dst, j=j, k=k: trade.copy(
                src.at[place.others[k]], dst.at[k], slot_of(j, k), place.peer(k)))
        if j == 0:
            trade.do(None, mine[2].start)
            for k in (2, 3, 1):
                trade.send(None, lambda k=k: trade.copy(small, sml.at[place.t], slot_of(2, k), place.peer(k)))
    for j, (src, dst) in enumerate(pairs_of_rows):
        trade.step()
        trade.do(None, mine[j].wait)
        for k in (2, 3, 1):
            trade.wait(None, lambda dst=dst, k=k: dst.at[k], slot_of(j, k), place.pair())
        if j == 0:
            trade.do(None, mine[2].wait)
            for k in (2, 3, 1):
                trade.wait(None, lambda k=k: sml.at[place.others[k]], slot_of(2, k), place.pair())

    def tell(i, device):
        pl.semaphore_signal(free.at[i], inc=1, device_id=device, device_id_type=MESH)

    def hear(i):
        pl.semaphore_wait(free.at[i], 1)

    pair_at = lambda h: 4 + 2 * h
    line_at = lambda h: 8 + line * h

    def release(h):
        def add(script):
            script.do(None, lambda: tell(pair_at(h), place.pair()))
            script.do(None, lambda: tell(pair_at(h) + 1, place.peer(2)))
            for k in range(1, line):
                to = place.at(lax.rem(place.a + k, line), place.b, place.t)
                script.do(None, lambda to=to: tell(line_at(h) + place.a, to))

        return add

    def before_far(i):
        return lambda script: script.do(None, lambda: hear(i))

    def before_cross(h):
        def add(script):
            script.do(None, lambda: hear(pair_at(h)))
            script.do(None, lambda: hear(pair_at(h) + 1))

        return add

    def before_line(h):
        def add(script):
            for k in range(1, line):
                script.do(None, lambda k=k: hear(line_at(h) + lax.rem(place.a + k, line)))

        return add

    base = rows_at + 12
    each = sums_of(line)
    nh = nq // 2
    two = lambda ref: ref.at[pl.ds(2, 2)]
    last = lambda ref, cols: ref.at[:, :, :, :, cols]
    scatter = lambda *args, **more: Scatter(place, ssem, rsem, *args, **more)
    sum_u, sum_d, sum_q = [], [], []
    for h in range(2):
        cols = pl.ds(h * TILE, TILE)
        cols_q = pl.ds(h * TILE, nh)
        cq, cu, cd = CUTS[h], CUTS[3 + h], CUTS[5 + h]
        rdx, rdy, rx, ry, near = bufs[3 + h]
        sum_u.append(scatter(
            lambda i, cols=cols: big1.at[i, :, :, :, cols], last(met1, cols), last(two(big1), cols), part_of(s1, h),
            bufs[1 + h], base + (1 + h) * each, cu, before_far=before_far(2 + h),
        ))
        sum_d.append(scatter(
            lambda i, cols=cols: big1.at[i, :, :, :, cols], last(met1, cols), last(acc2, cols), part_of(s2, h),
            (rdx.at[:, :, pl.ds(0, TILE - cd)], rdy.at[:, :, pl.ds(0, cd)], rx, ry, near),
            base + (3 + h) * each, cd, release=release(h),
        ))
        sum_q.append(scatter(
            lambda i, cols=cols_q: big1.at[i, :, :, :, cols], last(met1, cols_q), last(acc2, cols_q),
            sq.at[:, pl.ds(h * nh, nh)],
            (
                rdx.at[:, :, pl.ds(0, nh - cq)],
                rdy.at[:, :, pl.ds(0, cq)] if cq > 0 else rdy,
                *[ref.at[:, :, pl.ds(0, nh)] for ref in (rx, ry, near)],
            ),
            base + (5 + h) * each, cq,
            before_far=before_far(h), before_cross=before_cross(h), before_line=before_line(h),
        ))
    sum_o = scatter(lambda i: bigo.at[i], meto, two(bigo), so, bufs[0], base, CUTS[2])

    def rows_home(src, dst, first, sem):
        home = Trade(ssem, rsem)
        stay = pltpu.make_async_copy(src.at[pl.ds(0, part)], dst.at[place.t], sem)
        home.step()
        home.do(None, stay.start)
        for k in (2, 3, 1):
            home.send(None, lambda k=k: home.copy(
                src.at[pl.ds(k * part, part)], dst.at[place.t], first + k, place.peer(k)))
        home.step()
        home.do(None, stay.wait)
        for k in (2, 3, 1):
            home.wait(None, lambda k=k: dst.at[place.others[k]], first + k, place.pair())
        return home

    base = base + 7 * each
    token_rows = rows_home(low, gtok, base, lsem.at[rows_sem + 3])
    out_rows = rows_home(g, lo, base + 4, lsem.at[rows_sem + 4])

    base = base + 8
    few = Trade(ssem, rsem)
    hops = ((cold, place.peer(1)), (colx, place.pair()), (coly, place.peer(2)))

    def fold(i, land):
        here[i + 1] = here[i] + land[...]

    few.step()
    for i, (land, device) in enumerate(hops):
        few.send(None, lambda i=i, land=land, device=device: few.copy(here.at[i], land, base + i, device))
        few.step()
        few.wait(None, lambda land=land: land, base + i, place.pair())
        few.do(None, lambda i=i, land=land: fold(i, land))
    for k in range(1, line):
        far = lax.rem(place.a + k, line)
        few.send(None, lambda far=far, k=k: few.copy(
            here.at[3], far_sums.at[k], base + 3 + k, place.at(far, place.b, place.t)))
    few.step()
    for k in range(1, line):
        few.wait(None, lambda k=k: far_sums.at[k], base + 3 + k, place.pair())

    scripts = {str(i): w for i, w in enumerate(gathers)}
    scripts.update(
        {
            "r": trade, "q": sum_q[0], "w": sum_q[1], "o": sum_o, "u": sum_u[0], "v": sum_u[1], "d": sum_d[0],
            "e": sum_d[1], "s": token_rows, "t": out_rows, "f": few,
        }
    )
    plan = Schedule(ORDER, scripts)

    def tile_of(j):
        h, q = j // 4, lax.rem(j, 4)
        block = block_of(place, q)
        at = pl.ds(pl.multiple_of(h * TILE, TILE), TILE)
        return q, block, at, pl.ds(pl.multiple_of(block * n1 + h * TILE, TILE), TILE)

    def some(count, body, unroll=1):
        lax.fori_loop(0, count, lambda i, _: (body(i), 0)[1], 0, unroll=unroll)

    def by_rows(body):
        some(rows // ROWS, lambda i: body(i, pl.ds(pl.multiple_of(i * ROWS, ROWS), ROWS)), UNROLL)

    def fetch_rows(src, dst, sem):
        copies = [pltpu.make_async_copy(src.at[k], dst.at[pl.ds(k * part, part)], sem.at[k]) for k in range(4)]
        for c in copies:
            c.start()
        for c in copies:
            c.wait()

    for c in takes:
        c.wait()
    small[...] = jnp.zeros_like(small)
    small[0:1, :] = b_fc1[...].reshape(1, -1)
    small[1:2, :local] = b_qv[0:1, :]
    small[1:2, local : 2 * local] = b_qv[1:2, :]
    for h in range(2):
        for j in range(3):
            wq[:, (h * 3 + j) * 128 : (h * 3 + j + 1) * 128] = raw_q[j, :, h * 128 : (h + 1) * 128]
    plan.run()
    wo[...] = raw_o[...].T
    w2[...] = raw_2[...].T
    plan.run("K")
    for i, vector in enumerate(vectors):
        vecs[i : i + 1, :] = vector[...].reshape(1, -1)
    mark = marks[pl.ds(place.t, 1), :].astype(F32)
    marked[...] = jnp.broadcast_to(mark, (128, rows)).T
    for k in range(4):
        at = pl.ds(k * part, part)
        masks[0, at, :] = marked[pl.ds(pl.multiple_of(place.others[k] * part, 32), part), :]
    masks[1] = jnp.where(jnp.max(mark, axis=1, keepdims=True) > 0, masks[0], 1.0)
    here[0] = jnp.zeros_like(here[0])

    def heads_part(h1, wqv, pbuf, sem):
        fetch_rows(xin, low, sem)

        def first_norm(i, at):
            x = low[at, :].astype(F32)
            unit, _inv = norm_stats(x)
            h1[at, :] = (unit * vecs[0:1, :] + vecs[1:2, :]).astype(BF)
            real = masks[0, at, :1]
            here[0, 0:1, :] += jnp.sum(x * x * real, axis=0, keepdims=True)
            here[0, 2:3, :] += jnp.broadcast_to(jnp.sum(real, axis=0, keepdims=True), (1, width))

        by_rows(first_norm)
        save_h1 = pltpu.make_async_copy(h1, h1_kept, sem.at[4])
        save_h1.start()
        plan.run("L")
        block_at = lambda i: block_of(place, 3 - i)
        fetch = lambda i, slot: pltpu.make_async_copy(
            fq.at[:, :, :, pl.ds(pl.multiple_of(block_at(i) * nq, 128), nq)], wqv.at[slot], sem.at[5 + slot])
        fetch(0, 0).start()
        allowed = masks[1, :, :1] > 0
        save = lambda i, h: pltpu.make_async_copy(pbuf.at[h], probs.at[block_at(i) * 2 + h], sem.at[8 + h])

        def heads_block(i):
            block, slot = block_at(i), lax.rem(i, 2)
            fetch(i, slot).wait()
            got = jnp.dot(h1[...], wqv[slot].reshape(width, nq), preferred_element_type=F32)
            bias = sml[pl.ds(block, 1), 1, : 2 * local]
            for h in range(2):
                q, k, v = (slice((h * 3 + j) * 128, (h * 3 + j + 1) * 128) for j in range(3))
                bq, bv = bias[:, h * 128 : (h + 1) * 128], bias[:, local + h * 128 : local + (h + 1) * 128]
                dqkv[block, :, q] = (got[:, q] + bq).astype(BF) * jnp.asarray(HD ** (-0.5), BF)
                dqkv[block, :, k] = got[:, k].astype(BF)
                dqkv[block, :, v] = (got[:, v] + bv).astype(BF)
            plan.run_at("P", i)

            def pair_step(h):
                pl.when(i >= 1)(lambda: save(i - 1, h).wait())

                def keep(head, got, share):
                    pbuf[h, head] = got
                    shares[block * 2 + h, head : head + 1, :] = share

                cols = [pl.ds(pl.multiple_of((h * 3 + j) * 128, 128), 128) for j in range(3)]
                q, k, v = (dqkv[block, :, c] for c in cols)
                at = pl.ds(pl.multiple_of(block * local + h * 128, 128), 128)
                g1b[:, at] = heads_forward(q, k, v, allowed, keep)
                save(i, h).start()
                plan.run_at("H", 2 * i + h)
                pl.when(jnp.logical_and(h == 0, i < 3))(lambda: fetch(i + 1, 1 - slot).start())

            some(2, pair_step)

        some(4, heads_block)
        save_qkv = pltpu.make_async_copy(dqkv, qkv_kept, sem.at[7])
        save_qkv.start()
        for wait in (save_h1, save_qkv, save(3, 0), save(3, 1)):
            wait.wait()

    pl.run_scoped(
        heads_part,
        pltpu.VMEM((rows, width), BF),
        pltpu.VMEM((2,) + block_shape + (nq,), BF),
        pltpu.VMEM((2, 2, rows, rows), BF),
        pltpu.SemaphoreType.DMA((10,)),
    )

    def hidden_part(wov, h2, gt, w1t, actb, slopeb, sem):
        save_o = pltpu.make_async_copy(g1b, o_kept, sem.at[4])
        save_o.start()
        fetch_o = pltpu.make_async_copy(fo, wov, sem.at[5])
        fetch_o.start()
        fetch_rows(gin, g, sem)

        def mask_rows(i, at):
            masked = g[at, :].astype(F32) * masks[0, at, :1]
            here[0, 3:4, :] += jnp.sum(masked, axis=0, keepdims=True)
            g[at, :] = masked.astype(BF)

        by_rows(mask_rows)
        gt[...] = g[...].T
        plan.run("G")
        fetch_o.wait()
        half = rows // 2

        def join(i):
            at = pl.ds(pl.multiple_of(i * half, 64), half)
            branch = lax.dot_general(
                g1b[at, :], wov[...].reshape(width, width), (((1,), (1,)), ((), ())), preferred_element_type=F32
            ) + vecs[4:5, :]
            here[0, 1:2, :] += jnp.sum(branch * branch * masks[0, at, :1], axis=0, keepdims=True)
            middle = low[at, :].astype(F32) + branch
            dh2[at, :] = middle
            unit, _inv = norm_stats(middle)
            h2[at, :] = (unit * vecs[2:3, :] + vecs[3:4, :]).astype(BF)

        some(2, join)
        save_x1 = pltpu.make_async_copy(dh2, x1_kept, sem.at[6])
        save_h2 = pltpu.make_async_copy(h2, h2_kept, sem.at[7])
        save_x1.start()
        save_h2.start()
        plan.run("O")
        fetch = lambda j, slot: pltpu.make_async_copy(f1.at[:, :, :, tile_of(j)[3]], w1t.at[slot], sem.at[8 + slot])
        fetch(0, 0).start()

        def saves(j, slot):
            cols = tile_of(j)[3]
            return (
                pltpu.make_async_copy(actb.at[slot], act.at[:, cols], sem.at[10 + slot]),
                pltpu.make_async_copy(slopeb.at[slot], slope.at[:, cols], sem.at[12 + slot]),
            )

        def hidden_step(j):
            slot = lax.rem(j, 2)
            pl.when(j + 1 < tiles)(lambda: fetch(j + 1, 1 - slot).start())

            @pl.when(j >= 2)
            def _():
                for save in saves(j - 2, slot):
                    save.wait()

            q, block, at, cols = tile_of(j)
            fetch(j, slot).wait()
            hidden = jnp.dot(h2[...], w1t[slot].reshape(width, TILE), preferred_element_type=F32) + sml[block, 0:1, at]
            gate = jax.nn.sigmoid(1.702 * hidden)
            actb[slot] = (hidden * gate).astype(BF)
            slopeb[slot] = (gate + 1.702 * hidden * gate * (1.0 - gate)).astype(BF)
            for save in saves(j, slot):
                save.start()
            product = jnp.dot(gt[...], actb[slot], preferred_element_type=F32).reshape(block_shape + (TILE,))

            @pl.when(q < 2)
            def _():
                big1[q, :, :, :, at] = product.astype(BF)

            @pl.when(q >= 2)
            def _():
                acc2[q - 2, :, :, :, at] = (product + met1[q - 2, :, :, :, at].astype(F32)).astype(BF)

            plan.run_at("F", j)

        some(tiles, hidden_step)
        for wait in saves(tiles - 2, tiles % 2) + saves(tiles - 1, (tiles - 1) % 2) + (save_o, save_x1, save_h2):
            wait.wait()

    pl.run_scoped(
        hidden_part,
        pltpu.VMEM(fo.shape, BF),
        pltpu.VMEM((rows, width), BF),
        pltpu.VMEM((width, rows), BF),
        pltpu.VMEM((2,) + block_shape + (TILE,), BF),
        pltpu.VMEM((2, rows, TILE), BF),
        pltpu.VMEM((2, rows, TILE), BF),
        pltpu.SemaphoreType.DMA((14,)),
    )
    for h in range(2):
        tell(2 + h, place.peer(1))
        sum_d[h].wait_sent(2)

    dh2[...] = jnp.zeros_like(dh2)

    def feed_forward(ml, h2t, f1t, f2t, slopet, actt, sem):
        def fetch(j, slot):
            cols = tile_of(j)[3]
            return (
                pltpu.make_async_copy(f1.at[:, :, :, cols], f1t.at[slot], sem.at[slot]),
                pltpu.make_async_copy(f2.at[:, :, :, cols], f2t.at[slot], sem.at[2 + slot]),
                pltpu.make_async_copy(slope.at[:, cols], slopet.at[slot], sem.at[4 + slot]),
                pltpu.make_async_copy(act.at[:, cols], actt.at[slot], sem.at[7 + slot]),
            )

        ml[...] = jnp.zeros_like(ml)
        load = pltpu.make_async_copy(h2_kept, low, sem.at[6])
        load.start()
        for c in fetch(0, 0):
            c.start()
        load.wait()
        h2t[...] = low[...].T

        def tile(j):
            slot = lax.rem(j, 2)

            @pl.when(j + 1 < tiles)
            def _():
                for c in fetch(j + 1, 1 - slot):
                    c.start()

            for c in fetch(j, slot):
                c.wait()
            q, block, at, cols = tile_of(j)
            w2_tile = f2t[slot].reshape(width, TILE)
            du = jnp.dot(g[...], w2_tile, preferred_element_type=F32)
            du = (du * slopet[slot].astype(F32)).astype(BF)
            here[0, pl.ds(4 + block, 1), at] = jnp.sum(du.astype(F32), axis=0, keepdims=True)
            product = jnp.dot(h2t[...], du, preferred_element_type=F32).reshape(block_shape + (TILE,))

            @pl.when(q < 2)
            def _():
                big1[q, :, :, :, at] = product.astype(BF)

            @pl.when(q >= 2)
            def _():
                big1[q, :, :, :, at] = (product + met1[q - 2, :, :, :, at].astype(F32)).astype(BF)

            dh2[...] += lax.dot_general(
                du, f1t[slot].reshape(width, TILE), (((1,), (1,)), ((), ())), preferred_element_type=F32
            )
            ml[...] += lax.dot_general(actt[slot], w2_tile, (((1,), (1,)), ((), ())), preferred_element_type=F32)
            plan.run_at("T", j)

        some(tiles, tile)

    def second_norm(ml, xt, sem):
        fetch = lambda i, slot: pltpu.make_async_copy(
            x1_kept.at[pl.ds(pl.multiple_of(i * ROWS, ROWS), ROWS)], xt.at[slot], sem.at[slot])
        fetch(0, 0).start()

        def some_rows(i, at):
            slot = lax.rem(i, 2)
            pl.when(i + 1 < rows // ROWS)(lambda: fetch(i + 1, 1 - slot).start())
            fetch(i, slot).wait()
            x = xt[slot]
            unit, inv = norm_stats(x)
            up = dh2[at, :]
            here[0, 8:9, :] += jnp.sum(up * unit, axis=0, keepdims=True)
            here[0, 9:10, :] += jnp.sum(up, axis=0, keepdims=True)
            g1 = g[at, :].astype(F32) + norm_back(up, unit, inv, vecs[2:3, :])
            rounded = g1.astype(BF)
            g1b[at, :] = rounded
            here[0, 10:11, :] += jnp.sum(rounded.astype(F32), axis=0, keepdims=True)
            dh2[at, :] = g1
            m = ml[at, :] + vecs[5:6, :]
            g[at, :] = (x + m).astype(BF)
            here[0, 11:12, :] += jnp.sum(m * m * masks[0, at, :1], axis=0, keepdims=True)

        by_rows(some_rows)

    def middle(ml):
        tiles_of = lambda *shape: pltpu.VMEM((2,) + shape, BF)
        pl.run_scoped(
            functools.partial(feed_forward, ml),
            pltpu.VMEM((width, rows), BF),
            tiles_of(*block_shape, TILE),
            tiles_of(*block_shape, TILE),
            tiles_of(rows, TILE),
            tiles_of(rows, TILE),
            pltpu.SemaphoreType.DMA((9,)),
        )
        for h in range(2):
            tell(h, place.peer(1))
        pl.run_scoped(
            functools.partial(second_norm, ml), pltpu.VMEM((2, ROWS, width), F32), pltpu.SemaphoreType.DMA((2,))
        )

    pl.run_scoped(middle, pltpu.VMEM((rows, width), F32))
    plan.run("N")

    def heads(tall, o, wov, do, pt, qt, sem):
        load_o = pltpu.make_async_copy(o_kept, o, sem.at[0])
        load_w = pltpu.make_async_copy(fo, wov, sem.at[1])
        load_h = pltpu.make_async_copy(h1_kept, low, sem.at[6])
        for c in (load_o, load_w, load_h):
            c.start()

        def heads_of(i):
            return block_of(place, lax.rem(i, 4)) * 2 + i // 4

        def fetch(i, slot):
            cols = pl.ds(pl.multiple_of((i // 4) * nh, 128), nh)
            return [
                pltpu.make_async_copy(
                    qkv_kept.at[block_of(place, lax.rem(i, 4)), :, cols], qt.at[slot], sem.at[2 + slot]),
                pltpu.make_async_copy(probs.at[heads_of(i)], pt.at[slot], sem.at[4 + slot]),
            ]

        for c in fetch(0, 0):
            c.start()
        tall[...] = g1b[...].T
        load_o.wait()
        load_w.wait()

        def output_weight(q):
            cols = pl.ds(pl.multiple_of(block_of(place, q) * no, 128), no)
            product = jnp.dot(tall[...], o[:, cols], preferred_element_type=F32).reshape(bigo.shape[1:])

            @pl.when(q < 2)
            def _():
                bigo[q] = product.astype(BF)

            @pl.when(q >= 2)
            def _():
                bigo[q] = (product + meto[q - 2].astype(F32)).astype(BF)

            plan.run_at("U", q)

        some(4, output_weight)
        do[...] = jnp.dot(g1b[...], wov[...].reshape(width, width), preferred_element_type=F32).astype(BF)
        plan.run("D")
        load_h.wait()
        tall[...] = low[...].T
        for script in sum_u:
            script.wait_sent(2)

        def pair_step(i):
            slot = lax.rem(i, 2)
            h, q = i // 4, lax.rem(i, 4)

            @pl.when(i + 1 < pairs)
            def _():
                for c in fetch(i + 1, 1 - slot):
                    c.start()

            for c in fetch(i, slot):
                c.wait()
            cols = pl.ds(pl.multiple_of(heads_of(i) * 128, 128), 128)
            got = heads_backward(
                qt[slot, :, :128], qt[slot, :, 128:256], qt[slot, :, 256:], o[:, cols], do[:, cols], pt[slot],
                shares[heads_of(i)],
            )
            mine = pl.ds(pl.multiple_of(h * nh, 128), nh)
            dqkv[q, :, mine] = jnp.concatenate(got, axis=1)
            plan.run_at("A", i)
            block = block_of(place, q)
            got = dqkv[q, :, mine]
            product = jnp.dot(tall[...], got, preferred_element_type=F32).reshape(block_shape + (nh,))
            total = jnp.sum(got.astype(F32), axis=0, keepdims=True)
            at = pl.ds(pl.multiple_of(block * local + h * 128, 128), 128)
            here[0, 14:15, at] = total[:, :128]
            here[0, 15:16, at] = total[:, 256:]
            to = pl.ds(pl.multiple_of(h * TILE, 128), nh)

            @pl.when(q < 2)
            def _():
                big1[q, :, :, :, to] = product.astype(BF)

            @pl.when(q >= 2)
            def _():
                acc2[q - 2, :, :, :, to] = (product + met1[q - 2, :, :, :, to].astype(F32)).astype(BF)

            plan.run_at("W", i)

        some(pairs, pair_step)

    pl.run_scoped(
        heads,
        pltpu.VMEM((width, rows), BF),
        pltpu.VMEM((rows, width), BF),
        pltpu.VMEM(fo.shape, BF),
        pltpu.VMEM((rows, width), BF),
        pltpu.VMEM((2, 2, rows, rows), BF),
        pltpu.VMEM((2, rows, nh), BF),
        pltpu.SemaphoreType.DMA((7,)),
    )

    def last_part(dh1, wqv, x, sem):
        fetch_w = lambda q, slot: pltpu.make_async_copy(
            fq.at[:, :, :, pl.ds(pl.multiple_of(block_of(place, q) * nq, 128), nq)], wqv.at[slot], sem.at[slot])
        load_x = [pltpu.make_async_copy(xin.at[k], x.at[pl.ds(k * part, part)], sem.at[2 + k]) for k in range(4)]
        fetch_w(0, 0).start()
        for c in load_x:
            c.start()
        dh1[...] = jnp.zeros_like(dh1)

        def back(q):
            slot = lax.rem(q, 2)
            pl.when(q < 3)(lambda: fetch_w(q + 1, 1 - slot).start())
            fetch_w(q, slot).wait()
            dh1[...] += lax.dot_general(
                dqkv[q], wqv[slot].reshape(width, nq), (((1,), (1,)), ((), ())), preferred_element_type=F32
            )
            plan.run_at("E", q)

        some(4, back)
        for c in load_x:
            c.wait()

        def some_rows(i, at):
            unit, inv = norm_stats(x[at, :].astype(F32))
            up = dh1[at, :]
            here[0, 12:13, :] += jnp.sum(up * unit, axis=0, keepdims=True)
            here[0, 13:14, :] += jnp.sum(up, axis=0, keepdims=True)
            low[at, :] = (dh2[at, :] + norm_back(up, unit, inv, vecs[0:1, :])).astype(BF)

        by_rows(some_rows)
        plan.run("M")

    pl.run_scoped(
        last_part,
        pltpu.VMEM((rows, width), F32),
        pltpu.VMEM((2,) + block_shape + (nq,), BF),
        pltpu.VMEM((rows, width), BF),
        pltpu.SemaphoreType.DMA((6,)),
    )
    total = here[3]
    for k in range(1, line):
        total = total + far_sums[k]
    sums[...] = total
    gives = [pltpu.make_async_copy(src, dst, io_sem.at[i]) for i, (src, dst) in enumerate(zip(made, wanted))]
    for c in gives:
        c.start()
    for c in gives:
        c.wait()
    for script in scripts.values():
        script.finish()


def layer(line, toks, grads, w_qkv, w1, w_out, w_fc2, marks, b_fc1, b_qv, *vectors):
    images, part, width = toks.shape
    rows = 4 * part
    depth, n1 = w1.shape
    no, n2, nq = w_out.shape[0], w_fc2.shape[0], 3 * w_qkv.shape[2]
    hidden = 4 * n1
    hbm = pl.BlockSpec(memory_space=pl.ANY)
    sds = jax.ShapeDtypeStruct
    block = lambda count, n: pltpu.VMEM((count, line, 2, depth, n), BF)
    few = (16, width)
    count = 6 * slots_of(line) + 12 + 7 * sums_of(line) + 8 + 3 + line
    kept = [
        sds((4, part, width), BF),
        sds((4, part, width), BF),
        *[sds((line, 2, depth, 4 * n), BF) for n in (nq, no, n1, n2)],
        sds((4, rows, nq), BF),
        sds((width // 128, 2, rows, rows), BF),
        sds((rows, width), BF),
        sds((rows, width), F32),
        sds((rows, width), BF),
        sds((rows, width), BF),
        sds((rows, hidden), BF),
        sds((rows, hidden), BF),
    ]
    return pl.pallas_call(
        functools.partial(layer_kernel, line),
        out_shape=[
            sds((depth, nq), F32),
            sds((depth, no), F32),
            sds((depth, n1), F32),
            sds((depth, n2), F32),
            sds((4, part, width), BF),
            sds((4, part, width), BF),
            sds(few, F32),
            *kept,
        ],
        in_specs=[hbm] * 15,
        out_specs=[hbm] * (7 + len(kept)),
        scratch_shapes=[
            block(4, n1),
            block(2, n1),
            block(4, no),
            block(2, no),
            block(2, n2),
            pltpu.VMEM((4, rows, nq), BF),
            *landing(line, depth, no, no - CUTS[2], CUTS[2]),
            *landing(line, depth, TILE, TILE - CUTS[3], CUTS[3]),
            *landing(line, depth, TILE, TILE - CUTS[4], CUTS[4]),
            *landing(line, depth, TILE, max(TILE - CUTS[5], nq // 2 - CUTS[0]), max(CUTS[5], CUTS[0])),
            *landing(line, depth, TILE, max(TILE - CUTS[6], nq // 2 - CUTS[1]), max(CUTS[6], CUTS[1])),
            pltpu.VMEM((rows, width), BF),
            pltpu.VMEM((rows, width), F32),
            pltpu.VMEM((rows, width), BF),
            pltpu.VMEM((rows, width), BF),
            pltpu.VMEM((4,) + few, F32),
            pltpu.VMEM(few, F32),
            pltpu.VMEM(few, F32),
            pltpu.VMEM(few, F32),
            pltpu.VMEM((line,) + few, F32),
            pltpu.VMEM((4, 8, n1), F32),
            pltpu.VMEM((8, n1), F32),
            pltpu.VMEM((depth, nq), BF),
            pltpu.VMEM((depth, no), BF),
            pltpu.VMEM((depth, n2), BF),
            pltpu.VMEM((rows, 128), F32),
            pltpu.VMEM((8, width), F32),
            pltpu.VMEM((2, rows, 128), F32),
            pltpu.VMEM((width // 128, 2, rows), F32),
            pltpu.SemaphoreType.DMA((11,)),
            pltpu.SemaphoreType.DMA((count,)),
            pltpu.SemaphoreType.DMA((count,)),
            pltpu.SemaphoreType.REGULAR((8 + 2 * line,)),
            *[pltpu.VMEM(ref.shape, ref.dtype) for ref in (w_qkv, w_out, w_fc2, marks, b_fc1, b_qv, *vectors)],
            pltpu.VMEM((depth, nq), F32),
            pltpu.VMEM((depth, no), F32),
            pltpu.VMEM((depth, n1), F32),
            pltpu.VMEM((depth, n2), F32),
            pltpu.VMEM(few, F32),
            pltpu.SemaphoreType.DMA((12,)),
        ],
        compiler_params=pltpu.CompilerParams(collective_id=0, has_side_effects=True, vmem_limit_bytes=63 * MIB),
        name="layer",
    )(toks, grads, w_qkv, w1, w_out, w_fc2, marks, b_fc1, b_qv, *vectors)[:7]


def finish_kernel(*refs):
    sq, so, s1, s2, lo, gtok, sums = refs[:7]
    outs, rms = refs[7:21], refs[21]
    vq, vo, v1, v2, vs, rows = refs[22:28]
    made, (in_sem, out_sem) = refs[28:39], refs[39:]
    loads = [
        pltpu.make_async_copy(src, dst, in_sem.at[i])
        for i, (src, dst) in enumerate(
            ((sums, vs), (sq, vq), (so, vo), (s2, v2), (s1, v1), (lo, rows.at[0]), (gtok, rows.at[1]))
        )
    ]
    for c in loads:
        c.start()
    saves = []

    def save(src, dst):
        copy = pltpu.make_async_copy(src, dst, out_sem.at[len(saves)])
        copy.start()
        saves.append(copy)

    lo_out, gtok_out, g_ln1, b_ln1, q_out, qv_out, o_out, b_out, g_ln2, b_ln2, one, b_fc1, two, b_fc2 = outs
    tq, tqv, to, t2 = made[:4]
    vectors = made[4:]
    t = lax.axis_index("tensor")
    local = tqv.shape[1]
    loads[0].wait()
    for ref, dst, at in zip(vectors, (g_ln1, b_ln1, b_out, g_ln2, b_ln2, b_fc2), (12, 13, 10, 8, 9, 3)):
        ref[...] = vs[at, :]
        save(ref, dst)
    vectors[6][...] = vs[pl.ds(4 + t, 1), :].reshape(-1)
    save(vectors[6], b_fc1)
    at = pl.ds(pl.multiple_of(t * local, 128), local)
    tqv[0:1, :] = vs[14:15, at]
    tqv[1:2, :] = vs[15:16, at]
    save(tqv, qv_out)
    count = vs[2:3, 0:1] * vs.shape[1]
    for i, at in enumerate((0, 1, 11)):
        rms[i] = jnp.max(jnp.sqrt(jnp.sum(vs[at : at + 1, :], axis=1, keepdims=True) / count))
    loads[1].wait()
    for h in range(2):
        for j in range(3):
            tq[j, :, h * 128 : (h + 1) * 128] = vq[:, (h * 3 + j) * 128 : (h * 3 + j + 1) * 128]
    save(tq, q_out)
    loads[2].wait()
    to[...] = vo[...].T
    save(to, o_out)
    loads[3].wait()
    t2[...] = v2[...].T
    save(t2, two)
    for c, src, dst in ((loads[4], v1, one), (loads[5], rows.at[0], lo_out), (loads[6], rows.at[1], gtok_out)):
        c.wait()
        save(src, dst)
    for c in saves:
        c.wait()


def finish(sum_q, sum_o, sum_1, sum_2, layer_out, grad_tokens, sums):
    width = sums.shape[1]
    depth, no = sum_o.shape
    n1, n2 = sum_1.shape[1], sum_2.shape[1]
    sds = jax.ShapeDtypeStruct
    row = sds((width,), F32)
    hbm = pl.BlockSpec(memory_space=pl.ANY)
    vmem = lambda ref: pltpu.VMEM(ref.shape, ref.dtype)
    q, qv, o, two = sds((3, depth, no), F32), sds((2, no), F32), sds((no, depth), F32), sds((n2, depth), F32)
    b_fc1 = sds((n1,), F32)
    lo, gtok, g_ln1, b_ln1, q, b_qv, o, b_out, g_ln2, b_ln2, one, b_fc1, two, b_fc2, rms = pl.pallas_call(
        finish_kernel,
        out_shape=[
            sds(layer_out.shape, BF), sds(grad_tokens.shape, BF), row, row, q, qv, o, row, row, row,
            sds(sum_1.shape, F32), b_fc1, two, row, sds((3,), F32),
        ],
        in_specs=[hbm] * 7,
        out_specs=[hbm] * 14 + [pl.BlockSpec(memory_space=pltpu.SMEM)],
        scratch_shapes=[
            *[vmem(ref) for ref in (sum_q, sum_o, sum_1, sum_2, sums)],
            pltpu.VMEM((2,) + layer_out.shape, BF),
            *[vmem(ref) for ref in (q, qv, o, two) + (row,) * 6 + (b_fc1,)],
            pltpu.SemaphoreType.DMA((7,)),
            pltpu.SemaphoreType.DMA((14,)),
        ],
        compiler_params=pltpu.CompilerParams(vmem_limit_bytes=63 * MIB),
        name="finish",
    )(sum_q, sum_o, sum_1, sum_2, layer_out, grad_tokens, sums)
    return (
        lo, gtok, g_ln1, b_ln1, q.transpose(1, 0, 2), b_qv, o, b_out, g_ln2, b_ln2, one, b_fc1, two, b_fc2, rms
    )


def shards(
    tokens, token_mask, out_grad, ln1_gain, ln1_bias, w_qkv, b_qv, w_out, b_out,
    ln2_gain, ln2_bias, w_fc1, b_fc1, w_fc2, b_fc2,
):
    line = lax.axis_size("dp") // 2
    sums = layer(
        line, tokens, out_grad, w_qkv.transpose(1, 0, 2), w_fc1, w_out, w_fc2, token_mask, b_fc1, b_qv,
        ln1_gain, ln1_bias, ln2_gain, ln2_bias, b_out, b_fc2,
    )
    return finish(*sums)


def solution(mesh):
    rowwise = P("dp", "tensor", None)
    placed = (
        rowwise, P("dp", None), rowwise, P(), P(), P("dp", None, "tensor"), P(None, "tensor"), P("tensor", "dp"),
        P(), P(), P(), P("dp", "tensor"), P("tensor"), P("tensor", "dp"), P(),
    )
    return jax.shard_map(
        shards,
        mesh=mesh,
        in_specs=placed,
        out_specs=(
            rowwise, rowwise, P(), P(), P("dp", None, "tensor"), P(None, "tensor"), P("tensor", "dp"), P(),
            P(), P(), P("dp", "tensor"), P("tensor"), P("tensor", "dp"), P(), P(),
        ),
        check_vma=False,
    )
```

```python
import functools

import jax
import jax.numpy as jnp
from jax import lax
from jax.experimental import pallas as pl
from jax.experimental.pallas import tpu as pltpu
from jax.sharding import PartitionSpec as P

HD = 64
MESH = pl.DeviceIdType.MESH
BF = jnp.bfloat16
F32 = jnp.float32
ROWS = 64
TILE = 512
UNROLL = 2
MIB = 1024 * 1024


class Place:
    def __init__(self, line):
        self.line = line
        self.d = lax.axis_index("dp")
        self.t = lax.axis_index("tensor")
        self.a = self.d // 2
        self.b = lax.rem(self.d, 2)
        y, c = self.t // 2, lax.rem(self.t, 2)
        self.others = (self.t, y * 2 + 1 - c, (1 - y) * 2 + c, (1 - y) * 2 + 1 - c)
        self.low, self.high = self.a > 0, self.a < line - 1
        self.inner = jnp.logical_and(self.low, self.high)

    def at(self, a, b, t):
        return (a * 2 + b, t)

    def pair(self):
        return self.at(self.a, 1 - self.b, self.t)

    def peer(self, k):
        return (self.d, self.others[k])

    def up(self):
        return self.at(self.a + 1, self.b, self.t)

    def down(self):
        return self.at(self.a - 1, self.b, self.t)


def greet(place, whole_line=False):
    barrier = pltpu.get_barrier_semaphore()

    def hail(device):
        pl.semaphore_signal(barrier, inc=1, device_id=device, device_id_type=MESH)

    line = place.line
    hail(place.pair())
    for k in range(1, 4):
        hail(place.peer(k))
    if whole_line:
        for k in range(1, line):
            hail(place.at(lax.rem(place.a + k, line), place.b, place.t))
        pl.semaphore_wait(barrier, 3 + line)
        return
    pl.when(place.low)(lambda: hail(place.down()))
    pl.when(place.high)(lambda: hail(place.up()))
    pl.when(place.inner)(lambda: pl.semaphore_wait(barrier, 6))
    pl.when(jnp.logical_not(place.inner))(lambda: pl.semaphore_wait(barrier, 5))


def both(p, q):
    if p is None:
        return q
    if q is None:
        return p
    return jnp.logical_and(p, q)


def when(pred, act):
    if pred is None:
        act()
    else:
        pl.when(pred)(act)


class Script:
    def __init__(self, ssem, rsem):
        self.ssem, self.rsem = ssem, rsem
        self.sent = []
        self.steps = []

    def copy(self, src, dst, slot, device):
        return pltpu.make_async_remote_copy(
            src_ref=src,
            dst_ref=dst,
            send_sem=self.ssem.at[slot],
            recv_sem=self.rsem.at[slot],
            device_id=device,
            device_id_type=MESH,
        )

    def step(self):
        self.steps.append([])

    def do(self, pred, act):
        self.steps[-1].append((pred, act))

    def send(self, pred, make):
        self.do(pred, lambda: make().start())
        self.sent.append((pred, make))

    def wait(self, pred, ref, slot, device):
        self.do(pred, lambda: self.copy(ref(), ref(), slot, device).wait_recv())

    def run(self, count=1):
        for _ in range(count):
            for pred, act in self.steps.pop(0):
                when(pred, act)

    def wait_sent(self, count):
        for pred, make in self.sent[:count]:
            when(pred, lambda make=make: make().wait_send())
        self.sent = self.sent[count:]

    def finish(self):
        assert not self.steps
        for pred, make in self.sent:
            when(pred, lambda make=make: make().wait_send())


def thirds(line):
    return [1], [2] if line > 2 else [], list(range(3, line))


def order(place):
    yield None, place.a
    for k in range(1, place.line):
        yield place.a >= k, place.a - k
        yield place.a + k <= place.line - 1, place.a + k


class Gather(Script):
    def __init__(self, place, ssem, rsem, local_sem, shard, whole, base, cut, by_line, first=0):
        super().__init__(ssem, rsem)
        self.p = place
        self.shard, self.whole = shard, whole
        self.n = shard.shape[1]
        self.first, self.apart = first, whole.shape[3] // 4
        self.base, self.cut, self.by_line = base, cut, by_line
        line, few = place.line, 1 if by_line else place.line
        sizes = (line, line, line, line, few, few, 4, line if by_line else 0, 0)
        self.offsets = [sum(sizes[:kind]) for kind in range(9)]
        p = place
        t2 = p.others[2]
        local = pltpu.make_async_copy(shard, self.block(p.a, p.b, p.t), local_sem)
        own = lambda: self.shard
        groups = thirds(p.line)
        apart = list(order(p))
        rings = [[i for k in group for i in apart[2 * k - 1 : 2 * k + 1]] for group in groups]

        def along(group, kind, b, t, spread):
            for up in (True, False):
                self.step()
                for k in group:
                    self.receive(k, kind, b, t, spread, up)

        self.step()
        self.pass_line(None, p.a, 1, True, own, 0, p.b, p.t)
        self.pass_line(None, p.a, 1, False, own, 0, p.b, p.t)
        self.spread(None, p.a, own)
        self.do(None, local.start)
        along(groups[0], 0, p.b, p.t, True)
        self.step()
        self.cross(apart[:1])
        along(groups[1], 0, p.b, p.t, True)
        self.step()
        if by_line:
            self.landed(apart[:1])
            diagonal = lambda: self.block(p.a, 1 - p.b, t2)
            self.pass_line(None, p.a, 1, True, diagonal, 7, 1 - p.b, t2)
            self.pass_line(None, p.a, 1, False, diagonal, 7, 1 - p.b, t2)
        else:
            self.cross(rings[0])
        along(groups[2], 0, p.b, p.t, True)
        if by_line:
            for group in groups:
                along(group, 7, 1 - p.b, t2, False)
        for ring in rings if by_line else rings[1:]:
            self.step()
            (self.settle if by_line else self.cross)(ring)
        self.do(None, local.wait)
        for j in range(3):
            self.step()
            self.core((j,))
        self.step()
        if not by_line:
            self.landed(apart)
        self.core((3,))
        self.step()
        self.arrive()

    def block(self, a, b, t, lo=0, hi=None):
        hi = self.n if hi is None else hi
        start = pl.multiple_of(t * self.apart + self.first + lo, 128)
        return self.whole.at[a, b, :, pl.ds(start, hi - lo)]

    def plane(self, b, t):
        start = pl.multiple_of(t * self.apart + self.first, 128)
        return self.whole.at[:, b, :, pl.ds(start, self.n)]

    def slot(self, kind, i):
        return self.base + self.offsets[kind] + (0 if self.by_line and kind in (4, 5) else i)

    def spread(self, pred, a, src):
        p = self.p
        self.send(pred, lambda: self.copy(src(), self.block(a, p.b, p.t), self.slot(2, a), p.pair()))
        self.send(pred, lambda: self.copy(src(), self.block(a, p.b, p.t), self.slot(3, a), p.peer(2)))

    def pass_line(self, pred, a, step, up, src, kind, b, t):
        p = self.p
        if step > p.line - 1:
            return
        ok = both(pred, p.high if up else p.low)
        to = p.up if up else p.down
        slot = self.slot(kind if up else kind + 1, step)
        self.send(ok, lambda: self.copy(src(), self.block(a, b, t), slot, to()))

    def receive(self, k, kind, b, t, spread, up):
        p = self.p
        chunk = p.a - k if up else p.a + k
        pred = p.a >= k if up else p.a + k <= p.line - 1
        src = lambda: self.block(chunk, b, t)
        self.wait(pred, src, self.slot(kind if up else kind + 1, k), p.pair())
        self.pass_line(pred, chunk, k + 1, up, src, kind, b, t)
        if spread:
            self.spread(pred, chunk, src)

    def settle(self, chunks):
        p = self.p
        for pred, a in chunks:
            self.wait(pred, lambda a=a: self.block(a, 1 - p.b, p.t), self.slot(2, a), p.pair())
            self.wait(pred, lambda a=a: self.block(a, p.b, p.others[2]), self.slot(3, a), p.pair())

    def cross(self, chunks):
        p, t2 = self.p, self.p.others[2]
        for pred, a in chunks:
            self.settle([(pred, a)])
            one = lambda a=a: self.block(a, 1 - p.b, p.t, 0, self.cut)
            two = lambda a=a: self.block(a, p.b, t2, self.cut, self.n)
            if self.cut > 0:
                self.send(pred, lambda a=a, one=one: self.copy(one(), one(), self.slot(4, a), p.peer(2)))
            if self.cut < self.n:
                self.send(pred, lambda a=a, two=two: self.copy(two(), two(), self.slot(5, a), p.pair()))

    def planes(self, far):
        p = self.p
        t, t2 = (p.others[1], p.others[3]) if far else (p.t, p.others[2])
        return ((p.b, t), (1 - p.b, t), (p.b, t2), (1 - p.b, t2))

    def core(self, which):
        for j in which:
            b, t = self.planes(False)[j]
            src = lambda b=b, t=t: self.plane(b, t)
            self.send(None, lambda j=j, src=src: self.copy(src(), src(), self.slot(6, j), self.p.peer(1)))

    def landed(self, chunks):
        p, t2 = self.p, self.p.others[2]
        for pred, a in chunks:
            if self.cut > 0:
                self.wait(pred, lambda a=a: self.block(a, 1 - p.b, t2, 0, self.cut), self.slot(4, a), p.pair())
            if self.cut < self.n:
                self.wait(pred, lambda a=a: self.block(a, 1 - p.b, t2, self.cut, self.n), self.slot(5, a), p.pair())

    def arrive(self):
        for j, (b, t) in enumerate(self.planes(True)):
            self.wait(None, lambda b=b, t=t: self.plane(b, t), self.slot(6, j), self.p.pair())


GATHER_CUTS = (256, 0, 0, 0, 0, 0)
BY_LINE = (False, True, True, True, True, True)
CUTS = (0, 128, 128, 256, 128, 128, 256)


def slots_of(line):
    return 6 * line + 6


def add_into(dst, *others):
    rows = dst.shape[0]
    step = min(rows, 32)

    def body(i, _):
        at = pl.ds(pl.multiple_of(i * step, step), step)
        total = dst[at, :]
        for other in others:
            total = total + other[at, :]
        dst[at, :] = total
        return 0

    lax.fori_loop(0, rows // step, body, 0)


def block_of(place, q):
    y, c = place.t // 2, lax.rem(place.t, 2)
    return lax.rem(y + 1 + q, 2) * 2 + lax.rem(c + 1 - q // 2, 2)


class Scatter(Script):
    def __init__(
        self, place, ssem, rsem, far, met, acc, out, bufs, base, cut,
        before_far=None, before_cross=None, before_line=None, release=None,
    ):
        super().__init__(ssem, rsem)
        self.p = place
        self.acc, self.out = acc, out
        self.rdx, self.rdy, self.rx, self.ry, self.near = bufs
        self.n = out.shape[1]
        self.base, self.cut = base, cut
        self.own = lambda *at: acc.at[(1, at[0], place.b) + at[1:]]
        self.by_pair = lambda *at: acc.at[(1, at[0], 1 - place.b) + at[1:]]
        self.by_y = lambda *at: acc.at[(0, at[0], place.b) + at[1:]]
        self.by_both = lambda *at: acc.at[(0, at[0], 1 - place.b) + at[1:]]
        if far is not None:
            for i in range(2):
                self.step()
                if i == 0 and before_far is not None:
                    before_far(self)
                self.send(None, lambda i=i: self.copy(far(i), met.at[i], base + i, place.peer(1)))
            for i in range(2):
                self.step()
                self.wait(None, lambda i=i: met.at[i], base + i, place.pair())
        every, first, late = slice(None), pl.ds(0, cut), pl.ds(cut, self.n - cut)
        pair, y = place.pair(), place.peer(2)
        lines = range(place.line)

        def give(src, dst, slot, device):
            self.send(None, lambda: self.copy(src(), dst(), base + slot, device))

        def take(ref, slot):
            self.wait(None, ref, base + slot, pair)

        def add(dst, *others):
            for a in lines:
                self.do(None, lambda a=a: add_into(dst(a), *[other(a) for other in others]))

        some, rest = cut > 0, cut < self.n
        self.step()
        if before_cross is not None:
            before_cross(self)
        if some:
            give(lambda: self.by_both(every, every, first), lambda: self.rdy, 4, y)
        if rest:
            give(lambda: self.by_both(every, every, late), lambda: self.rdx, 5, pair)
        if some:
            give(lambda: self.by_y(every, every, first), lambda: self.ry.at[:, :, first], 7, y)
        self.step()
        if rest:
            give(lambda: self.by_pair(every, every, late), lambda: self.rx.at[:, :, late], 6, pair)
        self.step()
        if some:
            take(lambda: self.rdy, 4)
            add(lambda a: self.by_pair(a, every, first), lambda a: self.rdy.at[a])
            give(lambda: self.by_pair(every, every, first), lambda: self.rx.at[:, :, first], 8, pair)
        self.step()
        if rest:
            take(lambda: self.rdx, 5)
            add(lambda a: self.by_y(a, every, late), lambda a: self.rdx.at[a])
            give(lambda: self.by_y(every, every, late), lambda: self.ry.at[:, :, late], 9, y)
        self.step()
        if rest:
            take(lambda: self.rx.at[:, :, late], 6)
        if some:
            take(lambda: self.ry.at[:, :, first], 7)
            take(lambda: self.rx.at[:, :, first], 8)
        if rest:
            take(lambda: self.ry.at[:, :, late], 9)
        if before_line is not None:
            before_line(self)
        for pred, chunk in reversed(list(order(place))[1:]):
            self.do(pred, lambda chunk=chunk: add_into(self.own(chunk), self.rx.at[chunk], self.ry.at[chunk]))
            self.send(pred, lambda chunk=chunk: self.copy(
                self.own(chunk), self.near.at[place.a], base + 10 + place.a, place.at(chunk, place.b, place.t)))
        self.do(None, lambda: add_into(self.own(place.a), self.rx.at[place.a], self.ry.at[place.a]))
        self.step()
        for pred, a in list(order(place))[1:]:
            self.wait(pred, lambda a=a: self.near.at[a], base + 10 + a, pair)
        self.do(None, self.close)
        if release is not None:
            sent, self.sent = self.sent[2:], self.sent[:2]
            for pred, make in sent:
                self.do(pred, lambda make=make: make().wait_send())
            release(self)

    def close(self):
        p = self.p
        rows = self.out.shape[0]
        step = min(rows, 16)

        def body(i, _):
            at = pl.ds(pl.multiple_of(i * step, step), step)
            value = self.acc[1, p.a, p.b, at, :].astype(F32)
            for k in range(1, p.line):
                value = value + self.near[lax.rem(p.a + k, p.line), at, :].astype(F32)
            self.out[at, :] = value
            return 0

        lax.fori_loop(0, rows // step, body, 0)


def landing(line, depth, n, by_pair, by_y):
    widths = (max(by_pair, 128), max(by_y, 128), n, n, n)
    return [pltpu.VMEM((line, depth, width), BF) for width in widths]


def sums_of(line):
    return 10 + line


class Trade(Script):
    pass


def heads_forward(q, k, v, allowed, keep):
    lane = lax.broadcasted_iota(jnp.int32, k.shape, 1)
    outs = []
    for h in range(2):
        mine = (lane // HD) == h
        scores = lax.dot_general(
            jnp.where(mine, k, jnp.zeros_like(k)), q, (((1,), (1,)), ((), ())), preferred_element_type=F32
        )
        scores = jnp.where(allowed, scores, -1e30)
        expo = jnp.exp(scores - jnp.max(scores, axis=0, keepdims=True))
        share = 1.0 / jnp.sum(expo, axis=0, keepdims=True)
        expo = expo.astype(BF)
        keep(h, expo, share)
        out = lax.dot_general(v[:, h * HD : (h + 1) * HD], expo, (((0,), (0,)), ((), ())), preferred_element_type=F32)
        outs.append(out * share)
    return jnp.concatenate(outs, axis=0).T.astype(BF)


def norm_stats(values):
    row_mean = jnp.mean(values, axis=-1, keepdims=True)
    centred = values - row_mean
    variance = jnp.mean(centred * centred, axis=-1, keepdims=True)
    inv_std = lax.rsqrt(variance + 1e-05)
    return centred * inv_std, inv_std


class Schedule:
    def __init__(self, text, scripts):
        self.after = {}
        at = ("", 0)
        counts = {}
        for ch in "".join(text):
            if ch.isupper():
                at = (ch, counts.get(ch, 0))
                counts[ch] = at[1] + 1
            else:
                self.after.setdefault(at, []).extend(scripts[ch].steps.pop(0))

    def run(self, name="", i=0):
        for pred, act in self.after.pop((name, i), ()):
            when(pred, act)

    def run_at(self, name, i):
        for at in sorted(k for n, k in self.after if n == name):
            pl.when(i == at)(lambda at=at: self.run(name, at))


ORDER = (
    "0K12002020210114r002022041112042",
    "22413501210rr042LP22H104H112P4H4",
    "14310131H44221352211P5H2313H4142",
    "5PH3H312544345rG43344444O5Fd353F",
    "d55d3353333F34353ddF5Fe5Fedd5ed5",
    "555555FeF3eTuTeudueT5euTuuTvTvue",
    "vTvvTuNUoeUouvdoUvvoUoDAWqAoWqAv",
    "toqWAoqqWAWwqAWuwAqwqWAwowWEwEEq",
    "EwwtMffwvqofsfwsf",
)


def heads_backward(q, k, v, o, do, expo, shares):
    lane = lax.broadcasted_iota(jnp.int32, k.shape, 1)
    first = lane < HD
    column = shares.T
    do = (do.astype(F32) * jnp.where(first, column[:, :1], column[:, 1:2])).astype(BF)
    product = do.astype(F32) * o.astype(F32)
    zero = jnp.zeros_like(k)
    dq_t, dk, dv = [], [], []
    for h in range(2):
        mine = (lane // HD) == h
        inner = jnp.sum(jnp.where(mine, product, 0.0), axis=1, keepdims=True).T
        dprobs = lax.dot_general(
            jnp.where(mine, v, zero), do, (((1,), (1,)), ((), ())), preferred_element_type=F32
        )
        got = expo[h]
        dscores = (got.astype(F32) * (dprobs - inner)).astype(BF)
        dv.append(jnp.dot(got, do, preferred_element_type=F32))
        dk.append(jnp.dot(dscores, q, preferred_element_type=F32))
        dq_t.append(
            lax.dot_general(k[:, h * HD : (h + 1) * HD], dscores, (((0,), (0,)), ((), ())), preferred_element_type=F32)
        )
    return (
        (jnp.concatenate(dq_t, axis=0).T * HD ** (-0.5)).astype(BF),
        jnp.where(first, dk[0], dk[1]).astype(BF),
        jnp.where(first, dv[0], dv[1]).astype(BF),
    )


def norm_back(upstream, unit, inv_std, gain):
    scaled = upstream * gain
    inner_mean = jnp.mean(scaled, axis=-1, keepdims=True)
    cross_mean = jnp.mean(scaled * unit, axis=-1, keepdims=True)
    return inv_std * (scaled - inner_mean - unit * cross_mean)


def layer_kernel(line, *refs):
    toks, grads, w1 = refs[0], refs[1], refs[3]
    given, held = refs[2:3] + refs[4:15], refs[-18:-6]
    raw_q, raw_o, raw_2, marks, b_fc1, b_qv = held[:6]
    vectors = held[6:]
    lo, gtok = refs[19:21]
    wanted, made = refs[15:19] + refs[21:22], refs[-6:-1]
    sq, so, s1, s2, sums = made
    io_sem = refs[-1]
    refs = refs[:-18]
    takes = [pltpu.make_async_copy(src, dst, io_sem.at[i]) for i, (src, dst) in enumerate(zip(given, held))]
    for c in takes:
        c.start()
    xin, gin, fq, fo, f1, f2, qkv_kept, probs, o_kept, x1_kept, h1_kept, h2_kept, act, slope = refs[22:36]
    big1, met1, bigo, meto, acc2, dqkv = refs[36:42]
    bufs = [refs[42 + 5 * i : 47 + 5 * i] for i in range(5)]
    g, dh2, g1b, low, here, cold, colx, coly, far_sums = refs[67:76]
    sml, small, wq, wo, w2, marked, vecs, masks, shares, h2t, lsem, ssem, rsem, free = refs[76:]
    place = Place(line)
    rows, width = g.shape
    part = rows // 4
    n1, no, nq = s1.shape[1], so.shape[1], sq.shape[1]
    local = no
    pairs = width // 128
    half_block = n1 // TILE
    tiles = 4 * half_block
    block_shape = big1.shape[1:4]
    greet(place, whole_line=True)

    per = slots_of(line)
    part_of = lambda ref, h: ref.at[:, pl.ds(h * TILE, TILE)]
    pieces = [(wq, fq, 0), (wo, fo, 0)]
    for h in range(half_block):
        pieces += [(part_of(w1, h), f1, h * TILE), (part_of(w2, h), f2, h * TILE)]
    gathers = [
        Gather(place, ssem, rsem, lsem.at[i], shard, whole, i * per, GATHER_CUTS[i], BY_LINE[i], first)
        for i, (shard, whole, first) in enumerate(pieces)
    ]
    rows_at = len(pieces) * per
    rows_sem = len(pieces)
    trade = Trade(ssem, rsem)
    slot_of = lambda j, k: rows_at + j * 4 + k
    pairs_of_rows = ((toks, xin), (grads, gin))
    mine = [pltpu.make_async_copy(src.at[place.t], dst.at[0], lsem.at[rows_sem + j]) for j, (src, dst) in enumerate(pairs_of_rows)]
    mine.append(pltpu.make_async_copy(small, sml.at[place.t], lsem.at[rows_sem + 2]))
    for j, (src, dst) in enumerate(pairs_of_rows):
        trade.step()
        trade.do(None, mine[j].start)
        for k in (2, 3, 1):
            trade.send(None, lambda src=src, dst=dst, j=j, k=k: trade.copy(
                src.at[place.others[k]], dst.at[k], slot_of(j, k), place.peer(k)))
        if j == 0:
            trade.do(None, mine[2].start)
            for k in (2, 3, 1):
                trade.send(None, lambda k=k: trade.copy(small, sml.at[place.t], slot_of(2, k), place.peer(k)))
    for j, (src, dst) in enumerate(pairs_of_rows):
        trade.step()
        trade.do(None, mine[j].wait)
        for k in (2, 3, 1):
            trade.wait(None, lambda dst=dst, k=k: dst.at[k], slot_of(j, k), place.pair())
        if j == 0:
            trade.do(None, mine[2].wait)
            for k in (2, 3, 1):
                trade.wait(None, lambda k=k: sml.at[place.others[k]], slot_of(2, k), place.pair())

    def tell(i, device):
        pl.semaphore_signal(free.at[i], inc=1, device_id=device, device_id_type=MESH)

    def hear(i):
        pl.semaphore_wait(free.at[i], 1)

    pair_at = lambda h: 4 + 2 * h
    line_at = lambda h: 8 + line * h

    def release(h):
        def add(script):
            script.do(None, lambda: tell(pair_at(h), place.pair()))
            script.do(None, lambda: tell(pair_at(h) + 1, place.peer(2)))
            for k in range(1, line):
                to = place.at(lax.rem(place.a + k, line), place.b, place.t)
                script.do(None, lambda to=to: tell(line_at(h) + place.a, to))

        return add

    def before_far(i):
        return lambda script: script.do(None, lambda: hear(i))

    def before_cross(h):
        def add(script):
            script.do(None, lambda: hear(pair_at(h)))
            script.do(None, lambda: hear(pair_at(h) + 1))

        return add

    def before_line(h):
        def add(script):
            for k in range(1, line):
                script.do(None, lambda k=k: hear(line_at(h) + lax.rem(place.a + k, line)))

        return add

    base = rows_at + 12
    each = sums_of(line)
    nh = nq // 2
    two = lambda ref: ref.at[pl.ds(2, 2)]
    last = lambda ref, cols: ref.at[:, :, :, :, cols]
    scatter = lambda *args, **more: Scatter(place, ssem, rsem, *args, **more)
    sum_u, sum_d, sum_q = [], [], []
    for h in range(2):
        cols = pl.ds(h * TILE, TILE)
        cols_q = pl.ds(h * TILE, nh)
        cq, cu, cd = CUTS[h], CUTS[3 + h], CUTS[5 + h]
        rdx, rdy, rx, ry, near = bufs[3 + h]
        sum_u.append(scatter(
            lambda i, cols=cols: big1.at[i, :, :, :, cols], last(met1, cols), last(two(big1), cols), part_of(s1, h),
            bufs[1 + h], base + (1 + h) * each, cu, before_far=before_far(2 + h),
        ))
        sum_d.append(scatter(
            lambda i, cols=cols: big1.at[i, :, :, :, cols], last(met1, cols), last(acc2, cols), part_of(s2, h),
            (rdx.at[:, :, pl.ds(0, TILE - cd)], rdy.at[:, :, pl.ds(0, cd)], rx, ry, near),
            base + (3 + h) * each, cd, release=release(h),
        ))
        sum_q.append(scatter(
            lambda i, cols=cols_q: big1.at[i, :, :, :, cols], last(met1, cols_q), last(acc2, cols_q),
            sq.at[:, pl.ds(h * nh, nh)],
            (
                rdx.at[:, :, pl.ds(0, nh - cq)],
                rdy.at[:, :, pl.ds(0, cq)] if cq > 0 else rdy,
                *[ref.at[:, :, pl.ds(0, nh)] for ref in (rx, ry, near)],
            ),
            base + (5 + h) * each, cq,
            before_far=before_far(h), before_cross=before_cross(h), before_line=before_line(h),
        ))
    sum_o = scatter(lambda i: bigo.at[i], meto, two(bigo), so, bufs[0], base, CUTS[2])

    def rows_home(src, dst, first, sem):
        home = Trade(ssem, rsem)
        stay = pltpu.make_async_copy(src.at[pl.ds(0, part)], dst.at[place.t], sem)
        home.step()
        home.do(None, stay.start)
        for k in (2, 3, 1):
            home.send(None, lambda k=k: home.copy(
                src.at[pl.ds(k * part, part)], dst.at[place.t], first + k, place.peer(k)))
        home.step()
        home.do(None, stay.wait)
        for k in (2, 3, 1):
            home.wait(None, lambda k=k: dst.at[place.others[k]], first + k, place.pair())
        return home

    base = base + 7 * each
    token_rows = rows_home(low, gtok, base, lsem.at[rows_sem + 3])
    out_rows = rows_home(g, lo, base + 4, lsem.at[rows_sem + 4])

    base = base + 8
    few = Trade(ssem, rsem)
    hops = ((cold, place.peer(1)), (colx, place.pair()), (coly, place.peer(2)))

    def fold(i, land):
        here[i + 1] = here[i] + land[...]

    few.step()
    for i, (land, device) in enumerate(hops):
        few.send(None, lambda i=i, land=land, device=device: few.copy(here.at[i], land, base + i, device))
        few.step()
        few.wait(None, lambda land=land: land, base + i, place.pair())
        few.do(None, lambda i=i, land=land: fold(i, land))
    for k in range(1, line):
        far = lax.rem(place.a + k, line)
        few.send(None, lambda far=far, k=k: few.copy(
            here.at[3], far_sums.at[k], base + 3 + k, place.at(far, place.b, place.t)))
    few.step()
    for k in range(1, line):
        few.wait(None, lambda k=k: far_sums.at[k], base + 3 + k, place.pair())

    scripts = {str(i): w for i, w in enumerate(gathers)}
    scripts.update(
        {
            "r": trade, "q": sum_q[0], "w": sum_q[1], "o": sum_o, "u": sum_u[0], "v": sum_u[1], "d": sum_d[0],
            "e": sum_d[1], "s": token_rows, "t": out_rows, "f": few,
        }
    )
    plan = Schedule(ORDER, scripts)

    def tile_of(j):
        h, q = j // 4, lax.rem(j, 4)
        block = block_of(place, q)
        at = pl.ds(pl.multiple_of(h * TILE, TILE), TILE)
        return q, block, at, pl.ds(pl.multiple_of(block * n1 + h * TILE, TILE), TILE)

    def some(count, body, unroll=1):
        lax.fori_loop(0, count, lambda i, _: (body(i), 0)[1], 0, unroll=unroll)

    def by_rows(body):
        some(rows // ROWS, lambda i: body(i, pl.ds(pl.multiple_of(i * ROWS, ROWS), ROWS)), UNROLL)

    def fetch_rows(src, dst, sem):
        copies = [pltpu.make_async_copy(src.at[k], dst.at[pl.ds(k * part, part)], sem.at[k]) for k in range(4)]
        for c in copies:
            c.start()
        for c in copies:
            c.wait()

    for c in takes:
        c.wait()
    small[...] = jnp.zeros_like(small)
    small[0:1, :] = b_fc1[...].reshape(1, -1)
    small[1:2, :local] = b_qv[0:1, :]
    small[1:2, local : 2 * local] = b_qv[1:2, :]
    for h in range(2):
        for j in range(3):
            wq[:, (h * 3 + j) * 128 : (h * 3 + j + 1) * 128] = raw_q[j, :, h * 128 : (h + 1) * 128]
    plan.run()
    wo[...] = raw_o[...].T
    w2[...] = raw_2[...].T
    plan.run("K")
    for i, vector in enumerate(vectors):
        vecs[i : i + 1, :] = vector[...].reshape(1, -1)
    mark = marks[pl.ds(place.t, 1), :].astype(F32)
    marked[...] = jnp.broadcast_to(mark, (128, rows)).T
    for k in range(4):
        at = pl.ds(k * part, part)
        masks[0, at, :] = marked[pl.ds(pl.multiple_of(place.others[k] * part, 32), part), :]
    masks[1] = jnp.where(jnp.max(mark, axis=1, keepdims=True) > 0, masks[0], 1.0)
    here[0] = jnp.zeros_like(here[0])

    def heads_part(h1, wqv, pbuf, sem):
        fetch_rows(xin, low, sem)

        def first_norm(i, at):
            x = low[at, :].astype(F32)
            unit, _inv = norm_stats(x)
            h1[at, :] = (unit * vecs[0:1, :] + vecs[1:2, :]).astype(BF)
            real = masks[0, at, :1]
            here[0, 0:1, :] += jnp.sum(x * x * real, axis=0, keepdims=True)
            here[0, 2:3, :] += jnp.broadcast_to(jnp.sum(real, axis=0, keepdims=True), (1, width))

        by_rows(first_norm)
        save_h1 = pltpu.make_async_copy(h1, h1_kept, sem.at[4])
        save_h1.start()
        plan.run("L")
        block_at = lambda i: block_of(place, 3 - i)
        fetch = lambda i, slot: pltpu.make_async_copy(
            fq.at[:, :, :, pl.ds(pl.multiple_of(block_at(i) * nq, 128), nq)], wqv.at[slot], sem.at[5 + slot])
        fetch(0, 0).start()
        allowed = masks[1, :, :1] > 0
        save = lambda i, h: pltpu.make_async_copy(pbuf.at[h], probs.at[block_at(i) * 2 + h], sem.at[8 + h])

        def heads_block(i):
            block, slot = block_at(i), lax.rem(i, 2)
            fetch(i, slot).wait()
            got = jnp.dot(h1[...], wqv[slot].reshape(width, nq), preferred_element_type=F32)
            bias = sml[pl.ds(block, 1), 1, : 2 * local]
            for h in range(2):
                q, k, v = (slice((h * 3 + j) * 128, (h * 3 + j + 1) * 128) for j in range(3))
                bq, bv = bias[:, h * 128 : (h + 1) * 128], bias[:, local + h * 128 : local + (h + 1) * 128]
                dqkv[block, :, q] = (got[:, q] + bq).astype(BF) * jnp.asarray(HD ** (-0.5), BF)
                dqkv[block, :, k] = got[:, k].astype(BF)
                dqkv[block, :, v] = (got[:, v] + bv).astype(BF)
            plan.run_at("P", i)

            def pair_step(h):
                pl.when(i >= 1)(lambda: save(i - 1, h).wait())

                def keep(head, got, share):
                    pbuf[h, head] = got
                    shares[block * 2 + h, head : head + 1, :] = share

                cols = [pl.ds(pl.multiple_of((h * 3 + j) * 128, 128), 128) for j in range(3)]
                q, k, v = (dqkv[block, :, c] for c in cols)
                at = pl.ds(pl.multiple_of(block * local + h * 128, 128), 128)
                g1b[:, at] = heads_forward(q, k, v, allowed, keep)
                save(i, h).start()
                plan.run_at("H", 2 * i + h)
                pl.when(jnp.logical_and(h == 0, i < 3))(lambda: fetch(i + 1, 1 - slot).start())

            some(2, pair_step)

        some(4, heads_block)
        save_qkv = pltpu.make_async_copy(dqkv, qkv_kept, sem.at[7])
        save_qkv.start()
        for wait in (save_h1, save_qkv, save(3, 0), save(3, 1)):
            wait.wait()

    pl.run_scoped(
        heads_part,
        pltpu.VMEM((rows, width), BF),
        pltpu.VMEM((2,) + block_shape + (nq,), BF),
        pltpu.VMEM((2, 2, rows, rows), BF),
        pltpu.SemaphoreType.DMA((10,)),
    )

    def hidden_part(wov, h2, gt, w1t, actb, slopeb, sem):
        save_o = pltpu.make_async_copy(g1b, o_kept, sem.at[4])
        save_o.start()
        fetch_o = pltpu.make_async_copy(fo, wov, sem.at[5])
        fetch_o.start()
        fetch_rows(gin, g, sem)

        def mask_rows(i, at):
            masked = g[at, :].astype(F32) * masks[0, at, :1]
            here[0, 3:4, :] += jnp.sum(masked, axis=0, keepdims=True)
            g[at, :] = masked.astype(BF)

        by_rows(mask_rows)
        gt[...] = g[...].T
        plan.run("G")
        fetch_o.wait()
        half = rows // 2

        def join(i):
            at = pl.ds(pl.multiple_of(i * half, 64), half)
            branch = lax.dot_general(
                g1b[at, :], wov[...].reshape(width, width), (((1,), (1,)), ((), ())), preferred_element_type=F32
            ) + vecs[4:5, :]
            here[0, 1:2, :] += jnp.sum(branch * branch * masks[0, at, :1], axis=0, keepdims=True)
            middle = low[at, :].astype(F32) + branch
            dh2[at, :] = middle
            unit, _inv = norm_stats(middle)
            h2[at, :] = (unit * vecs[2:3, :] + vecs[3:4, :]).astype(BF)

        some(2, join)
        save_x1 = pltpu.make_async_copy(dh2, x1_kept, sem.at[6])
        save_h2 = pltpu.make_async_copy(h2, h2_kept, sem.at[7])
        save_x1.start()
        save_h2.start()
        plan.run("O")
        fetch = lambda j, slot: pltpu.make_async_copy(f1.at[:, :, :, tile_of(j)[3]], w1t.at[slot], sem.at[8 + slot])
        fetch(0, 0).start()

        def saves(j, slot):
            cols = tile_of(j)[3]
            return (
                pltpu.make_async_copy(actb.at[slot], act.at[:, cols], sem.at[10 + slot]),
                pltpu.make_async_copy(slopeb.at[slot], slope.at[:, cols], sem.at[12 + slot]),
            )

        def hidden_step(j):
            slot = lax.rem(j, 2)
            pl.when(j + 1 < tiles)(lambda: fetch(j + 1, 1 - slot).start())

            @pl.when(j >= 2)
            def _():
                for save in saves(j - 2, slot):
                    save.wait()

            q, block, at, cols = tile_of(j)
            fetch(j, slot).wait()
            hidden = jnp.dot(h2[...], w1t[slot].reshape(width, TILE), preferred_element_type=F32) + sml[block, 0:1, at]
            gate = jax.nn.sigmoid(1.702 * hidden)
            actb[slot] = (hidden * gate).astype(BF)
            slopeb[slot] = (gate + 1.702 * hidden * gate * (1.0 - gate)).astype(BF)
            for save in saves(j, slot):
                save.start()
            product = jnp.dot(gt[...], actb[slot], preferred_element_type=F32).reshape(block_shape + (TILE,))

            @pl.when(q < 2)
            def _():
                big1[q, :, :, :, at] = product.astype(BF)

            @pl.when(q >= 2)
            def _():
                acc2[q - 2, :, :, :, at] = (product + met1[q - 2, :, :, :, at].astype(F32)).astype(BF)

            plan.run_at("F", j)

        some(tiles, hidden_step)
        h2t[...] = h2[...].T
        for wait in saves(tiles - 2, tiles % 2) + saves(tiles - 1, (tiles - 1) % 2) + (save_o, save_x1, save_h2):
            wait.wait()

    pl.run_scoped(
        hidden_part,
        pltpu.VMEM(fo.shape, BF),
        pltpu.VMEM((rows, width), BF),
        pltpu.VMEM((width, rows), BF),
        pltpu.VMEM((2,) + block_shape + (TILE,), BF),
        pltpu.VMEM((2, rows, TILE), BF),
        pltpu.VMEM((2, rows, TILE), BF),
        pltpu.SemaphoreType.DMA((14,)),
    )
    for h in range(2):
        tell(2 + h, place.peer(1))
        sum_d[h].wait_sent(2)

    dh2[...] = jnp.zeros_like(dh2)

    def feed_forward(ml, f1t, f2t, slopet, actt, sem):
        def fetch(j, slot):
            cols = tile_of(j)[3]
            return (
                pltpu.make_async_copy(f1.at[:, :, :, cols], f1t.at[slot], sem.at[slot]),
                pltpu.make_async_copy(f2.at[:, :, :, cols], f2t.at[slot], sem.at[2 + slot]),
                pltpu.make_async_copy(slope.at[:, cols], slopet.at[slot], sem.at[4 + slot]),
                pltpu.make_async_copy(act.at[:, cols], actt.at[slot], sem.at[7 + slot]),
            )

        ml[...] = jnp.zeros_like(ml)
        for c in fetch(0, 0):
            c.start()

        def tile(j):
            slot = lax.rem(j, 2)

            @pl.when(j + 1 < tiles)
            def _():
                for c in fetch(j + 1, 1 - slot):
                    c.start()

            for c in fetch(j, slot):
                c.wait()
            q, block, at, cols = tile_of(j)
            w2_tile = f2t[slot].reshape(width, TILE)
            du = jnp.dot(g[...], w2_tile, preferred_element_type=F32)
            du = (du * slopet[slot].astype(F32)).astype(BF)
            here[0, pl.ds(4 + block, 1), at] = jnp.sum(du.astype(F32), axis=0, keepdims=True)
            product = jnp.dot(h2t[...], du, preferred_element_type=F32).reshape(block_shape + (TILE,))

            @pl.when(q < 2)
            def _():
                big1[q, :, :, :, at] = product.astype(BF)

            @pl.when(q >= 2)
            def _():
                big1[q, :, :, :, at] = (product + met1[q - 2, :, :, :, at].astype(F32)).astype(BF)

            dh2[...] += lax.dot_general(
                du, f1t[slot].reshape(width, TILE), (((1,), (1,)), ((), ())), preferred_element_type=F32
            )
            ml[...] += lax.dot_general(actt[slot], w2_tile, (((1,), (1,)), ((), ())), preferred_element_type=F32)
            plan.run_at("T", j)

        some(tiles, tile)

    def second_norm(ml, xt, sem):
        fetch = lambda i, slot: pltpu.make_async_copy(
            x1_kept.at[pl.ds(pl.multiple_of(i * ROWS, ROWS), ROWS)], xt.at[slot], sem.at[slot])
        fetch(0, 0).start()

        def some_rows(i, at):
            slot = lax.rem(i, 2)
            pl.when(i + 1 < rows // ROWS)(lambda: fetch(i + 1, 1 - slot).start())
            fetch(i, slot).wait()
            x = xt[slot]
            unit, inv = norm_stats(x)
            up = dh2[at, :]
            here[0, 8:9, :] += jnp.sum(up * unit, axis=0, keepdims=True)
            here[0, 9:10, :] += jnp.sum(up, axis=0, keepdims=True)
            g1 = g[at, :].astype(F32) + norm_back(up, unit, inv, vecs[2:3, :])
            rounded = g1.astype(BF)
            g1b[at, :] = rounded
            here[0, 10:11, :] += jnp.sum(rounded.astype(F32), axis=0, keepdims=True)
            dh2[at, :] = g1
            m = ml[at, :] + vecs[5:6, :]
            g[at, :] = (x + m).astype(BF)
            here[0, 11:12, :] += jnp.sum(m * m * masks[0, at, :1], axis=0, keepdims=True)

        by_rows(some_rows)

    def middle(ml):
        tiles_of = lambda *shape: pltpu.VMEM((2,) + shape, BF)
        pl.run_scoped(
            functools.partial(feed_forward, ml),
            tiles_of(*block_shape, TILE),
            tiles_of(*block_shape, TILE),
            tiles_of(rows, TILE),
            tiles_of(rows, TILE),
            pltpu.SemaphoreType.DMA((9,)),
        )
        for h in range(2):
            tell(h, place.peer(1))
        pl.run_scoped(
            functools.partial(second_norm, ml), pltpu.VMEM((2, ROWS, width), F32), pltpu.SemaphoreType.DMA((2,))
        )

    pl.run_scoped(middle, pltpu.VMEM((rows, width), F32))
    plan.run("N")

    def heads(tall, o, wov, do, pt, qt, sem):
        load_o = pltpu.make_async_copy(o_kept, o, sem.at[0])
        load_w = pltpu.make_async_copy(fo, wov, sem.at[1])
        load_h = pltpu.make_async_copy(h1_kept, low, sem.at[6])
        for c in (load_o, load_w, load_h):
            c.start()

        def heads_of(i):
            return block_of(place, lax.rem(i, 4)) * 2 + i // 4

        def fetch(i, slot):
            cols = pl.ds(pl.multiple_of((i // 4) * nh, 128), nh)
            return [
                pltpu.make_async_copy(
                    qkv_kept.at[block_of(place, lax.rem(i, 4)), :, cols], qt.at[slot], sem.at[2 + slot]),
                pltpu.make_async_copy(probs.at[heads_of(i)], pt.at[slot], sem.at[4 + slot]),
            ]

        for c in fetch(0, 0):
            c.start()
        tall[...] = g1b[...].T
        load_o.wait()
        load_w.wait()

        def output_weight(q):
            cols = pl.ds(pl.multiple_of(block_of(place, q) * no, 128), no)
            product = jnp.dot(tall[...], o[:, cols], preferred_element_type=F32).reshape(bigo.shape[1:])

            @pl.when(q < 2)
            def _():
                bigo[q] = product.astype(BF)

            @pl.when(q >= 2)
            def _():
                bigo[q] = (product + meto[q - 2].astype(F32)).astype(BF)

            plan.run_at("U", q)

        some(4, output_weight)
        do[...] = jnp.dot(g1b[...], wov[...].reshape(width, width), preferred_element_type=F32).astype(BF)
        plan.run("D")
        load_h.wait()
        tall[...] = low[...].T
        for script in sum_u:
            script.wait_sent(2)

        def pair_step(i):
            slot = lax.rem(i, 2)
            h, q = i // 4, lax.rem(i, 4)

            @pl.when(i + 1 < pairs)
            def _():
                for c in fetch(i + 1, 1 - slot):
                    c.start()

            for c in fetch(i, slot):
                c.wait()
            cols = pl.ds(pl.multiple_of(heads_of(i) * 128, 128), 128)
            got = heads_backward(
                qt[slot, :, :128], qt[slot, :, 128:256], qt[slot, :, 256:], o[:, cols], do[:, cols], pt[slot],
                shares[heads_of(i)],
            )
            mine = pl.ds(pl.multiple_of(h * nh, 128), nh)
            dqkv[q, :, mine] = jnp.concatenate(got, axis=1)
            plan.run_at("A", i)
            block = block_of(place, q)
            got = dqkv[q, :, mine]
            product = jnp.dot(tall[...], got, preferred_element_type=F32).reshape(block_shape + (nh,))
            total = jnp.sum(got.astype(F32), axis=0, keepdims=True)
            at = pl.ds(pl.multiple_of(block * local + h * 128, 128), 128)
            here[0, 14:15, at] = total[:, :128]
            here[0, 15:16, at] = total[:, 256:]
            to = pl.ds(pl.multiple_of(h * TILE, 128), nh)

            @pl.when(q < 2)
            def _():
                big1[q, :, :, :, to] = product.astype(BF)

            @pl.when(q >= 2)
            def _():
                acc2[q - 2, :, :, :, to] = (product + met1[q - 2, :, :, :, to].astype(F32)).astype(BF)

            plan.run_at("W", i)

        some(pairs, pair_step)

    pl.run_scoped(
        heads,
        pltpu.VMEM((width, rows), BF),
        pltpu.VMEM((rows, width), BF),
        pltpu.VMEM(fo.shape, BF),
        pltpu.VMEM((rows, width), BF),
        pltpu.VMEM((2, 2, rows, rows), BF),
        pltpu.VMEM((2, rows, nh), BF),
        pltpu.SemaphoreType.DMA((7,)),
    )

    def last_part(dh1, wqv, x, sem):
        fetch_w = lambda q, slot: pltpu.make_async_copy(
            fq.at[:, :, :, pl.ds(pl.multiple_of(block_of(place, q) * nq, 128), nq)], wqv.at[slot], sem.at[slot])
        load_x = [pltpu.make_async_copy(xin.at[k], x.at[pl.ds(k * part, part)], sem.at[2 + k]) for k in range(4)]
        fetch_w(0, 0).start()
        for c in load_x:
            c.start()
        dh1[...] = jnp.zeros_like(dh1)

        def back(q):
            slot = lax.rem(q, 2)
            pl.when(q < 3)(lambda: fetch_w(q + 1, 1 - slot).start())
            fetch_w(q, slot).wait()
            dh1[...] += lax.dot_general(
                dqkv[q], wqv[slot].reshape(width, nq), (((1,), (1,)), ((), ())), preferred_element_type=F32
            )
            plan.run_at("E", q)

        some(4, back)
        for c in load_x:
            c.wait()

        def some_rows(i, at):
            unit, inv = norm_stats(x[at, :].astype(F32))
            up = dh1[at, :]
            here[0, 12:13, :] += jnp.sum(up * unit, axis=0, keepdims=True)
            here[0, 13:14, :] += jnp.sum(up, axis=0, keepdims=True)
            low[at, :] = (dh2[at, :] + norm_back(up, unit, inv, vecs[0:1, :])).astype(BF)

        by_rows(some_rows)
        plan.run("M")

    pl.run_scoped(
        last_part,
        pltpu.VMEM((rows, width), F32),
        pltpu.VMEM((2,) + block_shape + (nq,), BF),
        pltpu.VMEM((rows, width), BF),
        pltpu.SemaphoreType.DMA((6,)),
    )
    total = here[3]
    for k in range(1, line):
        total = total + far_sums[k]
    sums[...] = total
    gives = [pltpu.make_async_copy(src, dst, io_sem.at[i]) for i, (src, dst) in enumerate(zip(made, wanted))]
    for c in gives:
        c.start()
    for c in gives:
        c.wait()
    for script in scripts.values():
        script.finish()


def layer(line, toks, grads, w_qkv, w1, w_out, w_fc2, marks, b_fc1, b_qv, *vectors):
    images, part, width = toks.shape
    rows = 4 * part
    depth, n1 = w1.shape
    no, n2, nq = w_out.shape[0], w_fc2.shape[0], 3 * w_qkv.shape[2]
    hidden = 4 * n1
    hbm = pl.BlockSpec(memory_space=pl.ANY)
    sds = jax.ShapeDtypeStruct
    block = lambda count, n: pltpu.VMEM((count, line, 2, depth, n), BF)
    few = (16, width)
    count = 6 * slots_of(line) + 12 + 7 * sums_of(line) + 8 + 3 + line
    kept = [
        sds((4, part, width), BF),
        sds((4, part, width), BF),
        *[sds((line, 2, depth, 4 * n), BF) for n in (nq, no, n1, n2)],
        sds((4, rows, nq), BF),
        sds((width // 128, 2, rows, rows), BF),
        sds((rows, width), BF),
        sds((rows, width), F32),
        sds((rows, width), BF),
        sds((rows, width), BF),
        sds((rows, hidden), BF),
        sds((rows, hidden), BF),
    ]
    return pl.pallas_call(
        functools.partial(layer_kernel, line),
        out_shape=[
            sds((depth, nq), F32),
            sds((depth, no), F32),
            sds((depth, n1), F32),
            sds((depth, n2), F32),
            sds((4, part, width), BF),
            sds((4, part, width), BF),
            sds(few, F32),
            *kept,
        ],
        in_specs=[hbm] * 15,
        out_specs=[hbm] * (7 + len(kept)),
        scratch_shapes=[
            block(4, n1),
            block(2, n1),
            block(4, no),
            block(2, no),
            block(2, n2),
            pltpu.VMEM((4, rows, nq), BF),
            *landing(line, depth, no, no - CUTS[2], CUTS[2]),
            *landing(line, depth, TILE, TILE - CUTS[3], CUTS[3]),
            *landing(line, depth, TILE, TILE - CUTS[4], CUTS[4]),
            *landing(line, depth, TILE, max(TILE - CUTS[5], nq // 2 - CUTS[0]), max(CUTS[5], CUTS[0])),
            *landing(line, depth, TILE, max(TILE - CUTS[6], nq // 2 - CUTS[1]), max(CUTS[6], CUTS[1])),
            pltpu.VMEM((rows, width), BF),
            pltpu.VMEM((rows, width), F32),
            pltpu.VMEM((rows, width), BF),
            pltpu.VMEM((rows, width), BF),
            pltpu.VMEM((4,) + few, F32),
            pltpu.VMEM(few, F32),
            pltpu.VMEM(few, F32),
            pltpu.VMEM(few, F32),
            pltpu.VMEM((line,) + few, F32),
            pltpu.VMEM((4, 8, n1), F32),
            pltpu.VMEM((8, n1), F32),
            pltpu.VMEM((depth, nq), BF),
            pltpu.VMEM((depth, no), BF),
            pltpu.VMEM((depth, n2), BF),
            pltpu.VMEM((rows, 128), F32),
            pltpu.VMEM((8, width), F32),
            pltpu.VMEM((2, rows, 128), F32),
            pltpu.VMEM((width // 128, 2, rows), F32),
            pltpu.VMEM((width, rows), BF),
            pltpu.SemaphoreType.DMA((11,)),
            pltpu.SemaphoreType.DMA((count,)),
            pltpu.SemaphoreType.DMA((count,)),
            pltpu.SemaphoreType.REGULAR((8 + 2 * line,)),
            *[pltpu.VMEM(ref.shape, ref.dtype) for ref in (w_qkv, w_out, w_fc2, marks, b_fc1, b_qv, *vectors)],
            pltpu.VMEM((depth, nq), F32),
            pltpu.VMEM((depth, no), F32),
            pltpu.VMEM((depth, n1), F32),
            pltpu.VMEM((depth, n2), F32),
            pltpu.VMEM(few, F32),
            pltpu.SemaphoreType.DMA((12,)),
        ],
        compiler_params=pltpu.CompilerParams(collective_id=0, has_side_effects=True, vmem_limit_bytes=63 * MIB),
        name="layer",
    )(toks, grads, w_qkv, w1, w_out, w_fc2, marks, b_fc1, b_qv, *vectors)[:7]


def finish_kernel(*refs):
    sq, so, s1, s2, lo, gtok, sums = refs[:7]
    outs, rms = refs[7:21], refs[21]
    vq, vo, v1, v2, vs, rows = refs[22:28]
    made, (in_sem, out_sem) = refs[28:39], refs[39:]
    loads = [
        pltpu.make_async_copy(src, dst, in_sem.at[i])
        for i, (src, dst) in enumerate(
            ((sums, vs), (sq, vq), (so, vo), (s2, v2), (s1, v1), (lo, rows.at[0]), (gtok, rows.at[1]))
        )
    ]
    for c in loads:
        c.start()
    saves = []

    def save(src, dst):
        copy = pltpu.make_async_copy(src, dst, out_sem.at[len(saves)])
        copy.start()
        saves.append(copy)

    lo_out, gtok_out, g_ln1, b_ln1, q_out, qv_out, o_out, b_out, g_ln2, b_ln2, one, b_fc1, two, b_fc2 = outs
    tq, tqv, to, t2 = made[:4]
    vectors = made[4:]
    t = lax.axis_index("tensor")
    local = tqv.shape[1]
    loads[0].wait()
    for ref, dst, at in zip(vectors, (g_ln1, b_ln1, b_out, g_ln2, b_ln2, b_fc2), (12, 13, 10, 8, 9, 3)):
        ref[...] = vs[at, :]
        save(ref, dst)
    vectors[6][...] = vs[pl.ds(4 + t, 1), :].reshape(-1)
    save(vectors[6], b_fc1)
    at = pl.ds(pl.multiple_of(t * local, 128), local)
    tqv[0:1, :] = vs[14:15, at]
    tqv[1:2, :] = vs[15:16, at]
    save(tqv, qv_out)
    count = vs[2:3, 0:1] * vs.shape[1]
    for i, at in enumerate((0, 1, 11)):
        rms[i] = jnp.max(jnp.sqrt(jnp.sum(vs[at : at + 1, :], axis=1, keepdims=True) / count))
    loads[1].wait()
    for h in range(2):
        for j in range(3):
            tq[j, :, h * 128 : (h + 1) * 128] = vq[:, (h * 3 + j) * 128 : (h * 3 + j + 1) * 128]
    save(tq, q_out)
    loads[2].wait()
    to[...] = vo[...].T
    save(to, o_out)
    loads[3].wait()
    t2[...] = v2[...].T
    save(t2, two)
    for c, src, dst in ((loads[4], v1, one), (loads[5], rows.at[0], lo_out), (loads[6], rows.at[1], gtok_out)):
        c.wait()
        save(src, dst)
    for c in saves:
        c.wait()


def finish(sum_q, sum_o, sum_1, sum_2, layer_out, grad_tokens, sums):
    width = sums.shape[1]
    depth, no = sum_o.shape
    n1, n2 = sum_1.shape[1], sum_2.shape[1]
    sds = jax.ShapeDtypeStruct
    row = sds((width,), F32)
    hbm = pl.BlockSpec(memory_space=pl.ANY)
    vmem = lambda ref: pltpu.VMEM(ref.shape, ref.dtype)
    q, qv, o, two = sds((3, depth, no), F32), sds((2, no), F32), sds((no, depth), F32), sds((n2, depth), F32)
    b_fc1 = sds((n1,), F32)
    lo, gtok, g_ln1, b_ln1, q, b_qv, o, b_out, g_ln2, b_ln2, one, b_fc1, two, b_fc2, rms = pl.pallas_call(
        finish_kernel,
        out_shape=[
            sds(layer_out.shape, BF), sds(grad_tokens.shape, BF), row, row, q, qv, o, row, row, row,
            sds(sum_1.shape, F32), b_fc1, two, row, sds((3,), F32),
        ],
        in_specs=[hbm] * 7,
        out_specs=[hbm] * 14 + [pl.BlockSpec(memory_space=pltpu.SMEM)],
        scratch_shapes=[
            *[vmem(ref) for ref in (sum_q, sum_o, sum_1, sum_2, sums)],
            pltpu.VMEM((2,) + layer_out.shape, BF),
            *[vmem(ref) for ref in (q, qv, o, two) + (row,) * 6 + (b_fc1,)],
            pltpu.SemaphoreType.DMA((7,)),
            pltpu.SemaphoreType.DMA((14,)),
        ],
        compiler_params=pltpu.CompilerParams(vmem_limit_bytes=63 * MIB),
        name="finish",
    )(sum_q, sum_o, sum_1, sum_2, layer_out, grad_tokens, sums)
    return (
        lo, gtok, g_ln1, b_ln1, q.transpose(1, 0, 2), b_qv, o, b_out, g_ln2, b_ln2, one, b_fc1, two, b_fc2, rms
    )


def shards(
    tokens, token_mask, out_grad, ln1_gain, ln1_bias, w_qkv, b_qv, w_out, b_out,
    ln2_gain, ln2_bias, w_fc1, b_fc1, w_fc2, b_fc2,
):
    line = lax.axis_size("dp") // 2
    sums = layer(
        line, tokens, out_grad, w_qkv.transpose(1, 0, 2), w_fc1, w_out, w_fc2, token_mask, b_fc1, b_qv,
        ln1_gain, ln1_bias, ln2_gain, ln2_bias, b_out, b_fc2,
    )
    return finish(*sums)


def solution(mesh):
    rowwise = P("dp", "tensor", None)
    placed = (
        rowwise, P("dp", None), rowwise, P(), P(), P("dp", None, "tensor"), P(None, "tensor"), P("tensor", "dp"),
        P(), P(), P(), P("dp", "tensor"), P("tensor"), P("tensor", "dp"), P(),
    )
    return jax.shard_map(
        shards,
        mesh=mesh,
        in_specs=placed,
        out_specs=(
            rowwise, rowwise, P(), P(), P("dp", None, "tensor"), P(None, "tensor"), P("tensor", "dp"), P(),
            P(), P(), P("dp", "tensor"), P("tensor"), P("tensor", "dp"), P(), P(),
        ),
        check_vma=False,
    )
```
